32 devices in a mesh: ctx: 8 (over z, y), exp: 4 (over x, core), dp: 1.
Axes of the slice: x: 2, y: 2, z: 4, core: 2. Of those that a mesh axis runs over, the one named last changes fastest.
Arguments:
- residual: bfloat16 [512, 4096], P(('dp', 'ctx', 'exp')), may hold values from -0.59765625 to 0.59765625
- encoded_query_rows: bfloat16 [512, 4096], P(('dp', 'ctx'), 'exp'), may hold values from -256 to 256
- quantized_key_rows: bfloat16 [512, 512], P(('dp', 'ctx')), may hold values from -8 to 8
- quantized_value_rows: bfloat16 [512, 512], P(('dp', 'ctx')), may hold values from -6 to 6
- key_block_exponent: int32 [8, 4], P(('dp', 'ctx')), may hold values from -2 to 1
- value_block_exponent: int32 [8, 4], P(('dp', 'ctx')), may hold values from -2 to 1
- block_order: int32 [8], replicated, may hold values from 0 to 7, each once
- out_weight: bfloat16 [4096, 4096], P('exp', 'ctx'), may hold values from -0.09375 to 0.09375
- norm_gain: float32 [4096], replicated, may hold values from 0.1 to 1.9
- expert_ids: int32 [512, 8], P(('dp', 'ctx', 'exp')), may hold values from 0 to 15, all different within a row; in each aligned block of 16 rows (0 to 15, 16 to 31, ...) at most 12 rows name the same one
- route_weight: float32 [512, 8], P(('dp', 'ctx', 'exp')), may hold values from 0.05 to 0.25
- gate_weight: bfloat16 [32, 4096, 384], P(('ctx', 'exp')), may hold values from -0.09375 to 0.09375
- gate_scale: int32 [32, 32, 3], P(('ctx', 'exp')), may hold values from -1 to 1
- up_weight: bfloat16 [32, 4096, 384], P(('ctx', 'exp')), may hold values from -0.09375 to 0.09375
- up_scale: int32 [32, 32, 3], P(('ctx', 'exp')), may hold values from -1 to 1
- down_weight: bfloat16 [32, 384, 4096], P(('ctx', 'exp')), may hold values from -0.21875 to 0.21875
- down_scale: int32 [32, 3, 32], P(('ctx', 'exp')), may hold values from -1 to 1
Outputs:
- layer_out: bfloat16 [512, 4096], P(('dp', 'ctx', 'exp'))
The draws below stay inside these ranges and needn't reach their ends.
Inputs may be any that keep to these rules, and one draw needn't show every extreme that they name: `expert_ids`: each row names 8 different experts. Among the rows of one device (16 aligned rows), no expert is named by more than 12 rows, a bound that some block reaches. `block_order`: A permutation of the ctx indices.
All inputs are finite; a program needn't handle non-finite values.
Results may differ from the reference program's by a relative error of at most 0.03.
Values may be sent and summed in bfloat16 or wider, within the bound.
No kernel may reach another device: no remote copies, remote signals or barrier semaphores. Data moves between devices by JAX's collectives and lax.ppermute only.
A program may use at most 128 MiB of HBM per device.

```python
import math
import jax
import jax.numpy as jnp
import numpy as np
from jax import lax

D = 4096
QUERY_HEADS = 32
KEY_VALUE_HEADS = 4
HEAD_SIZE = 128
FF = 768
TOP = 8
SCALE_POSITIONS = 64
WB = 128
TOK_DEV = 16
CONTEXT_SPAN = 64
SEQUENCE_TOKENS = 512
EXP = 16
CAP = 12
N_CTX = 8


def common_keys(key):
    return jnp.clip(jax.random.normal(key, (SEQUENCE_TOKENS, KEY_VALUE_HEADS * HEAD_SIZE), jnp.float32), -6.0, 6.0)


def draw_quantized_key_rows(key, part):
    start_offset = common_keys(key)
    return start_offset.astype(jnp.bfloat16)


def draw_encoded_query_rows(key, part):
    key = jax.random.fold_in(key, 7)
    first_key = jax.random.fold_in(key, 0)
    queries = jnp.clip(jax.random.normal(first_key, (SEQUENCE_TOKENS, QUERY_HEADS * HEAD_SIZE), jnp.float32), -6.0, 6.0)
    return queries.astype(jnp.bfloat16)


def place_ends(values, key, least, largest):
    shape = values.shape
    place = [jax.random.randint(jax.random.fold_in(key, axis), (), 0, shape[axis]) for axis in range(len(shape))]
    values = values.at[tuple(place)].set(least)
    longest = shape.index(max(shape))
    place[longest] = (place[longest] + 1) % shape[longest]
    return values.at[tuple(place)].set(largest)


def levels(key, shape, cuts, smallest, high):
    def one(dim, parts):
        steps = jax.random.uniform(jax.random.fold_in(jax.random.fold_in(key, 6), dim), (parts,), jnp.float32, smallest / len(cuts), high / len(cuts))
        return jnp.repeat(jnp.exp(steps), shape[dim] // parts).reshape((-1,) + (1,) * (len(shape) - dim - 1))

    level = one(*cuts[0])
    for cut in cuts[1:]:
        level = level * one(*cut)
    return level


def deal_out(key, own, number, rows, number_of, top, reach, lean):
    ranking = jax.random.permutation(key, number_of)
    heavy_load, ordinary = load_shares(number_of, rows * top, reach, lean, True), load_shares(number_of, rows * top, reach, lean, False)
    places = jnp.arange(number_of)

    def named(sizes, rotation):
        used = int((sizes > 0).sum())
        fixed = max(1, used // 4)
        shifted = fixed + (places - fixed + rotation * (used - fixed)) % max(1, number_of - fixed)
        return jnp.zeros((number_of,), jnp.int32).at[ranking[jnp.where(places < fixed, places, shifted)]].set(jnp.asarray(sizes, jnp.int32))

    sizes = jnp.where(number % 4 == 0, named(heavy_load, number // 4), named(ordinary, number - number // 4 - 1))
    mixed = jax.random.permutation(jax.random.fold_in(own, 3), number_of)
    source_of, receiver = mixed[0:number_of // 2 * 2:2], mixed[1:number_of // 2 * 2:2]
    margin = jnp.minimum(sizes[source_of] - 1, reach - sizes[receiver]) // 2
    margin = jnp.where((source_of == ranking[0]) | (receiver == ranking[0]) | (sizes[receiver] == 0), 0, jnp.maximum(margin, 0))
    shifted = jax.random.randint(jax.random.fold_in(own, 4), (number_of // 2,), 0, 1 << 20) % (margin + 1)
    sizes = sizes.at[source_of].add(-shifted).at[receiver].add(shifted)
    items = jnp.searchsorted(jnp.cumsum(sizes), jnp.arange(rows * top), side="right").astype(jnp.int32)
    listing = items.reshape(top, rows).T
    listing = listing[jax.random.permutation(jax.random.fold_in(own, 1), rows)]
    rotation = jax.random.randint(jax.random.fold_in(own, 2), (rows, 1), 0, top)
    return jnp.take_along_axis(listing, (jnp.arange(top)[None, :] + rotation) % top, axis=1)


def load_shares(amount, total, most, slope, full):
    loads = [(1 << 20) // math.isqrt(standing ** slope) + 1 for standing in range(1, amount + 1)]
    largest = most if full else min(most, max(-(-total // amount), total * loads[0] // sum(loads)))
    least = 1 if total - largest >= amount - 1 else 0
    counts, rest = [largest] + [least] * (amount - 1), total - largest - least * (amount - 1)
    while rest > 0:
        movable = [i for i in range(1, amount) if counts[i] < largest] or [i for i in range(1, amount) if counts[i] < most]
        whole, left = sum([loads[i] for i in movable]), rest
        for i in movable:
            more = min(most - counts[i], max(1, left * loads[i] // whole), rest)
            counts[i] = counts[i] + more
            rest = rest - more
    return np.array(counts)


def noise(stream_key, dims, deviation, most, cuts=(), kind=jnp.bfloat16):
    loudness = levels(stream_key, dims, cuts, -0.22, 0.18) if cuts else 1.0
    entries = jax.random.normal(stream_key, dims, jnp.float32) * deviation * loudness
    return jnp.minimum(jnp.maximum(entries, -most), most).astype(kind)


def setup_inputs(seed: int = 0, part: int = 0) -> dict:
    splits = jax.random.split(jax.random.key(seed), 18)
    own_keys = jax.random.split(jax.random.fold_in(splits[17], part), 18)
    residual = noise(own_keys[0], (SEQUENCE_TOKENS, D), 0.1, 0.59765625, ((0, 32),))
    encoded_query_rows = draw_encoded_query_rows(jax.random.fold_in(jax.random.fold_in(splits[17], part), 71), part)
    quantized_key_rows = draw_quantized_key_rows(jax.random.fold_in(jax.random.fold_in(splits[17], part), 71), part)
    quantized_value_rows = noise(own_keys[3], (SEQUENCE_TOKENS, KEY_VALUE_HEADS * HEAD_SIZE), 1.0, 6.0, ((0, 8),))
    key_block_exponent = place_ends(jax.random.randint(own_keys[4], (SEQUENCE_TOKENS // SCALE_POSITIONS, KEY_VALUE_HEADS), -2, 2), jax.random.fold_in(own_keys[4], 1), -2, 1).astype(jnp.int32)
    value_block_exponent = place_ends(jax.random.randint(own_keys[5], (SEQUENCE_TOKENS // SCALE_POSITIONS, KEY_VALUE_HEADS), -2, 2), jax.random.fold_in(own_keys[5], 1), -2, 1).astype(jnp.int32)
    block_order = jax.random.permutation(splits[6], N_CTX).astype(jnp.int32)
    out_weight = noise(splits[7], (QUERY_HEADS * HEAD_SIZE, D), (QUERY_HEADS * HEAD_SIZE) ** -0.5, 0.09375, ((0, 4), (1, 8)))
    norm_gain = jnp.clip(1.0 + 0.18 * jax.random.normal(splits[8], (D,), jnp.float32), 0.1, 1.9)
    expert_ids_keys = jax.random.split(jax.random.fold_in(own_keys[9], 1), SEQUENCE_TOKENS // TOK_DEV)
    expert_ids_turns = jax.random.permutation(jax.random.fold_in(own_keys[9], 3), SEQUENCE_TOKENS // TOK_DEV)
    expert_ids = jax.vmap(lambda own, number: deal_out(jax.random.fold_in(own_keys[9], 2), own, number, TOK_DEV, EXP, TOP, CAP, 2))(expert_ids_keys, expert_ids_turns).reshape((SEQUENCE_TOKENS, TOP))
    route_weight = jnp.clip(0.05 + 0.2 * jax.random.uniform(own_keys[10], (SEQUENCE_TOKENS, TOP), jnp.float32) ** levels(own_keys[10], (SEQUENCE_TOKENS, TOP), ((0, 32),), -0.2, 0.2), 0.05, 0.25)
    gate_weight = noise(splits[11], (2 * EXP, D, FF // 2), D ** -0.5, 0.09375, ((0, 32),))
    gate_scale = place_ends(jax.random.randint(splits[12], (2 * EXP, D // WB, FF // 2 // WB), -1, 2), jax.random.fold_in(splits[12], 1), -1, 1).astype(jnp.int32)
    up_weight = noise(splits[13], (2 * EXP, D, FF // 2), D ** -0.5, 0.09375, ((0, 32),))
    up_scale = place_ends(jax.random.randint(splits[14], (2 * EXP, D // WB, FF // 2 // WB), -1, 2), jax.random.fold_in(splits[14], 1), -1, 1).astype(jnp.int32)
    down_weight = noise(splits[15], (2 * EXP, FF // 2, D), FF ** -0.5, 0.21875, ((0, 32),))
    down_scale = place_ends(jax.random.randint(splits[16], (2 * EXP, FF // 2 // WB, D // WB), -1, 2), jax.random.fold_in(splits[16], 1), -1, 1).astype(jnp.int32)
    return dict(residual=residual, encoded_query_rows=encoded_query_rows, quantized_key_rows=quantized_key_rows, quantized_value_rows=quantized_value_rows, key_block_exponent=key_block_exponent, value_block_exponent=value_block_exponent, block_order=block_order, out_weight=out_weight, norm_gain=norm_gain, expert_ids=expert_ids, route_weight=route_weight, gate_weight=gate_weight, gate_scale=gate_scale, up_weight=up_weight, up_scale=up_scale, down_weight=down_weight, down_scale=down_scale)


def pow_two(exponent, lowest, highest):
    result_sum = jnp.zeros(exponent.shape, jnp.float32)
    for power_of in range(lowest, highest + 1):
        result_sum = result_sum + jnp.where(exponent == power_of, 2.0 ** power_of, 0.0)
    return result_sum

def dequant(values, exponents, lowest, highest):
    row_blocks = exponents.shape[-2]
    col_blocks = exponents.shape[-1]
    row_rep = values.shape[-2] // row_blocks
    col_rep = values.shape[-1] // col_blocks
    factor = pow_two(exponents, lowest, highest).astype(jnp.bfloat16)
    shaped = values.reshape(values.shape[:-2] + (row_blocks, row_rep, col_blocks, col_rep))
    return (shaped * factor[..., :, None, :, None]).reshape(values.shape)

def reference(residual, encoded_query_rows, quantized_key_rows, quantized_value_rows, key_block_exponent, value_block_exponent, block_order, out_weight, norm_gain, expert_ids, route_weight, gate_weight, gate_scale, up_weight, up_scale, down_weight, down_scale):
    query_group_width = QUERY_HEADS // KEY_VALUE_HEADS
    row_ids = jnp.arange(SEQUENCE_TOKENS, dtype=jnp.int32)
    places = block_order[row_ids // CONTEXT_SPAN] * CONTEXT_SPAN + row_ids % CONTEXT_SPAN
    key_multiplier = jnp.repeat(pow_two(key_block_exponent, -2, 1), SCALE_POSITIONS, axis=0)
    value_multiplier = jnp.repeat(pow_two(value_block_exponent, -2, 1), SCALE_POSITIONS, axis=0)
    key_restored = (quantized_key_rows.astype(jnp.float32).reshape(SEQUENCE_TOKENS, KEY_VALUE_HEADS, HEAD_SIZE) * key_multiplier[:, :, None]).astype(jnp.bfloat16)
    value_restored = (quantized_value_rows.astype(jnp.float32).reshape(SEQUENCE_TOKENS, KEY_VALUE_HEADS, HEAD_SIZE) * value_multiplier[:, :, None]).astype(jnp.bfloat16)
    key_float = key_restored.astype(jnp.float32)
    value_float = value_restored.astype(jnp.float32)
    query_tiles = encoded_query_rows.reshape(N_CTX, CONTEXT_SPAN, KEY_VALUE_HEADS, query_group_width, HEAD_SIZE)
    query_places = places.reshape(N_CTX, CONTEXT_SPAN)
    inv_scale = 1.0 / math.sqrt(HEAD_SIZE)

    def attend_block(inputs):
        query_block, query_place = inputs
        scores = jnp.einsum('qgjd,kgd->gjqk', query_block.astype(jnp.float32), key_float) * inv_scale
        visible_mask = places[None, None, None, :] <= query_place[None, None, :, None]
        scores = jnp.where(visible_mask, scores, -1e+30)
        row_max = lax.optimization_barrier(jnp.max(scores, axis=-1, keepdims=True))
        exp_vals = jnp.where(visible_mask, jnp.exp(scores - row_max), 0.0)
        row_sum = lax.optimization_barrier(jnp.sum(exp_vals, axis=-1))
        rounded = lax.optimization_barrier(exp_vals.astype(jnp.bfloat16)).astype(jnp.float32)
        head_mix = jnp.einsum('gjqk,kgd->qgjd', rounded, value_float)
        return (head_mix / jnp.transpose(row_sum, (2, 0, 1))[:, :, :, None]).astype(jnp.bfloat16)
    attended = lax.map(attend_block, (query_tiles, query_places)).reshape(SEQUENCE_TOKENS, QUERY_HEADS * HEAD_SIZE)
    state = residual.astype(jnp.float32) + jnp.dot(attended, out_weight, preferred_element_type=jnp.float32)
    mean_sq = lax.optimization_barrier(jnp.mean(state * state, axis=-1, keepdims=True))
    normed = (state * lax.rsqrt(mean_sq + 1e-06) * norm_gain).astype(jnp.bfloat16)
    source_count = SEQUENCE_TOKENS // TOK_DEV
    copies = TOK_DEV * TOP
    grouped_ids = expert_ids.reshape(source_count, copies)
    onehot = (grouped_ids[:, :, None] == jnp.arange(EXP, dtype=jnp.int32)[None, None, :]).astype(jnp.int32)
    before = jnp.cumsum(onehot, axis=1) - onehot
    slot_ids = lax.optimization_barrier(jnp.sum(before * onehot, axis=2))
    source = jnp.arange(source_count, dtype=jnp.int32)[:, None]
    token_ids = source * TOK_DEV + jnp.arange(copies, dtype=jnp.int32)[None, :] // TOP
    target = (grouped_ids * (source_count * CAP) + source * CAP + slot_ids).reshape(-1)
    slot_table = jnp.full((EXP * source_count * CAP,), SEQUENCE_TOKENS, jnp.int32).at[target].set(token_ids.reshape(-1)).reshape(EXP, source_count * CAP)
    slot_probs = jnp.zeros((EXP * source_count * CAP,), jnp.float32).at[target].set(route_weight.reshape(-1)).reshape(EXP, source_count * CAP)
    padded = jnp.concatenate([normed, jnp.zeros((1, D), jnp.bfloat16)], axis=0)

    def expert_step(accumulated, inputs):
        number, row_index, weight_row = inputs
        first = (2 * number).astype(jnp.int32)
        gate_pair = dequant(lax.dynamic_slice_in_dim(gate_weight, first, 2, 0), lax.dynamic_slice_in_dim(gate_scale, first, 2, 0), -1, 1)
        up_pair = dequant(lax.dynamic_slice_in_dim(up_weight, first, 2, 0), lax.dynamic_slice_in_dim(up_scale, first, 2, 0), -1, 1)
        down_pair = dequant(lax.dynamic_slice_in_dim(down_weight, first, 2, 0), lax.dynamic_slice_in_dim(down_scale, first, 2, 0), -1, 1)
        gate_full = jnp.concatenate([gate_pair[0], gate_pair[1]], axis=1)
        up_full = jnp.concatenate([up_pair[0], up_pair[1]], axis=1)
        down_full = jnp.concatenate([down_pair[0], down_pair[1]], axis=0)
        row_vals = padded[row_index]
        gate_act = jnp.dot(row_vals, gate_full, preferred_element_type=jnp.float32)
        up_act = jnp.dot(row_vals, up_full, preferred_element_type=jnp.float32)
        hidden = (jax.nn.silu(gate_act) * up_act).astype(jnp.bfloat16)
        expert_out = jnp.dot(hidden, down_full, preferred_element_type=jnp.float32).astype(jnp.bfloat16)
        accumulated = accumulated.at[row_index].add(weight_row[:, None] * expert_out.astype(jnp.float32))
        return (accumulated, None)
    numbers = jnp.arange(EXP, dtype=jnp.int32)
    accumulated, unused = lax.scan(expert_step, jnp.zeros((SEQUENCE_TOKENS + 1, D), jnp.float32), (numbers, slot_table, slot_probs))
    return (state + accumulated[:SEQUENCE_TOKENS]).astype(jnp.bfloat16)
```

```python
import functools
import math

import jax
import jax.numpy as jnp
from jax import lax
from jax.experimental import pallas as pl
from jax.experimental.pallas import tpu as pltpu
from jax.sharding import PartitionSpec as P

QUERY_HEADS = 32
KEY_VALUE_HEADS = 4
HEAD_SIZE = 128
TOP = 8
SCALE_POSITIONS = 64
WB = 128
MIB = 1 << 20


def from_partner(array, axis, bit):
    return lax.ppermute(array, axis, [(i, i ^ 1 << bit) for i in range(lax.axis_size(axis))])


def bits_of(count):
    return count.bit_length() - 1


def from_offset(array, offset):
    return lax.ppermute(array, "exp", [(i, i ^ offset) for i in range(lax.axis_size("exp"))])


def from_ctx(array, offset):
    return lax.ppermute(array, "ctx", [(i, i ^ offset) for i in range(lax.axis_size("ctx"))])


def gather_route(ctx_count, x_count, rows_only=False):
    transfers, arrival = [], {(0, 0): 0}

    def go(source, axis, bit, delay=0):
        move = (1 << bit, 0) if axis == "ctx" else (0, 1 << bit - 1)
        target = (source[0] ^ move[0], source[1] ^ move[1])
        arrival[target] = arrival[source] + 1 + delay
        transfers.append((arrival[target], source, target, axis, bit))

    for bit in range(bits_of(ctx_count) - 1, 0, -1):
        for source in list(arrival):
            go(source, "ctx", bit)
    x_steps = [] if rows_only else [("exp", bit + 1) for bit in range(bits_of(x_count))]
    for number, first in enumerate(sorted(arrival)):
        steps = [("ctx", 0)] + x_steps if number % 2 == 0 else x_steps + [("ctx", 0)]
        held = [first]
        for axis, bit in steps:
            before = len(transfers)
            for source in held:
                late = source != first and (ctx_count, x_count) == (8, 2) and number in (0, 2)
                go(source, axis, bit, 1 if late else 0)
            held = held + [transfer[2] for transfer in transfers[before:]]
    return sorted(transfers, key=lambda transfer: transfer[0])


def stages_of(route):
    return [[t for t in route if t[0] == stage] for stage in sorted({t[0] for t in route})]


def together(*values):
    return lax.optimization_barrier(values)


def block_factor(exponent, width):
    factor = jnp.where(exponent < 0, 0.5, jnp.where(exponent > 0, 2.0, 1.0))
    return jnp.full((1, width), factor, jnp.float32).astype(jnp.bfloat16)


def pack_kernel(plan, ctx_ref, exp_ref, key_scale_ref, value_scale_ref, query_ref, key_ref, value_ref,
                ids_ref, route_ref, residual_ref, packed_ref, *piece_refs):
    heads, group, experts = plan
    span, width = query_ref.shape
    my_ctx, my_exp = ctx_ref[0], exp_ref[0]
    kv_head = my_exp * heads // group
    at = pl.ds(pl.multiple_of(kv_head * HEAD_SIZE, HEAD_SIZE), HEAD_SIZE)
    blocks = key_scale_ref.shape[0]
    for place, (ref, scale_ref) in enumerate(((key_ref, key_scale_ref), (value_ref, value_scale_ref))):
        for block in range(blocks):
            exponent = scale_ref[block, kv_head]
            factor = jnp.where(
                exponent < -1,
                0.25,
                jnp.where(exponent < 0, 0.5, jnp.where(exponent < 1, 1.0, 2.0)),
            )
            rows = pl.ds(block * (span // blocks), span // blocks)
            scaled = ref[rows, at].astype(jnp.float32) * factor
            packed_ref[rows, pl.ds(place * HEAD_SIZE, HEAD_SIZE)] = scaled.astype(jnp.bfloat16)
    packed_ref[:, 2 * HEAD_SIZE : 2 * HEAD_SIZE + width] = query_ref[...]
    tok = ids_ref.shape[1]
    number = lax.broadcasted_iota(jnp.int32, (128, tok), 0)
    dense = jnp.zeros((128, tok), jnp.float32)
    for k in range(TOP):
        dense = dense + jnp.where(ids_ref[k : k + 1, :] == number, route_ref[k : k + 1, :], 0.0)
    dense = jnp.concatenate([dense, jnp.zeros((128, 128 - tok), jnp.float32)], axis=1)
    dense = jnp.transpose(dense)[:tok, :]
    high = dense.astype(jnp.bfloat16)
    packed_ref[0:tok, 2 * HEAD_SIZE + width :] = high
    packed_ref[tok : 2 * tok, 2 * HEAD_SIZE + width :] = (dense - high.astype(jnp.float32)).astype(
        jnp.bfloat16
    )
    packed_ref[2 * tok :, 2 * HEAD_SIZE + width :] = jnp.zeros((span - 2 * tok, 128), jnp.bfloat16)
    cols = piece_refs[0].shape[1]
    for offset, ref in enumerate(piece_refs):
        col = pl.multiple_of(lax.bitwise_xor(my_ctx, offset) * cols, cols)
        ref[...] = residual_ref[:, pl.ds(col, cols)]


def deq_in_kernel(exp_ref, gate_scale_ref, up_scale_ref, gate_ref, up_ref, _, own_ref, give_ref):
    step = pl.program_id(0)
    core = lax.bitwise_and(exp_ref[0], 1)
    rows, cols = own_ref.shape[0], gate_ref.shape[2]
    for half, (ref, scale_ref) in enumerate(((gate_ref, gate_scale_ref), (up_ref, up_scale_ref))):
        for out_ref, side in ((give_ref, 1 - core), (own_ref, core)):
            first = (2 * step + side) * (rows // WB)
            for i in range(rows // WB):
                row = pl.multiple_of(side * rows + i * WB, WB)
                for j in range(cols // WB):
                    factor = block_factor(scale_ref[j, 0, first + i], WB)
                    out_ref[pl.ds(i * WB, WB), pl.ds(half * cols + j * WB, WB)] = (
                        ref[0, pl.ds(row, WB), pl.ds(j * WB, WB)] * factor
                    )


def deq_in(my_exp, gate_weight, gate_scale, up_weight, up_scale, ctx_count, after):
    width, hidden = gate_weight.shape[1:]
    rows = width // (2 * ctx_count)
    spec = pl.BlockSpec((1, 2 * rows, hidden), lambda i, e, gs, us: (0, i, 0))
    out_spec = pl.BlockSpec((rows, 2 * hidden), lambda i, e, gs, us: (i, 0))
    shape = jax.ShapeDtypeStruct((width // 2, 2 * hidden), jnp.bfloat16)
    return pl.pallas_call(
        deq_in_kernel,
        grid_spec=pltpu.PrefetchScalarGridSpec(
            num_scalar_prefetch=3,
            grid=(ctx_count,),
            in_specs=[spec, spec, pl.BlockSpec(memory_space=pl.ANY)],
            out_specs=[out_spec, out_spec],
        ),
        out_shape=[shape, shape],
        compiler_params=pltpu.CompilerParams(vmem_limit_bytes=16 * MIB),
        cost_estimate=pl.CostEstimate(
            flops=2 * width * hidden, bytes_accessed=8 * width * hidden, transcendentals=0
        ),
        name="dequant_in",
    )(
        my_exp,
        jnp.transpose(gate_scale, (2, 0, 1)),
        jnp.transpose(up_scale, (2, 0, 1)),
        gate_weight,
        up_weight,
        after,
    )


def deq_down_kernel(exp_ref, scale_ref, down_ref, _, own_ref, give_ref):
    step = pl.program_id(0)
    core = lax.bitwise_and(exp_ref[0], 1)
    rows, cols = own_ref.shape
    for out_ref, side in ((give_ref, 1 - core), (own_ref, core)):
        first = (2 * step + side) * (cols // WB)
        for j in range(cols // WB):
            col = pl.multiple_of(side * cols + j * WB, WB)
            for i in range(rows // WB):
                factor = block_factor(scale_ref[i, 0, first + j], WB)
                out_ref[pl.ds(i * WB, WB), pl.ds(j * WB, WB)] = (
                    down_ref[0, pl.ds(i * WB, WB), pl.ds(col, WB)] * factor
                )


def deq_down(my_exp, down_weight, down_scale, ctx_count, after):
    hidden, width = down_weight.shape[1:]
    cols = width // (2 * ctx_count)
    out_spec = pl.BlockSpec((hidden, cols), lambda i, e, ds: (0, i))
    shape = jax.ShapeDtypeStruct((hidden, width // 2), jnp.bfloat16)
    return pl.pallas_call(
        deq_down_kernel,
        grid_spec=pltpu.PrefetchScalarGridSpec(
            num_scalar_prefetch=2,
            grid=(ctx_count,),
            in_specs=[
                pl.BlockSpec((1, hidden, 2 * cols), lambda i, e, ds: (0, 0, i)),
                pl.BlockSpec(memory_space=pl.ANY),
            ],
            out_specs=[out_spec, out_spec],
        ),
        out_shape=[shape, shape],
        compiler_params=pltpu.CompilerParams(vmem_limit_bytes=16 * MIB),
        cost_estimate=pl.CostEstimate(
            flops=width * hidden, bytes_accessed=4 * width * hidden, transcendentals=0
        ),
        name="dequant_down",
    )(my_exp, jnp.transpose(down_scale, (1, 0, 2)), down_weight, after)


def attend_kernel(plan, ctx_ref, exp_ref, order_ref, *refs):
    ctx_count, exp_count, tok, heads, x_off = plan
    packed, pieces = refs[:ctx_count], refs[ctx_count : 2 * ctx_count]
    weight_ref, _ = refs[2 * ctx_count : 2 * ctx_count + 2]
    rest = refs[2 * ctx_count + 2 :]
    out_refs, route_refs = rest[0:2], (rest[2:3] if x_off == 0 else rest[0:1]) + rest[1:2]
    key_scr, value_scr, place_scr, att_scr = rest[-4:]
    x_count = exp_count // 2
    span = packed[0].shape[0]
    positions = ctx_count * span
    per_ctx = 2 * tok
    my_ctx, my_exp = ctx_ref[0], exp_ref[0]
    my_x, my_core = lax.shift_right_logical(my_exp, 1), lax.bitwise_and(my_exp, 1)
    start = pl.multiple_of(lax.bitwise_xor(my_x, x_off) * per_ctx, per_ctx)
    lane = lax.broadcasted_iota(jnp.int32, (8, positions), 1)
    places = lane % span
    for offset, ref in enumerate(packed):
        key_scr[pl.ds(offset * span, span), :] = ref[:, 0:HEAD_SIZE]
        value_scr[pl.ds(offset * span, span), :] = ref[:, HEAD_SIZE : 2 * HEAD_SIZE]
        base = order_ref[lax.bitwise_xor(my_ctx, offset)] * span
        places = places + jnp.where(lane // span == offset, base, 0)
    place_scr[...] = places
    scale = 1.0 / math.sqrt(HEAD_SIZE)
    for offset, ref in enumerate(packed):
        source = lax.bitwise_xor(my_ctx, offset)
        queries = jnp.concatenate(
            [
                ref[pl.ds(start, per_ctx), (h + 2) * HEAD_SIZE : (h + 3) * HEAD_SIZE]
                for h in range(heads)
            ],
            axis=0,
        )
        scores = lax.dot_general(
            queries, key_scr[...], (((1,), (1,)), ((), ())), preferred_element_type=jnp.float32
        )
        own_place = (
            order_ref[source] * span + start + lax.broadcasted_iota(jnp.int32, (per_ctx, positions), 0)
        )
        bias = jnp.where(place_scr[0:1, :] <= own_place, 0.0, -1e30)
        scores = scores.reshape(heads, per_ctx, positions) * scale + bias[None]
        largest = jnp.max(scores, axis=-1, keepdims=True)
        exps = jnp.exp(scores - largest)
        total = jnp.sum(exps, axis=-1, keepdims=True)
        mixed = jnp.dot(
            exps.astype(jnp.bfloat16).reshape(heads * per_ctx, positions),
            value_scr[...],
            preferred_element_type=jnp.float32,
        ).reshape(heads, per_ctx, HEAD_SIZE)
        mixed = (mixed / total).astype(jnp.bfloat16)
        at = pl.ds(pl.multiple_of(source * per_ctx, per_ctx), per_ctx)
        for head in range(heads):
            att_scr[at, pl.ds(head * HEAD_SIZE, HEAD_SIZE)] = mixed[head]

    cols = weight_ref.shape[1] // 2
    per_x = ctx_count * per_ctx
    first = (heads + 2) * HEAD_SIZE
    route_lane = lax.broadcasted_iota(jnp.int32, (tok, HEAD_SIZE), 1)
    expert = my_ctx * x_count + lax.bitwise_xor(my_x, x_off)
    sides = [jnp.zeros((tok, HEAD_SIZE), jnp.float32)] * 2
    for offset, ref in enumerate(packed):
        for part_of in range(2):
            block = ref[part_of * tok : (part_of + 1) * tok, first:].astype(jnp.float32)
            column = jnp.sum(jnp.where(route_lane == expert, block, 0.0), axis=1, keepdims=True)
            sides[part_of] = sides[part_of] + jnp.where(
                route_lane == lax.bitwise_xor(my_ctx, offset), column, 0.0
            )
    for which, out_ref in enumerate(out_refs):
        side = lax.bitwise_xor(my_core, which)
        weight = weight_ref[:, pl.ds(pl.multiple_of(side * cols, cols), cols)]
        part = jnp.dot(att_scr[...], weight, preferred_element_type=jnp.float32)
        out_ref[0:per_x, :] = part.astype(out_ref.dtype)
        if x_off == 0:
            for offset, ref in enumerate(pieces):
                row = (lax.bitwise_xor(my_ctx, offset) * 2 + my_core) * tok
                at = pl.ds(pl.multiple_of(row, tok), tok)
                piece = ref[:, pl.ds(pl.multiple_of(side * cols, cols), cols)].astype(jnp.float32)
                out_ref[at, :] = (out_ref[at, :].astype(jnp.float32) + piece).astype(out_ref.dtype)
        route_out = route_refs[which]
        row = route_out.shape[0] - 2 * tok
        for part_of, values in enumerate(sides):
            at = pl.ds(row + part_of * tok, tok)
            route_out[at, 0:HEAD_SIZE] = values.astype(jnp.bfloat16)
            if route_out.shape[1] > HEAD_SIZE:
                rest_shape = (tok, route_out.shape[1] - HEAD_SIZE)
                route_out[at, HEAD_SIZE:] = jnp.zeros(rest_shape, jnp.bfloat16)


def fill_rows(plan, ctx_ref, exp_ref, gain_ref, chunk_refs, offsets, rows_scr, groups):
    ctx_count, x_count = plan
    half = ctx_count // 2
    my_ctx = ctx_ref[0]
    my_core = lax.bitwise_and(exp_ref[0], 1)
    mine = lax.shift_right_logical(my_ctx, bits_of(half))
    rows, cols = chunk_refs[0].shape
    rows = rows // 2
    sums = {}
    for ref, (c_off, x_off) in zip(chunk_refs, offsets):
        source = lax.bitwise_xor(my_ctx, c_off)
        gain_at = pl.multiple_of((source * 2 + my_core) * cols, cols)
        gain = gain_ref[:, pl.ds(gain_at, cols)]
        col = pl.multiple_of(lax.bitwise_and(source, half - 1) * cols, cols)
        for place, group in enumerate(groups):
            side = mine if group == 1 else 1 - mine
            chunk = ref[pl.ds(pl.multiple_of(side * rows, rows), rows), :].astype(jnp.float32)
            row = (place * x_count + x_off) * rows
            rows_scr[pl.ds(row, rows), pl.ds(col, cols)] = (chunk * gain).astype(jnp.bfloat16)
            square = jnp.sum(chunk * chunk, axis=-1, keepdims=True)
            sums[row] = sums[row] + square if row in sums else square
    return sums


def experts_in_first(plan, offsets, ctx_ref, exp_ref, *refs):
    chunk_refs, (gain_ref, own_ref, other_ref, _, act_ref, square_ref, rows_scr) = refs[:-7], refs[-7:]
    half = plan[0] // 2
    sums = fill_rows(plan, ctx_ref, exp_ref, gain_ref, chunk_refs, offsets, rows_scr, (0, 1))
    for row, square in sums.items():
        square_ref[pl.ds(row, square.shape[0]), :] = square
    depth, width = rows_scr.shape[1], own_ref.shape[1]
    start = lax.shift_right_logical(ctx_ref[0], bits_of(half)) * depth
    at = pl.ds(pl.multiple_of(start, depth), depth)
    for place, ref in enumerate((own_ref, other_ref)):
        act_ref[:, place * width : (place + 1) * width] = jnp.dot(
            rows_scr[...], ref[at, :], preferred_element_type=jnp.float32
        )


def experts_in_second(plan, offsets, group, ctx_ref, exp_ref, *refs):
    chunk_refs, rest = refs[:-8], refs[-8:]
    gain_ref, own_ref, other_ref, first_ref, square_ref, _, act_ref, rows_scr = rest
    half = plan[0] // 2
    sums = fill_rows(plan, ctx_ref, exp_ref, gain_ref, chunk_refs, offsets, rows_scr, (group,))
    count, depth = rows_scr.shape
    width = own_ref.shape[1]
    lane = lax.broadcasted_iota(jnp.int32, (1, HEAD_SIZE), 1)
    for row, square in sums.items():
        rows = square.shape[0]
        square = square + square_ref[pl.ds(group * count + row, rows), :]
        high = square.astype(jnp.bfloat16).astype(jnp.float32)
        act_ref[pl.ds(row, rows), 2 * width :] = jnp.where(lane == 0, high, square - high).astype(
            jnp.bfloat16
        )
    start = (1 - lax.shift_right_logical(ctx_ref[0], bits_of(half))) * depth
    at = pl.ds(pl.multiple_of(start, depth), depth)
    for place, ref in enumerate((own_ref, other_ref)):
        cols = slice(place * width, (place + 1) * width)
        act = first_ref[group * count : (group + 1) * count, cols] + jnp.dot(
            rows_scr[...], ref[at, :], preferred_element_type=jnp.float32
        )
        act_ref[:, cols] = act.astype(jnp.bfloat16)


def experts_out_kernel(plan, group, slots, model_width, ctx_ref, exp_ref, act_ref, came_ref, *refs):
    ctx_count, exp_count, tok = plan
    x_count, half = exp_count // 2, ctx_count // 2
    route_refs = refs[:exp_count]
    own_ref, other_ref, _ = refs[exp_count : exp_count + 3]
    rest = refs[exp_count + 3 :]
    state_refs, rest = (rest[:ctx_count], rest[ctx_count:]) if group == 1 else ((), rest)
    out_refs, hidden_scr = rest[:-1], rest[-1]
    my_ctx = ctx_ref[0]
    my_core = lax.bitwise_and(exp_ref[0], 1)
    mine = lax.shift_right_logical(my_ctx, bits_of(half))
    first_ctx = (mine if group == 1 else 1 - mine) * half
    width = (act_ref.shape[1] - HEAD_SIZE) // 2
    hidden = width // 2
    lane = lax.broadcasted_iota(jnp.int32, (tok, HEAD_SIZE), 1)
    blocks = []
    for ref in route_refs:
        row = ref.shape[0] - 2 * tok
        both = ref[row : row + 2 * tok, 0:HEAD_SIZE].astype(jnp.float32)
        blocks.append(both[:tok] + both[tok:])
    columns = []
    for x_off in range(x_count):
        for low in range(half):
            for core in range(2):
                same, swapped = blocks[2 * x_off + core], blocks[2 * x_off + 1 - core]
                block = jnp.where(my_core == 0, same, swapped)
                picked = jnp.where(lane == first_ctx + low, block, 0.0)
                columns.append(jnp.sum(picked, axis=1, keepdims=True))
    route = jnp.concatenate(columns, axis=0)
    squares = act_ref[:, 2 * width :].astype(jnp.float32) + came_ref[:, 2 * width :].astype(jnp.float32)
    norm = lax.rsqrt((squares[:, 0:1] + squares[:, 1:2]) / model_width + 1e-06)
    scaled_route = norm * route
    for side in range(2):
        acts = act_ref[:, side * width : (side + 1) * width].astype(jnp.float32) + came_ref[
            :, (1 - side) * width : (2 - side) * width
        ].astype(jnp.float32)
        gate = acts[:, :hidden] * norm
        value = gate / (1.0 + jnp.exp(-gate)) * (acts[:, hidden:] * scaled_route)
        hidden_scr[:, side * hidden : (side + 1) * hidden] = value.astype(jnp.bfloat16)
    picked = []
    for c_off, x_off in slots:
        low = lax.bitwise_and(lax.bitwise_xor(my_ctx, c_off), half - 1)
        row = pl.multiple_of((x_off * half + low) * (2 * tok), 2 * tok)
        picked.append(hidden_scr[pl.ds(row, 2 * tok), :])
    picked = jnp.concatenate(picked, axis=0)
    out_cols = own_ref.shape[1]
    step = min(512, out_cols)
    for col in range(0, out_cols, step):
        at = pl.ds(col, step)
        out = jnp.dot(picked[:, :hidden], own_ref[:, at], preferred_element_type=jnp.float32)
        out = out + jnp.dot(picked[:, hidden:], other_ref[:, at], preferred_element_type=jnp.float32)
        for place, ref in enumerate(out_refs):
            ref[:, at] = out[place * 2 * tok : (place + 1) * 2 * tok, :].astype(ref.dtype)
    for slot, ref in zip(slots, out_refs):
        if slot == (0, 0):
            for c_off, state_ref in enumerate(state_refs):
                cols = state_ref.shape[1]
                at = pl.ds(pl.multiple_of(lax.bitwise_xor(my_ctx, c_off) * cols, cols), cols)
                own_row = pl.multiple_of(my_ctx * (2 * tok), 2 * tok)
                ref[:, at] = ref[:, at] + state_ref[pl.ds(own_row, 2 * tok), :].astype(jnp.float32)


def shards(
    residual,
    encoded_query_rows,
    quantized_key_rows,
    quantized_value_rows,
    key_block_exponent,
    value_block_exponent,
    block_order,
    out_weight,
    norm_gain,
    expert_ids,
    route_weight,
    gate_weight,
    gate_scale,
    up_weight,
    up_scale,
    down_weight,
    down_scale,
):
    f32, bf16 = jnp.float32, jnp.bfloat16
    vmem = pl.BlockSpec(memory_space=pltpu.VMEM)
    smem = pl.BlockSpec(memory_space=pltpu.SMEM)
    anywhere = pl.BlockSpec(memory_space=pl.ANY)
    span, query_width = encoded_query_rows.shape
    heads = query_width // HEAD_SIZE
    group = QUERY_HEADS // KEY_VALUE_HEADS
    ctx_count = lax.axis_size("ctx")
    exp_count = lax.axis_size("exp")
    x_count = exp_count // 2
    experts = ctx_count * x_count
    tok, model_width = residual.shape
    half_width = model_width // 2
    cols = half_width // ctx_count
    my_ctx = lax.axis_index("ctx").astype(jnp.int32).reshape(1)
    my_exp = lax.axis_index("exp").astype(jnp.int32).reshape(1)
    route = gather_route(ctx_count, x_count)

    packed, *pieces = pl.pallas_call(
        functools.partial(pack_kernel, (heads, group, experts)),
        in_specs=[smem] * 4 + [vmem] * 6,
        out_specs=[vmem] * (1 + ctx_count),
        out_shape=[jax.ShapeDtypeStruct((span, query_width + 3 * HEAD_SIZE), bf16)]
        + [jax.ShapeDtypeStruct((tok, 2 * cols), bf16)] * ctx_count,
        compiler_params=pltpu.CompilerParams(vmem_limit_bytes=8 * MIB),
        name="pack",
    )(
        my_ctx,
        my_exp,
        key_block_exponent,
        value_block_exponent,
        encoded_query_rows,
        quantized_key_rows,
        quantized_value_rows,
        jnp.transpose(expert_ids),
        jnp.transpose(route_weight),
        residual,
    )
    held = {(0, 0): packed}
    stages = stages_of(gather_route(ctx_count, x_count, rows_only=True))
    for number, stage in enumerate(stages):
        came = [from_partner(held[source], axis, bit) for _, source, _, axis, bit in stage]
        if number == 0:
            in_own, in_give = deq_in(
                my_exp, gate_weight, gate_scale, up_weight, up_scale, ctx_count, packed
            )
            *came, in_own, in_give = together(*came, in_own, in_give)
        elif number == 1:
            in_other = from_offset(in_give, 1)
            pieces = [pieces[0]] + [from_ctx(pieces[offset], offset) for offset in range(1, ctx_count)]
            down_own, down_give = deq_down(my_exp, down_weight, down_scale, ctx_count, came_first)
            *came, down_own, down_give = together(*came, down_own, down_give)
        came_first = came[0]
        held.update({target: array for (_, _, target, _, _), array in zip(stage, came)})
    packed = [held[offset, 0] for offset in range(ctx_count)]
    down_other = from_offset(down_give, 1)

    positions = ctx_count * span
    per_x = 2 * ctx_count * tok
    gives, after = {}, out_weight
    for x_off in reversed(range(x_count)):
        give_shape = jax.ShapeDtypeStruct((per_x + 2 * tok, cols), bf16)
        first_shape = jax.ShapeDtypeStruct((per_x, cols), f32) if x_off == 0 else give_shape
        route_shape = [jax.ShapeDtypeStruct((2 * tok, HEAD_SIZE), bf16)] if x_off == 0 else []
        outs = pl.pallas_call(
            functools.partial(attend_kernel, (ctx_count, exp_count, tok, heads, x_off)),
            in_specs=[smem] * 3 + [vmem] * (2 * ctx_count + 1) + [anywhere],
            out_specs=[vmem] * (2 + len(route_shape)),
            out_shape=[first_shape, give_shape] + route_shape,
            scratch_shapes=[
                pltpu.VMEM((positions, HEAD_SIZE), bf16),
                pltpu.VMEM((positions, HEAD_SIZE), bf16),
                pltpu.VMEM((8, positions), jnp.int32),
                pltpu.VMEM((per_x, query_width), bf16),
            ],
            compiler_params=pltpu.CompilerParams(vmem_limit_bytes=2 * ctx_count * MIB),
            cost_estimate=pl.CostEstimate(
                flops=(4 * positions * positions + 4 * positions * cols) * query_width // x_count,
                bytes_accessed=4 * MIB,
                transcendentals=heads * positions * positions // x_count,
            ),
            name="attend",
        )(my_ctx, my_exp, block_order, *packed, *pieces, out_weight, after)
        gives[2 * x_off + 1] = from_offset(outs[1], 2 * x_off + 1)
        if x_off:
            gives[2 * x_off] = from_offset(outs[0], 2 * x_off)
            after = outs[0]
        else:
            keep, own_route = outs[0], outs[2]

    gives = [gives[offset] for offset in range(1, exp_count)]
    state = keep
    for give in gives:
        state = state + give[:per_x].astype(f32)
    state = state.astype(bf16)

    chunks = {(0, 0): state}
    for stage in stages_of(route):
        came = [from_partner(chunks[source], axis, bit) for _, source, _, axis, bit in stage]
        if stage[-1] != route[-1]:
            came = together(*came)
        chunks.update({target: array for (_, _, target, _, _), array in zip(stage, came)})
    gain = norm_gain.reshape(1, model_width)
    rows = x_count * per_x
    in_width = in_own.shape[1]
    near = tuple(sorted(key for key in chunks if key[0] < ctx_count // 2))
    far = tuple(sorted(key for key in chunks if key[0] >= ctx_count // 2))
    first_act, first_square = pl.pallas_call(
        functools.partial(experts_in_first, (ctx_count, x_count), near),
        in_specs=[smem] * 2 + [vmem] * (len(near) + 3) + [anywhere],
        out_specs=[vmem] * 2,
        out_shape=[
            jax.ShapeDtypeStruct((rows, 2 * in_width), f32),
            jax.ShapeDtypeStruct((rows, 1), f32),
        ],
        scratch_shapes=[pltpu.VMEM((rows, half_width // 2), bf16)],
        compiler_params=pltpu.CompilerParams(vmem_limit_bytes=2 * ctx_count * MIB),
        cost_estimate=pl.CostEstimate(
            flops=2 * rows * half_width * in_width, bytes_accessed=8 * MIB, transcendentals=0
        ),
        name="experts_in_first",
    )(my_ctx, my_exp, *[chunks[key] for key in near], gain, in_own, in_other, down_give)
    acts = []
    for part in range(2):
        acts.append(
            pl.pallas_call(
                functools.partial(experts_in_second, (ctx_count, x_count), far, part),
                in_specs=[smem] * 2 + [vmem] * (len(far) + 5) + [anywhere],
                out_specs=vmem,
                out_shape=jax.ShapeDtypeStruct((rows // 2, 2 * in_width + HEAD_SIZE), bf16),
                scratch_shapes=[pltpu.VMEM((rows // 2, half_width // 2), bf16)],
                compiler_params=pltpu.CompilerParams(vmem_limit_bytes=2 * ctx_count * MIB),
                cost_estimate=pl.CostEstimate(
                    flops=rows * half_width * in_width, bytes_accessed=8 * MIB, transcendentals=0
                ),
                name="experts_in_second",
            )(
                my_ctx,
                my_exp,
                *[chunks[key] for key in far],
                gain,
                in_own,
                in_other,
                first_act,
                first_square,
                acts[0] if part else first_square,
            )
        )
    leaves = {key for key in chunks} - {source for _, source, _, _, _ in route}
    sums = {}
    for part in range(2):
        slots = near if part == 1 else far
        states = [chunks[offset, 0] for offset in range(ctx_count)] if part == 1 else []
        outs = pl.pallas_call(
            functools.partial(experts_out_kernel, (ctx_count, exp_count, tok), part, slots, model_width),
            in_specs=[smem] * 2 + [vmem] * (4 + exp_count) + [anywhere] + [vmem] * len(states),
            out_specs=[vmem] * len(slots),
            out_shape=[
                jax.ShapeDtypeStruct((2 * tok, half_width), bf16 if slot in leaves else f32)
                for slot in slots
            ],
            scratch_shapes=[pltpu.VMEM((rows // 2, in_width), bf16)],
            compiler_params=pltpu.CompilerParams(vmem_limit_bytes=2 * ctx_count * MIB),
            cost_estimate=pl.CostEstimate(
                flops=rows * half_width * in_width,
                bytes_accessed=8 * MIB,
                transcendentals=rows * in_width // 2,
            ),
            name="experts_out",
        )(
            my_ctx,
            my_exp,
            acts[part],
            from_offset(acts[part], 1),
            own_route,
            *gives,
            down_own,
            down_other,
            sums[slots_done[0]] if part else acts[1],
            *states,
        )
        slots_done = slots
        sums.update(zip(slots, outs))

    backward = stages_of(route)[::-1]
    for number, stage in enumerate(backward):
        came = [from_partner(sums[target].astype(bf16), axis, bit) for _, _, target, axis, bit in stage]
        if number < len(backward) - 1:
            waiting = [key for key in near if key in sums] if number == 0 else []
            values = together(*came, *[sums[key] for key in waiting])
            came = values[: len(came)]
            sums.update(zip(waiting, values[len(came) :]))
        for (_, source, target, _, _), array in zip(stage, came):
            sums[source] = sums[source] + array.astype(f32)
    total = sums[0, 0]
    core = lax.bitwise_and(my_exp[0], 1)
    mine = jnp.where(core == 0, total[:tok], total[tok:]).astype(bf16)
    came = from_offset(jnp.where(core == 0, total[tok:], total[:tok]).astype(bf16), 1)
    mine = mine.reshape(tok, ctx_count, 1, cols)
    came = came.reshape(tok, ctx_count, 1, cols)
    result = jnp.where(core == 0, jnp.concatenate([mine, came], axis=2), jnp.concatenate([came, mine], axis=2))
    return result.reshape(tok, model_width)


def solution(mesh):
    return jax.shard_map(
        shards,
        mesh=mesh,
        in_specs=(
            P(("dp", "ctx", "exp"), None),
            P(("dp", "ctx"), "exp"),
            P(("dp", "ctx"), None),
            P(("dp", "ctx"), None),
            P(("dp", "ctx"), None),
            P(("dp", "ctx"), None),
            P(),
            P("exp", "ctx"),
            P(),
            P(("dp", "ctx", "exp"), None),
            P(("dp", "ctx", "exp"), None),
            P(("ctx", "exp"), None, None),
            P(("ctx", "exp"), None, None),
            P(("ctx", "exp"), None, None),
            P(("ctx", "exp"), None, None),
            P(("ctx", "exp"), None, None),
            P(("ctx", "exp"), None, None),
        ),
        out_specs=P(("dp", "ctx", "exp"), None),
        check_vma=False,
    )
```

```python
import functools
import math

import jax
import jax.numpy as jnp
from jax import lax
from jax.experimental import pallas as pl
from jax.experimental.pallas import tpu as pltpu
from jax.sharding import PartitionSpec as P

QUERY_HEADS = 32
KEY_VALUE_HEADS = 4
HEAD_SIZE = 128
TOP = 8
SCALE_POSITIONS = 64
WB = 128
MIB = 1 << 20


def from_partner(array, axis, bit):
    return lax.ppermute(array, axis, [(i, i ^ 1 << bit) for i in range(lax.axis_size(axis))])


def bits_of(count):
    return count.bit_length() - 1


def from_offset(array, offset):
    return lax.ppermute(array, "exp", [(i, i ^ offset) for i in range(lax.axis_size("exp"))])


def from_ctx(array, offset):
    return lax.ppermute(array, "ctx", [(i, i ^ offset) for i in range(lax.axis_size("ctx"))])


def gather_route(ctx_count, x_count, rows_only=False):
    transfers, arrival = [], {(0, 0): 0}

    def go(source, axis, bit, delay=0):
        move = (1 << bit, 0) if axis == "ctx" else (0, 1 << bit - 1)
        target = (source[0] ^ move[0], source[1] ^ move[1])
        arrival[target] = arrival[source] + 1 + delay
        transfers.append((arrival[target], source, target, axis, bit))

    for bit in range(bits_of(ctx_count) - 1, 0, -1):
        for source in list(arrival):
            go(source, "ctx", bit)
    x_steps = [] if rows_only else [("exp", bit + 1) for bit in range(bits_of(x_count))]
    for number, first in enumerate(sorted(arrival)):
        steps = [("ctx", 0)] + x_steps if number % 2 == 0 else x_steps + [("ctx", 0)]
        held = [first]
        for axis, bit in steps:
            before = len(transfers)
            for source in held:
                late = source != first and (ctx_count, x_count) == (8, 2) and number in (0, 2)
                go(source, axis, bit, 1 if late else 0)
            held = held + [transfer[2] for transfer in transfers[before:]]
    return sorted(transfers, key=lambda transfer: transfer[0])


def stages_of(route):
    return [[t for t in route if t[0] == stage] for stage in sorted({t[0] for t in route})]


def together(*values):
    return lax.optimization_barrier(values)


def block_factor(exponent, width):
    factor = jnp.where(exponent < 0, 0.5, jnp.where(exponent > 0, 2.0, 1.0))
    return jnp.full((1, width), factor, jnp.float32).astype(jnp.bfloat16)


def copy_all(sems, pairs):
    copies = [pltpu.make_async_copy(src, dst, sems.at[i]) for i, (src, dst) in enumerate(pairs)]
    for copy in copies:
        copy.start()
    return copies


def pack_kernel(plan, ctx_ref, exp_ref, key_scale_hbm, value_scale_hbm, query_hbm, key_hbm, value_hbm, ids_hbm,
                route_hbm, residual_hbm, packed_ref, near_ref, far_ref, key_scale_ref, value_scale_ref,
                key_ref, value_ref, ids_ref, route_ref, sems):
    heads, group = plan
    span, width = query_hbm.shape
    half, tok, cols = near_ref.shape
    my_ctx, my_exp = ctx_ref[0], exp_ref[0]
    kv_head = my_exp * heads // group
    at = pl.ds(pl.multiple_of(kv_head * HEAD_SIZE, HEAD_SIZE), HEAD_SIZE)
    pairs = [
        (key_scale_hbm, key_scale_ref),
        (value_scale_hbm, value_scale_ref),
        (key_hbm.at[:, at], key_ref),
        (value_hbm.at[:, at], value_ref),
        (ids_hbm, ids_ref),
        (route_hbm, route_ref),
        (query_hbm, packed_ref.at[:, 2 * HEAD_SIZE : 2 * HEAD_SIZE + width]),
    ]
    for offset in range(2 * half):
        col = pl.multiple_of(lax.bitwise_xor(my_ctx, offset) * cols, cols)
        pairs.append(
            (residual_hbm.at[:, pl.ds(col, cols)], (near_ref if offset < half else far_ref).at[offset % half])
        )
    copies = copy_all(sems, pairs)
    for copy in copies[:6]:
        copy.wait()
    lane = lax.broadcasted_iota(jnp.int32, key_scale_ref.shape, 1)
    blocks = key_scale_ref.shape[0]
    for place, (ref, scale_ref) in enumerate(((key_ref, key_scale_ref), (value_ref, value_scale_ref))):
        exponent = scale_ref[...]
        factor = jnp.where(
            exponent < -1, 0.25, jnp.where(exponent < 0, 0.5, jnp.where(exponent < 1, 1.0, 2.0))
        )
        factor = jnp.sum(jnp.where(lane == kv_head, factor, 0.0), axis=1, keepdims=True)
        for block in range(blocks):
            rows = pl.ds(block * (span // blocks), span // blocks)
            scaled = ref[rows, :].astype(jnp.float32) * factor[block : block + 1, :]
            packed_ref[rows, pl.ds(place * HEAD_SIZE, HEAD_SIZE)] = scaled.astype(jnp.bfloat16)
    number = lax.broadcasted_iota(jnp.int32, (128, tok), 0)
    dense = jnp.zeros((128, tok), jnp.float32)
    for k in range(TOP):
        dense = dense + jnp.where(ids_ref[k : k + 1, :] == number, route_ref[k : k + 1, :], 0.0)
    dense = jnp.concatenate([dense, jnp.zeros((128, 128 - tok), jnp.float32)], axis=1)
    dense = jnp.transpose(dense)[:tok, :]
    high = dense.astype(jnp.bfloat16)
    packed_ref[0:tok, 2 * HEAD_SIZE + width :] = high
    packed_ref[tok : 2 * tok, 2 * HEAD_SIZE + width :] = (dense - high.astype(jnp.float32)).astype(
        jnp.bfloat16
    )
    packed_ref[2 * tok :, 2 * HEAD_SIZE + width :] = jnp.zeros((span - 2 * tok, 128), jnp.bfloat16)
    for copy in copies[6:]:
        copy.wait()


def deq_in_kernel(ctx_count, exp_ref, gate_scale_hbm, up_scale_hbm, gate_hbm, up_hbm, _, own_ref, give_ref,
                  gate_ref, up_ref, gate_scale_ref, up_scale_ref, sems):
    core = lax.bitwise_and(exp_ref[0], 1)
    width, cols = gate_ref.shape
    rows = width // (2 * ctx_count)
    pairs = [(gate_scale_hbm, gate_scale_ref), (up_scale_hbm, up_scale_ref)]
    for step in range(ctx_count):
        at = pl.ds(step * 2 * rows, 2 * rows)
        pairs += [(gate_hbm.at[0, at], gate_ref.at[at]), (up_hbm.at[0, at], up_ref.at[at])]
    copies = copy_all(sems, pairs)
    for copy in copies[:2]:
        copy.wait()
    for step in range(ctx_count):
        for half, (ref, scale_ref) in enumerate(((gate_ref, gate_scale_ref), (up_ref, up_scale_ref))):
            copies[2 + 2 * step + half].wait()
            for out_ref, side in ((give_ref, 1 - core), (own_ref, core)):
                first = (2 * step + side) * (rows // WB)
                for i in range(rows // WB):
                    row = pl.multiple_of((2 * step + side) * rows + i * WB, WB)
                    for j in range(cols // WB):
                        factor = block_factor(scale_ref[j, 0, first + i], WB)
                        out_ref[pl.ds(step * rows + i * WB, WB), pl.ds(half * cols + j * WB, WB)] = (
                            ref[pl.ds(row, WB), pl.ds(j * WB, WB)] * factor
                        )


def deq_in(my_exp, gate_weight, gate_scale, up_weight, up_scale, ctx_count, after):
    width, hidden = gate_weight.shape[1:]
    shape = jax.ShapeDtypeStruct((width // 2, 2 * hidden), jnp.bfloat16)
    gate_scale = jnp.transpose(gate_scale, (2, 0, 1))
    up_scale = jnp.transpose(up_scale, (2, 0, 1))
    return pl.pallas_call(
        functools.partial(deq_in_kernel, ctx_count),
        in_specs=[pl.BlockSpec(memory_space=pltpu.SMEM)]
        + [pl.BlockSpec(memory_space=pltpu.HBM)] * 4
        + [pl.BlockSpec(memory_space=pl.ANY)],
        out_specs=[pl.BlockSpec(memory_space=pltpu.VMEM)] * 2,
        out_shape=[shape, shape],
        scratch_shapes=[
            pltpu.VMEM((width, hidden), jnp.bfloat16),
            pltpu.VMEM((width, hidden), jnp.bfloat16),
            pltpu.SMEM(gate_scale.shape, jnp.int32),
            pltpu.SMEM(up_scale.shape, jnp.int32),
            pltpu.SemaphoreType.DMA((2 + 2 * ctx_count,)),
        ],
        compiler_params=pltpu.CompilerParams(vmem_limit_bytes=20 * MIB),
        cost_estimate=pl.CostEstimate(
            flops=2 * width * hidden, bytes_accessed=8 * width * hidden, transcendentals=0
        ),
        name="dequant_in",
    )(my_exp, gate_scale, up_scale, gate_weight, up_weight, after)


def deq_down_kernel(ctx_count, exp_ref, scale_hbm, down_hbm, _, own_ref, give_ref, down_ref, scale_ref, sems):
    core = lax.bitwise_and(exp_ref[0], 1)
    rows, width = down_ref.shape
    cols = width // (2 * ctx_count)
    pairs = [(scale_hbm, scale_ref)]
    for step in range(ctx_count):
        at = pl.ds(step * 2 * cols, 2 * cols)
        pairs.append((down_hbm.at[0, :, at], down_ref.at[:, at]))
    copies = copy_all(sems, pairs)
    copies[0].wait()
    for step in range(ctx_count):
        copies[1 + step].wait()
        for out_ref, side in ((give_ref, 1 - core), (own_ref, core)):
            first = (2 * step + side) * (cols // WB)
            for j in range(cols // WB):
                col = pl.multiple_of((2 * step + side) * cols + j * WB, WB)
                for i in range(rows // WB):
                    factor = block_factor(scale_ref[i, 0, first + j], WB)
                    out_ref[pl.ds(i * WB, WB), pl.ds(step * cols + j * WB, WB)] = (
                        down_ref[pl.ds(i * WB, WB), pl.ds(col, WB)] * factor
                    )


def deq_down(my_exp, down_weight, down_scale, ctx_count, after):
    hidden, width = down_weight.shape[1:]
    shape = jax.ShapeDtypeStruct((hidden, width // 2), jnp.bfloat16)
    down_scale = jnp.transpose(down_scale, (1, 0, 2))
    return pl.pallas_call(
        functools.partial(deq_down_kernel, ctx_count),
        in_specs=[pl.BlockSpec(memory_space=pltpu.SMEM)]
        + [pl.BlockSpec(memory_space=pltpu.HBM)] * 2
        + [pl.BlockSpec(memory_space=pl.ANY)],
        out_specs=[pl.BlockSpec(memory_space=pltpu.VMEM)] * 2,
        out_shape=[shape, shape],
        scratch_shapes=[
            pltpu.VMEM((hidden, width), jnp.bfloat16),
            pltpu.SMEM(down_scale.shape, jnp.int32),
            pltpu.SemaphoreType.DMA((1 + ctx_count,)),
        ],
        compiler_params=pltpu.CompilerParams(vmem_limit_bytes=12 * MIB),
        cost_estimate=pl.CostEstimate(
            flops=width * hidden, bytes_accessed=4 * width * hidden, transcendentals=0
        ),
        name="dequant_down",
    )(my_exp, down_scale, down_weight, after)


def attend_kernel(plan, ctx_ref, exp_ref, order_ref, *refs):
    ctx_count, exp_count, tok, heads, piece_places = plan
    packed, refs = refs[:ctx_count], refs[ctx_count:]
    piece_refs, refs = refs[: 1 + bits_of(ctx_count)], refs[1 + bits_of(ctx_count) :]
    weight_ref, rest = refs[0], refs[2:]
    keep_ref, own_route_ref = rest[0:2]
    give_refs = rest[2 : 1 + exp_count]
    key_scr, value_scr, place_scr, att_scr = rest[1 + exp_count :]
    x_count = exp_count // 2
    span = packed[0].shape[0]
    positions = ctx_count * span
    my_ctx, my_exp = ctx_ref[0], exp_ref[0]
    my_x, my_core = lax.shift_right_logical(my_exp, 1), lax.bitwise_and(my_exp, 1)
    lane = lax.broadcasted_iota(jnp.int32, (8, positions), 1)
    places = lane % span
    for offset, ref in enumerate(packed):
        key_scr[pl.ds(offset * span, span), :] = ref[:, 0:HEAD_SIZE]
        value_scr[pl.ds(offset * span, span), :] = ref[:, HEAD_SIZE : 2 * HEAD_SIZE]
        base = order_ref[lax.bitwise_xor(my_ctx, offset)] * span
        places = places + jnp.where(lane // span == offset, base, 0)
    place_scr[...] = places
    scale = 1.0 / math.sqrt(HEAD_SIZE)
    for offset, ref in enumerate(packed):
        source = lax.bitwise_xor(my_ctx, offset)
        queries = jnp.concatenate(
            [ref[:, (h + 2) * HEAD_SIZE : (h + 3) * HEAD_SIZE] for h in range(heads)], axis=0
        )
        scores = lax.dot_general(
            queries, key_scr[...], (((1,), (1,)), ((), ())), preferred_element_type=jnp.float32
        )
        own_place = order_ref[source] * span + lax.broadcasted_iota(jnp.int32, (span, positions), 0)
        bias = jnp.where(place_scr[0:1, :] <= own_place, 0.0, -1e30)
        scores = scores.reshape(heads, span, positions) * scale + bias[None]
        largest = jnp.max(scores, axis=-1, keepdims=True)
        exps = jnp.exp(scores - largest)
        total = jnp.sum(exps, axis=-1, keepdims=True)
        mixed = jnp.dot(
            exps.astype(jnp.bfloat16).reshape(heads * span, positions),
            value_scr[...],
            preferred_element_type=jnp.float32,
        ).reshape(heads, span, HEAD_SIZE)
        mixed = (mixed / total).astype(jnp.bfloat16)
        for owner in range(exp_count):
            x_off = lax.bitwise_xor(my_x, owner // 2)
            row = pl.multiple_of(((x_off * ctx_count + source) * 2 + owner % 2) * tok, tok)
            for head in range(heads):
                att_scr[pl.ds(row, tok), pl.ds(head * HEAD_SIZE, HEAD_SIZE)] = mixed[
                    head, owner * tok : (owner + 1) * tok, :
                ]

    cols = weight_ref.shape[1] // 2
    per_x = 2 * ctx_count * tok
    first = (heads + 2) * HEAD_SIZE
    route_lane = lax.broadcasted_iota(jnp.int32, (tok, HEAD_SIZE), 1)
    for which in range(exp_count - 1, -1, -1):
        side = lax.bitwise_xor(my_core, which % 2)
        weight = weight_ref[:, pl.ds(pl.multiple_of(side * cols, cols), cols)]
        part = jnp.dot(
            att_scr[pl.ds(which // 2 * per_x, per_x), :], weight, preferred_element_type=jnp.float32
        )
        out_ref = give_refs[which - 1] if which else keep_ref
        out_ref[0:per_x, :] = part.astype(out_ref.dtype)
        if which < 2:
            for offset, (array, place) in enumerate(piece_places):
                row = (lax.bitwise_xor(my_ctx, offset) * 2 + my_core) * tok
                at = pl.ds(pl.multiple_of(row, tok), tok)
                piece = piece_refs[array][place, :, pl.ds(pl.multiple_of(side * cols, cols), cols)].astype(jnp.float32)
                out_ref[at, :] = (out_ref[at, :].astype(jnp.float32) + piece).astype(out_ref.dtype)
        expert = my_ctx * x_count + lax.bitwise_xor(my_x, which // 2)
        sides = [jnp.zeros((tok, HEAD_SIZE), jnp.float32)] * 2
        for offset, ref in enumerate(packed):
            for part_of in range(2):
                block = ref[part_of * tok : (part_of + 1) * tok, first:].astype(jnp.float32)
                column = jnp.sum(jnp.where(route_lane == expert, block, 0.0), axis=1, keepdims=True)
                sides[part_of] = sides[part_of] + jnp.where(
                    route_lane == lax.bitwise_xor(my_ctx, offset), column, 0.0
                )
        route_out, row = (give_refs[which - 1], per_x) if which else (own_route_ref, 0)
        for part_of, side in enumerate(sides):
            at = pl.ds(row + part_of * tok, tok)
            route_out[at, 0:HEAD_SIZE] = side.astype(jnp.bfloat16)
            if route_out.shape[1] > HEAD_SIZE:
                rest_shape = (tok, route_out.shape[1] - HEAD_SIZE)
                route_out[at, HEAD_SIZE:] = jnp.zeros(rest_shape, jnp.bfloat16)


def fill_rows(plan, ctx_ref, exp_ref, gain_ref, chunk_refs, offsets, rows_scr, groups):
    ctx_count, x_count = plan
    half = ctx_count // 2
    my_ctx = ctx_ref[0]
    my_core = lax.bitwise_and(exp_ref[0], 1)
    mine = lax.shift_right_logical(my_ctx, bits_of(half))
    rows, cols = chunk_refs[0].shape
    rows = rows // 2
    sums = {}
    for ref, (c_off, x_off) in zip(chunk_refs, offsets):
        source = lax.bitwise_xor(my_ctx, c_off)
        gain_at = pl.multiple_of((source * 2 + my_core) * cols, cols)
        gain = gain_ref[:, pl.ds(gain_at, cols)]
        col = pl.multiple_of(lax.bitwise_and(source, half - 1) * cols, cols)
        for place, group in enumerate(groups):
            side = mine if group == 1 else 1 - mine
            chunk = ref[pl.ds(pl.multiple_of(side * rows, rows), rows), :].astype(jnp.float32)
            row = (place * x_count + x_off) * rows
            rows_scr[pl.ds(row, rows), pl.ds(col, cols)] = (chunk * gain).astype(jnp.bfloat16)
            square = jnp.sum(chunk * chunk, axis=-1, keepdims=True)
            sums[row] = sums[row] + square if row in sums else square
    return sums


def experts_in_first(plan, offsets, ctx_ref, exp_ref, *refs):
    chunk_refs, (gain_ref, own_ref, other_ref, _, act_ref, square_ref, rows_scr) = refs[:-7], refs[-7:]
    half = plan[0] // 2
    sums = fill_rows(plan, ctx_ref, exp_ref, gain_ref, chunk_refs, offsets, rows_scr, (0, 1))
    for row, square in sums.items():
        square_ref[pl.ds(row, square.shape[0]), :] = square
    depth, width = rows_scr.shape[1], own_ref.shape[1]
    start = lax.shift_right_logical(ctx_ref[0], bits_of(half)) * depth
    at = pl.ds(pl.multiple_of(start, depth), depth)
    for place, ref in enumerate((own_ref, other_ref)):
        act_ref[:, place * width : (place + 1) * width] = jnp.dot(
            rows_scr[...], ref[at, :], preferred_element_type=jnp.float32
        )


def experts_in_second(plan, offsets, group, ctx_ref, exp_ref, *refs):
    chunk_refs, rest = refs[:-8], refs[-8:]
    gain_ref, own_ref, other_ref, first_ref, square_ref, _, act_ref, rows_scr = rest
    half = plan[0] // 2
    sums = fill_rows(plan, ctx_ref, exp_ref, gain_ref, chunk_refs, offsets, rows_scr, (group,))
    count, depth = rows_scr.shape
    width = own_ref.shape[1]
    lane = lax.broadcasted_iota(jnp.int32, (1, HEAD_SIZE), 1)
    for row, square in sums.items():
        rows = square.shape[0]
        square = square + square_ref[pl.ds(group * count + row, rows), :]
        high = square.astype(jnp.bfloat16).astype(jnp.float32)
        act_ref[pl.ds(row, rows), 2 * width :] = jnp.where(lane == 0, high, square - high).astype(
            jnp.bfloat16
        )
    start = (1 - lax.shift_right_logical(ctx_ref[0], bits_of(half))) * depth
    at = pl.ds(pl.multiple_of(start, depth), depth)
    for place, ref in enumerate((own_ref, other_ref)):
        cols = slice(place * width, (place + 1) * width)
        act = first_ref[group * count : (group + 1) * count, cols] + jnp.dot(
            rows_scr[...], ref[at, :], preferred_element_type=jnp.float32
        )
        act_ref[:, cols] = act.astype(jnp.bfloat16)


def experts_out_kernel(plan, group, slots, model_width, ctx_ref, exp_ref, act_ref, came_ref, *refs):
    ctx_count, exp_count, tok = plan
    x_count, half = exp_count // 2, ctx_count // 2
    route_refs = refs[:exp_count]
    own_ref, other_ref, _ = refs[exp_count : exp_count + 3]
    rest = refs[exp_count + 3 :]
    state_refs, rest = (rest[:ctx_count], rest[ctx_count:]) if group == 1 else ((), rest)
    out_refs, hidden_scr = rest[:-1], rest[-1]
    my_ctx = ctx_ref[0]
    my_core = lax.bitwise_and(exp_ref[0], 1)
    mine = lax.shift_right_logical(my_ctx, bits_of(half))
    first_ctx = (mine if group == 1 else 1 - mine) * half
    width = (act_ref.shape[1] - HEAD_SIZE) // 2
    hidden = width // 2
    lane = lax.broadcasted_iota(jnp.int32, (tok, HEAD_SIZE), 1)
    blocks = []
    for ref in route_refs:
        row = ref.shape[0] - 2 * tok
        both = ref[row : row + 2 * tok, 0:HEAD_SIZE].astype(jnp.float32)
        blocks.append(both[:tok] + both[tok:])
    columns = []
    for x_off in range(x_count):
        for low in range(half):
            for core in range(2):
                same, swapped = blocks[2 * x_off + core], blocks[2 * x_off + 1 - core]
                block = jnp.where(my_core == 0, same, swapped)
                picked = jnp.where(lane == first_ctx + low, block, 0.0)
                columns.append(jnp.sum(picked, axis=1, keepdims=True))
    route = jnp.concatenate(columns, axis=0)
    squares = act_ref[:, 2 * width :].astype(jnp.float32) + came_ref[:, 2 * width :].astype(jnp.float32)
    norm = lax.rsqrt((squares[:, 0:1] + squares[:, 1:2]) / model_width + 1e-06)
    scaled_route = norm * route
    for side in range(2):
        acts = act_ref[:, side * width : (side + 1) * width].astype(jnp.float32) + came_ref[
            :, (1 - side) * width : (2 - side) * width
        ].astype(jnp.float32)
        gate = acts[:, :hidden] * norm
        value = gate / (1.0 + jnp.exp(-gate)) * (acts[:, hidden:] * scaled_route)
        hidden_scr[:, side * hidden : (side + 1) * hidden] = value.astype(jnp.bfloat16)
    picked = []
    for c_off, x_off in slots:
        low = lax.bitwise_and(lax.bitwise_xor(my_ctx, c_off), half - 1)
        row = pl.multiple_of((x_off * half + low) * (2 * tok), 2 * tok)
        picked.append(hidden_scr[pl.ds(row, 2 * tok), :])
    picked = jnp.concatenate(picked, axis=0)
    out_cols = own_ref.shape[1]
    step = min(512, out_cols)
    for col in range(0, out_cols, step):
        at = pl.ds(col, step)
        out = jnp.dot(picked[:, :hidden], own_ref[:, at], preferred_element_type=jnp.float32)
        out = out + jnp.dot(picked[:, hidden:], other_ref[:, at], preferred_element_type=jnp.float32)
        for place, ref in enumerate(out_refs):
            ref[:, at] = out[place * 2 * tok : (place + 1) * 2 * tok, :].astype(ref.dtype)
    for slot, ref in zip(slots, out_refs):
        if slot == (0, 0):
            for c_off, state_ref in enumerate(state_refs):
                cols = state_ref.shape[1]
                at = pl.ds(pl.multiple_of(lax.bitwise_xor(my_ctx, c_off) * cols, cols), cols)
                own_row = pl.multiple_of(my_ctx * (2 * tok), 2 * tok)
                ref[:, at] = ref[:, at] + state_ref[pl.ds(own_row, 2 * tok), :].astype(jnp.float32)


def shards(
    residual,
    encoded_query_rows,
    quantized_key_rows,
    quantized_value_rows,
    key_block_exponent,
    value_block_exponent,
    block_order,
    out_weight,
    norm_gain,
    expert_ids,
    route_weight,
    gate_weight,
    gate_scale,
    up_weight,
    up_scale,
    down_weight,
    down_scale,
):
    f32, bf16 = jnp.float32, jnp.bfloat16
    vmem = pl.BlockSpec(memory_space=pltpu.VMEM)
    smem = pl.BlockSpec(memory_space=pltpu.SMEM)
    anywhere = pl.BlockSpec(memory_space=pl.ANY)
    span, query_width = encoded_query_rows.shape
    heads = query_width // HEAD_SIZE
    group = QUERY_HEADS // KEY_VALUE_HEADS
    ctx_count = lax.axis_size("ctx")
    exp_count = lax.axis_size("exp")
    x_count = exp_count // 2
    experts = ctx_count * x_count
    tok, model_width = residual.shape
    half_width = model_width // 2
    cols = half_width // ctx_count
    my_ctx = lax.axis_index("ctx").astype(jnp.int32).reshape(1)
    my_exp = lax.axis_index("exp").astype(jnp.int32).reshape(1)
    route = gather_route(ctx_count, x_count)

    hbm = pl.BlockSpec(memory_space=pltpu.HBM)
    piece_shape = jax.ShapeDtypeStruct((ctx_count // 2, tok, 2 * cols), bf16)
    packed, near, far = pl.pallas_call(
        functools.partial(pack_kernel, (heads, group)),
        in_specs=[smem] * 2 + [hbm] * 8,
        out_specs=[vmem] * 3,
        out_shape=[
            jax.ShapeDtypeStruct((span, query_width + 3 * HEAD_SIZE), bf16),
            piece_shape,
            piece_shape,
        ],
        scratch_shapes=[
            pltpu.VMEM(key_block_exponent.shape, jnp.int32),
            pltpu.VMEM(key_block_exponent.shape, jnp.int32),
            pltpu.VMEM((span, HEAD_SIZE), bf16),
            pltpu.VMEM((span, HEAD_SIZE), bf16),
            pltpu.VMEM((TOP, tok), jnp.int32),
            pltpu.VMEM((TOP, tok), f32),
            pltpu.SemaphoreType.DMA((7 + ctx_count,)),
        ],
        compiler_params=pltpu.CompilerParams(vmem_limit_bytes=8 * MIB),
        name="pack",
    )(
        my_ctx,
        my_exp,
        key_block_exponent,
        value_block_exponent,
        encoded_query_rows,
        quantized_key_rows,
        quantized_value_rows,
        jnp.transpose(expert_ids),
        jnp.transpose(route_weight),
        residual,
    )
    held = {(0, 0): packed}
    piece_arrays = [near]
    piece_at = {(0, offset): (0, offset) for offset in range(ctx_count // 2)}
    sending, send_keys = far, [(0, offset) for offset in range(ctx_count // 2, ctx_count)]
    stages = stages_of(gather_route(ctx_count, x_count, rows_only=True))
    for number, stage in enumerate(stages):
        came = [from_partner(held[source], axis, bit) for _, source, _, axis, bit in stage]
        piece_bit = bits_of(ctx_count) - 1 - number
        came.append(from_ctx(sending, 1 << piece_bit))
        if number == 0:
            in_own, in_give = deq_in(
                my_exp, gate_weight, gate_scale, up_weight, up_scale, ctx_count, packed
            )
            *came, in_own, in_give = together(*came, in_own, in_give)
        elif number == 1:
            in_other = from_offset(in_give, 1)
            down_own, down_give = deq_down(my_exp, down_weight, down_scale, ctx_count, came_first)
            *came, in_other, down_own, down_give = together(*came, in_other, down_own, down_give)
        elif number < len(stages) - 1:
            came = together(*came)
        came_first = came[0]
        held.update({target: array for (_, _, target, _, _), array in zip(stage, came)})
        piece_arrays.append(came[-1])
        for place, (source, target) in enumerate(send_keys):
            piece_at[source ^ 1 << piece_bit, target ^ 1 << piece_bit] = (number + 1, place)
        if piece_bit:
            send_keys = sorted(key for key in piece_at if key[1] == key[1] & ((2 << piece_bit - 1) - 1) and key[1] >> piece_bit - 1 & 1)
            sending = jnp.stack([piece_arrays[array][place] for array, place in map(piece_at.get, send_keys)])
    packed = [held[offset, 0] for offset in range(ctx_count)]
    piece_places = tuple(piece_at[offset, 0] for offset in range(ctx_count))
    down_other = from_offset(down_give, 1)

    positions = ctx_count * span
    per_x = 2 * ctx_count * tok
    keep, own_route, *gives = pl.pallas_call(
        functools.partial(attend_kernel, (ctx_count, exp_count, tok, heads, piece_places)),
        in_specs=[smem] * 3 + [vmem] * (ctx_count + len(piece_arrays) + 1) + [anywhere],
        out_specs=[vmem] * (1 + exp_count),
        out_shape=[
            jax.ShapeDtypeStruct((per_x, cols), f32),
            jax.ShapeDtypeStruct((2 * tok, HEAD_SIZE), bf16),
        ]
        + [jax.ShapeDtypeStruct((per_x + 2 * tok, cols), bf16)] * (exp_count - 1),
        scratch_shapes=[
            pltpu.VMEM((positions, HEAD_SIZE), bf16),
            pltpu.VMEM((positions, HEAD_SIZE), bf16),
            pltpu.VMEM((8, positions), jnp.int32),
            pltpu.VMEM((positions, query_width), bf16),
        ],
        compiler_params=pltpu.CompilerParams(vmem_limit_bytes=3 * ctx_count * MIB),
        cost_estimate=pl.CostEstimate(
            flops=4 * positions * positions * query_width + 4 * positions * query_width * cols,
            bytes_accessed=8 * MIB,
            transcendentals=heads * positions * positions,
        ),
        name="attend",
    )(my_ctx, my_exp, block_order, *packed, *piece_arrays, out_weight, down_other)

    gives = {offset: from_offset(gives[offset - 1], offset) for offset in reversed(range(1, exp_count))}
    gives = [gives[offset] for offset in range(1, exp_count)]
    state = keep
    for give in gives:
        state = state + give[:per_x].astype(f32)
    state = state.astype(bf16)

    chunks = {(0, 0): state}
    for stage in stages_of(route):
        came = [from_partner(chunks[source], axis, bit) for _, source, _, axis, bit in stage]
        if stage[-1] != route[-1]:
            came = together(*came)
        chunks.update({target: array for (_, _, target, _, _), array in zip(stage, came)})
    gain = norm_gain.reshape(1, model_width)
    rows = x_count * per_x
    in_width = in_own.shape[1]
    near = tuple(sorted(key for key in chunks if key[0] < ctx_count // 2))
    far = tuple(sorted(key for key in chunks if key[0] >= ctx_count // 2))
    first_act, first_square = pl.pallas_call(
        functools.partial(experts_in_first, (ctx_count, x_count), near),
        in_specs=[smem] * 2 + [vmem] * (len(near) + 3) + [anywhere],
        out_specs=[vmem] * 2,
        out_shape=[
            jax.ShapeDtypeStruct((rows, 2 * in_width), f32),
            jax.ShapeDtypeStruct((rows, 1), f32),
        ],
        scratch_shapes=[pltpu.VMEM((rows, half_width // 2), bf16)],
        compiler_params=pltpu.CompilerParams(vmem_limit_bytes=2 * ctx_count * MIB),
        cost_estimate=pl.CostEstimate(
            flops=2 * rows * half_width * in_width, bytes_accessed=8 * MIB, transcendentals=0
        ),
        name="experts_in_first",
    )(my_ctx, my_exp, *[chunks[key] for key in near], gain, in_own, in_other, down_give)
    acts = []
    for part in range(2):
        acts.append(
            pl.pallas_call(
                functools.partial(experts_in_second, (ctx_count, x_count), far, part),
                in_specs=[smem] * 2 + [vmem] * (len(far) + 5) + [anywhere],
                out_specs=vmem,
                out_shape=jax.ShapeDtypeStruct((rows // 2, 2 * in_width + HEAD_SIZE), bf16),
                scratch_shapes=[pltpu.VMEM((rows // 2, half_width // 2), bf16)],
                compiler_params=pltpu.CompilerParams(vmem_limit_bytes=2 * ctx_count * MIB),
                cost_estimate=pl.CostEstimate(
                    flops=rows * half_width * in_width, bytes_accessed=8 * MIB, transcendentals=0
                ),
                name="experts_in_second",
            )(
                my_ctx,
                my_exp,
                *[chunks[key] for key in far],
                gain,
                in_own,
                in_other,
                first_act,
                first_square,
                acts[0] if part else first_square,
            )
        )
    leaves = {key for key in chunks} - {source for _, source, _, _, _ in route}
    sums = {}
    for part in range(2):
        slots = near if part == 1 else far
        states = [chunks[offset, 0] for offset in range(ctx_count)] if part == 1 else []
        outs = pl.pallas_call(
            functools.partial(experts_out_kernel, (ctx_count, exp_count, tok), part, slots, model_width),
            in_specs=[smem] * 2 + [vmem] * (4 + exp_count) + [anywhere] + [vmem] * len(states),
            out_specs=[vmem] * len(slots),
            out_shape=[
                jax.ShapeDtypeStruct((2 * tok, half_width), bf16 if slot in leaves else f32)
                for slot in slots
            ],
            scratch_shapes=[pltpu.VMEM((rows // 2, in_width), bf16)],
            compiler_params=pltpu.CompilerParams(vmem_limit_bytes=2 * ctx_count * MIB),
            cost_estimate=pl.CostEstimate(
                flops=rows * half_width * in_width,
                bytes_accessed=8 * MIB,
                transcendentals=rows * in_width // 2,
            ),
            name="experts_out",
        )(
            my_ctx,
            my_exp,
            acts[part],
            from_offset(acts[part], 1),
            own_route,
            *gives,
            down_own,
            down_other,
            sums[slots_done[0]] if part else acts[1],
            *states,
        )
        slots_done = slots
        sums.update(zip(slots, outs))

    backward = stages_of(route)[::-1]
    for number, stage in enumerate(backward):
        came = [from_partner(sums[target].astype(bf16), axis, bit) for _, _, target, axis, bit in stage]
        if number < len(backward) - 1:
            waiting = [key for key in near if key in sums] if number == 0 else []
            values = together(*came, *[sums[key] for key in waiting])
            came = values[: len(came)]
            sums.update(zip(waiting, values[len(came) :]))
        for (_, source, target, _, _), array in zip(stage, came):
            sums[source] = sums[source] + array.astype(f32)
    total = sums[0, 0]
    core = lax.bitwise_and(my_exp[0], 1)
    mine = jnp.where(core == 0, total[:tok], total[tok:]).astype(bf16)
    came = from_offset(jnp.where(core == 0, total[tok:], total[:tok]).astype(bf16), 1)
    mine = mine.reshape(tok, ctx_count, 1, cols)
    came = came.reshape(tok, ctx_count, 1, cols)
    result = jnp.where(core == 0, jnp.concatenate([mine, came], axis=2), jnp.concatenate([came, mine], axis=2))
    return result.reshape(tok, model_width)


def solution(mesh):
    return jax.shard_map(
        shards,
        mesh=mesh,
        in_specs=(
            P(("dp", "ctx", "exp"), None),
            P(("dp", "ctx"), "exp"),
            P(("dp", "ctx"), None),
            P(("dp", "ctx"), None),
            P(("dp", "ctx"), None),
            P(("dp", "ctx"), None),
            P(),
            P("exp", "ctx"),
            P(),
            P(("dp", "ctx", "exp"), None),
            P(("dp", "ctx", "exp"), None),
            P(("ctx", "exp"), None, None),
            P(("ctx", "exp"), None, None),
            P(("ctx", "exp"), None, None),
            P(("ctx", "exp"), None, None),
            P(("ctx", "exp"), None, None),
            P(("ctx", "exp"), None, None),
        ),
        out_specs=P(("dp", "ctx", "exp"), None),
        check_vma=False,
    )
```

```python
import functools
import math

import jax
import jax.numpy as jnp
from jax import lax
from jax.experimental import pallas as pl
from jax.experimental.pallas import tpu as pltpu
from jax.sharding import PartitionSpec as P

QUERY_HEADS = 32
KEY_VALUE_HEADS = 4
HEAD_SIZE = 128
TOP = 8
SCALE_POSITIONS = 64
WB = 128
MIB = 1 << 20


def bits_of(count):
    return count.bit_length() - 1


def from_offset(array, offset):
    return lax.ppermute(array, "exp", [(i, i ^ offset) for i in range(lax.axis_size("exp"))])


def from_ctx(array, offset):
    return lax.ppermute(array, "ctx", [(i, i ^ offset) for i in range(lax.axis_size("ctx"))])


def moved(offset, move):
    return (offset[0] ^ move[0], offset[1] ^ move[1])


def gather_route(ctx_count, x_count, rows_only=False):
    transfers, arrival, places = [], {(0, 0): 0}, {(0, 0): ((0, 0), (0, 0))}

    def go(source, moves, delay=0):
        reached = tuple(moved(place, (c, e >> 1)) for place, (c, e) in zip(places[source], moves))
        target = reached[0]
        arrival[target], places[target] = arrival[source] + 1 + delay, reached
        transfers.append((arrival[target], source, target, moves))
        return target

    bits = bits_of(ctx_count)
    y_move = (1, 0)
    if rows_only:
        shared, steps = range(bits - 1, 1, -1), [(2, 0), y_move]
    else:
        shared, steps = range(bits - 1, 0, -1), [(0, 2 << bit) for bit in range(bits_of(x_count))] + [y_move]
    pairs = list(zip(steps, reversed(steps)))
    for bit in shared:
        for source in list(arrival):
            go(source, ((1 << bit, 0),) * 2)
    for number, first in enumerate(sorted(arrival)):
        held = [first]
        for moves in pairs:
            tuned = (ctx_count, x_count) == (8, 2) and not rows_only and number in (0, 2)
            held = held + [go(source, moves, 1 if tuned and source != first else 0) for source in held]
    return sorted(transfers, key=lambda transfer: transfer[0]), places


def follow(array, moves):
    exp_count = lax.axis_size("exp")
    pairs = []
    for c in range(lax.axis_size("ctx")):
        for e in range(exp_count):
            far = moved((c, e), moves[e % 2])
            pairs.append((far[0] * exp_count + far[1], c * exp_count + e))
    return lax.ppermute(array, ("ctx", "exp"), pairs)


def by_core(core, place, part):
    first, second = place[0][part], place[1][part]
    return first if first == second else jnp.where(core == 0, first, second)


def stages_of(route):
    return [[t for t in route if t[0] == stage] for stage in sorted({t[0] for t in route})]


def together(*values):
    return lax.optimization_barrier(values)


def block_factor(exponent, width):
    factor = jnp.where(exponent < 0, 0.5, jnp.where(exponent > 0, 2.0, 1.0))
    return jnp.full((1, width), factor, jnp.float32).astype(jnp.bfloat16)


def in_hbm(*arrays):
    return [pltpu.with_memory_space_constraint(array, pltpu.HBM) for array in arrays]


def copy_all(sems, pairs):
    copies = [pltpu.make_async_copy(src, dst, sems.at[i]) for i, (src, dst) in enumerate(pairs)]
    for copy in copies:
        copy.start()
    return copies


def pack_kernel(plan, ctx_ref, exp_ref, key_scale_hbm, value_scale_hbm, query_hbm, key_hbm, value_hbm, ids_hbm,
                route_hbm, residual_hbm, packed_ref, near_ref, far_ref, key_scale_ref, value_scale_ref,
                key_ref, value_ref, ids_ref, route_ref, sems):
    heads, group = plan
    span, width = query_hbm.shape
    half, tok, cols = near_ref.shape
    my_ctx, my_exp = ctx_ref[0], exp_ref[0]
    kv_head = my_exp * heads // group
    at = pl.ds(pl.multiple_of(kv_head * HEAD_SIZE, HEAD_SIZE), HEAD_SIZE)
    pairs = [
        (key_scale_hbm, key_scale_ref),
        (value_scale_hbm, value_scale_ref),
        (key_hbm.at[:, at], key_ref),
        (value_hbm.at[:, at], value_ref),
        (ids_hbm, ids_ref),
        (route_hbm, route_ref),
        (query_hbm, packed_ref.at[:, 2 * HEAD_SIZE : 2 * HEAD_SIZE + width]),
    ]
    for offset in range(2 * half):
        col = pl.multiple_of(lax.bitwise_xor(my_ctx, offset) * cols, cols)
        pairs.append(
            (residual_hbm.at[:, pl.ds(col, cols)], (near_ref if offset < half else far_ref).at[offset % half])
        )
    copies = copy_all(sems, pairs)
    for copy in copies[:6]:
        copy.wait()
    lane = lax.broadcasted_iota(jnp.int32, key_scale_ref.shape, 1)
    blocks = key_scale_ref.shape[0]
    for place, (ref, scale_ref) in enumerate(((key_ref, key_scale_ref), (value_ref, value_scale_ref))):
        exponent = scale_ref[...]
        factor = jnp.where(
            exponent < -1, 0.25, jnp.where(exponent < 0, 0.5, jnp.where(exponent < 1, 1.0, 2.0))
        )
        factor = jnp.sum(jnp.where(lane == kv_head, factor, 0.0), axis=1, keepdims=True)
        for block in range(blocks):
            rows = pl.ds(block * (span // blocks), span // blocks)
            scaled = ref[rows, :].astype(jnp.float32) * factor[block : block + 1, :]
            packed_ref[rows, pl.ds(place * HEAD_SIZE, HEAD_SIZE)] = scaled.astype(jnp.bfloat16)
    number = lax.broadcasted_iota(jnp.int32, (128, tok), 0)
    dense = jnp.zeros((128, tok), jnp.float32)
    for k in range(TOP):
        dense = dense + jnp.where(ids_ref[k : k + 1, :] == number, route_ref[k : k + 1, :], 0.0)
    dense = jnp.concatenate([dense, jnp.zeros((128, 128 - tok), jnp.float32)], axis=1)
    dense = jnp.transpose(dense)[:tok, :]
    high = dense.astype(jnp.bfloat16)
    packed_ref[0:tok, 2 * HEAD_SIZE + width :] = high
    packed_ref[tok : 2 * tok, 2 * HEAD_SIZE + width :] = (dense - high.astype(jnp.float32)).astype(
        jnp.bfloat16
    )
    packed_ref[2 * tok :, 2 * HEAD_SIZE + width :] = jnp.zeros((span - 2 * tok, 128), jnp.bfloat16)
    for copy in copies[6:]:
        copy.wait()


def deq_in_kernel(ctx_count, exp_ref, gate_scale_hbm, up_scale_hbm, gate_hbm, up_hbm, _, own_ref, give_ref,
                  gate_ref, up_ref, gate_scale_ref, up_scale_ref, sems):
    core = lax.bitwise_and(exp_ref[0], 1)
    width, cols = gate_ref.shape
    rows = width // (2 * ctx_count)
    pairs = [(gate_scale_hbm, gate_scale_ref), (up_scale_hbm, up_scale_ref)]
    for step in range(ctx_count):
        at = pl.ds(step * 2 * rows, 2 * rows)
        pairs += [(gate_hbm.at[0, at], gate_ref.at[at]), (up_hbm.at[0, at], up_ref.at[at])]
    copies = copy_all(sems, pairs)
    for copy in copies[:2]:
        copy.wait()
    for step in range(ctx_count):
        for half, (ref, scale_ref) in enumerate(((gate_ref, gate_scale_ref), (up_ref, up_scale_ref))):
            copies[2 + 2 * step + half].wait()
            for out_ref, side in ((give_ref, 1 - core), (own_ref, core)):
                first = (2 * step + side) * (rows // WB)
                for i in range(rows // WB):
                    row = pl.multiple_of((2 * step + side) * rows + i * WB, WB)
                    for j in range(cols // WB):
                        factor = block_factor(scale_ref[j, 0, first + i], WB)
                        out_ref[pl.ds(step * rows + i * WB, WB), pl.ds(half * cols + j * WB, WB)] = (
                            ref[pl.ds(row, WB), pl.ds(j * WB, WB)] * factor
                        )


def deq_in(my_exp, gate_weight, gate_scale, up_weight, up_scale, ctx_count, after):
    width, hidden = gate_weight.shape[1:]
    shape = jax.ShapeDtypeStruct((width // 2, 2 * hidden), jnp.bfloat16)
    gate_scale = jnp.transpose(gate_scale, (2, 0, 1))
    up_scale = jnp.transpose(up_scale, (2, 0, 1))
    return pl.pallas_call(
        functools.partial(deq_in_kernel, ctx_count),
        in_specs=[pl.BlockSpec(memory_space=pltpu.SMEM)]
        + [pl.BlockSpec(memory_space=pltpu.HBM)] * 4
        + [pl.BlockSpec(memory_space=pl.ANY)],
        out_specs=[pl.BlockSpec(memory_space=pltpu.VMEM)] * 2,
        out_shape=[shape, shape],
        scratch_shapes=[
            pltpu.VMEM((width, hidden), jnp.bfloat16),
            pltpu.VMEM((width, hidden), jnp.bfloat16),
            pltpu.SMEM(gate_scale.shape, jnp.int32),
            pltpu.SMEM(up_scale.shape, jnp.int32),
            pltpu.SemaphoreType.DMA((2 + 2 * ctx_count,)),
        ],
        compiler_params=pltpu.CompilerParams(vmem_limit_bytes=20 * MIB),
        cost_estimate=pl.CostEstimate(
            flops=2 * width * hidden, bytes_accessed=8 * width * hidden, transcendentals=0
        ),
        name="dequant_in",
    )(my_exp, *in_hbm(gate_scale, up_scale, gate_weight, up_weight), after)


def deq_down_kernel(ctx_count, exp_ref, scale_hbm, down_hbm, _, own_ref, give_ref, down_ref, scale_ref, sems):
    core = lax.bitwise_and(exp_ref[0], 1)
    rows, width = down_ref.shape
    cols = width // (2 * ctx_count)
    pairs = [(scale_hbm, scale_ref)]
    for step in range(ctx_count):
        at = pl.ds(step * 2 * cols, 2 * cols)
        pairs.append((down_hbm.at[0, :, at], down_ref.at[:, at]))
    copies = copy_all(sems, pairs)
    copies[0].wait()
    for step in range(ctx_count):
        copies[1 + step].wait()
        for out_ref, side in ((give_ref, 1 - core), (own_ref, core)):
            first = (2 * step + side) * (cols // WB)
            for j in range(cols // WB):
                col = pl.multiple_of((2 * step + side) * cols + j * WB, WB)
                for i in range(rows // WB):
                    factor = block_factor(scale_ref[i, 0, first + j], WB)
                    out_ref[pl.ds(i * WB, WB), pl.ds(step * cols + j * WB, WB)] = (
                        down_ref[pl.ds(i * WB, WB), pl.ds(col, WB)] * factor
                    )


def deq_down(my_exp, down_weight, down_scale, ctx_count, after):
    hidden, width = down_weight.shape[1:]
    shape = jax.ShapeDtypeStruct((hidden, width // 2), jnp.bfloat16)
    down_scale = jnp.transpose(down_scale, (1, 0, 2))
    return pl.pallas_call(
        functools.partial(deq_down_kernel, ctx_count),
        in_specs=[pl.BlockSpec(memory_space=pltpu.SMEM)]
        + [pl.BlockSpec(memory_space=pltpu.HBM)] * 2
        + [pl.BlockSpec(memory_space=pl.ANY)],
        out_specs=[pl.BlockSpec(memory_space=pltpu.VMEM)] * 2,
        out_shape=[shape, shape],
        scratch_shapes=[
            pltpu.VMEM((hidden, width), jnp.bfloat16),
            pltpu.SMEM(down_scale.shape, jnp.int32),
            pltpu.SemaphoreType.DMA((1 + ctx_count,)),
        ],
        compiler_params=pltpu.CompilerParams(vmem_limit_bytes=12 * MIB),
        cost_estimate=pl.CostEstimate(
            flops=width * hidden, bytes_accessed=4 * width * hidden, transcendentals=0
        ),
        name="dequant_down",
    )(my_exp, *in_hbm(down_scale, down_weight), after)


def attend_kernel(plan, ctx_ref, exp_ref, order_ref, *refs):
    ctx_count, exp_count, tok, heads, piece_places, places_of = plan
    packed, refs = refs[:ctx_count], refs[ctx_count:]
    piece_refs, refs = refs[: 1 + bits_of(ctx_count)], refs[1 + bits_of(ctx_count) :]
    weight_ref, rest = refs[0], refs[2:]
    keep_ref, own_route_ref = rest[0:2]
    give_refs = rest[2 : 1 + exp_count]
    key_scr, value_scr, place_scr, att_scr = rest[1 + exp_count :]
    x_count = exp_count // 2
    span = packed[0].shape[0]
    positions = ctx_count * span
    my_ctx, my_exp = ctx_ref[0], exp_ref[0]
    my_x, my_core = lax.shift_right_logical(my_exp, 1), lax.bitwise_and(my_exp, 1)
    lane = lax.broadcasted_iota(jnp.int32, (8, positions), 1)
    places = lane % span
    for offset, ref in enumerate(packed):
        key_scr[pl.ds(offset * span, span), :] = ref[:, 0:HEAD_SIZE]
        value_scr[pl.ds(offset * span, span), :] = ref[:, HEAD_SIZE : 2 * HEAD_SIZE]
        base = order_ref[lax.bitwise_xor(my_ctx, by_core(my_core, places_of[offset], 0))] * span
        places = places + jnp.where(lane // span == offset, base, 0)
    place_scr[...] = places
    scale = 1.0 / math.sqrt(HEAD_SIZE)
    for offset, ref in enumerate(packed):
        source = lax.bitwise_xor(my_ctx, by_core(my_core, places_of[offset], 0))
        queries = jnp.concatenate(
            [ref[:, (h + 2) * HEAD_SIZE : (h + 3) * HEAD_SIZE] for h in range(heads)], axis=0
        )
        scores = lax.dot_general(
            queries, key_scr[...], (((1,), (1,)), ((), ())), preferred_element_type=jnp.float32
        )
        own_place = order_ref[source] * span + lax.broadcasted_iota(jnp.int32, (span, positions), 0)
        bias = jnp.where(place_scr[0:1, :] <= own_place, 0.0, -1e30)
        scores = scores.reshape(heads, span, positions) * scale + bias[None]
        largest = jnp.max(scores, axis=-1, keepdims=True)
        exps = jnp.exp(scores - largest)
        total = jnp.sum(exps, axis=-1, keepdims=True)
        mixed = jnp.dot(
            exps.astype(jnp.bfloat16).reshape(heads * span, positions),
            value_scr[...],
            preferred_element_type=jnp.float32,
        ).reshape(heads, span, HEAD_SIZE)
        mixed = (mixed / total).astype(jnp.bfloat16)
        for owner in range(exp_count):
            x_off = lax.bitwise_xor(my_x, owner // 2)
            row = pl.multiple_of(((x_off * ctx_count + source) * 2 + owner % 2) * tok, tok)
            for head in range(heads):
                att_scr[pl.ds(row, tok), pl.ds(head * HEAD_SIZE, HEAD_SIZE)] = mixed[
                    head, owner * tok : (owner + 1) * tok, :
                ]

    cols = weight_ref.shape[1] // 2
    per_x = 2 * ctx_count * tok
    first = (heads + 2) * HEAD_SIZE
    route_lane = lax.broadcasted_iota(jnp.int32, (tok, HEAD_SIZE), 1)
    for which in range(exp_count - 1, -1, -1):
        side = lax.bitwise_xor(my_core, which % 2)
        weight = weight_ref[:, pl.ds(pl.multiple_of(side * cols, cols), cols)]
        part = jnp.dot(
            att_scr[pl.ds(which // 2 * per_x, per_x), :], weight, preferred_element_type=jnp.float32
        )
        out_ref = give_refs[which - 1] if which else keep_ref
        out_ref[0:per_x, :] = part.astype(out_ref.dtype)
        if which < 2:
            for offset, (array, place) in enumerate(piece_places):
                row = (lax.bitwise_xor(my_ctx, offset) * 2 + my_core) * tok
                at = pl.ds(pl.multiple_of(row, tok), tok)
                piece = piece_refs[array][place, :, pl.ds(pl.multiple_of(side * cols, cols), cols)].astype(jnp.float32)
                out_ref[at, :] = (out_ref[at, :].astype(jnp.float32) + piece).astype(out_ref.dtype)
        expert = my_ctx * x_count + lax.bitwise_xor(my_x, which // 2)
        sides = [jnp.zeros((tok, HEAD_SIZE), jnp.float32)] * 2
        for offset, ref in enumerate(packed):
            source = lax.bitwise_xor(my_ctx, by_core(my_core, places_of[offset], 0))
            for part_of in range(2):
                block = ref[part_of * tok : (part_of + 1) * tok, first:].astype(jnp.float32)
                column = jnp.sum(jnp.where(route_lane == expert, block, 0.0), axis=1, keepdims=True)
                sides[part_of] = sides[part_of] + jnp.where(route_lane == source, column, 0.0)
        route_out, row = (give_refs[which - 1], per_x) if which else (own_route_ref, 0)
        for part_of, side in enumerate(sides):
            at = pl.ds(row + part_of * tok, tok)
            route_out[at, 0:HEAD_SIZE] = side.astype(jnp.bfloat16)
            if route_out.shape[1] > HEAD_SIZE:
                rest_shape = (tok, route_out.shape[1] - HEAD_SIZE)
                route_out[at, HEAD_SIZE:] = jnp.zeros(rest_shape, jnp.bfloat16)


def fill_rows(plan, ctx_ref, exp_ref, gain_ref, chunk_refs, places, rows_scr, square_ref, groups):
    ctx_count, x_count = plan
    half = ctx_count // 2
    my_ctx = ctx_ref[0]
    my_core = lax.bitwise_and(exp_ref[0], 1)
    mine = lax.shift_right_logical(my_ctx, bits_of(half))
    rows, cols = chunk_refs[0].shape
    rows = rows // 2
    for ref, place_of in zip(chunk_refs, places):
        source = lax.bitwise_xor(my_ctx, by_core(my_core, place_of, 0))
        x_off = by_core(my_core, place_of, 1)
        gain_at = pl.multiple_of((source * 2 + my_core) * cols, cols)
        gain = gain_ref[:, pl.ds(gain_at, cols)]
        col = pl.multiple_of(lax.bitwise_and(source, half - 1) * cols, cols)
        for place, group in enumerate(groups):
            side = mine if group == 1 else 1 - mine
            chunk = ref[pl.ds(pl.multiple_of(side * rows, rows), rows), :].astype(jnp.float32)
            at = pl.ds(pl.multiple_of((place * x_count + x_off) * rows, rows), rows)
            rows_scr[at, pl.ds(col, cols)] = (chunk * gain).astype(jnp.bfloat16)
            square_ref[at, :] = square_ref[at, :] + jnp.sum(chunk * chunk, axis=-1, keepdims=True)


def experts_in_first(plan, offsets, ctx_ref, exp_ref, *refs):
    chunk_refs, (gain_ref, own_ref, other_ref, _, act_ref, square_ref, rows_scr) = refs[:-7], refs[-7:]
    half = plan[0] // 2
    square_ref[...] = jnp.zeros(square_ref.shape, jnp.float32)
    fill_rows(plan, ctx_ref, exp_ref, gain_ref, chunk_refs, offsets, rows_scr, square_ref, (0, 1))
    depth, width = rows_scr.shape[1], own_ref.shape[1]
    start = lax.shift_right_logical(ctx_ref[0], bits_of(half)) * depth
    at = pl.ds(pl.multiple_of(start, depth), depth)
    for place, ref in enumerate((own_ref, other_ref)):
        act_ref[:, place * width : (place + 1) * width] = jnp.dot(
            rows_scr[...], ref[at, :], preferred_element_type=jnp.float32
        )


def experts_in_second(plan, offsets, group, ctx_ref, exp_ref, *refs):
    chunk_refs, rest = refs[:-9], refs[-9:]
    gain_ref, own_ref, other_ref, first_ref, square_ref, _, act_ref, rows_scr, sum_scr = rest
    half = plan[0] // 2
    count, depth = rows_scr.shape
    width = own_ref.shape[1]
    sum_scr[...] = square_ref[group * count : (group + 1) * count, :]
    fill_rows(plan, ctx_ref, exp_ref, gain_ref, chunk_refs, offsets, rows_scr, sum_scr, (group,))
    lane = lax.broadcasted_iota(jnp.int32, (1, HEAD_SIZE), 1)
    square = sum_scr[...]
    high = square.astype(jnp.bfloat16).astype(jnp.float32)
    act_ref[:, 2 * width :] = jnp.where(lane == 0, high, square - high).astype(jnp.bfloat16)
    start = (1 - lax.shift_right_logical(ctx_ref[0], bits_of(half))) * depth
    at = pl.ds(pl.multiple_of(start, depth), depth)
    for place, ref in enumerate((own_ref, other_ref)):
        cols = slice(place * width, (place + 1) * width)
        act = first_ref[group * count : (group + 1) * count, cols] + jnp.dot(
            rows_scr[...], ref[at, :], preferred_element_type=jnp.float32
        )
        act_ref[:, cols] = act.astype(jnp.bfloat16)


def experts_out_kernel(plan, group, places, state_at, model_width, ctx_ref, exp_ref, act_ref, came_ref, *refs):
    ctx_count, exp_count, tok = plan
    x_count, half = exp_count // 2, ctx_count // 2
    route_refs = refs[:exp_count]
    own_ref, other_ref, _ = refs[exp_count : exp_count + 3]
    rest = refs[exp_count + 3 :]
    state_count = 1 + max((max(pair) for pair in state_at), default=-1)
    state_refs, rest = rest[:state_count], rest[state_count:]
    out_refs, hidden_scr = rest[:-1], rest[-1]
    my_ctx = ctx_ref[0]
    my_core = lax.bitwise_and(exp_ref[0], 1)
    mine = lax.shift_right_logical(my_ctx, bits_of(half))
    first_ctx = (mine if group == 1 else 1 - mine) * half
    width = (act_ref.shape[1] - HEAD_SIZE) // 2
    hidden = width // 2
    lane = lax.broadcasted_iota(jnp.int32, (tok, HEAD_SIZE), 1)
    blocks = []
    for ref in route_refs:
        row = ref.shape[0] - 2 * tok
        both = ref[row : row + 2 * tok, 0:HEAD_SIZE].astype(jnp.float32)
        blocks.append(both[:tok] + both[tok:])
    columns = []
    for x_off in range(x_count):
        for low in range(half):
            for core in range(2):
                same, swapped = blocks[2 * x_off + core], blocks[2 * x_off + 1 - core]
                block = jnp.where(my_core == 0, same, swapped)
                picked = jnp.where(lane == first_ctx + low, block, 0.0)
                columns.append(jnp.sum(picked, axis=1, keepdims=True))
    route = jnp.concatenate(columns, axis=0)
    squares = act_ref[:, 2 * width :].astype(jnp.float32) + came_ref[:, 2 * width :].astype(jnp.float32)
    norm = lax.rsqrt((squares[:, 0:1] + squares[:, 1:2]) / model_width + 1e-06)
    scaled_route = norm * route
    for side in range(2):
        acts = act_ref[:, side * width : (side + 1) * width].astype(jnp.float32) + came_ref[
            :, (1 - side) * width : (2 - side) * width
        ].astype(jnp.float32)
        gate = acts[:, :hidden] * norm
        value = gate / (1.0 + jnp.exp(-gate)) * (acts[:, hidden:] * scaled_route)
        hidden_scr[:, side * hidden : (side + 1) * hidden] = value.astype(jnp.bfloat16)
    picked = []
    for place in places:
        x_off = by_core(my_core, place, 1)
        low = lax.bitwise_and(lax.bitwise_xor(my_ctx, by_core(my_core, place, 0)), half - 1)
        row = pl.multiple_of((x_off * half + low) * (2 * tok), 2 * tok)
        picked.append(hidden_scr[pl.ds(row, 2 * tok), :])
    picked = jnp.concatenate(picked, axis=0)
    out_cols = own_ref.shape[1]
    step = min(512, out_cols)
    for col in range(0, out_cols, step):
        at = pl.ds(col, step)
        out = jnp.dot(picked[:, :hidden], own_ref[:, at], preferred_element_type=jnp.float32)
        out = out + jnp.dot(picked[:, hidden:], other_ref[:, at], preferred_element_type=jnp.float32)
        for place, ref in enumerate(out_refs):
            ref[:, at] = out[place * 2 * tok : (place + 1) * 2 * tok, :].astype(ref.dtype)
    for place, ref in zip(places, out_refs):
        if place[0] == (0, 0):
            own_rows = pl.ds(pl.multiple_of(my_ctx * (2 * tok), 2 * tok), 2 * tok)
            for c_off, (first, second) in enumerate(state_at):
                cols = state_refs[first].shape[1]
                at = pl.ds(pl.multiple_of(lax.bitwise_xor(my_ctx, c_off) * cols, cols), cols)
                state = state_refs[first][own_rows, :].astype(jnp.float32)
                if second != first:
                    other = state_refs[second][own_rows, :].astype(jnp.float32)
                    state = jnp.where(my_core == 0, state, other)
                ref[:, at] = ref[:, at] + state


def shards(
    residual,
    encoded_query_rows,
    quantized_key_rows,
    quantized_value_rows,
    key_block_exponent,
    value_block_exponent,
    block_order,
    out_weight,
    norm_gain,
    expert_ids,
    route_weight,
    gate_weight,
    gate_scale,
    up_weight,
    up_scale,
    down_weight,
    down_scale,
):
    f32, bf16 = jnp.float32, jnp.bfloat16
    vmem = pl.BlockSpec(memory_space=pltpu.VMEM)
    smem = pl.BlockSpec(memory_space=pltpu.SMEM)
    anywhere = pl.BlockSpec(memory_space=pl.ANY)
    span, query_width = encoded_query_rows.shape
    heads = query_width // HEAD_SIZE
    group = QUERY_HEADS // KEY_VALUE_HEADS
    ctx_count = lax.axis_size("ctx")
    exp_count = lax.axis_size("exp")
    x_count = exp_count // 2
    experts = ctx_count * x_count
    tok, model_width = residual.shape
    half_width = model_width // 2
    cols = half_width // ctx_count
    my_ctx = lax.axis_index("ctx").astype(jnp.int32).reshape(1)
    my_exp = lax.axis_index("exp").astype(jnp.int32).reshape(1)
    route, places = gather_route(ctx_count, x_count)

    hbm = pl.BlockSpec(memory_space=pltpu.HBM)
    piece_shape = jax.ShapeDtypeStruct((ctx_count // 2, tok, 2 * cols), bf16)
    packed, near, far = pl.pallas_call(
        functools.partial(pack_kernel, (heads, group)),
        in_specs=[smem] * 2 + [hbm] * 8,
        out_specs=[vmem] * 3,
        out_shape=[
            jax.ShapeDtypeStruct((span, query_width + 3 * HEAD_SIZE), bf16),
            piece_shape,
            piece_shape,
        ],
        scratch_shapes=[
            pltpu.VMEM(key_block_exponent.shape, jnp.int32),
            pltpu.VMEM(key_block_exponent.shape, jnp.int32),
            pltpu.VMEM((span, HEAD_SIZE), bf16),
            pltpu.VMEM((span, HEAD_SIZE), bf16),
            pltpu.VMEM((TOP, tok), jnp.int32),
            pltpu.VMEM((TOP, tok), f32),
            pltpu.SemaphoreType.DMA((7 + ctx_count,)),
        ],
        compiler_params=pltpu.CompilerParams(vmem_limit_bytes=8 * MIB),
        name="pack",
    )(
        my_ctx,
        my_exp,
        *in_hbm(
            key_block_exponent,
            value_block_exponent,
            encoded_query_rows,
            quantized_key_rows,
            quantized_value_rows,
            jnp.transpose(expert_ids),
            jnp.transpose(route_weight),
            residual,
        ),
    )
    held = {(0, 0): packed}
    piece_arrays = [near]
    piece_at = {(0, offset): (0, offset) for offset in range(ctx_count // 2)}
    sending, send_keys = far, [(0, offset) for offset in range(ctx_count // 2, ctx_count)]
    row_route, row_places = gather_route(ctx_count, x_count, rows_only=True)
    stages = stages_of(row_route)
    for number, stage in enumerate(stages):
        came = [follow(held[source], moves) for _, source, _, moves in stage]
        piece_bit = bits_of(ctx_count) - 1 - number
        came.append(from_ctx(sending, 1 << piece_bit))
        if number == 0:
            in_own, in_give = deq_in(
                my_exp, gate_weight, gate_scale, up_weight, up_scale, ctx_count, packed
            )
            *came, in_own, in_give = together(*came, in_own, in_give)
        elif number == 1:
            in_other = from_offset(in_give, 1)
            down_own, down_give = deq_down(my_exp, down_weight, down_scale, ctx_count, came_first)
            *came, in_other, down_own, down_give = together(*came, in_other, down_own, down_give)
        elif number < len(stages) - 1:
            came = together(*came)
        came_first = came[0]
        held.update({target: array for (_, _, target, _), array in zip(stage, came)})
        piece_arrays.append(came[-1])
        for place, (source, target) in enumerate(send_keys):
            piece_at[source ^ 1 << piece_bit, target ^ 1 << piece_bit] = (number + 1, place)
        if piece_bit:
            below = 1 << piece_bit
            send_keys = sorted(key for key in piece_at if below // 2 <= key[1] < below)
            sending = jnp.stack([piece_arrays[array][place] for array, place in map(piece_at.get, send_keys)])
    packed = [held[offset, 0] for offset in range(ctx_count)]
    attend_places = tuple(row_places[offset, 0] for offset in range(ctx_count))
    piece_places = tuple(piece_at[offset, 0] for offset in range(ctx_count))
    down_other = from_offset(down_give, 1)

    positions = ctx_count * span
    per_x = 2 * ctx_count * tok
    keep, own_route, *gives = pl.pallas_call(
        functools.partial(attend_kernel, (ctx_count, exp_count, tok, heads, piece_places, attend_places)),
        in_specs=[smem] * 3 + [vmem] * (ctx_count + len(piece_arrays) + 1) + [anywhere],
        out_specs=[vmem] * (1 + exp_count),
        out_shape=[
            jax.ShapeDtypeStruct((per_x, cols), f32),
            jax.ShapeDtypeStruct((2 * tok, HEAD_SIZE), bf16),
        ]
        + [jax.ShapeDtypeStruct((per_x + 2 * tok, cols), bf16)] * (exp_count - 1),
        scratch_shapes=[
            pltpu.VMEM((positions, HEAD_SIZE), bf16),
            pltpu.VMEM((positions, HEAD_SIZE), bf16),
            pltpu.VMEM((8, positions), jnp.int32),
            pltpu.VMEM((positions, query_width), bf16),
        ],
        compiler_params=pltpu.CompilerParams(vmem_limit_bytes=3 * ctx_count * MIB),
        cost_estimate=pl.CostEstimate(
            flops=4 * positions * positions * query_width + 4 * positions * query_width * cols,
            bytes_accessed=8 * MIB,
            transcendentals=heads * positions * positions,
        ),
        name="attend",
    )(my_ctx, my_exp, block_order, *packed, *piece_arrays, out_weight, down_other)

    gives = {offset: from_offset(gives[offset - 1], offset) for offset in reversed(range(1, exp_count))}
    gives = [gives[offset] for offset in range(1, exp_count)]
    state = keep
    for give in gives:
        state = state + give[:per_x].astype(f32)
    state = state.astype(bf16)

    chunks = {(0, 0): state}
    for stage in stages_of(route):
        came = [follow(chunks[source], moves) for _, source, _, moves in stage]
        if stage[-1] != route[-1]:
            came = together(*came)
        chunks.update({target: array for (_, _, target, _), array in zip(stage, came)})
    gain = norm_gain.reshape(1, model_width)
    rows = x_count * per_x
    in_width = in_own.shape[1]
    near = tuple(sorted(key for key in chunks if key[0] < ctx_count // 2))
    far = tuple(sorted(key for key in chunks if key[0] >= ctx_count // 2))
    near_places, far_places = (tuple(places[key] for key in keys) for keys in (near, far))
    first_act, first_square = pl.pallas_call(
        functools.partial(experts_in_first, (ctx_count, x_count), near_places),
        in_specs=[smem] * 2 + [vmem] * (len(near) + 3) + [anywhere],
        out_specs=[vmem] * 2,
        out_shape=[
            jax.ShapeDtypeStruct((rows, 2 * in_width), f32),
            jax.ShapeDtypeStruct((rows, 1), f32),
        ],
        scratch_shapes=[pltpu.VMEM((rows, half_width // 2), bf16)],
        compiler_params=pltpu.CompilerParams(vmem_limit_bytes=2 * ctx_count * MIB),
        cost_estimate=pl.CostEstimate(
            flops=2 * rows * half_width * in_width, bytes_accessed=8 * MIB, transcendentals=0
        ),
        name="experts_in_first",
    )(my_ctx, my_exp, *[chunks[key] for key in near], gain, in_own, in_other, down_give)
    acts = []
    for part in range(2):
        acts.append(
            pl.pallas_call(
                functools.partial(experts_in_second, (ctx_count, x_count), far_places, part),
                in_specs=[smem] * 2 + [vmem] * (len(far) + 5) + [anywhere],
                out_specs=vmem,
                out_shape=jax.ShapeDtypeStruct((rows // 2, 2 * in_width + HEAD_SIZE), bf16),
                scratch_shapes=[
                    pltpu.VMEM((rows // 2, half_width // 2), bf16),
                    pltpu.VMEM((rows // 2, 1), f32),
                ],
                compiler_params=pltpu.CompilerParams(vmem_limit_bytes=2 * ctx_count * MIB),
                cost_estimate=pl.CostEstimate(
                    flops=rows * half_width * in_width, bytes_accessed=8 * MIB, transcendentals=0
                ),
                name="experts_in_second",
            )(
                my_ctx,
                my_exp,
                *[chunks[key] for key in far],
                gain,
                in_own,
                in_other,
                first_act,
                first_square,
                acts[0] if part else first_square,
            )
        )
    leaves = set(chunks) - {source for _, source, _, _ in route}
    sums = {}
    for part in range(2):
        slots = near if part == 1 else far
        state_keys, state_at = [], []
        for offset in range(ctx_count) if part == 1 else ():
            pair = [next(key for key in chunks if places[key][core] == (offset, 0)) for core in range(2)]
            state_keys += [key for key in pair if key not in state_keys]
            state_at.append(tuple(state_keys.index(key) for key in pair))
        states = [chunks[key] for key in state_keys]
        outs = pl.pallas_call(
            functools.partial(
                experts_out_kernel,
                (ctx_count, exp_count, tok),
                part,
                tuple(places[key] for key in slots),
                tuple(state_at),
                model_width,
            ),
            in_specs=[smem] * 2 + [vmem] * (4 + exp_count) + [anywhere] + [vmem] * len(states),
            out_specs=[vmem] * len(slots),
            out_shape=[
                jax.ShapeDtypeStruct((2 * tok, half_width), bf16 if slot in leaves else f32)
                for slot in slots
            ],
            scratch_shapes=[pltpu.VMEM((rows // 2, in_width), bf16)],
            compiler_params=pltpu.CompilerParams(vmem_limit_bytes=2 * ctx_count * MIB),
            cost_estimate=pl.CostEstimate(
                flops=rows * half_width * in_width,
                bytes_accessed=8 * MIB,
                transcendentals=rows * in_width // 2,
            ),
            name="experts_out",
        )(
            my_ctx,
            my_exp,
            acts[part],
            from_offset(acts[part], 1),
            own_route,
            *gives,
            down_own,
            down_other,
            sums[slots_done[0]] if part else acts[1],
            *states,
        )
        slots_done = slots
        sums.update(zip(slots, outs))

    backward = stages_of(route)[::-1]
    for number, stage in enumerate(backward):
        came = [follow(sums[target].astype(bf16), moves) for _, _, target, moves in stage]
        if number < len(backward) - 1:
            waiting = [key for key in near if key in sums] if number == 0 else []
            values = together(*came, *[sums[key] for key in waiting])
            came = values[: len(came)]
            sums.update(zip(waiting, values[len(came) :]))
        for (_, source, target, _), array in zip(stage, came):
            sums[source] = sums[source] + array.astype(f32)
    total = sums[0, 0]
    core = lax.bitwise_and(my_exp[0], 1)
    mine = jnp.where(core == 0, total[:tok], total[tok:]).astype(bf16)
    came = from_offset(jnp.where(core == 0, total[tok:], total[:tok]).astype(bf16), 1)
    mine = mine.reshape(tok, ctx_count, 1, cols)
    came = came.reshape(tok, ctx_count, 1, cols)
    result = jnp.where(core == 0, jnp.concatenate([mine, came], axis=2), jnp.concatenate([came, mine], axis=2))
    return result.reshape(tok, model_width)


def solution(mesh):
    return jax.shard_map(
        shards,
        mesh=mesh,
        in_specs=(
            P(("dp", "ctx", "exp"), None),
            P(("dp", "ctx"), "exp"),
            P(("dp", "ctx"), None),
            P(("dp", "ctx"), None),
            P(("dp", "ctx"), None),
            P(("dp", "ctx"), None),
            P(),
            P("exp", "ctx"),
            P(),
            P(("dp", "ctx", "exp"), None),
            P(("dp", "ctx", "exp"), None),
            P(("ctx", "exp"), None, None),
            P(("ctx", "exp"), None, None),
            P(("ctx", "exp"), None, None),
            P(("ctx", "exp"), None, None),
            P(("ctx", "exp"), None, None),
            P(("ctx", "exp"), None, None),
        ),
        out_specs=P(("dp", "ctx", "exp"), None),
        check_vma=False,
    )
```

```python
import functools
import math

import jax
import jax.numpy as jnp
from jax import lax
from jax.experimental import pallas as pl
from jax.experimental.pallas import tpu as pltpu
from jax.sharding import PartitionSpec as P

QUERY_HEADS = 32
KEY_VALUE_HEADS = 4
HEAD_SIZE = 128
TOP = 8
SCALE_POSITIONS = 64
WB = 128
MIB = 1 << 20


def bits_of(count):
    return count.bit_length() - 1


def from_offset(array, offset):
    return lax.ppermute(array, "exp", [(i, i ^ offset) for i in range(lax.axis_size("exp"))])


def from_ctx(array, offset):
    return lax.ppermute(array, "ctx", [(i, i ^ offset) for i in range(lax.axis_size("ctx"))])


def moved(offset, move):
    return (offset[0] ^ move[0], offset[1] ^ move[1])


def gather_route(ctx_count, x_count, rows_only=False):
    transfers, arrival, places = [], {(0, 0): 0}, {(0, 0): ((0, 0), (0, 0))}

    def go(source, moves, delay=0):
        reached = tuple(moved(place, (c, e >> 1)) for place, (c, e) in zip(places[source], moves))
        target = reached[0]
        arrival[target], places[target] = arrival[source] + 1 + delay, reached
        transfers.append((arrival[target], source, target, moves))
        return target

    bits = bits_of(ctx_count)
    y_move = (1, 0)
    if rows_only:
        shared, steps = range(bits - 1, 1, -1), [(2, 0), y_move]
    else:
        shared, steps = range(bits - 1, 0, -1), [(0, 2 << bit) for bit in range(bits_of(x_count))] + [y_move]
    pairs = list(zip(steps, reversed(steps)))
    for bit in shared:
        for source in list(arrival):
            go(source, ((1 << bit, 0),) * 2)
    for number, first in enumerate(sorted(arrival)):
        held = [first]
        for moves in pairs:
            tuned = (ctx_count, x_count) == (8, 2) and not rows_only and number == 0
            held = held + [go(source, moves, 1 if tuned and source != first else 0) for source in held]
    return sorted(transfers, key=lambda transfer: transfer[0]), places


def follow(array, moves):
    exp_count = lax.axis_size("exp")
    pairs = []
    for c in range(lax.axis_size("ctx")):
        for e in range(exp_count):
            far = moved((c, e), moves[e % 2])
            pairs.append((far[0] * exp_count + far[1], c * exp_count + e))
    return lax.ppermute(array, ("ctx", "exp"), pairs)


def by_core(core, place, part):
    first, second = place[0][part], place[1][part]
    return first if first == second else jnp.where(core == 0, first, second)


def stages_of(route):
    stages, arrays = [], [((0, 0),)]
    for stage in sorted({transfer[0] for transfer in route}):
        sends = []
        for moves in sorted({t[3] for t in route if t[0] == stage}):
            left = {source: target for number, source, target, way in route if (number, way) == (stage, moves)}
            groups = [group for group in arrays if len(group) > 1 and all(key in left for key in group)]
            rest = tuple(sorted(key for key in left if not any(key in group for group in groups)))
            for group in groups + [rest] * bool(rest):
                sends.append((moves, group, tuple(left[key] for key in group)))
        arrays = arrays + [send[2] for send in sends]
        stages.append(sends)
    return stages


def spread(block, stages, beside=None):
    arrays, at, joined = [block], {(0, 0): (0, 0)}, {}
    rows = block.shape[0]
    for number, sends in enumerate(stages):
        came = []
        for moves, group, _ in sends:
            first, row = at[group[0]]
            whole = row == 0 and arrays[first].shape[0] == len(group) * rows
            if whole and all(at[key] == (first, place * rows) for place, key in enumerate(group)):
                joined[group] = arrays[first]
            elif group not in joined:
                parts = [arrays[at[key][0]][at[key][1] : at[key][1] + rows] for key in group]
                joined[group] = jnp.concatenate(parts, axis=0)
            came.append(follow(joined[group], moves))
        came = beside(number, came) if beside else (together(*came) if number < len(stages) - 1 else came)
        for (_, _, targets), array in zip(sends, came):
            at.update({key: (len(arrays), place * rows) for place, key in enumerate(targets)})
            arrays.append(array)
    return arrays, at


def together(*values):
    return lax.optimization_barrier(values)


def block_factor(exponent, width):
    factor = jnp.where(exponent < 0, 0.5, jnp.where(exponent > 0, 2.0, 1.0))
    return jnp.full((1, width), factor, jnp.float32).astype(jnp.bfloat16)


def in_hbm(*arrays):
    return [pltpu.with_memory_space_constraint(array, pltpu.HBM) for array in arrays]


def copy_all(sems, pairs):
    copies = [pltpu.make_async_copy(src, dst, sems.at[i]) for i, (src, dst) in enumerate(pairs)]
    for copy in copies:
        copy.start()
    return copies


def pack_kernel(plan, ctx_ref, exp_ref, key_scale_hbm, value_scale_hbm, query_hbm, key_hbm, value_hbm, ids_hbm,
                route_hbm, residual_hbm, packed_ref, near_ref, far_ref, key_scale_ref, value_scale_ref,
                key_ref, value_ref, ids_ref, route_ref, sems):
    heads, group, piece_places = plan
    span, width = query_hbm.shape
    half, tok, cols = near_ref.shape
    my_ctx, my_exp = ctx_ref[0], exp_ref[0]
    kv_head = my_exp * heads // group
    at = pl.ds(pl.multiple_of(kv_head * HEAD_SIZE, HEAD_SIZE), HEAD_SIZE)
    pairs = [
        (key_scale_hbm, key_scale_ref),
        (value_scale_hbm, value_scale_ref),
        (key_hbm.at[:, at], key_ref),
        (value_hbm.at[:, at], value_ref),
        (ids_hbm, ids_ref),
        (route_hbm, route_ref),
        (query_hbm, packed_ref.at[:, 2 * HEAD_SIZE : 2 * HEAD_SIZE + width]),
    ]
    core = lax.bitwise_and(my_exp, 1)
    for ref, places in zip((near_ref, far_ref), piece_places):
        for number, place in enumerate(places):
            col = pl.multiple_of(lax.bitwise_xor(my_ctx, by_core(core, place, 0)) * cols, cols)
            pairs.append((residual_hbm.at[:, pl.ds(col, cols)], ref.at[number]))
    copies = copy_all(sems, pairs)
    for copy in copies[:6]:
        copy.wait()
    lane = lax.broadcasted_iota(jnp.int32, key_scale_ref.shape, 1)
    blocks = key_scale_ref.shape[0]
    for place, (ref, scale_ref) in enumerate(((key_ref, key_scale_ref), (value_ref, value_scale_ref))):
        exponent = scale_ref[...]
        factor = jnp.where(
            exponent < -1, 0.25, jnp.where(exponent < 0, 0.5, jnp.where(exponent < 1, 1.0, 2.0))
        )
        factor = jnp.sum(jnp.where(lane == kv_head, factor, 0.0), axis=1, keepdims=True)
        for block in range(blocks):
            rows = pl.ds(block * (span // blocks), span // blocks)
            scaled = ref[rows, :].astype(jnp.float32) * factor[block : block + 1, :]
            packed_ref[rows, pl.ds(place * HEAD_SIZE, HEAD_SIZE)] = scaled.astype(jnp.bfloat16)
    number = lax.broadcasted_iota(jnp.int32, (128, tok), 0)
    dense = jnp.zeros((128, tok), jnp.float32)
    for k in range(TOP):
        dense = dense + jnp.where(ids_ref[k : k + 1, :] == number, route_ref[k : k + 1, :], 0.0)
    dense = jnp.concatenate([dense, jnp.zeros((128, 128 - tok), jnp.float32)], axis=1)
    dense = jnp.transpose(dense)[:tok, :]
    high = dense.astype(jnp.bfloat16)
    packed_ref[0:tok, 2 * HEAD_SIZE + width :] = high
    packed_ref[tok : 2 * tok, 2 * HEAD_SIZE + width :] = (dense - high.astype(jnp.float32)).astype(
        jnp.bfloat16
    )
    packed_ref[2 * tok :, 2 * HEAD_SIZE + width :] = jnp.zeros((span - 2 * tok, 128), jnp.bfloat16)
    for copy in copies[6:]:
        copy.wait()


def deq_in_kernel(ctx_count, exp_ref, gate_scale_hbm, up_scale_hbm, gate_hbm, up_hbm, _, own_ref, give_ref,
                  gate_ref, up_ref, gate_scale_ref, up_scale_ref, sems):
    core = lax.bitwise_and(exp_ref[0], 1)
    width, cols = gate_ref.shape
    rows = width // (2 * ctx_count)
    pairs = [(gate_scale_hbm, gate_scale_ref), (up_scale_hbm, up_scale_ref)]
    for step in range(ctx_count):
        at = pl.ds(step * 2 * rows, 2 * rows)
        pairs += [(gate_hbm.at[0, at], gate_ref.at[at]), (up_hbm.at[0, at], up_ref.at[at])]
    copies = copy_all(sems, pairs)
    for copy in copies[:2]:
        copy.wait()
    for step in range(ctx_count):
        for half, (ref, scale_ref) in enumerate(((gate_ref, gate_scale_ref), (up_ref, up_scale_ref))):
            copies[2 + 2 * step + half].wait()
            for out_ref, side in ((give_ref, 1 - core), (own_ref, core)):
                first = (2 * step + side) * (rows // WB)
                for i in range(rows // WB):
                    row = pl.multiple_of((2 * step + side) * rows + i * WB, WB)
                    for j in range(cols // WB):
                        factor = block_factor(scale_ref[j, 0, first + i], WB)
                        out_ref[pl.ds(step * rows + i * WB, WB), pl.ds(half * cols + j * WB, WB)] = (
                            ref[pl.ds(row, WB), pl.ds(j * WB, WB)] * factor
                        )


def deq_in(my_exp, gate_weight, gate_scale, up_weight, up_scale, ctx_count, after):
    width, hidden = gate_weight.shape[1:]
    shape = jax.ShapeDtypeStruct((width // 2, 2 * hidden), jnp.bfloat16)
    gate_scale = jnp.transpose(gate_scale, (2, 0, 1))
    up_scale = jnp.transpose(up_scale, (2, 0, 1))
    return pl.pallas_call(
        functools.partial(deq_in_kernel, ctx_count),
        in_specs=[pl.BlockSpec(memory_space=pltpu.SMEM)]
        + [pl.BlockSpec(memory_space=pltpu.HBM)] * 4
        + [pl.BlockSpec(memory_space=pl.ANY)],
        out_specs=[pl.BlockSpec(memory_space=pltpu.VMEM)] * 2,
        out_shape=[shape, shape],
        scratch_shapes=[
            pltpu.VMEM((width, hidden), jnp.bfloat16),
            pltpu.VMEM((width, hidden), jnp.bfloat16),
            pltpu.SMEM(gate_scale.shape, jnp.int32),
            pltpu.SMEM(up_scale.shape, jnp.int32),
            pltpu.SemaphoreType.DMA((2 + 2 * ctx_count,)),
        ],
        compiler_params=pltpu.CompilerParams(vmem_limit_bytes=20 * MIB),
        cost_estimate=pl.CostEstimate(
            flops=2 * width * hidden, bytes_accessed=8 * width * hidden, transcendentals=0
        ),
        name="dequant_in",
    )(my_exp, *in_hbm(gate_scale, up_scale, gate_weight, up_weight), after)


def deq_down_kernel(ctx_count, exp_ref, scale_hbm, down_hbm, _, own_ref, give_ref, down_ref, scale_ref, sems):
    core = lax.bitwise_and(exp_ref[0], 1)
    rows, width = down_ref.shape
    cols = width // (2 * ctx_count)
    pairs = [(scale_hbm, scale_ref)]
    for step in range(ctx_count):
        at = pl.ds(step * 2 * cols, 2 * cols)
        pairs.append((down_hbm.at[0, :, at], down_ref.at[:, at]))
    copies = copy_all(sems, pairs)
    copies[0].wait()
    for step in range(ctx_count):
        copies[1 + step].wait()
        for out_ref, side in ((give_ref, 1 - core), (own_ref, core)):
            first = (2 * step + side) * (cols // WB)
            for j in range(cols // WB):
                col = pl.multiple_of((2 * step + side) * cols + j * WB, WB)
                for i in range(rows // WB):
                    factor = block_factor(scale_ref[i, 0, first + j], WB)
                    out_ref[pl.ds(i * WB, WB), pl.ds(step * cols + j * WB, WB)] = (
                        down_ref[pl.ds(i * WB, WB), pl.ds(col, WB)] * factor
                    )


def deq_down(my_exp, down_weight, down_scale, ctx_count, after):
    hidden, width = down_weight.shape[1:]
    shape = jax.ShapeDtypeStruct((hidden, width // 2), jnp.bfloat16)
    down_scale = jnp.transpose(down_scale, (1, 0, 2))
    return pl.pallas_call(
        functools.partial(deq_down_kernel, ctx_count),
        in_specs=[pl.BlockSpec(memory_space=pltpu.SMEM)]
        + [pl.BlockSpec(memory_space=pltpu.HBM)] * 2
        + [pl.BlockSpec(memory_space=pl.ANY)],
        out_specs=[pl.BlockSpec(memory_space=pltpu.VMEM)] * 2,
        out_shape=[shape, shape],
        scratch_shapes=[
            pltpu.VMEM((hidden, width), jnp.bfloat16),
            pltpu.SMEM(down_scale.shape, jnp.int32),
            pltpu.SemaphoreType.DMA((1 + ctx_count,)),
        ],
        compiler_params=pltpu.CompilerParams(vmem_limit_bytes=12 * MIB),
        cost_estimate=pl.CostEstimate(
            flops=width * hidden, bytes_accessed=4 * width * hidden, transcendentals=0
        ),
        name="dequant_down",
    )(my_exp, *in_hbm(down_scale, down_weight), after)


def attend_kernel(plan, ctx_ref, exp_ref, order_ref, *refs):
    ctx_count, exp_count, tok, heads, piece_places, attend_at = plan
    packed_at, places_of = [at for at, _ in attend_at], [place for _, place in attend_at]
    array_count = 1 + max(array for array, _ in packed_at)
    span = exp_count * tok
    packed_refs, refs = refs[:array_count], refs[array_count:]
    packed = []
    for array, row in packed_at:
        packed.append(packed_refs[array].at[pl.ds(row, span)])
    piece_refs, refs = refs[: 1 + bits_of(ctx_count)], refs[1 + bits_of(ctx_count) :]
    weight_ref, rest = refs[0], refs[2:]
    x_count = exp_count // 2
    keep_refs, (give_ref, own_route_ref) = rest[:x_count], rest[x_count : x_count + 2]
    key_scr, value_scr, place_scr, att_scr = rest[x_count + 2 :]
    positions = ctx_count * span
    my_ctx, my_exp = ctx_ref[0], exp_ref[0]
    my_x, my_core = lax.shift_right_logical(my_exp, 1), lax.bitwise_and(my_exp, 1)
    lane = lax.broadcasted_iota(jnp.int32, (8, positions), 1)
    places = lane % span
    for offset, ref in enumerate(packed):
        key_scr[pl.ds(offset * span, span), :] = ref[:, 0:HEAD_SIZE]
        value_scr[pl.ds(offset * span, span), :] = ref[:, HEAD_SIZE : 2 * HEAD_SIZE]
        base = order_ref[lax.bitwise_xor(my_ctx, by_core(my_core, places_of[offset], 0))] * span
        places = places + jnp.where(lane // span == offset, base, 0)
    place_scr[...] = places
    scale = 1.0 / math.sqrt(HEAD_SIZE)
    for offset, ref in enumerate(packed):
        source = lax.bitwise_xor(my_ctx, by_core(my_core, places_of[offset], 0))
        queries = jnp.concatenate(
            [ref[:, (h + 2) * HEAD_SIZE : (h + 3) * HEAD_SIZE] for h in range(heads)], axis=0
        )
        scores = lax.dot_general(
            queries, key_scr[...], (((1,), (1,)), ((), ())), preferred_element_type=jnp.float32
        )
        own_place = order_ref[source] * span + lax.broadcasted_iota(jnp.int32, (span, positions), 0)
        bias = jnp.where(place_scr[0:1, :] <= own_place, 0.0, -1e30)
        scores = scores.reshape(heads, span, positions) * scale + bias[None]
        largest = jnp.max(scores, axis=-1, keepdims=True)
        exps = jnp.exp(scores - largest)
        total = jnp.sum(exps, axis=-1, keepdims=True)
        mixed = jnp.dot(
            exps.astype(jnp.bfloat16).reshape(heads * span, positions),
            value_scr[...],
            preferred_element_type=jnp.float32,
        ).reshape(heads, span, HEAD_SIZE)
        mixed = (mixed / total).astype(jnp.bfloat16)
        for owner in range(exp_count):
            x_off = lax.bitwise_xor(my_x, owner // 2)
            row = pl.multiple_of(((x_off * ctx_count + source) * 2 + owner % 2) * tok, tok)
            for head in range(heads):
                att_scr[pl.ds(row, tok), pl.ds(head * HEAD_SIZE, HEAD_SIZE)] = mixed[
                    head, owner * tok : (owner + 1) * tok, :
                ]

    cols = weight_ref.shape[1] // 2
    per_x = 2 * ctx_count * tok
    first = (heads + 2) * HEAD_SIZE
    route_lane = lax.broadcasted_iota(jnp.int32, (tok, HEAD_SIZE), 1)
    route_base = x_count * per_x
    for x_off in range(x_count):
        rows = pl.ds(x_off * per_x, per_x)
        for which in (1, 0):
            side = lax.bitwise_xor(my_core, which)
            weight = weight_ref[:, pl.ds(pl.multiple_of(side * cols, cols), cols)]
            part = jnp.dot(att_scr[rows, :], weight, preferred_element_type=jnp.float32)
            out_ref = give_ref if which else keep_refs[x_off]
            out_ref[pl.ds(x_off * per_x if which else 0, per_x), :] = part.astype(out_ref.dtype)
            if x_off == 0:
                for (array, place), place_of in zip(piece_places, places_of):
                    source = lax.bitwise_xor(my_ctx, by_core(my_core, place_of, 0))
                    at = pl.ds(pl.multiple_of((source * 2 + my_core) * tok, tok), tok)
                    piece = piece_refs[array][place, :, pl.ds(pl.multiple_of(side * cols, cols), cols)]
                    value = out_ref[at, :].astype(jnp.float32) + piece.astype(jnp.float32)
                    out_ref[at, :] = value.astype(out_ref.dtype)
        expert = my_ctx * x_count + lax.bitwise_xor(my_x, x_off)
        sides = [jnp.zeros((tok, HEAD_SIZE), jnp.float32)] * 2
        for offset, ref in enumerate(packed):
            source = lax.bitwise_xor(my_ctx, by_core(my_core, places_of[offset], 0))
            for part_of in range(2):
                block = ref[part_of * tok : (part_of + 1) * tok, first:].astype(jnp.float32)
                column = jnp.sum(jnp.where(route_lane == expert, block, 0.0), axis=1, keepdims=True)
                sides[part_of] = sides[part_of] + jnp.where(route_lane == source, column, 0.0)
        for part_of, side in enumerate(sides):
            row = (2 * x_off + part_of) * tok
            for ref, base in ((give_ref, route_base), (own_route_ref, 0)):
                at = pl.ds(base + row, tok)
                ref[at, 0:HEAD_SIZE] = side.astype(jnp.bfloat16)
                if cols > HEAD_SIZE:
                    ref[at, HEAD_SIZE:] = jnp.zeros((tok, cols - HEAD_SIZE), jnp.bfloat16)


def fill_rows(plan, ctx_ref, exp_ref, gain_ref, chunk_refs, places, rows_scr, square_ref, groups):
    ctx_count, x_count, tok = plan
    half = ctx_count // 2
    my_ctx = ctx_ref[0]
    my_core = lax.bitwise_and(exp_ref[0], 1)
    mine = lax.shift_right_logical(my_ctx, bits_of(half))
    cols = chunk_refs[0].shape[1]
    rows = ctx_count * tok
    for (array, first_row), place_of in places:
        ref = chunk_refs[array]
        source = lax.bitwise_xor(my_ctx, by_core(my_core, place_of, 0))
        x_off = by_core(my_core, place_of, 1)
        gain_at = pl.multiple_of((source * 2 + my_core) * cols, cols)
        gain = gain_ref[:, pl.ds(gain_at, cols)]
        col = pl.multiple_of(lax.bitwise_and(source, half - 1) * cols, cols)
        for place, group in enumerate(groups):
            side = mine if group == 1 else 1 - mine
            chunk_at = pl.ds(pl.multiple_of(first_row + side * rows, rows), rows)
            chunk = ref[chunk_at, :].astype(jnp.float32)
            at = pl.ds(pl.multiple_of((place * x_count + x_off) * rows, rows), rows)
            rows_scr[at, pl.ds(col, cols)] = (chunk * gain).astype(jnp.bfloat16)
            square_ref[at, :] = square_ref[at, :] + jnp.sum(chunk * chunk, axis=-1, keepdims=True)


def experts_in_first(plan, offsets, ctx_ref, exp_ref, *refs):
    chunk_refs, (gain_ref, own_ref, other_ref, _, act_ref, square_ref, rows_scr) = refs[:-7], refs[-7:]
    half = plan[0] // 2
    square_ref[...] = jnp.zeros(square_ref.shape, jnp.float32)
    fill_rows(plan, ctx_ref, exp_ref, gain_ref, chunk_refs, offsets, rows_scr, square_ref, (0, 1))
    depth, width = rows_scr.shape[1], own_ref.shape[1]
    start = lax.shift_right_logical(ctx_ref[0], bits_of(half)) * depth
    at = pl.ds(pl.multiple_of(start, depth), depth)
    for place, ref in enumerate((own_ref, other_ref)):
        act_ref[:, place * width : (place + 1) * width] = jnp.dot(
            rows_scr[...], ref[at, :], preferred_element_type=jnp.float32
        )


def experts_in_second(plan, offsets, group, ctx_ref, exp_ref, *refs):
    chunk_refs, rest = refs[:-9], refs[-9:]
    gain_ref, own_ref, other_ref, first_ref, square_ref, _, act_ref, rows_scr, sum_scr = rest
    half = plan[0] // 2
    count, depth = rows_scr.shape
    width = own_ref.shape[1]
    sum_scr[...] = square_ref[group * count : (group + 1) * count, :]
    fill_rows(plan, ctx_ref, exp_ref, gain_ref, chunk_refs, offsets, rows_scr, sum_scr, (group,))
    lane = lax.broadcasted_iota(jnp.int32, (1, HEAD_SIZE), 1)
    square = sum_scr[...]
    high = square.astype(jnp.bfloat16).astype(jnp.float32)
    act_ref[:, 2 * width :] = jnp.where(lane == 0, high, square - high).astype(jnp.bfloat16)
    start = (1 - lax.shift_right_logical(ctx_ref[0], bits_of(half))) * depth
    at = pl.ds(pl.multiple_of(start, depth), depth)
    for place, ref in enumerate((own_ref, other_ref)):
        cols = slice(place * width, (place + 1) * width)
        act = first_ref[group * count : (group + 1) * count, cols] + jnp.dot(
            rows_scr[...], ref[at, :], preferred_element_type=jnp.float32
        )
        act_ref[:, cols] = act.astype(jnp.bfloat16)


def experts_out_kernel(plan, group, places, state_at, route_at, model_width, ctx_ref, exp_ref, act_ref, came_ref, *refs):
    ctx_count, exp_count, tok = plan
    x_count, half = exp_count // 2, ctx_count // 2
    route_refs, refs = refs[: x_count + 1], refs[x_count + 1 :]
    (own_ref, other_ref, _), rest = refs[:3], refs[3:]
    state_count = 1 + max((array for pair in state_at for array, _ in pair), default=-1)
    state_refs, rest = rest[:state_count], rest[state_count:]
    out_refs, hidden_scr = rest[:-1], rest[-1]
    my_ctx = ctx_ref[0]
    my_core = lax.bitwise_and(exp_ref[0], 1)
    mine = lax.shift_right_logical(my_ctx, bits_of(half))
    first_ctx = (mine if group == 1 else 1 - mine) * half
    width = (act_ref.shape[1] - HEAD_SIZE) // 2
    hidden = width // 2
    lane = lax.broadcasted_iota(jnp.int32, (tok, HEAD_SIZE), 1)
    blocks = []
    for array, row in route_at:
        both = route_refs[array][row : row + 2 * tok, 0:HEAD_SIZE].astype(jnp.float32)
        blocks.append(both[:tok] + both[tok:])
    columns = []
    for x_off in range(x_count):
        for low in range(half):
            for core in range(2):
                same, swapped = blocks[2 * x_off + core], blocks[2 * x_off + 1 - core]
                block = jnp.where(my_core == 0, same, swapped)
                picked = jnp.where(lane == first_ctx + low, block, 0.0)
                columns.append(jnp.sum(picked, axis=1, keepdims=True))
    route = jnp.concatenate(columns, axis=0)
    squares = act_ref[:, 2 * width :].astype(jnp.float32) + came_ref[:, 2 * width :].astype(jnp.float32)
    norm = lax.rsqrt((squares[:, 0:1] + squares[:, 1:2]) / model_width + 1e-06)
    scaled_route = norm * route
    for side in range(2):
        acts = act_ref[:, side * width : (side + 1) * width].astype(jnp.float32) + came_ref[
            :, (1 - side) * width : (2 - side) * width
        ].astype(jnp.float32)
        gate = acts[:, :hidden] * norm
        value = gate / (1.0 + jnp.exp(-gate)) * (acts[:, hidden:] * scaled_route)
        hidden_scr[:, side * hidden : (side + 1) * hidden] = value.astype(jnp.bfloat16)
    picked = []
    for place in places:
        x_off = by_core(my_core, place, 1)
        low = lax.bitwise_and(lax.bitwise_xor(my_ctx, by_core(my_core, place, 0)), half - 1)
        row = pl.multiple_of((x_off * half + low) * (2 * tok), 2 * tok)
        picked.append(hidden_scr[pl.ds(row, 2 * tok), :])
    picked = jnp.concatenate(picked, axis=0)
    out_cols = own_ref.shape[1]
    step = min(512, out_cols)
    for col in range(0, out_cols, step):
        at = pl.ds(col, step)
        out = jnp.dot(picked[:, :hidden], own_ref[:, at], preferred_element_type=jnp.float32)
        out = out + jnp.dot(picked[:, hidden:], other_ref[:, at], preferred_element_type=jnp.float32)
        for place, ref in enumerate(out_refs):
            ref[:, at] = out[place * 2 * tok : (place + 1) * 2 * tok, :].astype(ref.dtype)
    for place, ref in zip(places, out_refs):
        if place[0] == (0, 0):
            for c_off, pair in enumerate(state_at):
                states = []
                for array, first_row in pair:
                    own_row = pl.multiple_of(first_row + my_ctx * (2 * tok), 2 * tok)
                    states.append(state_refs[array][pl.ds(own_row, 2 * tok), :].astype(jnp.float32))
                state = states[0] if pair[0] == pair[1] else jnp.where(my_core == 0, *states)
                cols = state.shape[1]
                at = pl.ds(pl.multiple_of(lax.bitwise_xor(my_ctx, c_off) * cols, cols), cols)
                ref[:, at] = ref[:, at] + state


def shards(
    residual,
    encoded_query_rows,
    quantized_key_rows,
    quantized_value_rows,
    key_block_exponent,
    value_block_exponent,
    block_order,
    out_weight,
    norm_gain,
    expert_ids,
    route_weight,
    gate_weight,
    gate_scale,
    up_weight,
    up_scale,
    down_weight,
    down_scale,
):
    f32, bf16 = jnp.float32, jnp.bfloat16
    vmem = pl.BlockSpec(memory_space=pltpu.VMEM)
    smem = pl.BlockSpec(memory_space=pltpu.SMEM)
    anywhere = pl.BlockSpec(memory_space=pl.ANY)
    span, query_width = encoded_query_rows.shape
    heads = query_width // HEAD_SIZE
    group = QUERY_HEADS // KEY_VALUE_HEADS
    ctx_count = lax.axis_size("ctx")
    exp_count = lax.axis_size("exp")
    x_count = exp_count // 2
    experts = ctx_count * x_count
    tok, model_width = residual.shape
    half_width = model_width // 2
    cols = half_width // ctx_count
    my_ctx = lax.axis_index("ctx").astype(jnp.int32).reshape(1)
    my_exp = lax.axis_index("exp").astype(jnp.int32).reshape(1)
    route, places = gather_route(ctx_count, x_count)

    hbm = pl.BlockSpec(memory_space=pltpu.HBM)
    piece_shape = jax.ShapeDtypeStruct((ctx_count // 2, tok, 2 * cols), bf16)
    row_route, row_places = gather_route(ctx_count, x_count, rows_only=True)
    names = sorted(row_places)
    piece_names = [[key for key in names if bool(key[0] & 2) == sent] for sent in (False, True)]
    piece_places = tuple(tuple(row_places[key] for key in keys) for keys in piece_names)
    packed, near, far = pl.pallas_call(
        functools.partial(pack_kernel, (heads, group, piece_places)),
        in_specs=[smem] * 2 + [hbm] * 8,
        out_specs=[vmem] * 3,
        out_shape=[
            jax.ShapeDtypeStruct((span, query_width + 3 * HEAD_SIZE), bf16),
            piece_shape,
            piece_shape,
        ],
        scratch_shapes=[
            pltpu.VMEM(key_block_exponent.shape, jnp.int32),
            pltpu.VMEM(key_block_exponent.shape, jnp.int32),
            pltpu.VMEM((span, HEAD_SIZE), bf16),
            pltpu.VMEM((span, HEAD_SIZE), bf16),
            pltpu.VMEM((TOP, tok), jnp.int32),
            pltpu.VMEM((TOP, tok), f32),
            pltpu.SemaphoreType.DMA((7 + ctx_count,)),
        ],
        compiler_params=pltpu.CompilerParams(vmem_limit_bytes=8 * MIB),
        name="pack",
    )(
        my_ctx,
        my_exp,
        *in_hbm(
            key_block_exponent,
            value_block_exponent,
            encoded_query_rows,
            quantized_key_rows,
            quantized_value_rows,
            jnp.transpose(expert_ids),
            jnp.transpose(route_weight),
            residual,
        ),
    )
    piece_arrays = [near]
    piece_at = {(0, key[0]): (0, place) for place, key in enumerate(piece_names[0])}
    piece_bits = [1, *range(bits_of(ctx_count) - 1, 1, -1), 0]
    sending, weights = far, {}

    def beside(number, came):
        nonlocal sending
        bit = 1 << piece_bits[number]
        moves = {1: ((2, 0), (1, 0)), 0: ((1, 0), (2, 0))}.get(piece_bits[number], ((bit, 0),) * 2)
        if number == 0:
            keys = [(0, key[0]) for key in piece_names[1]]
        else:
            keys = sorted(key for key in piece_at if key[1] & bit)
            sending = jnp.stack([piece_arrays[array][place] for array, place in map(piece_at.pop, keys)])
        pieces = follow(sending, moves)
        if number == 0:
            own, give = deq_in(my_exp, gate_weight, gate_scale, up_weight, up_scale, ctx_count, packed)
            *came, pieces, weights["in_own"], weights["in_give"] = together(*came, pieces, own, give)
        elif number == 1:
            other = from_offset(weights["in_give"], 1)
            own, give = deq_down(my_exp, down_weight, down_scale, ctx_count, piece_arrays[-1])
            *came, pieces, weights["in_other"], weights["down_own"], weights["down_give"] = together(
                *came, pieces, other, own, give
            )
        elif number < len(piece_bits) - 1:
            *came, pieces = together(*came, pieces)
        for place, (source, target) in enumerate(keys):
            piece_at[source ^ bit, target ^ bit] = (len(piece_arrays), place)
        piece_arrays.append(pieces)
        return came

    packed, packed_at = spread(packed, stages_of(row_route), beside)
    attend_at = tuple((packed_at[key], row_places[key]) for key in names)
    attend_pieces = tuple(piece_at[key[0], 0] for key in names)
    in_own, in_other, down_own = weights["in_own"], weights["in_other"], weights["down_own"]
    down_other = from_offset(weights["down_give"], 1)

    positions = ctx_count * span
    per_x = 2 * ctx_count * tok
    *keeps, give, own_route = pl.pallas_call(
        functools.partial(attend_kernel, (ctx_count, exp_count, tok, heads, attend_pieces, attend_at)),
        in_specs=[smem] * 3 + [vmem] * (len(packed) + len(piece_arrays) + 1) + [anywhere],
        out_specs=[vmem] * (2 + x_count),
        out_shape=[jax.ShapeDtypeStruct((per_x, cols), f32)] * x_count
        + [
            jax.ShapeDtypeStruct((x_count * (per_x + 2 * tok), cols), bf16),
            jax.ShapeDtypeStruct((x_count * 2 * tok, cols), bf16),
        ],
        scratch_shapes=[
            pltpu.VMEM((positions, HEAD_SIZE), bf16),
            pltpu.VMEM((positions, HEAD_SIZE), bf16),
            pltpu.VMEM((8, positions), jnp.int32),
            pltpu.VMEM((positions, query_width), bf16),
        ],
        compiler_params=pltpu.CompilerParams(vmem_limit_bytes=3 * ctx_count * MIB),
        cost_estimate=pl.CostEstimate(
            flops=4 * positions * positions * query_width + 4 * positions * query_width * cols,
            bytes_accessed=8 * MIB,
            transcendentals=heads * positions * positions,
        ),
        name="attend",
    )(my_ctx, my_exp, block_order, *packed, *piece_arrays, out_weight, down_other)

    given = from_offset(give, 1)
    routes, route_at, state = [own_route, given], [(0, 0), (1, x_count * per_x)], keeps[0]
    state = state + given[:per_x].astype(f32)
    for x_off in range(1, x_count):
        part = keeps[x_off] + given[x_off * per_x : (x_off + 1) * per_x].astype(f32)
        row = x_count * per_x + x_off * 2 * tok
        own = own_route[x_off * 2 * tok : (x_off + 1) * 2 * tok]
        sent = jnp.concatenate([part.astype(bf16), own, given[row : row + 2 * tok]], axis=0)
        came = from_offset(sent, 2 * x_off)
        state = state + came[:per_x].astype(f32)
        route_at += [(len(routes), per_x), (len(routes), per_x + 2 * tok)]
        routes.append(came)
    state = state.astype(bf16)

    stages = stages_of(route)
    chunks, chunk_at = spread(state, stages)
    gain = norm_gain.reshape(1, model_width)
    rows = x_count * per_x
    in_width = in_own.shape[1]
    near = tuple(sorted(key for key in places if key[0] < ctx_count // 2))
    far = tuple(sorted(key for key in places if key[0] >= ctx_count // 2))

    def picked(keys):
        arrays = sorted({chunk_at[key][0] for key in keys})
        at = tuple(((arrays.index(chunk_at[key][0]), chunk_at[key][1]), places[key]) for key in keys)
        return [chunks[array] for array in arrays], at

    near_chunks, near_places = picked(near)
    far_chunks, far_places = picked(far)
    first_act, first_square = pl.pallas_call(
        functools.partial(experts_in_first, (ctx_count, x_count, tok), near_places),
        in_specs=[smem] * 2 + [vmem] * (len(near_chunks) + 3) + [anywhere],
        out_specs=[vmem] * 2,
        out_shape=[
            jax.ShapeDtypeStruct((rows, 2 * in_width), f32),
            jax.ShapeDtypeStruct((rows, 1), f32),
        ],
        scratch_shapes=[pltpu.VMEM((rows, half_width // 2), bf16)],
        compiler_params=pltpu.CompilerParams(vmem_limit_bytes=2 * ctx_count * MIB),
        cost_estimate=pl.CostEstimate(
            flops=2 * rows * half_width * in_width, bytes_accessed=8 * MIB, transcendentals=0
        ),
        name="experts_in_first",
    )(my_ctx, my_exp, *near_chunks, gain, in_own, in_other, down_other)
    acts = []
    for part in range(2):
        acts.append(
            pl.pallas_call(
                functools.partial(experts_in_second, (ctx_count, x_count, tok), far_places, part),
                in_specs=[smem] * 2 + [vmem] * (len(far_chunks) + 5) + [anywhere],
                out_specs=vmem,
                out_shape=jax.ShapeDtypeStruct((rows // 2, 2 * in_width + HEAD_SIZE), bf16),
                scratch_shapes=[
                    pltpu.VMEM((rows // 2, half_width // 2), bf16),
                    pltpu.VMEM((rows // 2, 1), f32),
                ],
                compiler_params=pltpu.CompilerParams(vmem_limit_bytes=2 * ctx_count * MIB),
                cost_estimate=pl.CostEstimate(
                    flops=rows * half_width * in_width, bytes_accessed=8 * MIB, transcendentals=0
                ),
                name="experts_in_second",
            )(
                my_ctx,
                my_exp,
                *far_chunks,
                gain,
                in_own,
                in_other,
                first_act,
                first_square,
                acts[0] if part else first_square,
            )
        )
    leaves = set(places) - {source for _, source, _, _ in route}
    sums = {}
    for part in range(2):
        slots = near if part == 1 else far
        state_keys = [
            next(key for key in places if places[key][core] == (offset, 0))
            for offset in (range(ctx_count) if part == 1 else ())
            for core in range(2)
        ]
        states, state_at = picked(state_keys)
        state_at = tuple((state_at[i][0], state_at[i + 1][0]) for i in range(0, len(state_at), 2))
        outs = pl.pallas_call(
            functools.partial(
                experts_out_kernel,
                (ctx_count, exp_count, tok),
                part,
                tuple(places[key] for key in slots),
                state_at,
                tuple(route_at),
                model_width,
            ),
            in_specs=[smem] * 2 + [vmem] * (5 + x_count) + [anywhere] + [vmem] * len(states),
            out_specs=[vmem] * len(slots),
            out_shape=[
                jax.ShapeDtypeStruct((2 * tok, half_width), bf16 if slot in leaves else f32)
                for slot in slots
            ],
            scratch_shapes=[pltpu.VMEM((rows // 2, in_width), bf16)],
            compiler_params=pltpu.CompilerParams(vmem_limit_bytes=2 * ctx_count * MIB),
            cost_estimate=pl.CostEstimate(
                flops=rows * half_width * in_width,
                bytes_accessed=8 * MIB,
                transcendentals=rows * in_width // 2,
            ),
            name="experts_out",
        )(
            my_ctx,
            my_exp,
            acts[part],
            from_offset(acts[part], 1),
            *routes,
            down_own,
            down_other,
            sums[slots_done[0]] if part else acts[1],
            *states,
        )
        slots_done = slots
        sums.update(zip(slots, outs))

    for number, sends in enumerate(reversed(stages)):
        came = []
        for moves, _, targets in sends:
            sent = [sums[key].astype(bf16) for key in targets]
            came.append(follow(sent[0] if len(sent) == 1 else jnp.concatenate(sent, axis=0), moves))
        if number < len(stages) - 1:
            waiting = list(near) if number == 0 else []
            values = together(*came, *[sums[key] for key in waiting])
            came = values[: len(came)]
            sums.update(zip(waiting, values[len(came) :]))
        for (_, sources, _), array in zip(sends, came):
            for place, key in enumerate(sources):
                part = array[place * 2 * tok : (place + 1) * 2 * tok]
                sums[key] = sums[key] + part.astype(f32)
    total = sums[0, 0]
    core = lax.bitwise_and(my_exp[0], 1)
    mine = jnp.where(core == 0, total[:tok], total[tok:]).astype(bf16)
    came = from_offset(jnp.where(core == 0, total[tok:], total[:tok]).astype(bf16), 1)
    mine = mine.reshape(tok, ctx_count, 1, cols)
    came = came.reshape(tok, ctx_count, 1, cols)
    result = jnp.where(core == 0, jnp.concatenate([mine, came], axis=2), jnp.concatenate([came, mine], axis=2))
    return result.reshape(tok, model_width)


def solution(mesh):
    return jax.shard_map(
        shards,
        mesh=mesh,
        in_specs=(
            P(("dp", "ctx", "exp"), None),
            P(("dp", "ctx"), "exp"),
            P(("dp", "ctx"), None),
            P(("dp", "ctx"), None),
            P(("dp", "ctx"), None),
            P(("dp", "ctx"), None),
            P(),
            P("exp", "ctx"),
            P(),
            P(("dp", "ctx", "exp"), None),
            P(("dp", "ctx", "exp"), None),
            P(("ctx", "exp"), None, None),
            P(("ctx", "exp"), None, None),
            P(("ctx", "exp"), None, None),
            P(("ctx", "exp"), None, None),
            P(("ctx", "exp"), None, None),
            P(("ctx", "exp"), None, None),
        ),
        out_specs=P(("dp", "ctx", "exp"), None),
        check_vma=False,
    )
```

```python
import functools
import math

import jax
import jax.numpy as jnp
from jax import lax
from jax.experimental import pallas as pl
from jax.experimental.pallas import tpu as pltpu
from jax.sharding import PartitionSpec as P

QUERY_HEADS = 32
KEY_VALUE_HEADS = 4
HEAD_SIZE = 128
TOP = 8
SCALE_POSITIONS = 64
WB = 128
MIB = 1 << 20


def bits_of(count):
    return count.bit_length() - 1


def from_offset(array, offset):
    return lax.ppermute(array, "exp", [(i, i ^ offset) for i in range(lax.axis_size("exp"))])


def from_ctx(array, offset):
    return lax.ppermute(array, "ctx", [(i, i ^ offset) for i in range(lax.axis_size("ctx"))])


def moved(offset, move):
    return (offset[0] ^ move[0], offset[1] ^ move[1])


def gather_route(ctx_count, x_count, rows_only=False):
    transfers, arrival, places = [], {(0, 0): 0}, {(0, 0): ((0, 0), (0, 0))}

    def go(source, moves, delay=0):
        reached = tuple(moved(place, (c, e >> 1)) for place, (c, e) in zip(places[source], moves))
        target = reached[0]
        arrival[target], places[target] = arrival[source] + 1 + delay, reached
        transfers.append((arrival[target], source, target, moves))
        return target

    bits = bits_of(ctx_count)
    y_move = (1, 0)
    if rows_only:
        shared, steps = range(bits - 1, 1, -1), [(2, 0), y_move]
    else:
        shared, steps = range(bits - 1, 0, -1), [(0, 2 << bit) for bit in range(bits_of(x_count))] + [y_move]
    pairs = list(zip(steps, reversed(steps)))
    for bit in shared:
        for source in list(arrival):
            go(source, ((1 << bit, 0),) * 2)
    for number, first in enumerate(sorted(arrival)):
        held = [first]
        for moves in pairs:
            tuned = (ctx_count, x_count) == (8, 2) and not rows_only and number == 0
            held = held + [go(source, moves, 1 if tuned and source != first else 0) for source in held]
    return sorted(transfers, key=lambda transfer: transfer[0]), places


def follow(array, moves):
    exp_count = lax.axis_size("exp")
    pairs = []
    for c in range(lax.axis_size("ctx")):
        for e in range(exp_count):
            far = moved((c, e), moves[e % 2])
            pairs.append((far[0] * exp_count + far[1], c * exp_count + e))
    return lax.ppermute(array, ("ctx", "exp"), pairs)


def by_core(core, place, part):
    first, second = place[0][part], place[1][part]
    return first if first == second else jnp.where(core == 0, first, second)


def stages_of(route):
    stages, arrays = [], [((0, 0),)]
    top = max(moves[0][0] for _, _, _, moves in route)
    for stage in sorted({transfer[0] for transfer in route}):
        sends = []
        for moves in sorted({t[3] for t in route if t[0] == stage}):
            left = {source: target for number, source, target, way in route if (number, way) == (stage, moves)}
            groups = [group for group in arrays if len(group) > 1 and all(key in left for key in group)]
            rest = tuple(sorted(key for key in left if not any(key in group for group in groups)))
            for group in groups + [rest] * bool(rest):
                sends.append((moves, group, tuple(left[key] for key in group)))
        sends.sort(key=lambda send: -len(send[1]) * (2 if send[0][0][0] == top > 2 else 1))
        arrays = arrays + [send[2] for send in sends]
        stages.append(sends)
    return stages


def spread(block, stages, beside=None):
    arrays, at, joined = [block], {(0, 0): (0, 0)}, {}
    rows = block.shape[0]
    for number, sends in enumerate(stages):
        came = []
        for moves, group, _ in sends:
            first, row = at[group[0]]
            whole = row == 0 and arrays[first].shape[0] == len(group) * rows
            if whole and all(at[key] == (first, place * rows) for place, key in enumerate(group)):
                joined[group] = arrays[first]
            elif group not in joined:
                parts = [arrays[at[key][0]][at[key][1] : at[key][1] + rows] for key in group]
                joined[group] = jnp.concatenate(parts, axis=0)
            came.append(follow(joined[group], moves))
        came = beside(number, came) if beside else (together(*came) if number < len(stages) - 1 else came)
        for (_, _, targets), array in zip(sends, came):
            at.update({key: (len(arrays), place * rows) for place, key in enumerate(targets)})
            arrays.append(array)
    return arrays, at


def together(*values):
    return lax.optimization_barrier(values)


def block_factor(exponent, width):
    factor = jnp.where(exponent < 0, 0.5, jnp.where(exponent > 0, 2.0, 1.0))
    return jnp.full((1, width), factor, jnp.float32).astype(jnp.bfloat16)


def in_hbm(*arrays):
    return [pltpu.with_memory_space_constraint(array, pltpu.HBM) for array in arrays]


def copy_all(sems, pairs):
    copies = [pltpu.make_async_copy(src, dst, sems.at[i]) for i, (src, dst) in enumerate(pairs)]
    for copy in copies:
        copy.start()
    return copies


def pack_kernel(plan, ctx_ref, exp_ref, key_scale_hbm, value_scale_hbm, query_hbm, key_hbm, value_hbm, ids_hbm,
                route_hbm, residual_hbm, packed_ref, near_ref, far_ref, key_scale_ref, value_scale_ref,
                key_ref, value_ref, ids_ref, route_ref, sems):
    heads, group, piece_places = plan
    span, width = query_hbm.shape
    half, tok, cols = near_ref.shape
    my_ctx, my_exp = ctx_ref[0], exp_ref[0]
    kv_head = my_exp * heads // group
    at = pl.ds(pl.multiple_of(kv_head * HEAD_SIZE, HEAD_SIZE), HEAD_SIZE)
    pairs = [
        (key_scale_hbm, key_scale_ref),
        (value_scale_hbm, value_scale_ref),
        (key_hbm.at[:, at], key_ref),
        (value_hbm.at[:, at], value_ref),
        (ids_hbm, ids_ref),
        (route_hbm, route_ref),
        (query_hbm, packed_ref.at[:, 2 * HEAD_SIZE : 2 * HEAD_SIZE + width]),
    ]
    core = lax.bitwise_and(my_exp, 1)
    for ref, places in zip((near_ref, far_ref), piece_places):
        for number, place in enumerate(places):
            col = pl.multiple_of(lax.bitwise_xor(my_ctx, by_core(core, place, 0)) * cols, cols)
            pairs.append((residual_hbm.at[:, pl.ds(col, cols)], ref.at[number]))
    copies = copy_all(sems, pairs)
    for copy in copies[:6]:
        copy.wait()
    lane = lax.broadcasted_iota(jnp.int32, key_scale_ref.shape, 1)
    blocks = key_scale_ref.shape[0]
    for place, (ref, scale_ref) in enumerate(((key_ref, key_scale_ref), (value_ref, value_scale_ref))):
        exponent = scale_ref[...]
        factor = jnp.where(
            exponent < -1, 0.25, jnp.where(exponent < 0, 0.5, jnp.where(exponent < 1, 1.0, 2.0))
        )
        factor = jnp.sum(jnp.where(lane == kv_head, factor, 0.0), axis=1, keepdims=True)
        for block in range(blocks):
            rows = pl.ds(block * (span // blocks), span // blocks)
            scaled = ref[rows, :].astype(jnp.float32) * factor[block : block + 1, :]
            packed_ref[rows, pl.ds(place * HEAD_SIZE, HEAD_SIZE)] = scaled.astype(jnp.bfloat16)
    number = lax.broadcasted_iota(jnp.int32, (128, tok), 0)
    dense = jnp.zeros((128, tok), jnp.float32)
    for k in range(TOP):
        dense = dense + jnp.where(ids_ref[k : k + 1, :] == number, route_ref[k : k + 1, :], 0.0)
    dense = jnp.concatenate([dense, jnp.zeros((128, 128 - tok), jnp.float32)], axis=1)
    dense = jnp.transpose(dense)[:tok, :]
    high = dense.astype(jnp.bfloat16)
    packed_ref[0:tok, 2 * HEAD_SIZE + width :] = high
    packed_ref[tok : 2 * tok, 2 * HEAD_SIZE + width :] = (dense - high.astype(jnp.float32)).astype(
        jnp.bfloat16
    )
    packed_ref[2 * tok :, 2 * HEAD_SIZE + width :] = jnp.zeros((span - 2 * tok, 128), jnp.bfloat16)
    for copy in copies[6:]:
        copy.wait()


def deq_in_kernel(ctx_count, exp_ref, gate_scale_hbm, up_scale_hbm, gate_hbm, up_hbm, _, own_ref, give_ref,
                  gate_ref, up_ref, gate_scale_ref, up_scale_ref, sems):
    core = lax.bitwise_and(exp_ref[0], 1)
    width, cols = gate_ref.shape
    rows = width // (2 * ctx_count)
    pairs = [(gate_scale_hbm, gate_scale_ref), (up_scale_hbm, up_scale_ref)]
    for step in range(ctx_count):
        at = pl.ds(step * 2 * rows, 2 * rows)
        pairs += [(gate_hbm.at[0, at], gate_ref.at[at]), (up_hbm.at[0, at], up_ref.at[at])]
    copies = copy_all(sems, pairs)
    for copy in copies[:2]:
        copy.wait()
    for step in range(ctx_count):
        for half, (ref, scale_ref) in enumerate(((gate_ref, gate_scale_ref), (up_ref, up_scale_ref))):
            copies[2 + 2 * step + half].wait()
            for out_ref, side in ((give_ref, 1 - core), (own_ref, core)):
                first = (2 * step + side) * (rows // WB)
                for i in range(rows // WB):
                    row = pl.multiple_of((2 * step + side) * rows + i * WB, WB)
                    for j in range(cols // WB):
                        factor = block_factor(scale_ref[j, 0, first + i], WB)
                        out_ref[pl.ds(step * rows + i * WB, WB), pl.ds(half * cols + j * WB, WB)] = (
                            ref[pl.ds(row, WB), pl.ds(j * WB, WB)] * factor
                        )


def deq_in(my_exp, gate_weight, gate_scale, up_weight, up_scale, ctx_count, after):
    width, hidden = gate_weight.shape[1:]
    shape = jax.ShapeDtypeStruct((width // 2, 2 * hidden), jnp.bfloat16)
    gate_scale = jnp.transpose(gate_scale, (2, 0, 1))
    up_scale = jnp.transpose(up_scale, (2, 0, 1))
    return pl.pallas_call(
        functools.partial(deq_in_kernel, ctx_count),
        in_specs=[pl.BlockSpec(memory_space=pltpu.SMEM)]
        + [pl.BlockSpec(memory_space=pltpu.HBM)] * 4
        + [pl.BlockSpec(memory_space=pl.ANY)],
        out_specs=[pl.BlockSpec(memory_space=pltpu.VMEM)] * 2,
        out_shape=[shape, shape],
        scratch_shapes=[
            pltpu.VMEM((width, hidden), jnp.bfloat16),
            pltpu.VMEM((width, hidden), jnp.bfloat16),
            pltpu.SMEM(gate_scale.shape, jnp.int32),
            pltpu.SMEM(up_scale.shape, jnp.int32),
            pltpu.SemaphoreType.DMA((2 + 2 * ctx_count,)),
        ],
        compiler_params=pltpu.CompilerParams(vmem_limit_bytes=20 * MIB),
        cost_estimate=pl.CostEstimate(
            flops=2 * width * hidden, bytes_accessed=8 * width * hidden, transcendentals=0
        ),
        name="dequant_in",
    )(my_exp, *in_hbm(gate_scale, up_scale, gate_weight, up_weight), after)


def deq_down_kernel(ctx_count, exp_ref, scale_hbm, down_hbm, _, own_ref, give_ref, down_ref, scale_ref, sems):
    core = lax.bitwise_and(exp_ref[0], 1)
    rows, width = down_ref.shape
    cols = width // (2 * ctx_count)
    pairs = [(scale_hbm, scale_ref)]
    for step in range(ctx_count):
        at = pl.ds(step * 2 * cols, 2 * cols)
        pairs.append((down_hbm.at[0, :, at], down_ref.at[:, at]))
    copies = copy_all(sems, pairs)
    copies[0].wait()
    for step in range(ctx_count):
        copies[1 + step].wait()
        for out_ref, side in ((give_ref, 1 - core), (own_ref, core)):
            first = (2 * step + side) * (cols // WB)
            for j in range(cols // WB):
                col = pl.multiple_of((2 * step + side) * cols + j * WB, WB)
                for i in range(rows // WB):
                    factor = block_factor(scale_ref[i, 0, first + j], WB)
                    out_ref[pl.ds(i * WB, WB), pl.ds(step * cols + j * WB, WB)] = (
                        down_ref[pl.ds(i * WB, WB), pl.ds(col, WB)] * factor
                    )


def deq_down(my_exp, down_weight, down_scale, ctx_count, after):
    hidden, width = down_weight.shape[1:]
    shape = jax.ShapeDtypeStruct((hidden, width // 2), jnp.bfloat16)
    down_scale = jnp.transpose(down_scale, (1, 0, 2))
    return pl.pallas_call(
        functools.partial(deq_down_kernel, ctx_count),
        in_specs=[pl.BlockSpec(memory_space=pltpu.SMEM)]
        + [pl.BlockSpec(memory_space=pltpu.HBM)] * 2
        + [pl.BlockSpec(memory_space=pl.ANY)],
        out_specs=[pl.BlockSpec(memory_space=pltpu.VMEM)] * 2,
        out_shape=[shape, shape],
        scratch_shapes=[
            pltpu.VMEM((hidden, width), jnp.bfloat16),
            pltpu.SMEM(down_scale.shape, jnp.int32),
            pltpu.SemaphoreType.DMA((1 + ctx_count,)),
        ],
        compiler_params=pltpu.CompilerParams(vmem_limit_bytes=12 * MIB),
        cost_estimate=pl.CostEstimate(
            flops=width * hidden, bytes_accessed=4 * width * hidden, transcendentals=0
        ),
        name="dequant_down",
    )(my_exp, *in_hbm(down_scale, down_weight), after)


def attend_kernel(plan, ctx_ref, exp_ref, order_ref, *refs):
    ctx_count, exp_count, tok, heads, piece_places, attend_at = plan
    packed_at, places_of = [at for at, _ in attend_at], [place for _, place in attend_at]
    array_count = 1 + max(array for array, _ in packed_at)
    span = exp_count * tok
    packed_refs, refs = refs[:array_count], refs[array_count:]
    packed = []
    for array, row in packed_at:
        packed.append(packed_refs[array].at[pl.ds(row, span)])
    piece_refs, refs = refs[: 1 + bits_of(ctx_count)], refs[1 + bits_of(ctx_count) :]
    weight_ref, rest = refs[0], refs[2:]
    x_count = exp_count // 2
    keep_refs, (give_ref, own_route_ref) = rest[:x_count], rest[x_count : x_count + 2]
    key_scr, value_scr, place_scr, att_scr = rest[x_count + 2 :]
    positions = ctx_count * span
    my_ctx, my_exp = ctx_ref[0], exp_ref[0]
    my_x, my_core = lax.shift_right_logical(my_exp, 1), lax.bitwise_and(my_exp, 1)
    lane = lax.broadcasted_iota(jnp.int32, (8, positions), 1)
    places = lane % span
    for offset, ref in enumerate(packed):
        key_scr[pl.ds(offset * span, span), :] = ref[:, 0:HEAD_SIZE]
        value_scr[pl.ds(offset * span, span), :] = ref[:, HEAD_SIZE : 2 * HEAD_SIZE]
        base = order_ref[lax.bitwise_xor(my_ctx, by_core(my_core, places_of[offset], 0))] * span
        places = places + jnp.where(lane // span == offset, base, 0)
    place_scr[...] = places
    scale = 1.0 / math.sqrt(HEAD_SIZE)
    for offset, ref in enumerate(packed):
        source = lax.bitwise_xor(my_ctx, by_core(my_core, places_of[offset], 0))
        queries = jnp.concatenate(
            [ref[:, (h + 2) * HEAD_SIZE : (h + 3) * HEAD_SIZE] for h in range(heads)], axis=0
        )
        scores = lax.dot_general(
            queries, key_scr[...], (((1,), (1,)), ((), ())), preferred_element_type=jnp.float32
        )
        own_place = order_ref[source] * span + lax.broadcasted_iota(jnp.int32, (span, positions), 0)
        bias = jnp.where(place_scr[0:1, :] <= own_place, 0.0, -1e30)
        scores = scores.reshape(heads, span, positions) * scale + bias[None]
        largest = jnp.max(scores, axis=-1, keepdims=True)
        exps = jnp.exp(scores - largest)
        total = jnp.sum(exps, axis=-1, keepdims=True)
        mixed = jnp.dot(
            exps.astype(jnp.bfloat16).reshape(heads * span, positions),
            value_scr[...],
            preferred_element_type=jnp.float32,
        ).reshape(heads, span, HEAD_SIZE)
        mixed = (mixed / total).astype(jnp.bfloat16)
        for owner in range(exp_count):
            x_off = lax.bitwise_xor(my_x, owner // 2)
            row = pl.multiple_of(((x_off * ctx_count + source) * 2 + owner % 2) * tok, tok)
            for head in range(heads):
                att_scr[pl.ds(row, tok), pl.ds(head * HEAD_SIZE, HEAD_SIZE)] = mixed[
                    head, owner * tok : (owner + 1) * tok, :
                ]

    cols = weight_ref.shape[1] // 2
    per_x = 2 * ctx_count * tok
    first = (heads + 2) * HEAD_SIZE
    route_lane = lax.broadcasted_iota(jnp.int32, (tok, HEAD_SIZE), 1)
    route_base = x_count * per_x
    for x_off in range(x_count):
        rows = pl.ds(x_off * per_x, per_x)
        for which in (1, 0):
            side = lax.bitwise_xor(my_core, which)
            weight = weight_ref[:, pl.ds(pl.multiple_of(side * cols, cols), cols)]
            part = jnp.dot(att_scr[rows, :], weight, preferred_element_type=jnp.float32)
            out_ref = give_ref if which else keep_refs[x_off]
            out_ref[pl.ds(x_off * per_x if which else 0, per_x), :] = part.astype(out_ref.dtype)
            if x_off == 0:
                for (array, place), place_of in zip(piece_places, places_of):
                    source = lax.bitwise_xor(my_ctx, by_core(my_core, place_of, 0))
                    at = pl.ds(pl.multiple_of((source * 2 + my_core) * tok, tok), tok)
                    piece = piece_refs[array][place, :, pl.ds(pl.multiple_of(side * cols, cols), cols)]
                    value = out_ref[at, :].astype(jnp.float32) + piece.astype(jnp.float32)
                    out_ref[at, :] = value.astype(out_ref.dtype)
        expert = my_ctx * x_count + lax.bitwise_xor(my_x, x_off)
        sides = [jnp.zeros((tok, HEAD_SIZE), jnp.float32)] * 2
        for offset, ref in enumerate(packed):
            source = lax.bitwise_xor(my_ctx, by_core(my_core, places_of[offset], 0))
            for part_of in range(2):
                block = ref[part_of * tok : (part_of + 1) * tok, first:].astype(jnp.float32)
                column = jnp.sum(jnp.where(route_lane == expert, block, 0.0), axis=1, keepdims=True)
                sides[part_of] = sides[part_of] + jnp.where(route_lane == source, column, 0.0)
        for part_of, side in enumerate(sides):
            row = (2 * x_off + part_of) * tok
            for ref, base in ((give_ref, route_base), (own_route_ref, 0)):
                at = pl.ds(base + row, tok)
                ref[at, 0:HEAD_SIZE] = side.astype(jnp.bfloat16)
                if cols > HEAD_SIZE:
                    ref[at, HEAD_SIZE:] = jnp.zeros((tok, cols - HEAD_SIZE), jnp.bfloat16)


def fill_rows(plan, ctx_ref, exp_ref, gain_ref, chunk_refs, places, rows_scr, square_ref, groups):
    ctx_count, x_count, tok = plan
    half = ctx_count // 2
    my_ctx = ctx_ref[0]
    my_core = lax.bitwise_and(exp_ref[0], 1)
    mine = lax.shift_right_logical(my_ctx, bits_of(half))
    cols = chunk_refs[0].shape[1]
    rows = ctx_count * tok
    for (array, first_row), place_of in places:
        ref = chunk_refs[array]
        source = lax.bitwise_xor(my_ctx, by_core(my_core, place_of, 0))
        x_off = by_core(my_core, place_of, 1)
        gain_at = pl.multiple_of((source * 2 + my_core) * cols, cols)
        gain = gain_ref[:, pl.ds(gain_at, cols)]
        col = pl.multiple_of(lax.bitwise_and(source, half - 1) * cols, cols)
        for place, group in enumerate(groups):
            side = mine if group == 1 else 1 - mine
            chunk_at = pl.ds(pl.multiple_of(first_row + side * rows, rows), rows)
            chunk = ref[chunk_at, :].astype(jnp.float32)
            at = pl.ds(pl.multiple_of((place * x_count + x_off) * rows, rows), rows)
            rows_scr[at, pl.ds(col, cols)] = (chunk * gain).astype(jnp.bfloat16)
            square_ref[at, :] = square_ref[at, :] + jnp.sum(chunk * chunk, axis=-1, keepdims=True)


def experts_in_first(plan, offsets, ctx_ref, exp_ref, *refs):
    chunk_refs, (gain_ref, own_ref, other_ref, _, act_ref, square_ref, rows_scr) = refs[:-7], refs[-7:]
    half = plan[0] // 2
    square_ref[...] = jnp.zeros(square_ref.shape, jnp.float32)
    fill_rows(plan, ctx_ref, exp_ref, gain_ref, chunk_refs, offsets, rows_scr, square_ref, (0, 1))
    depth, width = rows_scr.shape[1], own_ref.shape[1]
    start = lax.shift_right_logical(ctx_ref[0], bits_of(half)) * depth
    at = pl.ds(pl.multiple_of(start, depth), depth)
    for place, ref in enumerate((own_ref, other_ref)):
        act_ref[:, place * width : (place + 1) * width] = jnp.dot(
            rows_scr[...], ref[at, :], preferred_element_type=jnp.float32
        )


def experts_in_second(plan, offsets, group, ctx_ref, exp_ref, *refs):
    chunk_refs, rest = refs[:-9], refs[-9:]
    gain_ref, own_ref, other_ref, first_ref, square_ref, _, act_ref, rows_scr, sum_scr = rest
    half = plan[0] // 2
    count, depth = rows_scr.shape
    width = own_ref.shape[1]
    sum_scr[...] = square_ref[group * count : (group + 1) * count, :]
    fill_rows(plan, ctx_ref, exp_ref, gain_ref, chunk_refs, offsets, rows_scr, sum_scr, (group,))
    lane = lax.broadcasted_iota(jnp.int32, (1, HEAD_SIZE), 1)
    square = sum_scr[...]
    high = square.astype(jnp.bfloat16).astype(jnp.float32)
    act_ref[:, 2 * width :] = jnp.where(lane == 0, high, square - high).astype(jnp.bfloat16)
    start = (1 - lax.shift_right_logical(ctx_ref[0], bits_of(half))) * depth
    at = pl.ds(pl.multiple_of(start, depth), depth)
    for place, ref in enumerate((own_ref, other_ref)):
        cols = slice(place * width, (place + 1) * width)
        act = first_ref[group * count : (group + 1) * count, cols] + jnp.dot(
            rows_scr[...], ref[at, :], preferred_element_type=jnp.float32
        )
        act_ref[:, cols] = act.astype(jnp.bfloat16)


def experts_out_kernel(plan, group, places, state_at, route_at, model_width, ctx_ref, exp_ref, act_ref, came_ref, *refs):
    ctx_count, exp_count, tok = plan
    x_count, half = exp_count // 2, ctx_count // 2
    route_refs, refs = refs[: x_count + 1], refs[x_count + 1 :]
    (own_ref, other_ref, _), rest = refs[:3], refs[3:]
    state_count = 1 + max((array for pair in state_at for array, _ in pair), default=-1)
    state_refs, rest = rest[:state_count], rest[state_count:]
    out_refs, hidden_scr = rest[:-1], rest[-1]
    my_ctx = ctx_ref[0]
    my_core = lax.bitwise_and(exp_ref[0], 1)
    mine = lax.shift_right_logical(my_ctx, bits_of(half))
    first_ctx = (mine if group == 1 else 1 - mine) * half
    width = (act_ref.shape[1] - HEAD_SIZE) // 2
    hidden = width // 2
    lane = lax.broadcasted_iota(jnp.int32, (tok, HEAD_SIZE), 1)
    blocks = []
    for array, row in route_at:
        both = route_refs[array][row : row + 2 * tok, 0:HEAD_SIZE].astype(jnp.float32)
        blocks.append(both[:tok] + both[tok:])
    columns = []
    for x_off in range(x_count):
        for low in range(half):
            for core in range(2):
                same, swapped = blocks[2 * x_off + core], blocks[2 * x_off + 1 - core]
                block = jnp.where(my_core == 0, same, swapped)
                picked = jnp.where(lane == first_ctx + low, block, 0.0)
                columns.append(jnp.sum(picked, axis=1, keepdims=True))
    route = jnp.concatenate(columns, axis=0)
    squares = act_ref[:, 2 * width :].astype(jnp.float32) + came_ref[:, 2 * width :].astype(jnp.float32)
    norm = lax.rsqrt((squares[:, 0:1] + squares[:, 1:2]) / model_width + 1e-06)
    scaled_route = norm * route
    for side in range(2):
        acts = act_ref[:, side * width : (side + 1) * width].astype(jnp.float32) + came_ref[
            :, (1 - side) * width : (2 - side) * width
        ].astype(jnp.float32)
        gate = acts[:, :hidden] * norm
        value = gate / (1.0 + jnp.exp(-gate)) * (acts[:, hidden:] * scaled_route)
        hidden_scr[:, side * hidden : (side + 1) * hidden] = value.astype(jnp.bfloat16)
    picked = []
    for place in places:
        x_off = by_core(my_core, place, 1)
        low = lax.bitwise_and(lax.bitwise_xor(my_ctx, by_core(my_core, place, 0)), half - 1)
        row = pl.multiple_of((x_off * half + low) * (2 * tok), 2 * tok)
        picked.append(hidden_scr[pl.ds(row, 2 * tok), :])
    picked = jnp.concatenate(picked, axis=0)
    out_cols = own_ref.shape[1]
    step = min(512, out_cols)
    for col in range(0, out_cols, step):
        at = pl.ds(col, step)
        out = jnp.dot(picked[:, :hidden], own_ref[:, at], preferred_element_type=jnp.float32)
        out = out + jnp.dot(picked[:, hidden:], other_ref[:, at], preferred_element_type=jnp.float32)
        for place, ref in enumerate(out_refs):
            ref[:, at] = out[place * 2 * tok : (place + 1) * 2 * tok, :].astype(ref.dtype)
    for place, ref in zip(places, out_refs):
        if place[0] == (0, 0):
            for c_off, pair in enumerate(state_at):
                states = []
                for array, first_row in pair:
                    own_row = pl.multiple_of(first_row + my_ctx * (2 * tok), 2 * tok)
                    states.append(state_refs[array][pl.ds(own_row, 2 * tok), :].astype(jnp.float32))
                state = states[0] if pair[0] == pair[1] else jnp.where(my_core == 0, *states)
                cols = state.shape[1]
                at = pl.ds(pl.multiple_of(lax.bitwise_xor(my_ctx, c_off) * cols, cols), cols)
                ref[:, at] = ref[:, at] + state


def shards(
    residual,
    encoded_query_rows,
    quantized_key_rows,
    quantized_value_rows,
    key_block_exponent,
    value_block_exponent,
    block_order,
    out_weight,
    norm_gain,
    expert_ids,
    route_weight,
    gate_weight,
    gate_scale,
    up_weight,
    up_scale,
    down_weight,
    down_scale,
):
    f32, bf16 = jnp.float32, jnp.bfloat16
    vmem = pl.BlockSpec(memory_space=pltpu.VMEM)
    smem = pl.BlockSpec(memory_space=pltpu.SMEM)
    anywhere = pl.BlockSpec(memory_space=pl.ANY)
    span, query_width = encoded_query_rows.shape
    heads = query_width // HEAD_SIZE
    group = QUERY_HEADS // KEY_VALUE_HEADS
    ctx_count = lax.axis_size("ctx")
    exp_count = lax.axis_size("exp")
    x_count = exp_count // 2
    experts = ctx_count * x_count
    tok, model_width = residual.shape
    half_width = model_width // 2
    cols = half_width // ctx_count
    my_ctx = lax.axis_index("ctx").astype(jnp.int32).reshape(1)
    my_exp = lax.axis_index("exp").astype(jnp.int32).reshape(1)
    route, places = gather_route(ctx_count, x_count)

    hbm = pl.BlockSpec(memory_space=pltpu.HBM)
    piece_shape = jax.ShapeDtypeStruct((ctx_count // 2, tok, 2 * cols), bf16)
    row_route, row_places = gather_route(ctx_count, x_count, rows_only=True)
    names = sorted(row_places)
    piece_names = [[key for key in names if bool(key[0] & 2) == sent] for sent in (False, True)]
    piece_places = tuple(tuple(row_places[key] for key in keys) for keys in piece_names)
    packed, near, far = pl.pallas_call(
        functools.partial(pack_kernel, (heads, group, piece_places)),
        in_specs=[smem] * 2 + [hbm] * 8,
        out_specs=[vmem] * 3,
        out_shape=[
            jax.ShapeDtypeStruct((span, query_width + 3 * HEAD_SIZE), bf16),
            piece_shape,
            piece_shape,
        ],
        scratch_shapes=[
            pltpu.VMEM(key_block_exponent.shape, jnp.int32),
            pltpu.VMEM(key_block_exponent.shape, jnp.int32),
            pltpu.VMEM((span, HEAD_SIZE), bf16),
            pltpu.VMEM((span, HEAD_SIZE), bf16),
            pltpu.VMEM((TOP, tok), jnp.int32),
            pltpu.VMEM((TOP, tok), f32),
            pltpu.SemaphoreType.DMA((7 + ctx_count,)),
        ],
        compiler_params=pltpu.CompilerParams(vmem_limit_bytes=8 * MIB),
        name="pack",
    )(
        my_ctx,
        my_exp,
        *in_hbm(
            key_block_exponent,
            value_block_exponent,
            encoded_query_rows,
            quantized_key_rows,
            quantized_value_rows,
            jnp.transpose(expert_ids),
            jnp.transpose(route_weight),
            residual,
        ),
    )
    piece_arrays = [near]
    piece_at = {(0, key[0]): (0, place) for place, key in enumerate(piece_names[0])}
    piece_bits = [1, *range(bits_of(ctx_count) - 1, 1, -1), 0]
    sending, weights = far, {}

    def beside(number, came):
        nonlocal sending
        bit = 1 << piece_bits[number]
        moves = {1: ((2, 0), (1, 0)), 0: ((1, 0), (2, 0))}.get(piece_bits[number], ((bit, 0),) * 2)
        if number == 0:
            keys = [(0, key[0]) for key in piece_names[1]]
        else:
            keys = sorted(key for key in piece_at if key[1] & bit)
            sending = jnp.stack([piece_arrays[array][place] for array, place in map(piece_at.pop, keys)])
        pieces = follow(sending, moves)
        if number == 0:
            own, give = deq_in(my_exp, gate_weight, gate_scale, up_weight, up_scale, ctx_count, packed)
            *came, pieces, weights["in_own"], weights["in_give"] = together(*came, pieces, own, give)
        elif number == 1:
            other = from_offset(weights["in_give"], 1)
            own, give = deq_down(my_exp, down_weight, down_scale, ctx_count, piece_arrays[-1])
            *came, pieces, weights["in_other"], weights["down_own"], weights["down_give"] = together(
                *came, pieces, other, own, give
            )
        elif number < len(piece_bits) - 1:
            *came, pieces = together(*came, pieces)
        for place, (source, target) in enumerate(keys):
            piece_at[source ^ bit, target ^ bit] = (len(piece_arrays), place)
        piece_arrays.append(pieces)
        return came

    packed, packed_at = spread(packed, stages_of(row_route), beside)
    attend_at = tuple((packed_at[key], row_places[key]) for key in names)
    attend_pieces = tuple(piece_at[key[0], 0] for key in names)
    in_own, in_other, down_own = weights["in_own"], weights["in_other"], weights["down_own"]
    down_other = from_offset(weights["down_give"], 1)

    positions = ctx_count * span
    per_x = 2 * ctx_count * tok
    *keeps, give, own_route = pl.pallas_call(
        functools.partial(attend_kernel, (ctx_count, exp_count, tok, heads, attend_pieces, attend_at)),
        in_specs=[smem] * 3 + [vmem] * (len(packed) + len(piece_arrays) + 1) + [anywhere],
        out_specs=[vmem] * (2 + x_count),
        out_shape=[jax.ShapeDtypeStruct((per_x, cols), f32)] * x_count
        + [
            jax.ShapeDtypeStruct((x_count * (per_x + 2 * tok), cols), bf16),
            jax.ShapeDtypeStruct((x_count * 2 * tok, cols), bf16),
        ],
        scratch_shapes=[
            pltpu.VMEM((positions, HEAD_SIZE), bf16),
            pltpu.VMEM((positions, HEAD_SIZE), bf16),
            pltpu.VMEM((8, positions), jnp.int32),
            pltpu.VMEM((positions, query_width), bf16),
        ],
        compiler_params=pltpu.CompilerParams(vmem_limit_bytes=3 * ctx_count * MIB),
        cost_estimate=pl.CostEstimate(
            flops=4 * positions * positions * query_width + 4 * positions * query_width * cols,
            bytes_accessed=8 * MIB,
            transcendentals=heads * positions * positions,
        ),
        name="attend",
    )(my_ctx, my_exp, block_order, *packed, *piece_arrays, out_weight, down_other)

    given = from_offset(give, 1)
    routes, route_at, state = [own_route, given], [(0, 0), (1, x_count * per_x)], keeps[0]
    state = state + given[:per_x].astype(f32)
    for x_off in range(1, x_count):
        part = keeps[x_off] + given[x_off * per_x : (x_off + 1) * per_x].astype(f32)
        row = x_count * per_x + x_off * 2 * tok
        own = own_route[x_off * 2 * tok : (x_off + 1) * 2 * tok]
        sent = jnp.concatenate([part.astype(bf16), own, given[row : row + 2 * tok]], axis=0)
        came = from_offset(sent, 2 * x_off)
        state = state + came[:per_x].astype(f32)
        route_at += [(len(routes), per_x), (len(routes), per_x + 2 * tok)]
        routes.append(came)
    state = state.astype(bf16)

    stages = stages_of(route)
    chunks, chunk_at = spread(state, stages)
    gain = norm_gain.reshape(1, model_width)
    rows = x_count * per_x
    in_width = in_own.shape[1]
    near = tuple(sorted(key for key in places if key[0] < ctx_count // 2))
    far = tuple(sorted(key for key in places if key[0] >= ctx_count // 2))

    def picked(keys):
        arrays = sorted({chunk_at[key][0] for key in keys})
        at = tuple(((arrays.index(chunk_at[key][0]), chunk_at[key][1]), places[key]) for key in keys)
        return [chunks[array] for array in arrays], at

    near_chunks, near_places = picked(near)
    far_chunks, far_places = picked(far)
    first_act, first_square = pl.pallas_call(
        functools.partial(experts_in_first, (ctx_count, x_count, tok), near_places),
        in_specs=[smem] * 2 + [vmem] * (len(near_chunks) + 3) + [anywhere],
        out_specs=[vmem] * 2,
        out_shape=[
            jax.ShapeDtypeStruct((rows, 2 * in_width), f32),
            jax.ShapeDtypeStruct((rows, 1), f32),
        ],
        scratch_shapes=[pltpu.VMEM((rows, half_width // 2), bf16)],
        compiler_params=pltpu.CompilerParams(vmem_limit_bytes=2 * ctx_count * MIB),
        cost_estimate=pl.CostEstimate(
            flops=2 * rows * half_width * in_width, bytes_accessed=8 * MIB, transcendentals=0
        ),
        name="experts_in_first",
    )(my_ctx, my_exp, *near_chunks, gain, in_own, in_other, down_other)
    acts = []
    for part in range(2):
        acts.append(
            pl.pallas_call(
                functools.partial(experts_in_second, (ctx_count, x_count, tok), far_places, part),
                in_specs=[smem] * 2 + [vmem] * (len(far_chunks) + 5) + [anywhere],
                out_specs=vmem,
                out_shape=jax.ShapeDtypeStruct((rows // 2, 2 * in_width + HEAD_SIZE), bf16),
                scratch_shapes=[
                    pltpu.VMEM((rows // 2, half_width // 2), bf16),
                    pltpu.VMEM((rows // 2, 1), f32),
                ],
                compiler_params=pltpu.CompilerParams(vmem_limit_bytes=2 * ctx_count * MIB),
                cost_estimate=pl.CostEstimate(
                    flops=rows * half_width * in_width, bytes_accessed=8 * MIB, transcendentals=0
                ),
                name="experts_in_second",
            )(
                my_ctx,
                my_exp,
                *far_chunks,
                gain,
                in_own,
                in_other,
                first_act,
                first_square,
                acts[0] if part else first_square,
            )
        )
    leaves = set(places) - {source for _, source, _, _ in route}
    sums = {}
    for part in range(2):
        slots = near if part == 1 else far
        state_keys = [
            next(key for key in places if places[key][core] == (offset, 0))
            for offset in (range(ctx_count) if part == 1 else ())
            for core in range(2)
        ]
        states, state_at = picked(state_keys)
        state_at = tuple((state_at[i][0], state_at[i + 1][0]) for i in range(0, len(state_at), 2))
        outs = pl.pallas_call(
            functools.partial(
                experts_out_kernel,
                (ctx_count, exp_count, tok),
                part,
                tuple(places[key] for key in slots),
                state_at,
                tuple(route_at),
                model_width,
            ),
            in_specs=[smem] * 2 + [vmem] * (5 + x_count) + [anywhere] + [vmem] * len(states),
            out_specs=[vmem] * len(slots),
            out_shape=[
                jax.ShapeDtypeStruct((2 * tok, half_width), bf16 if slot in leaves else f32)
                for slot in slots
            ],
            scratch_shapes=[pltpu.VMEM((rows // 2, in_width), bf16)],
            compiler_params=pltpu.CompilerParams(vmem_limit_bytes=2 * ctx_count * MIB),
            cost_estimate=pl.CostEstimate(
                flops=rows * half_width * in_width,
                bytes_accessed=8 * MIB,
                transcendentals=rows * in_width // 2,
            ),
            name="experts_out",
        )(
            my_ctx,
            my_exp,
            acts[part],
            from_offset(acts[part], 1),
            *routes,
            down_own,
            down_other,
            sums[slots_done[0]] if part else acts[1],
            *states,
        )
        slots_done = slots
        sums.update(zip(slots, outs))

    for number, sends in enumerate(reversed(stages)):
        came = []
        for moves, _, targets in sends:
            sent = [sums[key].astype(bf16) for key in targets]
            came.append(follow(sent[0] if len(sent) == 1 else jnp.concatenate(sent, axis=0), moves))
        if number < len(stages) - 1:
            waiting = list(near) if number == 0 else []
            values = together(*came, *[sums[key] for key in waiting])
            came = values[: len(came)]
            sums.update(zip(waiting, values[len(came) :]))
        for (_, sources, _), array in zip(sends, came):
            for place, key in enumerate(sources):
                part = array[place * 2 * tok : (place + 1) * 2 * tok]
                sums[key] = sums[key] + part.astype(f32)
    total = sums[0, 0]
    core = lax.bitwise_and(my_exp[0], 1)
    mine = jnp.where(core == 0, total[:tok], total[tok:]).astype(bf16)
    came = from_offset(jnp.where(core == 0, total[tok:], total[:tok]).astype(bf16), 1)
    mine = mine.reshape(tok, ctx_count, 1, cols)
    came = came.reshape(tok, ctx_count, 1, cols)
    result = jnp.where(core == 0, jnp.concatenate([mine, came], axis=2), jnp.concatenate([came, mine], axis=2))
    return result.reshape(tok, model_width)


def solution(mesh):
    return jax.shard_map(
        shards,
        mesh=mesh,
        in_specs=(
            P(("dp", "ctx", "exp"), None),
            P(("dp", "ctx"), "exp"),
            P(("dp", "ctx"), None),
            P(("dp", "ctx"), None),
            P(("dp", "ctx"), None),
            P(("dp", "ctx"), None),
            P(),
            P("exp", "ctx"),
            P(),
            P(("dp", "ctx", "exp"), None),
            P(("dp", "ctx", "exp"), None),
            P(("ctx", "exp"), None, None),
            P(("ctx", "exp"), None, None),
            P(("ctx", "exp"), None, None),
            P(("ctx", "exp"), None, None),
            P(("ctx", "exp"), None, None),
            P(("ctx", "exp"), None, None),
        ),
        out_specs=P(("dp", "ctx", "exp"), None),
        check_vma=False,
    )
```

```python
import functools
import math

import jax
import jax.numpy as jnp
from jax import lax
from jax.experimental import pallas as pl
from jax.experimental.pallas import tpu as pltpu
from jax.sharding import PartitionSpec as P

QUERY_HEADS = 32
KEY_VALUE_HEADS = 4
HEAD_SIZE = 128
TOP = 8
SCALE_POSITIONS = 64
WB = 128
MIB = 1 << 20


def bits_of(count):
    return count.bit_length() - 1


def from_offset(array, offset):
    return lax.ppermute(array, "exp", [(i, i ^ offset) for i in range(lax.axis_size("exp"))])


def from_ctx(array, offset):
    return lax.ppermute(array, "ctx", [(i, i ^ offset) for i in range(lax.axis_size("ctx"))])


def moved(offset, move):
    return (offset[0] ^ move[0], offset[1] ^ move[1])


def gather_route(ctx_count, x_count, rows_only=False):
    transfers, arrival, places = [], {(0, 0): 0}, {(0, 0): ((0, 0), (0, 0))}

    def go(source, moves, delay=0):
        reached = tuple(moved(place, (c, e >> 1)) for place, (c, e) in zip(places[source], moves))
        target = reached[0]
        arrival[target], places[target] = arrival[source] + 1 + delay, reached
        transfers.append((arrival[target], source, target, moves))
        return target

    bits = bits_of(ctx_count)
    y_move = (1, 0)
    if (ctx_count, x_count) == (8, 2) and not rows_only:
        z_far, z_near = ((4, 0),) * 2, ((2, 0),) * 2
        first, second = ((0, 2), y_move), (y_move, (0, 2))
        at = {"0": (0, 0)}
        for stage, moves, hops in (
            (1, z_far, "0>4"),
            (1, z_near, "0>2"),
            (1, first, "0>0a"),
            (1, second, "0>0b"),
            (2, z_near, "4>6 0b>2b"),
            (2, first, "2>2a 4>4a"),
            (2, second, "4>4b 0a>0ab"),
            (3, z_near, "4a>6a"),
            (3, second, "2a>2ab 4a>4ab 6>6b"),
            (4, second, "6a>6ab"),
        ):
            for hop in hops.split():
                source, target = hop.split(">")
                at[target] = go(at[source], moves, stage - 1 - arrival[at[source]])
        return sorted(transfers, key=lambda transfer: transfer[0]), places
    if rows_only:
        shared, steps = range(bits - 1, 1, -1), [(2, 0), y_move]
    else:
        shared, steps = range(bits - 1, 0, -1), [(0, 2 << bit) for bit in range(bits_of(x_count))] + [y_move]
    pairs = list(zip(steps, reversed(steps)))
    for bit in shared:
        for source in list(arrival):
            go(source, ((1 << bit, 0),) * 2)
    for first in sorted(arrival):
        held = [first]
        for moves in pairs:
            held = held + [go(source, moves) for source in held]
    return sorted(transfers, key=lambda transfer: transfer[0]), places


def follow(array, moves):
    exp_count = lax.axis_size("exp")
    pairs = []
    for c in range(lax.axis_size("ctx")):
        for e in range(exp_count):
            far = moved((c, e), moves[e % 2])
            pairs.append((far[0] * exp_count + far[1], c * exp_count + e))
    return lax.ppermute(array, ("ctx", "exp"), pairs)


def by_core(core, place, part):
    first, second = place[0][part], place[1][part]
    return first if first == second else jnp.where(core == 0, first, second)


def stages_of(route):
    stages, arrays = [], [((0, 0),)]
    top = max(moves[0][0] for _, _, _, moves in route)
    for stage in sorted({transfer[0] for transfer in route}):
        sends = []
        for moves in sorted({t[3] for t in route if t[0] == stage}):
            left = {source: target for number, source, target, way in route if (number, way) == (stage, moves)}
            groups = [group for group in arrays if len(group) > 1 and all(key in left for key in group)]
            rest = tuple(sorted(key for key in left if not any(key in group for group in groups)))
            for group in groups + [rest] * bool(rest):
                sends.append((moves, group, tuple(left[key] for key in group)))
        sends.sort(key=lambda send: -len(send[1]) * (2 if send[0][0][0] == top > 2 else 1))
        arrays = arrays + [send[2] for send in sends]
        stages.append(sends)
    return stages


def spread(block, stages, beside=None):
    arrays, at, joined = [block], {(0, 0): (0, 0)}, {}
    rows = block.shape[0]
    for number, sends in enumerate(stages):
        came = []
        for moves, group, _ in sends:
            first, row = at[group[0]]
            whole = row == 0 and arrays[first].shape[0] == len(group) * rows
            if whole and all(at[key] == (first, place * rows) for place, key in enumerate(group)):
                joined[group] = arrays[first]
            elif group not in joined:
                parts = [arrays[at[key][0]][at[key][1] : at[key][1] + rows] for key in group]
                joined[group] = jnp.concatenate(parts, axis=0)
            came.append(follow(joined[group], moves))
        came = beside(number, came) if beside else (together(*came) if number < len(stages) - 1 else came)
        for (_, _, targets), array in zip(sends, came):
            at.update({key: (len(arrays), place * rows) for place, key in enumerate(targets)})
            arrays.append(array)
    return arrays, at


def together(*values):
    return lax.optimization_barrier(values)


def block_factor(exponent, width):
    factor = jnp.where(exponent < 0, 0.5, jnp.where(exponent > 0, 2.0, 1.0))
    return jnp.full((1, width), factor, jnp.float32).astype(jnp.bfloat16)


def in_hbm(*arrays):
    return [pltpu.with_memory_space_constraint(array, pltpu.HBM) for array in arrays]


def copy_all(sems, pairs):
    copies = [pltpu.make_async_copy(src, dst, sems.at[i]) for i, (src, dst) in enumerate(pairs)]
    for copy in copies:
        copy.start()
    return copies


def pack_kernel(plan, ctx_ref, exp_ref, key_scale_hbm, value_scale_hbm, query_hbm, key_hbm, value_hbm, ids_hbm,
                route_hbm, residual_hbm, packed_ref, near_ref, far_ref, key_scale_ref, value_scale_ref,
                key_ref, value_ref, ids_ref, route_ref, sems):
    heads, group, piece_places = plan
    span, width = query_hbm.shape
    half, tok, cols = near_ref.shape
    my_ctx, my_exp = ctx_ref[0], exp_ref[0]
    kv_head = my_exp * heads // group
    at = pl.ds(pl.multiple_of(kv_head * HEAD_SIZE, HEAD_SIZE), HEAD_SIZE)
    pairs = [
        (key_scale_hbm, key_scale_ref),
        (value_scale_hbm, value_scale_ref),
        (key_hbm.at[:, at], key_ref),
        (value_hbm.at[:, at], value_ref),
        (ids_hbm, ids_ref),
        (route_hbm, route_ref),
        (query_hbm, packed_ref.at[:, 2 * HEAD_SIZE : 2 * HEAD_SIZE + width]),
    ]
    core = lax.bitwise_and(my_exp, 1)
    for ref, places in zip((near_ref, far_ref), piece_places):
        for number, place in enumerate(places):
            col = pl.multiple_of(lax.bitwise_xor(my_ctx, by_core(core, place, 0)) * cols, cols)
            pairs.append((residual_hbm.at[:, pl.ds(col, cols)], ref.at[number]))
    copies = copy_all(sems, pairs)
    for copy in copies[:6]:
        copy.wait()
    lane = lax.broadcasted_iota(jnp.int32, key_scale_ref.shape, 1)
    blocks = key_scale_ref.shape[0]
    for place, (ref, scale_ref) in enumerate(((key_ref, key_scale_ref), (value_ref, value_scale_ref))):
        exponent = scale_ref[...]
        factor = jnp.where(
            exponent < -1, 0.25, jnp.where(exponent < 0, 0.5, jnp.where(exponent < 1, 1.0, 2.0))
        )
        factor = jnp.sum(jnp.where(lane == kv_head, factor, 0.0), axis=1, keepdims=True)
        for block in range(blocks):
            rows = pl.ds(block * (span // blocks), span // blocks)
            scaled = ref[rows, :].astype(jnp.float32) * factor[block : block + 1, :]
            packed_ref[rows, pl.ds(place * HEAD_SIZE, HEAD_SIZE)] = scaled.astype(jnp.bfloat16)
    number = lax.broadcasted_iota(jnp.int32, (128, tok), 0)
    dense = jnp.zeros((128, tok), jnp.float32)
    for k in range(TOP):
        dense = dense + jnp.where(ids_ref[k : k + 1, :] == number, route_ref[k : k + 1, :], 0.0)
    dense = jnp.concatenate([dense, jnp.zeros((128, 128 - tok), jnp.float32)], axis=1)
    dense = jnp.transpose(dense)[:tok, :]
    high = dense.astype(jnp.bfloat16)
    packed_ref[0:tok, 2 * HEAD_SIZE + width :] = high
    packed_ref[tok : 2 * tok, 2 * HEAD_SIZE + width :] = (dense - high.astype(jnp.float32)).astype(
        jnp.bfloat16
    )
    packed_ref[2 * tok :, 2 * HEAD_SIZE + width :] = jnp.zeros((span - 2 * tok, 128), jnp.bfloat16)
    for copy in copies[6:]:
        copy.wait()


def deq_in_kernel(ctx_count, exp_ref, gate_scale_hbm, up_scale_hbm, gate_hbm, up_hbm, _, own_ref, give_ref,
                  gate_ref, up_ref, gate_scale_ref, up_scale_ref, sems):
    core = lax.bitwise_and(exp_ref[0], 1)
    width, cols = gate_ref.shape
    rows = width // (2 * ctx_count)
    pairs = [(gate_scale_hbm, gate_scale_ref), (up_scale_hbm, up_scale_ref)]
    for step in range(ctx_count):
        at = pl.ds(step * 2 * rows, 2 * rows)
        pairs += [(gate_hbm.at[0, at], gate_ref.at[at]), (up_hbm.at[0, at], up_ref.at[at])]
    copies = copy_all(sems, pairs)
    for copy in copies[:2]:
        copy.wait()
    for step in range(ctx_count):
        for half, (ref, scale_ref) in enumerate(((gate_ref, gate_scale_ref), (up_ref, up_scale_ref))):
            copies[2 + 2 * step + half].wait()
            for out_ref, side in ((give_ref, 1 - core), (own_ref, core)):
                first = (2 * step + side) * (rows // WB)
                for i in range(rows // WB):
                    row = pl.multiple_of((2 * step + side) * rows + i * WB, WB)
                    for j in range(cols // WB):
                        factor = block_factor(scale_ref[j, 0, first + i], WB)
                        out_ref[pl.ds(step * rows + i * WB, WB), pl.ds(half * cols + j * WB, WB)] = (
                            ref[pl.ds(row, WB), pl.ds(j * WB, WB)] * factor
                        )


def deq_in(my_exp, gate_weight, gate_scale, up_weight, up_scale, ctx_count, after):
    width, hidden = gate_weight.shape[1:]
    shape = jax.ShapeDtypeStruct((width // 2, 2 * hidden), jnp.bfloat16)
    gate_scale = jnp.transpose(gate_scale, (2, 0, 1))
    up_scale = jnp.transpose(up_scale, (2, 0, 1))
    return pl.pallas_call(
        functools.partial(deq_in_kernel, ctx_count),
        in_specs=[pl.BlockSpec(memory_space=pltpu.SMEM)]
        + [pl.BlockSpec(memory_space=pltpu.HBM)] * 4
        + [pl.BlockSpec(memory_space=pl.ANY)],
        out_specs=[pl.BlockSpec(memory_space=pltpu.VMEM)] * 2,
        out_shape=[shape, shape],
        scratch_shapes=[
            pltpu.VMEM((width, hidden), jnp.bfloat16),
            pltpu.VMEM((width, hidden), jnp.bfloat16),
            pltpu.SMEM(gate_scale.shape, jnp.int32),
            pltpu.SMEM(up_scale.shape, jnp.int32),
            pltpu.SemaphoreType.DMA((2 + 2 * ctx_count,)),
        ],
        compiler_params=pltpu.CompilerParams(vmem_limit_bytes=20 * MIB),
        cost_estimate=pl.CostEstimate(
            flops=2 * width * hidden, bytes_accessed=8 * width * hidden, transcendentals=0
        ),
        name="dequant_in",
    )(my_exp, *in_hbm(gate_scale, up_scale, gate_weight, up_weight), after)


def deq_down_kernel(ctx_count, exp_ref, scale_hbm, down_hbm, _, own_ref, give_ref, down_ref, scale_ref, sems):
    core = lax.bitwise_and(exp_ref[0], 1)
    rows, width = down_ref.shape
    cols = width // (2 * ctx_count)
    pairs = [(scale_hbm, scale_ref)]
    for step in range(ctx_count):
        at = pl.ds(step * 2 * cols, 2 * cols)
        pairs.append((down_hbm.at[0, :, at], down_ref.at[:, at]))
    copies = copy_all(sems, pairs)
    copies[0].wait()
    for step in range(ctx_count):
        copies[1 + step].wait()
        for out_ref, side in ((give_ref, 1 - core), (own_ref, core)):
            first = (2 * step + side) * (cols // WB)
            for j in range(cols // WB):
                col = pl.multiple_of((2 * step + side) * cols + j * WB, WB)
                for i in range(rows // WB):
                    factor = block_factor(scale_ref[i, 0, first + j], WB)
                    out_ref[pl.ds(i * WB, WB), pl.ds(step * cols + j * WB, WB)] = (
                        down_ref[pl.ds(i * WB, WB), pl.ds(col, WB)] * factor
                    )


def deq_down(my_exp, down_weight, down_scale, ctx_count, after):
    hidden, width = down_weight.shape[1:]
    shape = jax.ShapeDtypeStruct((hidden, width // 2), jnp.bfloat16)
    down_scale = jnp.transpose(down_scale, (1, 0, 2))
    return pl.pallas_call(
        functools.partial(deq_down_kernel, ctx_count),
        in_specs=[pl.BlockSpec(memory_space=pltpu.SMEM)]
        + [pl.BlockSpec(memory_space=pltpu.HBM)] * 2
        + [pl.BlockSpec(memory_space=pl.ANY)],
        out_specs=[pl.BlockSpec(memory_space=pltpu.VMEM)] * 2,
        out_shape=[shape, shape],
        scratch_shapes=[
            pltpu.VMEM((hidden, width), jnp.bfloat16),
            pltpu.SMEM(down_scale.shape, jnp.int32),
            pltpu.SemaphoreType.DMA((1 + ctx_count,)),
        ],
        compiler_params=pltpu.CompilerParams(vmem_limit_bytes=12 * MIB),
        cost_estimate=pl.CostEstimate(
            flops=width * hidden, bytes_accessed=4 * width * hidden, transcendentals=0
        ),
        name="dequant_down",
    )(my_exp, *in_hbm(down_scale, down_weight), after)


def attend_kernel(plan, ctx_ref, exp_ref, order_ref, *refs):
    ctx_count, exp_count, tok, heads, piece_places, attend_at = plan
    packed_at, places_of = [at for at, _ in attend_at], [place for _, place in attend_at]
    array_count = 1 + max(array for array, _ in packed_at)
    span = exp_count * tok
    packed_refs, refs = refs[:array_count], refs[array_count:]
    packed = []
    for array, row in packed_at:
        packed.append(packed_refs[array].at[pl.ds(row, span)])
    piece_refs, refs = refs[: 1 + bits_of(ctx_count)], refs[1 + bits_of(ctx_count) :]
    weight_ref, rest = refs[0], refs[2:]
    x_count = exp_count // 2
    keep_refs, (give_ref, own_route_ref) = rest[:x_count], rest[x_count : x_count + 2]
    key_scr, value_scr, place_scr, att_scr = rest[x_count + 2 :]
    positions = ctx_count * span
    my_ctx, my_exp = ctx_ref[0], exp_ref[0]
    my_x, my_core = lax.shift_right_logical(my_exp, 1), lax.bitwise_and(my_exp, 1)
    lane = lax.broadcasted_iota(jnp.int32, (8, positions), 1)
    places = lane % span
    for offset, ref in enumerate(packed):
        key_scr[pl.ds(offset * span, span), :] = ref[:, 0:HEAD_SIZE]
        value_scr[pl.ds(offset * span, span), :] = ref[:, HEAD_SIZE : 2 * HEAD_SIZE]
        base = order_ref[lax.bitwise_xor(my_ctx, by_core(my_core, places_of[offset], 0))] * span
        places = places + jnp.where(lane // span == offset, base, 0)
    place_scr[...] = places
    scale = 1.0 / math.sqrt(HEAD_SIZE)
    for offset, ref in enumerate(packed):
        source = lax.bitwise_xor(my_ctx, by_core(my_core, places_of[offset], 0))
        queries = jnp.concatenate(
            [ref[:, (h + 2) * HEAD_SIZE : (h + 3) * HEAD_SIZE] for h in range(heads)], axis=0
        )
        scores = lax.dot_general(
            queries, key_scr[...], (((1,), (1,)), ((), ())), preferred_element_type=jnp.float32
        )
        own_place = order_ref[source] * span + lax.broadcasted_iota(jnp.int32, (span, positions), 0)
        bias = jnp.where(place_scr[0:1, :] <= own_place, 0.0, -1e30)
        scores = scores.reshape(heads, span, positions) * scale + bias[None]
        largest = jnp.max(scores, axis=-1, keepdims=True)
        exps = jnp.exp(scores - largest)
        total = jnp.sum(exps, axis=-1, keepdims=True)
        mixed = jnp.dot(
            exps.astype(jnp.bfloat16).reshape(heads * span, positions),
            value_scr[...],
            preferred_element_type=jnp.float32,
        ).reshape(heads, span, HEAD_SIZE)
        mixed = (mixed / total).astype(jnp.bfloat16)
        for owner in range(exp_count):
            x_off = lax.bitwise_xor(my_x, owner // 2)
            row = pl.multiple_of(((x_off * ctx_count + source) * 2 + owner % 2) * tok, tok)
            for head in range(heads):
                att_scr[pl.ds(row, tok), pl.ds(head * HEAD_SIZE, HEAD_SIZE)] = mixed[
                    head, owner * tok : (owner + 1) * tok, :
                ]

    cols = weight_ref.shape[1] // 2
    per_x = 2 * ctx_count * tok
    first = (heads + 2) * HEAD_SIZE
    route_lane = lax.broadcasted_iota(jnp.int32, (tok, HEAD_SIZE), 1)
    route_base = x_count * per_x
    for x_off in range(x_count):
        rows = pl.ds(x_off * per_x, per_x)
        for which in (1, 0):
            side = lax.bitwise_xor(my_core, which)
            weight = weight_ref[:, pl.ds(pl.multiple_of(side * cols, cols), cols)]
            part = jnp.dot(att_scr[rows, :], weight, preferred_element_type=jnp.float32)
            out_ref = give_ref if which else keep_refs[x_off]
            out_ref[pl.ds(x_off * per_x if which else 0, per_x), :] = part.astype(out_ref.dtype)
            if x_off == 0:
                for (array, place), place_of in zip(piece_places, places_of):
                    source = lax.bitwise_xor(my_ctx, by_core(my_core, place_of, 0))
                    at = pl.ds(pl.multiple_of((source * 2 + my_core) * tok, tok), tok)
                    piece = piece_refs[array][place, :, pl.ds(pl.multiple_of(side * cols, cols), cols)]
                    value = out_ref[at, :].astype(jnp.float32) + piece.astype(jnp.float32)
                    out_ref[at, :] = value.astype(out_ref.dtype)
        expert = my_ctx * x_count + lax.bitwise_xor(my_x, x_off)
        block_out = jnp.zeros((tok, HEAD_SIZE), jnp.float32)
        for offset, ref in enumerate(packed):
            source = lax.bitwise_xor(my_ctx, by_core(my_core, places_of[offset], 0))
            for part_of in range(2):
                block = ref[part_of * tok : (part_of + 1) * tok, first:].astype(jnp.float32)
                column = jnp.sum(jnp.where(route_lane == expert, block, 0.0), axis=1, keepdims=True)
                block_out = jnp.where(route_lane == source + part_of * ctx_count, column, block_out)
        for ref, base in ((give_ref, route_base), (own_route_ref, 0)):
            at = pl.ds(base + x_off * tok, tok)
            ref[at, 0:HEAD_SIZE] = block_out.astype(jnp.bfloat16)
            if cols > HEAD_SIZE:
                ref[at, HEAD_SIZE:] = jnp.zeros((tok, cols - HEAD_SIZE), jnp.bfloat16)


def fill_rows(plan, ctx_ref, exp_ref, gain_ref, chunk_refs, places, rows_scr, square_ref, groups):
    ctx_count, x_count, tok = plan
    half = ctx_count // 2
    my_ctx = ctx_ref[0]
    my_core = lax.bitwise_and(exp_ref[0], 1)
    mine = lax.shift_right_logical(my_ctx, bits_of(half))
    cols = chunk_refs[0].shape[1]
    rows = ctx_count * tok
    for (array, first_row), place_of in places:
        ref = chunk_refs[array]
        source = lax.bitwise_xor(my_ctx, by_core(my_core, place_of, 0))
        x_off = by_core(my_core, place_of, 1)
        gain_at = pl.multiple_of((source * 2 + my_core) * cols, cols)
        gain = gain_ref[:, pl.ds(gain_at, cols)]
        col = pl.multiple_of(lax.bitwise_and(source, half - 1) * cols, cols)
        for place, group in enumerate(groups):
            side = mine if group == 1 else 1 - mine
            chunk_at = pl.ds(pl.multiple_of(first_row + side * rows, rows), rows)
            chunk = ref[chunk_at, :].astype(jnp.float32)
            at = pl.ds(pl.multiple_of((place * x_count + x_off) * rows, rows), rows)
            rows_scr[at, pl.ds(col, cols)] = (chunk * gain).astype(jnp.bfloat16)
            square_ref[at, :] = square_ref[at, :] + jnp.sum(chunk * chunk, axis=-1, keepdims=True)


def experts_in_first(plan, offsets, ctx_ref, exp_ref, *refs):
    chunk_refs, (gain_ref, own_ref, other_ref, _, act_ref, square_ref, rows_scr) = refs[:-7], refs[-7:]
    half = plan[0] // 2
    square_ref[...] = jnp.zeros(square_ref.shape, jnp.float32)
    fill_rows(plan, ctx_ref, exp_ref, gain_ref, chunk_refs, offsets, rows_scr, square_ref, (0, 1))
    depth, width = rows_scr.shape[1], own_ref.shape[1]
    start = lax.shift_right_logical(ctx_ref[0], bits_of(half)) * depth
    at = pl.ds(pl.multiple_of(start, depth), depth)
    for place, ref in enumerate((own_ref, other_ref)):
        act_ref[:, place * width : (place + 1) * width] = jnp.dot(
            rows_scr[...], ref[at, :], preferred_element_type=jnp.float32
        )


def experts_in_second(plan, offsets, group, ctx_ref, exp_ref, *refs):
    chunk_refs, rest = refs[:-9], refs[-9:]
    gain_ref, own_ref, other_ref, first_ref, square_ref, _, act_ref, rows_scr, sum_scr = rest
    half = plan[0] // 2
    count, depth = rows_scr.shape
    width = own_ref.shape[1]
    sum_scr[...] = square_ref[group * count : (group + 1) * count, :]
    fill_rows(plan, ctx_ref, exp_ref, gain_ref, chunk_refs, offsets, rows_scr, sum_scr, (group,))
    lane = lax.broadcasted_iota(jnp.int32, (1, HEAD_SIZE), 1)
    square = sum_scr[...]
    high = square.astype(jnp.bfloat16).astype(jnp.float32)
    act_ref[:, 2 * width :] = jnp.where(lane == 0, high, square - high).astype(jnp.bfloat16)
    start = (1 - lax.shift_right_logical(ctx_ref[0], bits_of(half))) * depth
    at = pl.ds(pl.multiple_of(start, depth), depth)
    for place, ref in enumerate((own_ref, other_ref)):
        cols = slice(place * width, (place + 1) * width)
        act = first_ref[group * count : (group + 1) * count, cols] + jnp.dot(
            rows_scr[...], ref[at, :], preferred_element_type=jnp.float32
        )
        act_ref[:, cols] = act.astype(jnp.bfloat16)


def experts_out_kernel(plan, group, places, state_at, route_at, model_width, ctx_ref, exp_ref, act_ref, came_ref, *refs):
    ctx_count, exp_count, tok = plan
    x_count, half = exp_count // 2, ctx_count // 2
    route_refs, refs = refs[: x_count + 1], refs[x_count + 1 :]
    (own_ref, other_ref, _), rest = refs[:3], refs[3:]
    state_count = 1 + max((array for pair in state_at for array, _ in pair), default=-1)
    state_refs, rest = rest[:state_count], rest[state_count:]
    out_refs, hidden_scr = rest[:-1], rest[-1]
    my_ctx = ctx_ref[0]
    my_core = lax.bitwise_and(exp_ref[0], 1)
    mine = lax.shift_right_logical(my_ctx, bits_of(half))
    first_ctx = (mine if group == 1 else 1 - mine) * half
    width = (act_ref.shape[1] - HEAD_SIZE) // 2
    hidden = width // 2
    lane = lax.broadcasted_iota(jnp.int32, (tok, HEAD_SIZE), 1)
    blocks = []
    for array, row in route_at:
        blocks.append(route_refs[array][row : row + tok, 0:HEAD_SIZE].astype(jnp.float32))
    columns = []
    for x_off in range(x_count):
        for low in range(half):
            for core in range(2):
                same, swapped = blocks[2 * x_off + core], blocks[2 * x_off + 1 - core]
                block = jnp.where(my_core == 0, same, swapped)
                picked = jnp.where(lane % ctx_count == first_ctx + low, block, 0.0)
                columns.append(jnp.sum(picked, axis=1, keepdims=True))
    route = jnp.concatenate(columns, axis=0)
    squares = act_ref[:, 2 * width :].astype(jnp.float32) + came_ref[:, 2 * width :].astype(jnp.float32)
    norm = lax.rsqrt((squares[:, 0:1] + squares[:, 1:2]) / model_width + 1e-06)
    scaled_route = norm * route
    for side in range(2):
        acts = act_ref[:, side * width : (side + 1) * width].astype(jnp.float32) + came_ref[
            :, (1 - side) * width : (2 - side) * width
        ].astype(jnp.float32)
        gate = acts[:, :hidden] * norm
        value = gate / (1.0 + jnp.exp(-gate)) * (acts[:, hidden:] * scaled_route)
        hidden_scr[:, side * hidden : (side + 1) * hidden] = value.astype(jnp.bfloat16)
    picked = []
    for place in places:
        x_off = by_core(my_core, place, 1)
        low = lax.bitwise_and(lax.bitwise_xor(my_ctx, by_core(my_core, place, 0)), half - 1)
        row = pl.multiple_of((x_off * half + low) * (2 * tok), 2 * tok)
        picked.append(hidden_scr[pl.ds(row, 2 * tok), :])
    picked = jnp.concatenate(picked, axis=0)
    out_cols = own_ref.shape[1]
    step = min(512, out_cols)
    for col in range(0, out_cols, step):
        at = pl.ds(col, step)
        out = jnp.dot(picked[:, :hidden], own_ref[:, at], preferred_element_type=jnp.float32)
        out = out + jnp.dot(picked[:, hidden:], other_ref[:, at], preferred_element_type=jnp.float32)
        for place, ref in enumerate(out_refs):
            ref[:, at] = out[place * 2 * tok : (place + 1) * 2 * tok, :].astype(ref.dtype)
    for place, ref in zip(places, out_refs):
        if place[0] == (0, 0):
            for c_off, pair in enumerate(state_at):
                states = []
                for array, first_row in pair:
                    own_row = pl.multiple_of(first_row + my_ctx * (2 * tok), 2 * tok)
                    states.append(state_refs[array][pl.ds(own_row, 2 * tok), :].astype(jnp.float32))
                state = states[0] if pair[0] == pair[1] else jnp.where(my_core == 0, *states)
                cols = state.shape[1]
                at = pl.ds(pl.multiple_of(lax.bitwise_xor(my_ctx, c_off) * cols, cols), cols)
                ref[:, at] = ref[:, at] + state


def shards(
    residual,
    encoded_query_rows,
    quantized_key_rows,
    quantized_value_rows,
    key_block_exponent,
    value_block_exponent,
    block_order,
    out_weight,
    norm_gain,
    expert_ids,
    route_weight,
    gate_weight,
    gate_scale,
    up_weight,
    up_scale,
    down_weight,
    down_scale,
):
    f32, bf16 = jnp.float32, jnp.bfloat16
    vmem = pl.BlockSpec(memory_space=pltpu.VMEM)
    smem = pl.BlockSpec(memory_space=pltpu.SMEM)
    anywhere = pl.BlockSpec(memory_space=pl.ANY)
    span, query_width = encoded_query_rows.shape
    heads = query_width // HEAD_SIZE
    group = QUERY_HEADS // KEY_VALUE_HEADS
    ctx_count = lax.axis_size("ctx")
    exp_count = lax.axis_size("exp")
    x_count = exp_count // 2
    experts = ctx_count * x_count
    tok, model_width = residual.shape
    half_width = model_width // 2
    cols = half_width // ctx_count
    my_ctx = lax.axis_index("ctx").astype(jnp.int32).reshape(1)
    my_exp = lax.axis_index("exp").astype(jnp.int32).reshape(1)
    route, places = gather_route(ctx_count, x_count)

    hbm = pl.BlockSpec(memory_space=pltpu.HBM)
    piece_shape = jax.ShapeDtypeStruct((ctx_count // 2, tok, 2 * cols), bf16)
    row_route, row_places = gather_route(ctx_count, x_count, rows_only=True)
    names = sorted(row_places)
    piece_names = [[key for key in names if bool(key[0] & 2) == sent] for sent in (False, True)]
    piece_places = tuple(tuple(row_places[key] for key in keys) for keys in piece_names)
    packed, near, far = pl.pallas_call(
        functools.partial(pack_kernel, (heads, group, piece_places)),
        in_specs=[smem] * 2 + [hbm] * 8,
        out_specs=[vmem] * 3,
        out_shape=[
            jax.ShapeDtypeStruct((span, query_width + 3 * HEAD_SIZE), bf16),
            piece_shape,
            piece_shape,
        ],
        scratch_shapes=[
            pltpu.VMEM(key_block_exponent.shape, jnp.int32),
            pltpu.VMEM(key_block_exponent.shape, jnp.int32),
            pltpu.VMEM((span, HEAD_SIZE), bf16),
            pltpu.VMEM((span, HEAD_SIZE), bf16),
            pltpu.VMEM((TOP, tok), jnp.int32),
            pltpu.VMEM((TOP, tok), f32),
            pltpu.SemaphoreType.DMA((7 + ctx_count,)),
        ],
        compiler_params=pltpu.CompilerParams(vmem_limit_bytes=8 * MIB),
        name="pack",
    )(
        my_ctx,
        my_exp,
        *in_hbm(
            key_block_exponent,
            value_block_exponent,
            encoded_query_rows,
            quantized_key_rows,
            quantized_value_rows,
            jnp.transpose(expert_ids),
            jnp.transpose(route_weight),
            residual,
        ),
    )
    piece_arrays = [near]
    piece_at = {(0, key[0]): (0, place) for place, key in enumerate(piece_names[0])}
    piece_bits = [1, *range(bits_of(ctx_count) - 1, 1, -1), 0]
    sending, weights = far, {}

    def beside(number, came):
        nonlocal sending
        bit = 1 << piece_bits[number]
        moves = {1: ((2, 0), (1, 0)), 0: ((1, 0), (2, 0))}.get(piece_bits[number], ((bit, 0),) * 2)
        if number == 0:
            keys = [(0, key[0]) for key in piece_names[1]]
        else:
            keys = sorted(key for key in piece_at if key[1] & bit)
            sending = jnp.stack([piece_arrays[array][place] for array, place in map(piece_at.pop, keys)])
        pieces = follow(sending, moves)
        if number == 0:
            own, give = deq_in(my_exp, gate_weight, gate_scale, up_weight, up_scale, ctx_count, packed)
            *came, pieces, weights["in_own"], weights["in_give"] = together(*came, pieces, own, give)
        elif number == 1:
            other = from_offset(weights["in_give"], 1)
            own, give = deq_down(my_exp, down_weight, down_scale, ctx_count, piece_arrays[-1])
            *came, pieces, weights["in_other"], weights["down_own"], weights["down_give"] = together(
                *came, pieces, other, own, give
            )
        elif number < len(piece_bits) - 1:
            *came, pieces = together(*came, pieces)
        for place, (source, target) in enumerate(keys):
            piece_at[source ^ bit, target ^ bit] = (len(piece_arrays), place)
        piece_arrays.append(pieces)
        return came

    packed, packed_at = spread(packed, stages_of(row_route), beside)
    attend_at = tuple((packed_at[key], row_places[key]) for key in names)
    attend_pieces = tuple(piece_at[key[0], 0] for key in names)
    in_own, in_other, down_own = weights["in_own"], weights["in_other"], weights["down_own"]
    down_other = from_offset(weights["down_give"], 1)

    positions = ctx_count * span
    per_x = 2 * ctx_count * tok
    *keeps, give, own_route = pl.pallas_call(
        functools.partial(attend_kernel, (ctx_count, exp_count, tok, heads, attend_pieces, attend_at)),
        in_specs=[smem] * 3 + [vmem] * (len(packed) + len(piece_arrays) + 1) + [anywhere],
        out_specs=[vmem] * (2 + x_count),
        out_shape=[jax.ShapeDtypeStruct((per_x, cols), f32)] * x_count
        + [
            jax.ShapeDtypeStruct((x_count * (per_x + tok), cols), bf16),
            jax.ShapeDtypeStruct((x_count * tok, cols), bf16),
        ],
        scratch_shapes=[
            pltpu.VMEM((positions, HEAD_SIZE), bf16),
            pltpu.VMEM((positions, HEAD_SIZE), bf16),
            pltpu.VMEM((8, positions), jnp.int32),
            pltpu.VMEM((positions, query_width), bf16),
        ],
        compiler_params=pltpu.CompilerParams(vmem_limit_bytes=3 * ctx_count * MIB),
        cost_estimate=pl.CostEstimate(
            flops=4 * positions * positions * query_width + 4 * positions * query_width * cols,
            bytes_accessed=8 * MIB,
            transcendentals=heads * positions * positions,
        ),
        name="attend",
    )(my_ctx, my_exp, block_order, *packed, *piece_arrays, out_weight, down_other)

    given = from_offset(give, 1)
    routes, route_at, state = [own_route, given], [(0, 0), (1, x_count * per_x)], keeps[0]
    state = state + given[:per_x].astype(f32)
    for x_off in range(1, x_count):
        part = keeps[x_off] + given[x_off * per_x : (x_off + 1) * per_x].astype(f32)
        row = x_count * per_x + x_off * tok
        own = own_route[x_off * tok : (x_off + 1) * tok]
        sent = jnp.concatenate([part.astype(bf16), own, given[row : row + tok]], axis=0)
        came = from_offset(sent, 2 * x_off)
        state = state + came[:per_x].astype(f32)
        route_at += [(len(routes), per_x), (len(routes), per_x + tok)]
        routes.append(came)
    state = state.astype(bf16)

    stages = stages_of(route)
    chunks, chunk_at = spread(state, stages)
    gain = norm_gain.reshape(1, model_width)
    rows = x_count * per_x
    in_width = in_own.shape[1]
    near = tuple(sorted(key for key in places if key[0] < ctx_count // 2))
    far = tuple(sorted(key for key in places if key[0] >= ctx_count // 2))

    def picked(keys):
        arrays = sorted({chunk_at[key][0] for key in keys})
        at = tuple(((arrays.index(chunk_at[key][0]), chunk_at[key][1]), places[key]) for key in keys)
        return [chunks[array] for array in arrays], at

    near_chunks, near_places = picked(near)
    far_chunks, far_places = picked(far)
    first_act, first_square = pl.pallas_call(
        functools.partial(experts_in_first, (ctx_count, x_count, tok), near_places),
        in_specs=[smem] * 2 + [vmem] * (len(near_chunks) + 3) + [anywhere],
        out_specs=[vmem] * 2,
        out_shape=[
            jax.ShapeDtypeStruct((rows, 2 * in_width), f32),
            jax.ShapeDtypeStruct((rows, 1), f32),
        ],
        scratch_shapes=[pltpu.VMEM((rows, half_width // 2), bf16)],
        compiler_params=pltpu.CompilerParams(vmem_limit_bytes=2 * ctx_count * MIB),
        cost_estimate=pl.CostEstimate(
            flops=2 * rows * half_width * in_width, bytes_accessed=8 * MIB, transcendentals=0
        ),
        name="experts_in_first",
    )(my_ctx, my_exp, *near_chunks, gain, in_own, in_other, down_other)
    acts = []
    for part in range(2):
        acts.append(
            pl.pallas_call(
                functools.partial(experts_in_second, (ctx_count, x_count, tok), far_places, part),
                in_specs=[smem] * 2 + [vmem] * (len(far_chunks) + 5) + [anywhere],
                out_specs=vmem,
                out_shape=jax.ShapeDtypeStruct((rows // 2, 2 * in_width + HEAD_SIZE), bf16),
                scratch_shapes=[
                    pltpu.VMEM((rows // 2, half_width // 2), bf16),
                    pltpu.VMEM((rows // 2, 1), f32),
                ],
                compiler_params=pltpu.CompilerParams(vmem_limit_bytes=2 * ctx_count * MIB),
                cost_estimate=pl.CostEstimate(
                    flops=rows * half_width * in_width, bytes_accessed=8 * MIB, transcendentals=0
                ),
                name="experts_in_second",
            )(
                my_ctx,
                my_exp,
                *far_chunks,
                gain,
                in_own,
                in_other,
                first_act,
                first_square,
                acts[0] if part else first_square,
            )
        )
    leaves = set(places) - {source for _, source, _, _ in route}
    sums = {}
    for part in range(2):
        slots = near if part == 1 else far
        state_keys = [
            next(key for key in places if places[key][core] == (offset, 0))
            for offset in (range(ctx_count) if part == 1 else ())
            for core in range(2)
        ]
        states, state_at = picked(state_keys)
        state_at = tuple((state_at[i][0], state_at[i + 1][0]) for i in range(0, len(state_at), 2))
        outs = pl.pallas_call(
            functools.partial(
                experts_out_kernel,
                (ctx_count, exp_count, tok),
                part,
                tuple(places[key] for key in slots),
                state_at,
                tuple(route_at),
                model_width,
            ),
            in_specs=[smem] * 2 + [vmem] * (5 + x_count) + [anywhere] + [vmem] * len(states),
            out_specs=[vmem] * len(slots),
            out_shape=[
                jax.ShapeDtypeStruct((2 * tok, half_width), bf16 if slot in leaves else f32)
                for slot in slots
            ],
            scratch_shapes=[pltpu.VMEM((rows // 2, in_width), bf16)],
            compiler_params=pltpu.CompilerParams(vmem_limit_bytes=2 * ctx_count * MIB),
            cost_estimate=pl.CostEstimate(
                flops=rows * half_width * in_width,
                bytes_accessed=8 * MIB,
                transcendentals=rows * in_width // 2,
            ),
            name="experts_out",
        )(
            my_ctx,
            my_exp,
            acts[part],
            from_offset(acts[part], 1),
            *routes,
            down_own,
            down_other,
            sums[slots_done[0]] if part else acts[1],
            *states,
        )
        slots_done = slots
        sums.update(zip(slots, outs))

    for number, sends in enumerate(reversed(stages)):
        came = []
        for moves, _, targets in sends:
            sent = [sums[key].astype(bf16) for key in targets]
            came.append(follow(sent[0] if len(sent) == 1 else jnp.concatenate(sent, axis=0), moves))
        if number < len(stages) - 1:
            waiting = list(near) if number == 0 else []
            values = together(*came, *[sums[key] for key in waiting])
            came = values[: len(came)]
            sums.update(zip(waiting, values[len(came) :]))
        for (_, sources, _), array in zip(sends, came):
            for place, key in enumerate(sources):
                part = array[place * 2 * tok : (place + 1) * 2 * tok]
                sums[key] = sums[key] + part.astype(f32)
    total = sums[0, 0]
    core = lax.bitwise_and(my_exp[0], 1)
    mine = jnp.where(core == 0, total[:tok], total[tok:]).astype(bf16)
    came = from_offset(jnp.where(core == 0, total[tok:], total[:tok]).astype(bf16), 1)
    mine = mine.reshape(tok, ctx_count, 1, cols)
    came = came.reshape(tok, ctx_count, 1, cols)
    result = jnp.where(core == 0, jnp.concatenate([mine, came], axis=2), jnp.concatenate([came, mine], axis=2))
    return result.reshape(tok, model_width)


def solution(mesh):
    return jax.shard_map(
        shards,
        mesh=mesh,
        in_specs=(
            P(("dp", "ctx", "exp"), None),
            P(("dp", "ctx"), "exp"),
            P(("dp", "ctx"), None),
            P(("dp", "ctx"), None),
            P(("dp", "ctx"), None),
            P(("dp", "ctx"), None),
            P(),
            P("exp", "ctx"),
            P(),
            P(("dp", "ctx", "exp"), None),
            P(("dp", "ctx", "exp"), None),
            P(("ctx", "exp"), None, None),
            P(("ctx", "exp"), None, None),
            P(("ctx", "exp"), None, None),
            P(("ctx", "exp"), None, None),
            P(("ctx", "exp"), None, None),
            P(("ctx", "exp"), None, None),
        ),
        out_specs=P(("dp", "ctx", "exp"), None),
        check_vma=False,
    )
```

```python
import functools
import math

import jax
import jax.numpy as jnp
from jax import lax
from jax.experimental import pallas as pl
from jax.experimental.pallas import tpu as pltpu
from jax.sharding import PartitionSpec as P

QUERY_HEADS = 32
KEY_VALUE_HEADS = 4
HEAD_SIZE = 128
TOP = 8
SCALE_POSITIONS = 64
WB = 128
MIB = 1 << 20


def bits_of(count):
    return count.bit_length() - 1


def from_offset(array, offset):
    return lax.ppermute(array, "exp", [(i, i ^ offset) for i in range(lax.axis_size("exp"))])


def from_ctx(array, offset):
    return lax.ppermute(array, "ctx", [(i, i ^ offset) for i in range(lax.axis_size("ctx"))])


def moved(offset, move):
    return (offset[0] ^ move[0], offset[1] ^ move[1])


def gather_route(ctx_count, x_count, rows_only=False):
    transfers, arrival, places = [], {(0, 0): 0}, {(0, 0): ((0, 0), (0, 0))}

    def go(source, moves, delay=0):
        reached = tuple(moved(place, (c, e >> 1)) for place, (c, e) in zip(places[source], moves))
        target = reached[0]
        arrival[target], places[target] = arrival[source] + 1 + delay, reached
        transfers.append((arrival[target], source, target, moves))
        return target

    bits = bits_of(ctx_count)
    y_move = (1, 0)
    if (ctx_count, x_count) == (8, 2) and not rows_only:
        z_far, z_near = ((4, 0),) * 2, ((2, 0),) * 2
        first, second = ((0, 2), y_move), (y_move, (0, 2))
        at = {"0": (0, 0)}
        for stage, moves, hops in (
            (1, z_far, "0>4"),
            (1, z_near, "0>2"),
            (1, first, "0>0a"),
            (1, second, "0>0b"),
            (2, z_near, "4>6 0b>2b"),
            (2, first, "2>2a 4>4a"),
            (2, second, "4>4b 0a>0ab"),
            (3, z_near, "4a>6a"),
            (3, second, "2a>2ab 4a>4ab 6>6b"),
            (4, second, "6a>6ab"),
        ):
            for hop in hops.split():
                source, target = hop.split(">")
                at[target] = go(at[source], moves, stage - 1 - arrival[at[source]])
        return sorted(transfers, key=lambda transfer: transfer[0]), places
    if rows_only:
        shared, steps = range(bits - 1, 1, -1), [(2, 0), y_move]
    else:
        shared, steps = range(bits - 1, 0, -1), [(0, 2 << bit) for bit in range(bits_of(x_count))] + [y_move]
    pairs = list(zip(steps, reversed(steps)))
    for bit in shared:
        for source in list(arrival):
            go(source, ((1 << bit, 0),) * 2)
    for first in sorted(arrival):
        held = [first]
        for moves in pairs:
            held = held + [go(source, moves) for source in held]
    return sorted(transfers, key=lambda transfer: transfer[0]), places


def follow(array, moves):
    exp_count = lax.axis_size("exp")
    pairs = []
    for c in range(lax.axis_size("ctx")):
        for e in range(exp_count):
            far = moved((c, e), moves[e % 2])
            pairs.append((far[0] * exp_count + far[1], c * exp_count + e))
    return lax.ppermute(array, ("ctx", "exp"), pairs)


def by_core(core, place, part):
    first, second = place[0][part], place[1][part]
    return first if first == second else jnp.where(core == 0, first, second)


def stages_of(route):
    stages, arrays = [], [((0, 0),)]
    top = max(moves[0][0] for _, _, _, moves in route)
    for stage in sorted({transfer[0] for transfer in route}):
        sends = []
        for moves in sorted({t[3] for t in route if t[0] == stage}):
            left = {source: target for number, source, target, way in route if (number, way) == (stage, moves)}
            groups = [group for group in arrays if len(group) > 1 and all(key in left for key in group)]
            rest = tuple(sorted(key for key in left if not any(key in group for group in groups)))
            for group in groups + [rest] * bool(rest):
                sends.append((moves, group, tuple(left[key] for key in group)))
        def load(send):
            share = 1 if send[0][0] == send[0][1] else 0.5
            return len(send[1]) * (2 if send[0][0][0] == top > 2 else share)

        sends.sort(key=lambda send: (-load(send), send[0][0] != send[0][1]))
        arrays = arrays + [send[2] for send in sends]
        stages.append(sends)
    return stages


def spread(block, stages, beside=None):
    arrays, at, joined = [block], {(0, 0): (0, 0)}, {}
    rows = block.shape[0]
    for number, sends in enumerate(stages):
        came = []
        for moves, group, _ in sends:
            first, row = at[group[0]]
            whole = row == 0 and arrays[first].shape[0] == len(group) * rows
            if whole and all(at[key] == (first, place * rows) for place, key in enumerate(group)):
                joined[group] = arrays[first]
            elif group not in joined:
                parts = [arrays[at[key][0]][at[key][1] : at[key][1] + rows] for key in group]
                joined[group] = jnp.concatenate(parts, axis=0)
            came.append(follow(joined[group], moves))
        came = beside(number, came) if beside else (together(*came) if number < len(stages) - 1 else came)
        for (_, _, targets), array in zip(sends, came):
            at.update({key: (len(arrays), place * rows) for place, key in enumerate(targets)})
            arrays.append(array)
    return arrays, at


def together(*values):
    return lax.optimization_barrier(values)


def block_factor(exponent, width):
    factor = jnp.where(exponent < 0, 0.5, jnp.where(exponent > 0, 2.0, 1.0))
    return jnp.full((1, width), factor, jnp.float32).astype(jnp.bfloat16)


def in_hbm(*arrays):
    return [pltpu.with_memory_space_constraint(array, pltpu.HBM) for array in arrays]


def copy_all(sems, pairs):
    copies = [pltpu.make_async_copy(src, dst, sems.at[i]) for i, (src, dst) in enumerate(pairs)]
    for copy in copies:
        copy.start()
    return copies


def pack_kernel(plan, ctx_ref, exp_ref, key_scale_hbm, value_scale_hbm, query_hbm, key_hbm, value_hbm, ids_hbm,
                route_hbm, residual_hbm, packed_ref, near_ref, far_ref, key_scale_ref, value_scale_ref,
                key_ref, value_ref, ids_ref, route_ref, sems):
    heads, group, x_count, piece_places = plan
    span, width = query_hbm.shape
    half, tok, cols = near_ref.shape
    cols = cols - HEAD_SIZE
    my_ctx, my_exp = ctx_ref[0], exp_ref[0]
    kv_head = my_exp * heads // group
    at = pl.ds(pl.multiple_of(kv_head * HEAD_SIZE, HEAD_SIZE), HEAD_SIZE)
    pairs = [
        (key_scale_hbm, key_scale_ref),
        (value_scale_hbm, value_scale_ref),
        (key_hbm.at[:, at], key_ref),
        (value_hbm.at[:, at], value_ref),
        (ids_hbm, ids_ref),
        (route_hbm, route_ref),
        (query_hbm, packed_ref.at[:, 2 * HEAD_SIZE : 2 * HEAD_SIZE + width]),
    ]
    core = lax.bitwise_and(my_exp, 1)
    for ref, places in zip((near_ref, far_ref), piece_places):
        for number, place in enumerate(places):
            col = pl.multiple_of(lax.bitwise_xor(my_ctx, by_core(core, place, 0)) * cols, cols)
            pairs.append((residual_hbm.at[:, pl.ds(col, cols)], ref.at[number, :, 0:cols]))
    copies = copy_all(sems, pairs)
    for copy in copies[:6]:
        copy.wait()
    lane = lax.broadcasted_iota(jnp.int32, key_scale_ref.shape, 1)
    blocks = key_scale_ref.shape[0]
    for place, (ref, scale_ref) in enumerate(((key_ref, key_scale_ref), (value_ref, value_scale_ref))):
        exponent = scale_ref[...]
        factor = jnp.where(
            exponent < -1, 0.25, jnp.where(exponent < 0, 0.5, jnp.where(exponent < 1, 1.0, 2.0))
        )
        factor = jnp.sum(jnp.where(lane == kv_head, factor, 0.0), axis=1, keepdims=True)
        for block in range(blocks):
            rows = pl.ds(block * (span // blocks), span // blocks)
            scaled = ref[rows, :].astype(jnp.float32) * factor[block : block + 1, :]
            packed_ref[rows, pl.ds(place * HEAD_SIZE, HEAD_SIZE)] = scaled.astype(jnp.bfloat16)
    number = lax.broadcasted_iota(jnp.int32, (128, tok), 0)
    dense = jnp.zeros((128, tok), jnp.float32)
    for k in range(TOP):
        dense = dense + jnp.where(ids_ref[k : k + 1, :] == number, route_ref[k : k + 1, :], 0.0)
    dense = jnp.concatenate([dense, jnp.zeros((128, 128 - tok), jnp.float32)], axis=1)
    dense = jnp.transpose(dense)[:tok, :]
    lane = lax.broadcasted_iota(jnp.int32, (tok, HEAD_SIZE), 1)
    for ref, places in zip((near_ref, far_ref), piece_places):
        for number, place in enumerate(places):
            expert = lax.bitwise_xor(my_ctx, by_core(core, place, 0)) * x_count
            block = jnp.zeros((tok, HEAD_SIZE), jnp.float32)
            for x in range(x_count):
                column = jnp.sum(jnp.where(lane == expert + x, dense, 0.0), axis=1, keepdims=True)
                high = column.astype(jnp.bfloat16).astype(jnp.float32)
                block = jnp.where(lane == x, high, jnp.where(lane == x_count + x, column - high, block))
            ref[number, :, cols:] = block.astype(jnp.bfloat16)
    for copy in copies[6:]:
        copy.wait()


def deq_in_kernel(ctx_count, exp_ref, gate_scale_hbm, up_scale_hbm, gate_hbm, up_hbm, _, own_ref, give_ref,
                  gate_ref, up_ref, gate_scale_ref, up_scale_ref, sems):
    core = lax.bitwise_and(exp_ref[0], 1)
    width, cols = gate_ref.shape
    rows = width // (2 * ctx_count)
    pairs = [(gate_scale_hbm, gate_scale_ref), (up_scale_hbm, up_scale_ref)]
    for step in range(ctx_count):
        at = pl.ds(step * 2 * rows, 2 * rows)
        pairs += [(gate_hbm.at[0, at], gate_ref.at[at]), (up_hbm.at[0, at], up_ref.at[at])]
    copies = copy_all(sems, pairs)
    for copy in copies[:2]:
        copy.wait()
    for step in range(ctx_count):
        for half, (ref, scale_ref) in enumerate(((gate_ref, gate_scale_ref), (up_ref, up_scale_ref))):
            copies[2 + 2 * step + half].wait()
            for out_ref, side in ((give_ref, 1 - core), (own_ref, core)):
                first = (2 * step + side) * (rows // WB)
                for i in range(rows // WB):
                    row = pl.multiple_of((2 * step + side) * rows + i * WB, WB)
                    for j in range(cols // WB):
                        factor = block_factor(scale_ref[j, 0, first + i], WB)
                        out_ref[pl.ds(step * rows + i * WB, WB), pl.ds(half * cols + j * WB, WB)] = (
                            ref[pl.ds(row, WB), pl.ds(j * WB, WB)] * factor
                        )


def deq_in(my_exp, gate_weight, gate_scale, up_weight, up_scale, ctx_count, after):
    width, hidden = gate_weight.shape[1:]
    shape = jax.ShapeDtypeStruct((width // 2, 2 * hidden), jnp.bfloat16)
    gate_scale = jnp.transpose(gate_scale, (2, 0, 1))
    up_scale = jnp.transpose(up_scale, (2, 0, 1))
    return pl.pallas_call(
        functools.partial(deq_in_kernel, ctx_count),
        in_specs=[pl.BlockSpec(memory_space=pltpu.SMEM)]
        + [pl.BlockSpec(memory_space=pltpu.HBM)] * 4
        + [pl.BlockSpec(memory_space=pl.ANY)],
        out_specs=[pl.BlockSpec(memory_space=pltpu.VMEM)] * 2,
        out_shape=[shape, shape],
        scratch_shapes=[
            pltpu.VMEM((width, hidden), jnp.bfloat16),
            pltpu.VMEM((width, hidden), jnp.bfloat16),
            pltpu.SMEM(gate_scale.shape, jnp.int32),
            pltpu.SMEM(up_scale.shape, jnp.int32),
            pltpu.SemaphoreType.DMA((2 + 2 * ctx_count,)),
        ],
        compiler_params=pltpu.CompilerParams(vmem_limit_bytes=20 * MIB),
        cost_estimate=pl.CostEstimate(
            flops=2 * width * hidden, bytes_accessed=8 * width * hidden, transcendentals=0
        ),
        name="dequant_in",
    )(my_exp, *in_hbm(gate_scale, up_scale, gate_weight, up_weight), after)


def deq_down_kernel(ctx_count, exp_ref, scale_hbm, down_hbm, _, own_ref, give_ref, down_ref, scale_ref, sems):
    core = lax.bitwise_and(exp_ref[0], 1)
    rows, width = down_ref.shape
    cols = width // (2 * ctx_count)
    pairs = [(scale_hbm, scale_ref)]
    for step in range(ctx_count):
        at = pl.ds(step * 2 * cols, 2 * cols)
        pairs.append((down_hbm.at[0, :, at], down_ref.at[:, at]))
    copies = copy_all(sems, pairs)
    copies[0].wait()
    for step in range(ctx_count):
        copies[1 + step].wait()
        for out_ref, side in ((give_ref, 1 - core), (own_ref, core)):
            first = (2 * step + side) * (cols // WB)
            for j in range(cols // WB):
                col = pl.multiple_of((2 * step + side) * cols + j * WB, WB)
                for i in range(rows // WB):
                    factor = block_factor(scale_ref[i, 0, first + j], WB)
                    out_ref[pl.ds(i * WB, WB), pl.ds(step * cols + j * WB, WB)] = (
                        down_ref[pl.ds(i * WB, WB), pl.ds(col, WB)] * factor
                    )


def deq_down(my_exp, down_weight, down_scale, ctx_count, after):
    hidden, width = down_weight.shape[1:]
    shape = jax.ShapeDtypeStruct((hidden, width // 2), jnp.bfloat16)
    down_scale = jnp.transpose(down_scale, (1, 0, 2))
    return pl.pallas_call(
        functools.partial(deq_down_kernel, ctx_count),
        in_specs=[pl.BlockSpec(memory_space=pltpu.SMEM)]
        + [pl.BlockSpec(memory_space=pltpu.HBM)] * 2
        + [pl.BlockSpec(memory_space=pl.ANY)],
        out_specs=[pl.BlockSpec(memory_space=pltpu.VMEM)] * 2,
        out_shape=[shape, shape],
        scratch_shapes=[
            pltpu.VMEM((hidden, width), jnp.bfloat16),
            pltpu.SMEM(down_scale.shape, jnp.int32),
            pltpu.SemaphoreType.DMA((1 + ctx_count,)),
        ],
        compiler_params=pltpu.CompilerParams(vmem_limit_bytes=12 * MIB),
        cost_estimate=pl.CostEstimate(
            flops=width * hidden, bytes_accessed=4 * width * hidden, transcendentals=0
        ),
        name="dequant_down",
    )(my_exp, *in_hbm(down_scale, down_weight), after)


def attend_kernel(plan, ctx_ref, exp_ref, order_ref, *refs):
    ctx_count, exp_count, tok, heads, piece_places, attend_at = plan
    packed_at, places_of = [at for at, _ in attend_at], [place for _, place in attend_at]
    array_count = 1 + max(array for array, _ in packed_at)
    span = exp_count * tok
    packed_refs, refs = refs[:array_count], refs[array_count:]
    packed = []
    for array, row in packed_at:
        packed.append(packed_refs[array].at[pl.ds(row, span)])
    piece_refs, refs = refs[: 1 + bits_of(ctx_count)], refs[1 + bits_of(ctx_count) :]
    weight_ref, rest = refs[0], refs[2:]
    x_count = exp_count // 2
    keep_refs, (give_ref, own_route_ref) = rest[:x_count], rest[x_count : x_count + 2]
    key_scr, value_scr, place_scr, att_scr = rest[x_count + 2 :]
    positions = ctx_count * span
    my_ctx, my_exp = ctx_ref[0], exp_ref[0]
    my_x, my_core = lax.shift_right_logical(my_exp, 1), lax.bitwise_and(my_exp, 1)
    lane = lax.broadcasted_iota(jnp.int32, (8, positions), 1)
    places = lane % span
    for offset, ref in enumerate(packed):
        key_scr[pl.ds(offset * span, span), :] = ref[:, 0:HEAD_SIZE]
        value_scr[pl.ds(offset * span, span), 0:HEAD_SIZE] = ref[:, HEAD_SIZE : 2 * HEAD_SIZE]
        base = order_ref[lax.bitwise_xor(my_ctx, by_core(my_core, places_of[offset], 0))] * span
        places = places + jnp.where(lane // span == offset, base, 0)
    place_scr[...] = places
    scale = math.log2(math.e) / math.sqrt(HEAD_SIZE)
    value_scr[:, HEAD_SIZE:] = jnp.ones((positions, HEAD_SIZE), jnp.bfloat16)
    for offset, ref in enumerate(packed):
        source = lax.bitwise_xor(my_ctx, by_core(my_core, places_of[offset], 0))
        queries = jnp.concatenate(
            [ref[:, (h + 2) * HEAD_SIZE : (h + 3) * HEAD_SIZE] for h in range(heads)], axis=0
        )
        scores = lax.dot_general(
            queries, key_scr[...], (((1,), (1,)), ((), ())), preferred_element_type=jnp.float32
        )
        own_place = order_ref[source] * span + lax.broadcasted_iota(jnp.int32, (span, positions), 0)
        bias = jnp.where(place_scr[0:1, :] <= own_place, 0.0, -1e30)
        scores = scores.reshape(heads, span, positions) * scale + bias[None]
        exps = jnp.exp2(scores - jnp.max(scores, axis=-1, keepdims=True))
        mixed = jnp.dot(
            exps.astype(jnp.bfloat16).reshape(heads * span, positions),
            value_scr[...],
            preferred_element_type=jnp.float32,
        )
        mixed = mixed[:, :HEAD_SIZE] * (1.0 / mixed[:, HEAD_SIZE : HEAD_SIZE + 1])
        mixed = mixed.astype(jnp.bfloat16).reshape(heads, span, HEAD_SIZE)
        for owner in range(exp_count):
            x_off = lax.bitwise_xor(my_x, owner // 2)
            row = pl.multiple_of(((x_off * ctx_count + source) * 2 + owner % 2) * tok, tok)
            for head in range(heads):
                att_scr[pl.ds(row, tok), pl.ds(head * HEAD_SIZE, HEAD_SIZE)] = mixed[
                    head, owner * tok : (owner + 1) * tok, :
                ]

    cols = weight_ref.shape[1] // 2
    per_x = 2 * ctx_count * tok
    route_lane = lax.broadcasted_iota(jnp.int32, (tok, HEAD_SIZE), 1)
    route_base = x_count * per_x
    for x_off in range(x_count):
        rows = pl.ds(x_off * per_x, per_x)
        for which in (1, 0):
            side = lax.bitwise_xor(my_core, which)
            weight = weight_ref[:, pl.ds(pl.multiple_of(side * cols, cols), cols)]
            part = jnp.dot(att_scr[rows, :], weight, preferred_element_type=jnp.float32)
            out_ref = give_ref if which else keep_refs[x_off]
            out_ref[pl.ds(x_off * per_x if which else 0, per_x), :] = part.astype(out_ref.dtype)
            if x_off == 0:
                for (array, place), place_of in zip(piece_places, places_of):
                    source = lax.bitwise_xor(my_ctx, by_core(my_core, place_of, 0))
                    at = pl.ds(pl.multiple_of((source * 2 + my_core) * tok, tok), tok)
                    piece = piece_refs[array][place, :, pl.ds(pl.multiple_of(side * cols, cols), cols)]
                    value = out_ref[at, :].astype(jnp.float32) + piece.astype(jnp.float32)
                    out_ref[at, :] = value.astype(out_ref.dtype)
        block_out = jnp.zeros((tok, HEAD_SIZE), jnp.float32)
        for (array, place), place_of in zip(piece_places, places_of):
            source = lax.bitwise_xor(my_ctx, by_core(my_core, place_of, 0))
            block = piece_refs[array][place, :, 2 * cols :].astype(jnp.float32)
            for part_of in range(2):
                wanted = lax.bitwise_xor(my_x, x_off) + part_of * x_count
                column = jnp.sum(jnp.where(route_lane == wanted, block, 0.0), axis=1, keepdims=True)
                block_out = jnp.where(route_lane == source + part_of * ctx_count, column, block_out)
        for ref, base in ((give_ref, route_base), (own_route_ref, 0)):
            at = pl.ds(base + x_off * tok, tok)
            ref[at, 0:HEAD_SIZE] = block_out.astype(jnp.bfloat16)
            if cols > HEAD_SIZE:
                ref[at, HEAD_SIZE:] = jnp.zeros((tok, cols - HEAD_SIZE), jnp.bfloat16)


def fill_rows(plan, ctx_ref, exp_ref, gain_ref, chunk_refs, places, rows_scr, square_ref, groups):
    ctx_count, x_count, tok = plan
    half = ctx_count // 2
    my_ctx = ctx_ref[0]
    my_core = lax.bitwise_and(exp_ref[0], 1)
    mine = lax.shift_right_logical(my_ctx, bits_of(half))
    cols = chunk_refs[0].shape[1]
    rows = ctx_count * tok
    for (array, first_row), place_of in places:
        ref = chunk_refs[array]
        source = lax.bitwise_xor(my_ctx, by_core(my_core, place_of, 0))
        x_off = by_core(my_core, place_of, 1)
        gain_at = pl.multiple_of((source * 2 + my_core) * cols, cols)
        gain = gain_ref[:, pl.ds(gain_at, cols)]
        col = pl.multiple_of(lax.bitwise_and(source, half - 1) * cols, cols)
        for place, group in enumerate(groups):
            side = mine if group == 1 else 1 - mine
            chunk_at = pl.ds(pl.multiple_of(first_row + side * rows, rows), rows)
            chunk = ref[chunk_at, :].astype(jnp.float32)
            at = pl.ds(pl.multiple_of((place * x_count + x_off) * rows, rows), rows)
            rows_scr[at, pl.ds(col, cols)] = (chunk * gain).astype(jnp.bfloat16)
            square_ref[at, :] = square_ref[at, :] + jnp.sum(chunk * chunk, axis=-1, keepdims=True)


def experts_in_first(plan, offsets, ctx_ref, exp_ref, *refs):
    chunk_refs, (gain_ref, own_ref, other_ref, _, act_ref, square_ref, rows_scr) = refs[:-7], refs[-7:]
    half = plan[0] // 2
    square_ref[...] = jnp.zeros(square_ref.shape, jnp.float32)
    fill_rows(plan, ctx_ref, exp_ref, gain_ref, chunk_refs, offsets, rows_scr, square_ref, (0, 1))
    depth, width = rows_scr.shape[1], own_ref.shape[1]
    start = lax.shift_right_logical(ctx_ref[0], bits_of(half)) * depth
    at = pl.ds(pl.multiple_of(start, depth), depth)
    for place, ref in enumerate((own_ref, other_ref)):
        act_ref[:, place * width : (place + 1) * width] = jnp.dot(
            rows_scr[...], ref[at, :], preferred_element_type=jnp.float32
        )


def experts_in_second(plan, offsets, group, ctx_ref, exp_ref, *refs):
    chunk_refs, rest = refs[:-9], refs[-9:]
    gain_ref, own_ref, other_ref, first_ref, square_ref, _, act_ref, rows_scr, sum_scr = rest
    half = plan[0] // 2
    count, depth = rows_scr.shape
    width = own_ref.shape[1]
    sum_scr[...] = square_ref[group * count : (group + 1) * count, :]
    fill_rows(plan, ctx_ref, exp_ref, gain_ref, chunk_refs, offsets, rows_scr, sum_scr, (group,))
    lane = lax.broadcasted_iota(jnp.int32, (1, HEAD_SIZE), 1)
    square = sum_scr[...]
    high = square.astype(jnp.bfloat16).astype(jnp.float32)
    act_ref[:, 2 * width :] = jnp.where(lane == 0, high, square - high).astype(jnp.bfloat16)
    start = (1 - lax.shift_right_logical(ctx_ref[0], bits_of(half))) * depth
    at = pl.ds(pl.multiple_of(start, depth), depth)
    for place, ref in enumerate((own_ref, other_ref)):
        cols = slice(place * width, (place + 1) * width)
        act = first_ref[group * count : (group + 1) * count, cols] + jnp.dot(
            rows_scr[...], ref[at, :], preferred_element_type=jnp.float32
        )
        act_ref[:, cols] = act.astype(jnp.bfloat16)


def experts_out_kernel(plan, group, places, state_at, route_at, model_width, ctx_ref, exp_ref, act_ref, came_ref, *refs):
    ctx_count, exp_count, tok = plan
    x_count, half = exp_count // 2, ctx_count // 2
    route_refs, refs = refs[: x_count + 1], refs[x_count + 1 :]
    (own_ref, other_ref, _), rest = refs[:3], refs[3:]
    state_count = 1 + max((array for pair in state_at for array, _ in pair), default=-1)
    state_refs, rest = rest[:state_count], rest[state_count:]
    out_refs, hidden_scr = rest[:-1], rest[-1]
    my_ctx = ctx_ref[0]
    my_core = lax.bitwise_and(exp_ref[0], 1)
    mine = lax.shift_right_logical(my_ctx, bits_of(half))
    first_ctx = (mine if group == 1 else 1 - mine) * half
    width = (act_ref.shape[1] - HEAD_SIZE) // 2
    hidden = width // 2
    lane = lax.broadcasted_iota(jnp.int32, (tok, HEAD_SIZE), 1)
    blocks = []
    for array, row in route_at:
        blocks.append(route_refs[array][row : row + tok, 0:HEAD_SIZE].astype(jnp.float32))
    columns = []
    for x_off in range(x_count):
        for low in range(half):
            for core in range(2):
                same, swapped = blocks[2 * x_off + core], blocks[2 * x_off + 1 - core]
                block = jnp.where(my_core == 0, same, swapped)
                picked = jnp.where(lane % ctx_count == first_ctx + low, block, 0.0)
                columns.append(jnp.sum(picked, axis=1, keepdims=True))
    route = jnp.concatenate(columns, axis=0)
    squares = act_ref[:, 2 * width :].astype(jnp.float32) + came_ref[:, 2 * width :].astype(jnp.float32)
    norm = lax.rsqrt((squares[:, 0:1] + squares[:, 1:2]) / model_width + 1e-06)
    scaled_route = norm * route
    for side in range(2):
        acts = act_ref[:, side * width : (side + 1) * width].astype(jnp.float32) + came_ref[
            :, (1 - side) * width : (2 - side) * width
        ].astype(jnp.float32)
        gate = acts[:, :hidden] * norm
        value = gate / (1.0 + jnp.exp(-gate)) * (acts[:, hidden:] * scaled_route)
        hidden_scr[:, side * hidden : (side + 1) * hidden] = value.astype(jnp.bfloat16)
    picked = []
    for place in places:
        x_off = by_core(my_core, place, 1)
        low = lax.bitwise_and(lax.bitwise_xor(my_ctx, by_core(my_core, place, 0)), half - 1)
        row = pl.multiple_of((x_off * half + low) * (2 * tok), 2 * tok)
        picked.append(hidden_scr[pl.ds(row, 2 * tok), :])
    picked = jnp.concatenate(picked, axis=0)
    out_cols = own_ref.shape[1]
    step = min(512, out_cols)
    for col in range(0, out_cols, step):
        at = pl.ds(col, step)
        out = jnp.dot(picked[:, :hidden], own_ref[:, at], preferred_element_type=jnp.float32)
        out = out + jnp.dot(picked[:, hidden:], other_ref[:, at], preferred_element_type=jnp.float32)
        for place, ref in enumerate(out_refs):
            ref[:, at] = out[place * 2 * tok : (place + 1) * 2 * tok, :].astype(ref.dtype)
    for place, ref in zip(places, out_refs):
        if place[0] == (0, 0):
            for c_off, pair in enumerate(state_at):
                states = []
                for array, first_row in pair:
                    own_row = pl.multiple_of(first_row + my_ctx * (2 * tok), 2 * tok)
                    states.append(state_refs[array][pl.ds(own_row, 2 * tok), :].astype(jnp.float32))
                state = states[0] if pair[0] == pair[1] else jnp.where(my_core == 0, *states)
                cols = state.shape[1]
                at = pl.ds(pl.multiple_of(lax.bitwise_xor(my_ctx, c_off) * cols, cols), cols)
                ref[:, at] = ref[:, at] + state


def shards(
    residual,
    encoded_query_rows,
    quantized_key_rows,
    quantized_value_rows,
    key_block_exponent,
    value_block_exponent,
    block_order,
    out_weight,
    norm_gain,
    expert_ids,
    route_weight,
    gate_weight,
    gate_scale,
    up_weight,
    up_scale,
    down_weight,
    down_scale,
):
    f32, bf16 = jnp.float32, jnp.bfloat16
    vmem = pl.BlockSpec(memory_space=pltpu.VMEM)
    smem = pl.BlockSpec(memory_space=pltpu.SMEM)
    anywhere = pl.BlockSpec(memory_space=pl.ANY)
    span, query_width = encoded_query_rows.shape
    heads = query_width // HEAD_SIZE
    group = QUERY_HEADS // KEY_VALUE_HEADS
    ctx_count = lax.axis_size("ctx")
    exp_count = lax.axis_size("exp")
    x_count = exp_count // 2
    experts = ctx_count * x_count
    tok, model_width = residual.shape
    half_width = model_width // 2
    cols = half_width // ctx_count
    my_ctx = lax.axis_index("ctx").astype(jnp.int32).reshape(1)
    my_exp = lax.axis_index("exp").astype(jnp.int32).reshape(1)
    route, places = gather_route(ctx_count, x_count)

    hbm = pl.BlockSpec(memory_space=pltpu.HBM)
    piece_shape = jax.ShapeDtypeStruct((ctx_count // 2, tok, 2 * cols + HEAD_SIZE), bf16)
    row_route, row_places = gather_route(ctx_count, x_count, rows_only=True)
    names = sorted(row_places)
    piece_names = [[key for key in names if bool(key[0] & 2) == sent] for sent in (False, True)]
    piece_places = tuple(tuple(row_places[key] for key in keys) for keys in piece_names)
    packed, near, far = pl.pallas_call(
        functools.partial(pack_kernel, (heads, group, x_count, piece_places)),
        in_specs=[smem] * 2 + [hbm] * 8,
        out_specs=[vmem] * 3,
        out_shape=[
            jax.ShapeDtypeStruct((span, query_width + 2 * HEAD_SIZE), bf16),
            piece_shape,
            piece_shape,
        ],
        scratch_shapes=[
            pltpu.VMEM(key_block_exponent.shape, jnp.int32),
            pltpu.VMEM(key_block_exponent.shape, jnp.int32),
            pltpu.VMEM((span, HEAD_SIZE), bf16),
            pltpu.VMEM((span, HEAD_SIZE), bf16),
            pltpu.VMEM((TOP, tok), jnp.int32),
            pltpu.VMEM((TOP, tok), f32),
            pltpu.SemaphoreType.DMA((7 + ctx_count,)),
        ],
        compiler_params=pltpu.CompilerParams(vmem_limit_bytes=8 * MIB),
        name="pack",
    )(
        my_ctx,
        my_exp,
        *in_hbm(
            key_block_exponent,
            value_block_exponent,
            encoded_query_rows,
            quantized_key_rows,
            quantized_value_rows,
            jnp.transpose(expert_ids),
            jnp.transpose(route_weight),
            residual,
        ),
    )
    piece_arrays = [near]
    piece_at = {(0, key[0]): (0, place) for place, key in enumerate(piece_names[0])}
    piece_bits = [1, 0, *range(bits_of(ctx_count) - 1, 1, -1)]
    sending, weights = far, {}

    def beside(number, came):
        nonlocal sending
        bit = 1 << piece_bits[number]
        moves = {1: ((2, 0), (1, 0)), 0: ((1, 0), (2, 0))}.get(piece_bits[number], ((bit, 0),) * 2)
        if number == 0:
            keys = [(0, key[0]) for key in piece_names[1]]
        else:
            keys = sorted(key for key in piece_at if key[1] & bit)
            sending = jnp.stack([piece_arrays[array][place] for array, place in map(piece_at.pop, keys)])
        pieces = follow(sending, moves)
        if number == 0:
            own, give = deq_in(my_exp, gate_weight, gate_scale, up_weight, up_scale, ctx_count, packed)
            *came, pieces, weights["in_own"], weights["in_give"] = together(*came, pieces, own, give)
        elif number == 1:
            other = from_offset(weights["in_give"], 1)
            own, give = deq_down(my_exp, down_weight, down_scale, ctx_count, piece_arrays[-1])
            *came, pieces, weights["in_other"], weights["down_own"], weights["down_give"] = together(
                *came, pieces, other, own, give
            )
        elif number < len(piece_bits) - 1:
            *came, pieces = together(*came, pieces)
        for place, (source, target) in enumerate(keys):
            piece_at[source ^ bit, target ^ bit] = (len(piece_arrays), place)
        piece_arrays.append(pieces)
        return came

    packed, packed_at = spread(packed, stages_of(row_route), beside)
    attend_at = tuple((packed_at[key], row_places[key]) for key in names)
    attend_pieces = tuple(piece_at[key[0], 0] for key in names)
    in_own, in_other, down_own = weights["in_own"], weights["in_other"], weights["down_own"]
    down_other = from_offset(weights["down_give"], 1)

    positions = ctx_count * span
    per_x = 2 * ctx_count * tok
    *keeps, give, own_route = pl.pallas_call(
        functools.partial(attend_kernel, (ctx_count, exp_count, tok, heads, attend_pieces, attend_at)),
        in_specs=[smem] * 3 + [vmem] * (len(packed) + len(piece_arrays) + 1) + [anywhere],
        out_specs=[vmem] * (2 + x_count),
        out_shape=[jax.ShapeDtypeStruct((per_x, cols), f32)] * x_count
        + [
            jax.ShapeDtypeStruct((x_count * (per_x + tok), cols), bf16),
            jax.ShapeDtypeStruct((x_count * tok, cols), bf16),
        ],
        scratch_shapes=[
            pltpu.VMEM((positions, HEAD_SIZE), bf16),
            pltpu.VMEM((positions, 2 * HEAD_SIZE), bf16),
            pltpu.VMEM((8, positions), jnp.int32),
            pltpu.VMEM((positions, query_width), bf16),
        ],
        compiler_params=pltpu.CompilerParams(vmem_limit_bytes=3 * ctx_count * MIB),
        cost_estimate=pl.CostEstimate(
            flops=4 * positions * positions * query_width + 4 * positions * query_width * cols,
            bytes_accessed=8 * MIB,
            transcendentals=heads * positions * positions,
        ),
        name="attend",
    )(my_ctx, my_exp, block_order, *packed, *piece_arrays, out_weight, down_other)

    given = from_offset(give, 1)
    routes, route_at, state = [own_route, given], [(0, 0), (1, x_count * per_x)], keeps[0]
    state = state + given[:per_x].astype(f32)
    for x_off in range(1, x_count):
        part = keeps[x_off] + given[x_off * per_x : (x_off + 1) * per_x].astype(f32)
        row = x_count * per_x + x_off * tok
        own = own_route[x_off * tok : (x_off + 1) * tok]
        sent = jnp.concatenate([part.astype(bf16), own, given[row : row + tok]], axis=0)
        came = from_offset(sent, 2 * x_off)
        state = state + came[:per_x].astype(f32)
        route_at += [(len(routes), per_x), (len(routes), per_x + tok)]
        routes.append(came)
    state = state.astype(bf16)

    stages = stages_of(route)
    chunks, chunk_at = spread(state, stages)
    gain = norm_gain.reshape(1, model_width)
    rows = x_count * per_x
    in_width = in_own.shape[1]
    near = tuple(sorted(key for key in places if key[0] < ctx_count // 2))
    far = tuple(sorted(key for key in places if key[0] >= ctx_count // 2))

    def picked(keys):
        arrays = sorted({chunk_at[key][0] for key in keys})
        at = tuple(((arrays.index(chunk_at[key][0]), chunk_at[key][1]), places[key]) for key in keys)
        return [chunks[array] for array in arrays], at

    near_chunks, near_places = picked(near)
    far_chunks, far_places = picked(far)
    first_act, first_square = pl.pallas_call(
        functools.partial(experts_in_first, (ctx_count, x_count, tok), near_places),
        in_specs=[smem] * 2 + [vmem] * (len(near_chunks) + 3) + [anywhere],
        out_specs=[vmem] * 2,
        out_shape=[
            jax.ShapeDtypeStruct((rows, 2 * in_width), f32),
            jax.ShapeDtypeStruct((rows, 1), f32),
        ],
        scratch_shapes=[pltpu.VMEM((rows, half_width // 2), bf16)],
        compiler_params=pltpu.CompilerParams(vmem_limit_bytes=2 * ctx_count * MIB),
        cost_estimate=pl.CostEstimate(
            flops=2 * rows * half_width * in_width, bytes_accessed=8 * MIB, transcendentals=0
        ),
        name="experts_in_first",
    )(my_ctx, my_exp, *near_chunks, gain, in_own, in_other, down_other)
    acts = []
    for part in range(2):
        acts.append(
            pl.pallas_call(
                functools.partial(experts_in_second, (ctx_count, x_count, tok), far_places, part),
                in_specs=[smem] * 2 + [vmem] * (len(far_chunks) + 5) + [anywhere],
                out_specs=vmem,
                out_shape=jax.ShapeDtypeStruct((rows // 2, 2 * in_width + HEAD_SIZE), bf16),
                scratch_shapes=[
                    pltpu.VMEM((rows // 2, half_width // 2), bf16),
                    pltpu.VMEM((rows // 2, 1), f32),
                ],
                compiler_params=pltpu.CompilerParams(vmem_limit_bytes=2 * ctx_count * MIB),
                cost_estimate=pl.CostEstimate(
                    flops=rows * half_width * in_width, bytes_accessed=8 * MIB, transcendentals=0
                ),
                name="experts_in_second",
            )(
                my_ctx,
                my_exp,
                *far_chunks,
                gain,
                in_own,
                in_other,
                first_act,
                first_square,
                acts[0] if part else first_square,
            )
        )
    leaves = set(places) - {source for _, source, _, _ in route}
    sums = {}
    for part in range(2):
        slots = near if part == 1 else far
        state_keys = [
            next(key for key in places if places[key][core] == (offset, 0))
            for offset in (range(ctx_count) if part == 1 else ())
            for core in range(2)
        ]
        states, state_at = picked(state_keys)
        state_at = tuple((state_at[i][0], state_at[i + 1][0]) for i in range(0, len(state_at), 2))
        outs = pl.pallas_call(
            functools.partial(
                experts_out_kernel,
                (ctx_count, exp_count, tok),
                part,
                tuple(places[key] for key in slots),
                state_at,
                tuple(route_at),
                model_width,
            ),
            in_specs=[smem] * 2 + [vmem] * (5 + x_count) + [anywhere] + [vmem] * len(states),
            out_specs=[vmem] * len(slots),
            out_shape=[
                jax.ShapeDtypeStruct((2 * tok, half_width), bf16 if slot in leaves else f32)
                for slot in slots
            ],
            scratch_shapes=[pltpu.VMEM((rows // 2, in_width), bf16)],
            compiler_params=pltpu.CompilerParams(vmem_limit_bytes=2 * ctx_count * MIB),
            cost_estimate=pl.CostEstimate(
                flops=rows * half_width * in_width,
                bytes_accessed=8 * MIB,
                transcendentals=rows * in_width // 2,
            ),
            name="experts_out",
        )(
            my_ctx,
            my_exp,
            acts[part],
            from_offset(acts[part], 1),
            *routes,
            down_own,
            down_other,
            sums[slots_done[0]] if part else acts[1],
            *states,
        )
        slots_done = slots
        sums.update(zip(slots, outs))

    for number, sends in enumerate(reversed(stages)):
        came = []
        for moves, _, targets in sends:
            sent = [sums[key].astype(bf16) for key in targets]
            came.append(follow(sent[0] if len(sent) == 1 else jnp.concatenate(sent, axis=0), moves))
        if number < len(stages) - 1:
            waiting = list(near) if number == 0 else []
            values = together(*came, *[sums[key] for key in waiting])
            came = values[: len(came)]
            sums.update(zip(waiting, values[len(came) :]))
        for (_, sources, _), array in zip(sends, came):
            for place, key in enumerate(sources):
                part = array[place * 2 * tok : (place + 1) * 2 * tok]
                sums[key] = sums[key] + part.astype(f32)
    total = sums[0, 0]
    core = lax.bitwise_and(my_exp[0], 1)
    mine = jnp.where(core == 0, total[:tok], total[tok:]).astype(bf16)
    came = from_offset(jnp.where(core == 0, total[tok:], total[:tok]).astype(bf16), 1)
    mine = mine.reshape(tok, ctx_count, 1, cols)
    came = came.reshape(tok, ctx_count, 1, cols)
    result = jnp.where(core == 0, jnp.concatenate([mine, came], axis=2), jnp.concatenate([came, mine], axis=2))
    return result.reshape(tok, model_width)


def solution(mesh):
    return jax.shard_map(
        shards,
        mesh=mesh,
        in_specs=(
            P(("dp", "ctx", "exp"), None),
            P(("dp", "ctx"), "exp"),
            P(("dp", "ctx"), None),
            P(("dp", "ctx"), None),
            P(("dp", "ctx"), None),
            P(("dp", "ctx"), None),
            P(),
            P("exp", "ctx"),
            P(),
            P(("dp", "ctx", "exp"), None),
            P(("dp", "ctx", "exp"), None),
            P(("ctx", "exp"), None, None),
            P(("ctx", "exp"), None, None),
            P(("ctx", "exp"), None, None),
            P(("ctx", "exp"), None, None),
            P(("ctx", "exp"), None, None),
            P(("ctx", "exp"), None, None),
        ),
        out_specs=P(("dp", "ctx", "exp"), None),
        check_vma=False,
    )
```

```python
import functools
import math

import jax
import jax.numpy as jnp
from jax import lax
from jax.experimental import pallas as pl
from jax.experimental.pallas import tpu as pltpu
from jax.sharding import PartitionSpec as P

QUERY_HEADS = 32
KEY_VALUE_HEADS = 4
HEAD_SIZE = 128
TOP = 8
SCALE_POSITIONS = 64
WB = 128
MIB = 1 << 20


def bits_of(count):
    return count.bit_length() - 1


def from_offset(array, offset):
    return lax.ppermute(array, "exp", [(i, i ^ offset) for i in range(lax.axis_size("exp"))])


def from_ctx(array, offset):
    return lax.ppermute(array, "ctx", [(i, i ^ offset) for i in range(lax.axis_size("ctx"))])


def moved(offset, move):
    return (offset[0] ^ move[0], offset[1] ^ move[1])


def gather_route(ctx_count, x_count, rows_only=False):
    transfers, arrival, places = [], {(0, 0): 0}, {(0, 0): ((0, 0), (0, 0))}

    def go(source, moves, delay=0):
        reached = tuple(moved(place, (c, e >> 1)) for place, (c, e) in zip(places[source], moves))
        target = reached[0]
        arrival[target], places[target] = arrival[source] + 1 + delay, reached
        transfers.append((arrival[target], source, target, moves))
        return target

    bits = bits_of(ctx_count)
    y_move = (1, 0)
    if (ctx_count, x_count) == (8, 2) and not rows_only:
        z_far, z_near = ((4, 0),) * 2, ((2, 0),) * 2
        first, second = ((0, 2), y_move), (y_move, (0, 2))
        at = {"0": (0, 0)}
        for stage, moves, hops in (
            (1, z_far, "0>4"),
            (1, z_near, "0>2"),
            (1, first, "0>0a"),
            (1, second, "0>0b"),
            (2, z_near, "4>6 0b>2b"),
            (2, first, "2>2a 4>4a"),
            (2, second, "4>4b 0a>0ab"),
            (3, z_near, "4a>6a"),
            (3, second, "2a>2ab 4a>4ab 6>6b"),
            (4, second, "6a>6ab"),
        ):
            for hop in hops.split():
                source, target = hop.split(">")
                at[target] = go(at[source], moves, stage - 1 - arrival[at[source]])
        return sorted(transfers, key=lambda transfer: transfer[0]), places
    if rows_only:
        shared, steps = range(bits - 1, 1, -1), [(2, 0), y_move]
    else:
        shared, steps = range(bits - 1, 0, -1), [(0, 2 << bit) for bit in range(bits_of(x_count))] + [y_move]
    pairs = list(zip(steps, reversed(steps)))
    for bit in shared:
        for source in list(arrival):
            go(source, ((1 << bit, 0),) * 2)
    for first in sorted(arrival):
        held = [first]
        for moves in pairs:
            held = held + [go(source, moves) for source in held]
    return sorted(transfers, key=lambda transfer: transfer[0]), places


def follow(array, moves):
    exp_count = lax.axis_size("exp")
    pairs = []
    for c in range(lax.axis_size("ctx")):
        for e in range(exp_count):
            far = moved((c, e), moves[e % 2])
            pairs.append((far[0] * exp_count + far[1], c * exp_count + e))
    return lax.ppermute(array, ("ctx", "exp"), pairs)


def by_core(core, place, part):
    first, second = place[0][part], place[1][part]
    return first if first == second else jnp.where(core == 0, first, second)


def stages_of(route):
    stages, arrays = [], [((0, 0),)]
    top = max(moves[0][0] for _, _, _, moves in route)
    for stage in sorted({transfer[0] for transfer in route}):
        sends = []
        for moves in sorted({t[3] for t in route if t[0] == stage}):
            left = {source: target for number, source, target, way in route if (number, way) == (stage, moves)}
            groups = [group for group in arrays if len(group) > 1 and all(key in left for key in group)]
            rest = tuple(sorted(key for key in left if not any(key in group for group in groups)))
            for group in groups + [rest] * bool(rest):
                sends.append((moves, group, tuple(left[key] for key in group)))
        def order(send):
            moves, group, _ = send
            shared, load = moves[0] == moves[1], len(group) * (2 if moves[0][0] == top > 2 else 1)
            rank = (0 if shared else 1) if len(group) == 1 else (1 if shared else 2 * moves[0][0])
            return -load, rank

        sends.sort(key=order)
        arrays = arrays + [send[2] for send in sends]
        stages.append(sends)
    return stages


def spread(block, stages, beside=None):
    arrays, at, joined = [block], {(0, 0): (0, 0)}, {}
    rows = block.shape[0]
    for number, sends in enumerate(stages):
        came = []
        for moves, group, _ in sends:
            first, row = at[group[0]]
            whole = row == 0 and arrays[first].shape[0] == len(group) * rows
            if whole and all(at[key] == (first, place * rows) for place, key in enumerate(group)):
                joined[group] = arrays[first]
            elif group not in joined:
                parts = [arrays[at[key][0]][at[key][1] : at[key][1] + rows] for key in group]
                joined[group] = jnp.concatenate(parts, axis=0)
            came.append(follow(joined[group], moves))
        came = beside(number, came) if beside else (together(*came) if number < len(stages) - 1 else came)
        for (_, _, targets), array in zip(sends, came):
            at.update({key: (len(arrays), place * rows) for place, key in enumerate(targets)})
            arrays.append(array)
    return arrays, at


def together(*values):
    return lax.optimization_barrier(values)


def block_factor(exponent, width):
    factor = jnp.where(exponent < 0, 0.5, jnp.where(exponent > 0, 2.0, 1.0))
    return jnp.full((1, width), factor, jnp.float32).astype(jnp.bfloat16)


def in_hbm(*arrays):
    return [pltpu.with_memory_space_constraint(array, pltpu.HBM) for array in arrays]


def copy_all(sems, pairs):
    copies = [pltpu.make_async_copy(src, dst, sems.at[i]) for i, (src, dst) in enumerate(pairs)]
    for copy in copies:
        copy.start()
    return copies


def pack_kernel(plan, ctx_ref, exp_ref, key_scale_hbm, value_scale_hbm, query_hbm, key_hbm, value_hbm, ids_hbm,
                route_hbm, residual_hbm, packed_ref, near_ref, far_ref, key_scale_ref, value_scale_ref,
                key_ref, value_ref, ids_ref, route_ref, sems):
    heads, group, x_count, piece_places = plan
    span, width = query_hbm.shape
    half, tok, cols = near_ref.shape
    cols = cols - HEAD_SIZE
    my_ctx, my_exp = ctx_ref[0], exp_ref[0]
    kv_head = my_exp * heads // group
    at = pl.ds(pl.multiple_of(kv_head * HEAD_SIZE, HEAD_SIZE), HEAD_SIZE)
    pairs = [
        (key_scale_hbm, key_scale_ref),
        (value_scale_hbm, value_scale_ref),
        (key_hbm.at[:, at], key_ref),
        (value_hbm.at[:, at], value_ref),
        (ids_hbm, ids_ref),
        (route_hbm, route_ref),
        (query_hbm, packed_ref.at[:, 2 * HEAD_SIZE : 2 * HEAD_SIZE + width]),
    ]
    core = lax.bitwise_and(my_exp, 1)
    for ref, places in zip((near_ref, far_ref), piece_places):
        for number, place in enumerate(places):
            col = pl.multiple_of(lax.bitwise_xor(my_ctx, by_core(core, place, 0)) * cols, cols)
            pairs.append((residual_hbm.at[:, pl.ds(col, cols)], ref.at[number, :, 0:cols]))
    copies = copy_all(sems, pairs)
    for copy in copies[:6]:
        copy.wait()
    lane = lax.broadcasted_iota(jnp.int32, key_scale_ref.shape, 1)
    blocks = key_scale_ref.shape[0]
    for place, (ref, scale_ref) in enumerate(((key_ref, key_scale_ref), (value_ref, value_scale_ref))):
        exponent = scale_ref[...]
        factor = jnp.where(
            exponent < -1, 0.25, jnp.where(exponent < 0, 0.5, jnp.where(exponent < 1, 1.0, 2.0))
        )
        factor = jnp.sum(jnp.where(lane == kv_head, factor, 0.0), axis=1, keepdims=True)
        for block in range(blocks):
            rows = pl.ds(block * (span // blocks), span // blocks)
            scaled = ref[rows, :].astype(jnp.float32) * factor[block : block + 1, :]
            packed_ref[rows, pl.ds(place * HEAD_SIZE, HEAD_SIZE)] = scaled.astype(jnp.bfloat16)
    number = lax.broadcasted_iota(jnp.int32, (128, tok), 0)
    dense = jnp.zeros((128, tok), jnp.float32)
    for k in range(TOP):
        dense = dense + jnp.where(ids_ref[k : k + 1, :] == number, route_ref[k : k + 1, :], 0.0)
    dense = jnp.concatenate([dense, jnp.zeros((128, 128 - tok), jnp.float32)], axis=1)
    dense = jnp.transpose(dense)[:tok, :]
    lane = lax.broadcasted_iota(jnp.int32, (tok, HEAD_SIZE), 1)
    for ref, places in zip((near_ref, far_ref), piece_places):
        for number, place in enumerate(places):
            expert = lax.bitwise_xor(my_ctx, by_core(core, place, 0)) * x_count
            block = jnp.zeros((tok, HEAD_SIZE), jnp.float32)
            for x in range(x_count):
                column = jnp.sum(jnp.where(lane == expert + x, dense, 0.0), axis=1, keepdims=True)
                high = column.astype(jnp.bfloat16).astype(jnp.float32)
                block = jnp.where(lane == x, high, jnp.where(lane == x_count + x, column - high, block))
            ref[number, :, cols:] = block.astype(jnp.bfloat16)
    for copy in copies[6:]:
        copy.wait()


def deq_in_kernel(ctx_count, exp_ref, gate_scale_hbm, up_scale_hbm, gate_hbm, up_hbm, _, own_ref, give_ref,
                  gate_ref, up_ref, gate_scale_ref, up_scale_ref, sems):
    core = lax.bitwise_and(exp_ref[0], 1)
    width, cols = gate_ref.shape
    rows = width // (2 * ctx_count)
    pairs = [(gate_scale_hbm, gate_scale_ref), (up_scale_hbm, up_scale_ref)]
    for step in range(ctx_count):
        at = pl.ds(step * 2 * rows, 2 * rows)
        pairs += [(gate_hbm.at[0, at], gate_ref.at[at]), (up_hbm.at[0, at], up_ref.at[at])]
    copies = copy_all(sems, pairs)
    for copy in copies[:2]:
        copy.wait()
    for step in range(ctx_count):
        for half, (ref, scale_ref) in enumerate(((gate_ref, gate_scale_ref), (up_ref, up_scale_ref))):
            copies[2 + 2 * step + half].wait()
            for out_ref, side in ((give_ref, 1 - core), (own_ref, core)):
                first = (2 * step + side) * (rows // WB)
                for i in range(rows // WB):
                    row = pl.multiple_of((2 * step + side) * rows + i * WB, WB)
                    for j in range(cols // WB):
                        factor = block_factor(scale_ref[j, 0, first + i], WB)
                        out_ref[pl.ds(step * rows + i * WB, WB), pl.ds(half * cols + j * WB, WB)] = (
                            ref[pl.ds(row, WB), pl.ds(j * WB, WB)] * factor
                        )


def deq_in(my_exp, gate_weight, gate_scale, up_weight, up_scale, ctx_count, after):
    width, hidden = gate_weight.shape[1:]
    shape = jax.ShapeDtypeStruct((width // 2, 2 * hidden), jnp.bfloat16)
    gate_scale = jnp.transpose(gate_scale, (2, 0, 1))
    up_scale = jnp.transpose(up_scale, (2, 0, 1))
    return pl.pallas_call(
        functools.partial(deq_in_kernel, ctx_count),
        in_specs=[pl.BlockSpec(memory_space=pltpu.SMEM)]
        + [pl.BlockSpec(memory_space=pltpu.HBM)] * 4
        + [pl.BlockSpec(memory_space=pl.ANY)],
        out_specs=[pl.BlockSpec(memory_space=pltpu.VMEM)] * 2,
        out_shape=[shape, shape],
        scratch_shapes=[
            pltpu.VMEM((width, hidden), jnp.bfloat16),
            pltpu.VMEM((width, hidden), jnp.bfloat16),
            pltpu.SMEM(gate_scale.shape, jnp.int32),
            pltpu.SMEM(up_scale.shape, jnp.int32),
            pltpu.SemaphoreType.DMA((2 + 2 * ctx_count,)),
        ],
        compiler_params=pltpu.CompilerParams(vmem_limit_bytes=20 * MIB),
        cost_estimate=pl.CostEstimate(
            flops=2 * width * hidden, bytes_accessed=8 * width * hidden, transcendentals=0
        ),
        name="dequant_in",
    )(my_exp, *in_hbm(gate_scale, up_scale, gate_weight, up_weight), after)


def deq_down_kernel(ctx_count, exp_ref, scale_hbm, down_hbm, _, own_ref, give_ref, down_ref, scale_ref, sems):
    core = lax.bitwise_and(exp_ref[0], 1)
    rows, width = down_ref.shape
    cols = width // (2 * ctx_count)
    pairs = [(scale_hbm, scale_ref)]
    for step in range(ctx_count):
        at = pl.ds(step * 2 * cols, 2 * cols)
        pairs.append((down_hbm.at[0, :, at], down_ref.at[:, at]))
    copies = copy_all(sems, pairs)
    copies[0].wait()
    for step in range(ctx_count):
        copies[1 + step].wait()
        for out_ref, side in ((give_ref, 1 - core), (own_ref, core)):
            first = (2 * step + side) * (cols // WB)
            for j in range(cols // WB):
                col = pl.multiple_of((2 * step + side) * cols + j * WB, WB)
                for i in range(rows // WB):
                    factor = block_factor(scale_ref[i, 0, first + j], WB)
                    out_ref[pl.ds(i * WB, WB), pl.ds(step * cols + j * WB, WB)] = (
                        down_ref[pl.ds(i * WB, WB), pl.ds(col, WB)] * factor
                    )


def deq_down(my_exp, down_weight, down_scale, ctx_count, after):
    hidden, width = down_weight.shape[1:]
    shape = jax.ShapeDtypeStruct((hidden, width // 2), jnp.bfloat16)
    down_scale = jnp.transpose(down_scale, (1, 0, 2))
    return pl.pallas_call(
        functools.partial(deq_down_kernel, ctx_count),
        in_specs=[pl.BlockSpec(memory_space=pltpu.SMEM)]
        + [pl.BlockSpec(memory_space=pltpu.HBM)] * 2
        + [pl.BlockSpec(memory_space=pl.ANY)],
        out_specs=[pl.BlockSpec(memory_space=pltpu.VMEM)] * 2,
        out_shape=[shape, shape],
        scratch_shapes=[
            pltpu.VMEM((hidden, width), jnp.bfloat16),
            pltpu.SMEM(down_scale.shape, jnp.int32),
            pltpu.SemaphoreType.DMA((1 + ctx_count,)),
        ],
        compiler_params=pltpu.CompilerParams(vmem_limit_bytes=12 * MIB),
        cost_estimate=pl.CostEstimate(
            flops=width * hidden, bytes_accessed=4 * width * hidden, transcendentals=0
        ),
        name="dequant_down",
    )(my_exp, *in_hbm(down_scale, down_weight), after)


def attend_kernel(plan, ctx_ref, exp_ref, order_ref, *refs):
    ctx_count, exp_count, tok, heads, attend_at = plan
    packed_at, places_of = [at for at, _ in attend_at], [place for _, place in attend_at]
    array_count = 1 + max(array for array, _ in packed_at)
    span = exp_count * tok
    packed_refs, refs = refs[:array_count], refs[array_count:]
    packed = []
    for array, row in packed_at:
        packed.append(packed_refs[array].at[pl.ds(row, span)])
    weight_ref, rest = refs[0], refs[2:]
    x_count = exp_count // 2
    keep_refs, give_ref = rest[:x_count], rest[x_count]
    key_scr, value_scr, place_scr, att_scr = rest[x_count + 1 :]
    positions = ctx_count * span
    my_ctx, my_exp = ctx_ref[0], exp_ref[0]
    my_x, my_core = lax.shift_right_logical(my_exp, 1), lax.bitwise_and(my_exp, 1)
    lane = lax.broadcasted_iota(jnp.int32, (8, positions), 1)
    places = lane % span
    for offset, ref in enumerate(packed):
        key_scr[pl.ds(offset * span, span), :] = ref[:, 0:HEAD_SIZE]
        value_scr[pl.ds(offset * span, span), 0:HEAD_SIZE] = ref[:, HEAD_SIZE : 2 * HEAD_SIZE]
        base = order_ref[lax.bitwise_xor(my_ctx, by_core(my_core, places_of[offset], 0))] * span
        places = places + jnp.where(lane // span == offset, base, 0)
    place_scr[...] = places
    scale = math.log2(math.e) / math.sqrt(HEAD_SIZE)
    value_scr[:, HEAD_SIZE:] = jnp.ones((positions, HEAD_SIZE), jnp.bfloat16)
    for offset, ref in enumerate(packed):
        source = lax.bitwise_xor(my_ctx, by_core(my_core, places_of[offset], 0))
        queries = jnp.concatenate(
            [ref[:, (h + 2) * HEAD_SIZE : (h + 3) * HEAD_SIZE] for h in range(heads)], axis=0
        )
        scores = lax.dot_general(
            queries, key_scr[...], (((1,), (1,)), ((), ())), preferred_element_type=jnp.float32
        )
        own_place = order_ref[source] * span + lax.broadcasted_iota(jnp.int32, (span, positions), 0)
        bias = jnp.where(place_scr[0:1, :] <= own_place, 0.0, -1e30)
        scores = scores.reshape(heads, span, positions) * scale + bias[None]
        exps = jnp.exp2(scores - jnp.max(scores, axis=-1, keepdims=True))
        mixed = jnp.dot(
            exps.astype(jnp.bfloat16).reshape(heads * span, positions),
            value_scr[...],
            preferred_element_type=jnp.float32,
        )
        mixed = mixed[:, :HEAD_SIZE] * (1.0 / mixed[:, HEAD_SIZE : HEAD_SIZE + 1])
        mixed = mixed.astype(jnp.bfloat16).reshape(heads, span, HEAD_SIZE)
        for owner in range(exp_count):
            x_off = lax.bitwise_xor(my_x, owner // 2)
            row = pl.multiple_of(((x_off * ctx_count + source) * 2 + owner % 2) * tok, tok)
            for head in range(heads):
                att_scr[pl.ds(row, tok), pl.ds(head * HEAD_SIZE, HEAD_SIZE)] = mixed[
                    head, owner * tok : (owner + 1) * tok, :
                ]

    cols = weight_ref.shape[1] // 2
    per_x = 2 * ctx_count * tok
    for x_off in range(x_count):
        rows = pl.ds(x_off * per_x, per_x)
        for which in (1, 0):
            side = lax.bitwise_xor(my_core, which)
            weight = weight_ref[:, pl.ds(pl.multiple_of(side * cols, cols), cols)]
            part = jnp.dot(att_scr[rows, :], weight, preferred_element_type=jnp.float32)
            out_ref = give_ref if which else keep_refs[x_off]
            out_ref[pl.ds(x_off * per_x if which else 0, per_x), :] = part.astype(out_ref.dtype)


def finish_kernel(plan, ctx_ref, exp_ref, keep_in, give_in, *refs):
    ctx_count, x_count, tok, piece_places, places_of = plan
    piece_refs, (keep_ref, give_ref, own_route_ref) = refs[:-3], refs[-3:]
    my_ctx, my_exp = ctx_ref[0], exp_ref[0]
    my_x, my_core = lax.shift_right_logical(my_exp, 1), lax.bitwise_and(my_exp, 1)
    cols = keep_ref.shape[1]
    route_base = give_in.shape[0]
    keep_ref[...] = keep_in[...]
    give_ref[0:route_base, :] = give_in[...]
    blocks = [jnp.zeros((tok, HEAD_SIZE), jnp.float32)] * x_count
    lane = lax.broadcasted_iota(jnp.int32, (tok, HEAD_SIZE), 1)
    for (array, place), place_of in zip(piece_places, places_of):
        source = lax.bitwise_xor(my_ctx, by_core(my_core, place_of, 0))
        at = pl.ds(pl.multiple_of((source * 2 + my_core) * tok, tok), tok)
        for which, ref in enumerate((keep_ref, give_ref)):
            side = lax.bitwise_xor(my_core, which)
            piece = piece_refs[array][place, :, pl.ds(pl.multiple_of(side * cols, cols), cols)]
            value = ref[at, :].astype(jnp.float32) + piece.astype(jnp.float32)
            ref[at, :] = value.astype(ref.dtype)
        block = piece_refs[array][place, :, 2 * cols :].astype(jnp.float32)
        for x_off in range(x_count):
            for part in range(2):
                wanted = lax.bitwise_xor(my_x, x_off) + part * x_count
                column = jnp.sum(jnp.where(lane == wanted, block, 0.0), axis=1, keepdims=True)
                blocks[x_off] = jnp.where(lane == source + part * ctx_count, column, blocks[x_off])
    for x_off, block in enumerate(blocks):
        for ref, base in ((give_ref, route_base), (own_route_ref, 0)):
            at = pl.ds(base + x_off * tok, tok)
            ref[at, 0:HEAD_SIZE] = block.astype(jnp.bfloat16)
            if cols > HEAD_SIZE:
                ref[at, HEAD_SIZE:] = jnp.zeros((tok, cols - HEAD_SIZE), jnp.bfloat16)


def fill_rows(plan, ctx_ref, exp_ref, gain_ref, chunk_refs, places, rows_scr, square_ref, groups):
    ctx_count, x_count, tok = plan
    half = ctx_count // 2
    my_ctx = ctx_ref[0]
    my_core = lax.bitwise_and(exp_ref[0], 1)
    mine = lax.shift_right_logical(my_ctx, bits_of(half))
    cols = chunk_refs[0].shape[1]
    rows = ctx_count * tok
    for (array, first_row), place_of in places:
        ref = chunk_refs[array]
        source = lax.bitwise_xor(my_ctx, by_core(my_core, place_of, 0))
        x_off = by_core(my_core, place_of, 1)
        gain_at = pl.multiple_of((source * 2 + my_core) * cols, cols)
        gain = gain_ref[:, pl.ds(gain_at, cols)]
        col = pl.multiple_of(lax.bitwise_and(source, half - 1) * cols, cols)
        for place, group in enumerate(groups):
            side = mine if group == 1 else 1 - mine
            chunk_at = pl.ds(pl.multiple_of(first_row + side * rows, rows), rows)
            chunk = ref[chunk_at, :].astype(jnp.float32)
            at = pl.ds(pl.multiple_of((place * x_count + x_off) * rows, rows), rows)
            rows_scr[at, pl.ds(col, cols)] = (chunk * gain).astype(jnp.bfloat16)
            square_ref[at, :] = square_ref[at, :] + jnp.sum(chunk * chunk, axis=-1, keepdims=True)


def experts_in_first(plan, offsets, ctx_ref, exp_ref, *refs):
    chunk_refs, (gain_ref, own_ref, other_ref, _, act_ref, square_ref, rows_scr) = refs[:-7], refs[-7:]
    half = plan[0] // 2
    square_ref[...] = jnp.zeros(square_ref.shape, jnp.float32)
    fill_rows(plan, ctx_ref, exp_ref, gain_ref, chunk_refs, offsets, rows_scr, square_ref, (0, 1))
    depth, width = rows_scr.shape[1], own_ref.shape[1]
    start = lax.shift_right_logical(ctx_ref[0], bits_of(half)) * depth
    at = pl.ds(pl.multiple_of(start, depth), depth)
    for place, ref in enumerate((own_ref, other_ref)):
        act_ref[:, place * width : (place + 1) * width] = jnp.dot(
            rows_scr[...], ref[at, :], preferred_element_type=jnp.float32
        )


def experts_in_second(plan, offsets, group, ctx_ref, exp_ref, *refs):
    chunk_refs, rest = refs[:-9], refs[-9:]
    gain_ref, own_ref, other_ref, first_ref, square_ref, _, act_ref, rows_scr, sum_scr = rest
    half = plan[0] // 2
    count, depth = rows_scr.shape
    width = own_ref.shape[1]
    sum_scr[...] = square_ref[group * count : (group + 1) * count, :]
    fill_rows(plan, ctx_ref, exp_ref, gain_ref, chunk_refs, offsets, rows_scr, sum_scr, (group,))
    lane = lax.broadcasted_iota(jnp.int32, (1, HEAD_SIZE), 1)
    square = sum_scr[...]
    high = square.astype(jnp.bfloat16).astype(jnp.float32)
    act_ref[:, 2 * width :] = jnp.where(lane == 0, high, square - high).astype(jnp.bfloat16)
    start = (1 - lax.shift_right_logical(ctx_ref[0], bits_of(half))) * depth
    at = pl.ds(pl.multiple_of(start, depth), depth)
    for place, ref in enumerate((own_ref, other_ref)):
        cols = slice(place * width, (place + 1) * width)
        act = first_ref[group * count : (group + 1) * count, cols] + jnp.dot(
            rows_scr[...], ref[at, :], preferred_element_type=jnp.float32
        )
        act_ref[:, cols] = act.astype(jnp.bfloat16)


def experts_out_kernel(plan, group, places, state_at, route_at, model_width, ctx_ref, exp_ref, act_ref, came_ref, *refs):
    ctx_count, exp_count, tok = plan
    x_count, half = exp_count // 2, ctx_count // 2
    route_refs, refs = refs[: x_count + 1], refs[x_count + 1 :]
    (own_ref, other_ref, _), rest = refs[:3], refs[3:]
    state_count = 1 + max((array for pair in state_at for array, _ in pair), default=-1)
    state_refs, rest = rest[:state_count], rest[state_count:]
    out_refs, hidden_scr = rest[:-1], rest[-1]
    my_ctx = ctx_ref[0]
    my_core = lax.bitwise_and(exp_ref[0], 1)
    mine = lax.shift_right_logical(my_ctx, bits_of(half))
    first_ctx = (mine if group == 1 else 1 - mine) * half
    width = (act_ref.shape[1] - HEAD_SIZE) // 2
    hidden = width // 2
    lane = lax.broadcasted_iota(jnp.int32, (tok, HEAD_SIZE), 1)
    blocks = []
    for array, row in route_at:
        blocks.append(route_refs[array][row : row + tok, 0:HEAD_SIZE].astype(jnp.float32))
    columns = []
    for x_off in range(x_count):
        for low in range(half):
            for core in range(2):
                same, swapped = blocks[2 * x_off + core], blocks[2 * x_off + 1 - core]
                block = jnp.where(my_core == 0, same, swapped)
                picked = jnp.where(lane % ctx_count == first_ctx + low, block, 0.0)
                columns.append(jnp.sum(picked, axis=1, keepdims=True))
    route = jnp.concatenate(columns, axis=0)
    squares = act_ref[:, 2 * width :].astype(jnp.float32) + came_ref[:, 2 * width :].astype(jnp.float32)
    norm = lax.rsqrt((squares[:, 0:1] + squares[:, 1:2]) / model_width + 1e-06)
    scaled_route = norm * route
    for side in range(2):
        acts = act_ref[:, side * width : (side + 1) * width].astype(jnp.float32) + came_ref[
            :, (1 - side) * width : (2 - side) * width
        ].astype(jnp.float32)
        gate = acts[:, :hidden] * norm
        value = gate / (1.0 + jnp.exp(-gate)) * (acts[:, hidden:] * scaled_route)
        hidden_scr[:, side * hidden : (side + 1) * hidden] = value.astype(jnp.bfloat16)
    picked = []
    for place in places:
        x_off = by_core(my_core, place, 1)
        low = lax.bitwise_and(lax.bitwise_xor(my_ctx, by_core(my_core, place, 0)), half - 1)
        row = pl.multiple_of((x_off * half + low) * (2 * tok), 2 * tok)
        picked.append(hidden_scr[pl.ds(row, 2 * tok), :])
    picked = jnp.concatenate(picked, axis=0)
    out_cols = own_ref.shape[1]
    step = min(512, out_cols)
    for col in range(0, out_cols, step):
        at = pl.ds(col, step)
        out = jnp.dot(picked[:, :hidden], own_ref[:, at], preferred_element_type=jnp.float32)
        out = out + jnp.dot(picked[:, hidden:], other_ref[:, at], preferred_element_type=jnp.float32)
        for place, ref in enumerate(out_refs):
            ref[:, at] = out[place * 2 * tok : (place + 1) * 2 * tok, :].astype(ref.dtype)
    for place, ref in zip(places, out_refs):
        if place[0] == (0, 0):
            for c_off, pair in enumerate(state_at):
                states = []
                for array, first_row in pair:
                    own_row = pl.multiple_of(first_row + my_ctx * (2 * tok), 2 * tok)
                    states.append(state_refs[array][pl.ds(own_row, 2 * tok), :].astype(jnp.float32))
                state = states[0] if pair[0] == pair[1] else jnp.where(my_core == 0, *states)
                cols = state.shape[1]
                at = pl.ds(pl.multiple_of(lax.bitwise_xor(my_ctx, c_off) * cols, cols), cols)
                ref[:, at] = ref[:, at] + state


def shards(
    residual,
    encoded_query_rows,
    quantized_key_rows,
    quantized_value_rows,
    key_block_exponent,
    value_block_exponent,
    block_order,
    out_weight,
    norm_gain,
    expert_ids,
    route_weight,
    gate_weight,
    gate_scale,
    up_weight,
    up_scale,
    down_weight,
    down_scale,
):
    f32, bf16 = jnp.float32, jnp.bfloat16
    vmem = pl.BlockSpec(memory_space=pltpu.VMEM)
    smem = pl.BlockSpec(memory_space=pltpu.SMEM)
    anywhere = pl.BlockSpec(memory_space=pl.ANY)
    span, query_width = encoded_query_rows.shape
    heads = query_width // HEAD_SIZE
    group = QUERY_HEADS // KEY_VALUE_HEADS
    ctx_count = lax.axis_size("ctx")
    exp_count = lax.axis_size("exp")
    x_count = exp_count // 2
    experts = ctx_count * x_count
    tok, model_width = residual.shape
    half_width = model_width // 2
    cols = half_width // ctx_count
    my_ctx = lax.axis_index("ctx").astype(jnp.int32).reshape(1)
    my_exp = lax.axis_index("exp").astype(jnp.int32).reshape(1)
    route, places = gather_route(ctx_count, x_count)

    hbm = pl.BlockSpec(memory_space=pltpu.HBM)
    piece_shape = jax.ShapeDtypeStruct((ctx_count // 2, tok, 2 * cols + HEAD_SIZE), bf16)
    row_route, row_places = gather_route(ctx_count, x_count, rows_only=True)
    names = sorted(row_places)
    piece_names = [[key for key in names if bool(key[0] & 2) == sent] for sent in (False, True)]
    piece_places = tuple(tuple(row_places[key] for key in keys) for keys in piece_names)
    packed, near, far = pl.pallas_call(
        functools.partial(pack_kernel, (heads, group, x_count, piece_places)),
        in_specs=[smem] * 2 + [hbm] * 8,
        out_specs=[vmem] * 3,
        out_shape=[
            jax.ShapeDtypeStruct((span, query_width + 2 * HEAD_SIZE), bf16),
            piece_shape,
            piece_shape,
        ],
        scratch_shapes=[
            pltpu.VMEM(key_block_exponent.shape, jnp.int32),
            pltpu.VMEM(key_block_exponent.shape, jnp.int32),
            pltpu.VMEM((span, HEAD_SIZE), bf16),
            pltpu.VMEM((span, HEAD_SIZE), bf16),
            pltpu.VMEM((TOP, tok), jnp.int32),
            pltpu.VMEM((TOP, tok), f32),
            pltpu.SemaphoreType.DMA((7 + ctx_count,)),
        ],
        compiler_params=pltpu.CompilerParams(vmem_limit_bytes=8 * MIB),
        name="pack",
    )(
        my_ctx,
        my_exp,
        *in_hbm(
            key_block_exponent,
            value_block_exponent,
            encoded_query_rows,
            quantized_key_rows,
            quantized_value_rows,
            jnp.transpose(expert_ids),
            jnp.transpose(route_weight),
            residual,
        ),
    )
    piece_arrays = [near]
    piece_at = {(0, key[0]): (0, place) for place, key in enumerate(piece_names[0])}
    piece_bits = [1, 0, *range(bits_of(ctx_count) - 1, 1, -1)]
    sending, weights = far, {}

    def beside(number, came):
        nonlocal sending
        bit = 1 << piece_bits[number]
        moves = {1: ((2, 0), (1, 0)), 0: ((1, 0), (2, 0))}.get(piece_bits[number], ((bit, 0),) * 2)
        if number == 0:
            keys = [(0, key[0]) for key in piece_names[1]]
        else:
            keys = sorted(key for key in piece_at if key[1] & bit)
            sending = jnp.stack([piece_arrays[array][place] for array, place in map(piece_at.pop, keys)])
        pieces = follow(sending, moves)
        if number == 0:
            own, give = deq_in(my_exp, gate_weight, gate_scale, up_weight, up_scale, ctx_count, packed)
            *came, pieces, weights["in_own"], weights["in_give"] = together(*came, pieces, own, give)
        elif number == 1:
            other = from_offset(weights["in_give"], 1)
            own, give = deq_down(my_exp, down_weight, down_scale, ctx_count, piece_arrays[-1])
            *came, pieces, weights["in_other"], weights["down_own"], weights["down_give"] = together(
                *came, pieces, other, own, give
            )
        elif number < len(piece_bits) - 1:
            *came, pieces = together(*came, pieces)
        for place, (source, target) in enumerate(keys):
            piece_at[source ^ bit, target ^ bit] = (len(piece_arrays), place)
        piece_arrays.append(pieces)
        return came

    packed, packed_at = spread(packed, stages_of(row_route), beside)
    attend_at = tuple((packed_at[key], row_places[key]) for key in names)
    attend_pieces = tuple(piece_at[key[0], 0] for key in names)
    in_own, in_other, down_own = weights["in_own"], weights["in_other"], weights["down_own"]
    down_other = from_offset(weights["down_give"], 1)

    positions = ctx_count * span
    per_x = 2 * ctx_count * tok
    *keeps, give = pl.pallas_call(
        functools.partial(attend_kernel, (ctx_count, exp_count, tok, heads, attend_at)),
        in_specs=[smem] * 3 + [vmem] * (len(packed) + 1) + [anywhere],
        out_specs=[vmem] * (1 + x_count),
        out_shape=[jax.ShapeDtypeStruct((per_x, cols), f32)] * x_count
        + [jax.ShapeDtypeStruct((x_count * per_x, cols), bf16)],
        scratch_shapes=[
            pltpu.VMEM((positions, HEAD_SIZE), bf16),
            pltpu.VMEM((positions, 2 * HEAD_SIZE), bf16),
            pltpu.VMEM((8, positions), jnp.int32),
            pltpu.VMEM((positions, query_width), bf16),
        ],
        compiler_params=pltpu.CompilerParams(vmem_limit_bytes=3 * ctx_count * MIB),
        cost_estimate=pl.CostEstimate(
            flops=4 * positions * positions * query_width + 4 * positions * query_width * cols,
            bytes_accessed=8 * MIB,
            transcendentals=heads * positions * positions,
        ),
        name="attend",
    )(my_ctx, my_exp, block_order, *packed, out_weight, down_other)
    keeps[0], give, own_route = pl.pallas_call(
        functools.partial(
            finish_kernel,
            (ctx_count, x_count, tok, attend_pieces, tuple(place for _, place in attend_at)),
        ),
        in_specs=[smem] * 2 + [vmem] * (2 + len(piece_arrays)),
        out_specs=[vmem] * 3,
        out_shape=[
            jax.ShapeDtypeStruct((per_x, cols), f32),
            jax.ShapeDtypeStruct((x_count * (per_x + tok), cols), bf16),
            jax.ShapeDtypeStruct((x_count * tok, cols), bf16),
        ],
        compiler_params=pltpu.CompilerParams(vmem_limit_bytes=8 * MIB),
        name="finish",
    )(my_ctx, my_exp, keeps[0], give, *piece_arrays)

    given = from_offset(give, 1)
    routes, route_at, state = [own_route, given], [(0, 0), (1, x_count * per_x)], keeps[0]
    state = state + given[:per_x].astype(f32)
    for x_off in range(1, x_count):
        part = keeps[x_off] + given[x_off * per_x : (x_off + 1) * per_x].astype(f32)
        row = x_count * per_x + x_off * tok
        own = own_route[x_off * tok : (x_off + 1) * tok]
        sent = jnp.concatenate([part.astype(bf16), own, given[row : row + tok]], axis=0)
        came = from_offset(sent, 2 * x_off)
        state = state + came[:per_x].astype(f32)
        route_at += [(len(routes), per_x), (len(routes), per_x + tok)]
        routes.append(came)
    state = state.astype(bf16)

    stages = stages_of(route)
    chunks, chunk_at = spread(state, stages)
    gain = norm_gain.reshape(1, model_width)
    rows = x_count * per_x
    in_width = in_own.shape[1]
    near = tuple(sorted(key for key in places if key[0] < ctx_count // 2))
    far = tuple(sorted(key for key in places if key[0] >= ctx_count // 2))

    def picked(keys):
        arrays = sorted({chunk_at[key][0] for key in keys})
        at = tuple(((arrays.index(chunk_at[key][0]), chunk_at[key][1]), places[key]) for key in keys)
        return [chunks[array] for array in arrays], at

    near_chunks, near_places = picked(near)
    far_chunks, far_places = picked(far)
    first_act, first_square = pl.pallas_call(
        functools.partial(experts_in_first, (ctx_count, x_count, tok), near_places),
        in_specs=[smem] * 2 + [vmem] * (len(near_chunks) + 3) + [anywhere],
        out_specs=[vmem] * 2,
        out_shape=[
            jax.ShapeDtypeStruct((rows, 2 * in_width), f32),
            jax.ShapeDtypeStruct((rows, 1), f32),
        ],
        scratch_shapes=[pltpu.VMEM((rows, half_width // 2), bf16)],
        compiler_params=pltpu.CompilerParams(vmem_limit_bytes=2 * ctx_count * MIB),
        cost_estimate=pl.CostEstimate(
            flops=2 * rows * half_width * in_width, bytes_accessed=8 * MIB, transcendentals=0
        ),
        name="experts_in_first",
    )(my_ctx, my_exp, *near_chunks, gain, in_own, in_other, down_other)
    acts = []
    for part in range(2):
        acts.append(
            pl.pallas_call(
                functools.partial(experts_in_second, (ctx_count, x_count, tok), far_places, part),
                in_specs=[smem] * 2 + [vmem] * (len(far_chunks) + 5) + [anywhere],
                out_specs=vmem,
                out_shape=jax.ShapeDtypeStruct((rows // 2, 2 * in_width + HEAD_SIZE), bf16),
                scratch_shapes=[
                    pltpu.VMEM((rows // 2, half_width // 2), bf16),
                    pltpu.VMEM((rows // 2, 1), f32),
                ],
                compiler_params=pltpu.CompilerParams(vmem_limit_bytes=2 * ctx_count * MIB),
                cost_estimate=pl.CostEstimate(
                    flops=rows * half_width * in_width, bytes_accessed=8 * MIB, transcendentals=0
                ),
                name="experts_in_second",
            )(
                my_ctx,
                my_exp,
                *far_chunks,
                gain,
                in_own,
                in_other,
                first_act,
                first_square,
                acts[0] if part else first_square,
            )
        )
    leaves = set(places) - {source for _, source, _, _ in route}
    sums = {}
    for part in range(2):
        slots = near if part == 1 else far
        state_keys = [
            next(key for key in places if places[key][core] == (offset, 0))
            for offset in (range(ctx_count) if part == 1 else ())
            for core in range(2)
        ]
        states, state_at = picked(state_keys)
        state_at = tuple((state_at[i][0], state_at[i + 1][0]) for i in range(0, len(state_at), 2))
        outs = pl.pallas_call(
            functools.partial(
                experts_out_kernel,
                (ctx_count, exp_count, tok),
                part,
                tuple(places[key] for key in slots),
                state_at,
                tuple(route_at),
                model_width,
            ),
            in_specs=[smem] * 2 + [vmem] * (5 + x_count) + [anywhere] + [vmem] * len(states),
            out_specs=[vmem] * len(slots),
            out_shape=[
                jax.ShapeDtypeStruct((2 * tok, half_width), bf16 if slot in leaves else f32)
                for slot in slots
            ],
            scratch_shapes=[pltpu.VMEM((rows // 2, in_width), bf16)],
            compiler_params=pltpu.CompilerParams(vmem_limit_bytes=2 * ctx_count * MIB),
            cost_estimate=pl.CostEstimate(
                flops=rows * half_width * in_width,
                bytes_accessed=8 * MIB,
                transcendentals=rows * in_width // 2,
            ),
            name="experts_out",
        )(
            my_ctx,
            my_exp,
            acts[part],
            from_offset(acts[part], 1),
            *routes,
            down_own,
            down_other,
            sums[slots_done[0]] if part else acts[1],
            *states,
        )
        slots_done = slots
        sums.update(zip(slots, outs))

    for number, sends in enumerate(reversed(stages)):
        came = []
        for moves, _, targets in sends:
            sent = [sums[key].astype(bf16) for key in targets]
            came.append(follow(sent[0] if len(sent) == 1 else jnp.concatenate(sent, axis=0), moves))
        if number < len(stages) - 1:
            waiting = list(near) if number == 0 else []
            values = together(*came, *[sums[key] for key in waiting])
            came = values[: len(came)]
            sums.update(zip(waiting, values[len(came) :]))
        for (_, sources, _), array in zip(sends, came):
            for place, key in enumerate(sources):
                part = array[place * 2 * tok : (place + 1) * 2 * tok]
                sums[key] = sums[key] + part.astype(f32)
    total = sums[0, 0]
    core = lax.bitwise_and(my_exp[0], 1)
    mine = jnp.where(core == 0, total[:tok], total[tok:]).astype(bf16)
    came = from_offset(jnp.where(core == 0, total[tok:], total[:tok]).astype(bf16), 1)
    mine = mine.reshape(tok, ctx_count, 1, cols)
    came = came.reshape(tok, ctx_count, 1, cols)
    result = jnp.where(core == 0, jnp.concatenate([mine, came], axis=2), jnp.concatenate([came, mine], axis=2))
    return result.reshape(tok, model_width)


def solution(mesh):
    return jax.shard_map(
        shards,
        mesh=mesh,
        in_specs=(
            P(("dp", "ctx", "exp"), None),
            P(("dp", "ctx"), "exp"),
            P(("dp", "ctx"), None),
            P(("dp", "ctx"), None),
            P(("dp", "ctx"), None),
            P(("dp", "ctx"), None),
            P(),
            P("exp", "ctx"),
            P(),
            P(("dp", "ctx", "exp"), None),
            P(("dp", "ctx", "exp"), None),
            P(("ctx", "exp"), None, None),
            P(("ctx", "exp"), None, None),
            P(("ctx", "exp"), None, None),
            P(("ctx", "exp"), None, None),
            P(("ctx", "exp"), None, None),
            P(("ctx", "exp"), None, None),
        ),
        out_specs=P(("dp", "ctx", "exp"), None),
        check_vma=False,
    )
```

```python
import functools
import math

import jax
import jax.numpy as jnp
from jax import lax
from jax.experimental import pallas as pl
from jax.experimental.pallas import tpu as pltpu
from jax.sharding import PartitionSpec as P

QUERY_HEADS = 32
KEY_VALUE_HEADS = 4
HEAD_SIZE = 128
TOP = 8
SCALE_POSITIONS = 64
WB = 128
MIB = 1 << 20


def bits_of(count):
    return count.bit_length() - 1


def from_offset(array, offset):
    return lax.ppermute(array, "exp", [(i, i ^ offset) for i in range(lax.axis_size("exp"))])


def from_ctx(array, offset):
    return lax.ppermute(array, "ctx", [(i, i ^ offset) for i in range(lax.axis_size("ctx"))])


def moved(offset, move):
    return (offset[0] ^ move[0], offset[1] ^ move[1])


def gather_route(ctx_count, x_count, rows_only=False):
    transfers, arrival, places = [], {(0, 0): 0}, {(0, 0): ((0, 0), (0, 0))}

    def go(source, moves, delay=0):
        reached = tuple(moved(place, (c, e >> 1)) for place, (c, e) in zip(places[source], moves))
        target = reached[0]
        arrival[target], places[target] = arrival[source] + 1 + delay, reached
        transfers.append((arrival[target], source, target, moves))
        return target

    bits = bits_of(ctx_count)
    y_move = (1, 0)
    if (ctx_count, x_count) == (8, 2) and not rows_only:
        z_far, z_near = ((4, 0),) * 2, ((2, 0),) * 2
        first, second, both = ((0, 2), y_move), (y_move, (0, 2)), ((1, 2),) * 2
        at = {"0": (0, 0)}
        for stage, moves, hops in (
            (1, z_far, "0>4"),
            (1, z_near, "0>2"),
            (1, first, "0>0a"),
            (1, second, "0>0b"),
            (1, both, "0>0ab"),
            (2, z_far, "0ab>4ab"),
            (2, z_near, "4>6"),
            (2, first, "2>2a 4>4a"),
            (2, second, "2>2b 4>4b"),
            (3, z_near, "4ab>6ab"),
            (3, first, "6>6a"),
            (3, second, "6>6b 2a>2ab"),
        ):
            for hop in hops.split():
                source, target = hop.split(">")
                at[target] = go(at[source], moves, stage - 1 - arrival[at[source]])
        return sorted(transfers, key=lambda transfer: transfer[0]), places
    if rows_only:
        shared, steps = range(bits - 1, 1, -1), [(2, 0), y_move]
    else:
        shared, steps = range(bits - 1, 0, -1), [(0, 2 << bit) for bit in range(bits_of(x_count))] + [y_move]
    pairs = list(zip(steps, reversed(steps)))
    for bit in shared:
        for source in list(arrival):
            go(source, ((1 << bit, 0),) * 2)
    for first in sorted(arrival):
        held = [first]
        for moves in pairs:
            held = held + [go(source, moves) for source in held]
    return sorted(transfers, key=lambda transfer: transfer[0]), places


def follow(array, moves):
    exp_count = lax.axis_size("exp")
    pairs = []
    for c in range(lax.axis_size("ctx")):
        for e in range(exp_count):
            far = moved((c, e), moves[e % 2])
            pairs.append((far[0] * exp_count + far[1], c * exp_count + e))
    return lax.ppermute(array, ("ctx", "exp"), pairs)


def side_of(index, bit):
    return (index >> bit) & 1


def without(index, bit):
    return (index & ((1 << bit) - 1)) | ((index >> bit + 1) << bit)


def runs(ctx_count, bit, side, each):
    length = each << bit
    return [
        (pl.multiple_of((2 * k + side) * length, length), k * length, length) for k in range(ctx_count >> bit + 1)
    ]


def by_core(core, place, part):
    first, second = place[0][part], place[1][part]
    return first if first == second else jnp.where(core == 0, first, second)


def stages_of(route):
    stages, arrays = [], [((0, 0),)]
    top = max(moves[0][0] for _, _, _, moves in route)
    for stage in sorted({transfer[0] for transfer in route}):
        sends = []
        for moves in sorted({t[3] for t in route if t[0] == stage}):
            left = {source: target for number, source, target, way in route if (number, way) == (stage, moves)}
            groups = [group for group in arrays if len(group) > 1 and all(key in left for key in group)]
            rest = tuple(sorted(key for key in left if not any(key in group for group in groups)))
            for group in groups + [rest] * bool(rest):
                sends.append((moves, group, tuple(left[key] for key in group)))
        def order(send):
            moves, group, _ = send
            shared, far = moves[0] == moves[1], moves[0][0] == top > 2
            rank = (0 if shared else 1) if len(group) == 1 else (1 if shared else 2 * moves[0][0])
            return -len(group) * (2 if far else 1), -1 if far else rank

        sends.sort(key=order)
        arrays = arrays + [send[2] for send in sends]
        stages.append(sends)
    return stages


def spread(block, stages, beside=None):
    arrays, at, joined = [block], {(0, 0): (0, 0)}, {}
    rows = block.shape[0]
    for number, sends in enumerate(stages):
        came = []
        for moves, group, _ in sends:
            first, row = at[group[0]]
            whole = row == 0 and arrays[first].shape[0] == len(group) * rows
            if whole and all(at[key] == (first, place * rows) for place, key in enumerate(group)):
                joined[group] = arrays[first]
            elif group not in joined:
                parts = [arrays[at[key][0]][at[key][1] : at[key][1] + rows] for key in group]
                joined[group] = jnp.concatenate(parts, axis=0)
            came.append(follow(joined[group], moves))
        came = beside(number, came) if beside else (together(*came) if number < len(stages) - 1 else came)
        for (_, _, targets), array in zip(sends, came):
            at.update({key: (len(arrays), place * rows) for place, key in enumerate(targets)})
            arrays.append(array)
    return arrays, at


def together(*values):
    return lax.optimization_barrier(values)


def block_factor(exponent, width):
    factor = jnp.where(exponent < 0, 0.5, jnp.where(exponent > 0, 2.0, 1.0))
    return jnp.full((1, width), factor, jnp.float32).astype(jnp.bfloat16)


def in_hbm(*arrays):
    return [pltpu.with_memory_space_constraint(array, pltpu.HBM) for array in arrays]


def copy_all(sems, pairs):
    copies = [pltpu.make_async_copy(src, dst, sems.at[i]) for i, (src, dst) in enumerate(pairs)]
    for copy in copies:
        copy.start()
    return copies


def pack_kernel(plan, ctx_ref, exp_ref, key_scale_hbm, value_scale_hbm, query_hbm, key_hbm, value_hbm, ids_hbm,
                route_hbm, residual_hbm, packed_ref, near_ref, far_ref, key_scale_ref, value_scale_ref,
                key_ref, value_ref, ids_ref, route_ref, sems):
    heads, group, x_count, piece_places = plan
    span, width = query_hbm.shape
    half, tok, cols = near_ref.shape
    cols = cols - HEAD_SIZE
    my_ctx, my_exp = ctx_ref[0], exp_ref[0]
    kv_head = my_exp * heads // group
    at = pl.ds(pl.multiple_of(kv_head * HEAD_SIZE, HEAD_SIZE), HEAD_SIZE)
    pairs = [
        (key_scale_hbm, key_scale_ref),
        (value_scale_hbm, value_scale_ref),
        (key_hbm.at[:, at], key_ref),
        (value_hbm.at[:, at], value_ref),
        (ids_hbm, ids_ref),
        (route_hbm, route_ref),
        (query_hbm, packed_ref.at[:, 2 * HEAD_SIZE : 2 * HEAD_SIZE + width]),
    ]
    core = lax.bitwise_and(my_exp, 1)
    for ref, places in zip((near_ref, far_ref), piece_places):
        for number, place in enumerate(places):
            col = pl.multiple_of(lax.bitwise_xor(my_ctx, by_core(core, place, 0)) * cols, cols)
            pairs.append((residual_hbm.at[:, pl.ds(col, cols)], ref.at[number, :, 0:cols]))
    copies = copy_all(sems, pairs)
    for copy in copies[:6]:
        copy.wait()
    lane = lax.broadcasted_iota(jnp.int32, key_scale_ref.shape, 1)
    blocks = key_scale_ref.shape[0]
    for place, (ref, scale_ref) in enumerate(((key_ref, key_scale_ref), (value_ref, value_scale_ref))):
        exponent = scale_ref[...]
        factor = jnp.where(
            exponent < -1, 0.25, jnp.where(exponent < 0, 0.5, jnp.where(exponent < 1, 1.0, 2.0))
        )
        factor = jnp.sum(jnp.where(lane == kv_head, factor, 0.0), axis=1, keepdims=True)
        for block in range(blocks):
            rows = pl.ds(block * (span // blocks), span // blocks)
            scaled = ref[rows, :].astype(jnp.float32) * factor[block : block + 1, :]
            packed_ref[rows, pl.ds(place * HEAD_SIZE, HEAD_SIZE)] = scaled.astype(jnp.bfloat16)
    number = lax.broadcasted_iota(jnp.int32, (128, tok), 0)
    dense = jnp.zeros((128, tok), jnp.float32)
    for k in range(TOP):
        dense = dense + jnp.where(ids_ref[k : k + 1, :] == number, route_ref[k : k + 1, :], 0.0)
    dense = jnp.concatenate([dense, jnp.zeros((128, 128 - tok), jnp.float32)], axis=1)
    dense = jnp.transpose(dense)[:tok, :]
    lane = lax.broadcasted_iota(jnp.int32, (tok, HEAD_SIZE), 1)
    for ref, places in zip((near_ref, far_ref), piece_places):
        for number, place in enumerate(places):
            expert = lax.bitwise_xor(my_ctx, by_core(core, place, 0)) * x_count
            block = jnp.zeros((tok, HEAD_SIZE), jnp.float32)
            for x in range(x_count):
                column = jnp.sum(jnp.where(lane == expert + x, dense, 0.0), axis=1, keepdims=True)
                high = column.astype(jnp.bfloat16).astype(jnp.float32)
                block = jnp.where(lane == x, high, jnp.where(lane == x_count + x, column - high, block))
            ref[number, :, cols:] = block.astype(jnp.bfloat16)
    for copy in copies[6:]:
        copy.wait()


def deq_in_kernel(ctx_count, exp_ref, gate_scale_hbm, up_scale_hbm, gate_hbm, up_hbm, _, own_ref, give_ref,
                  gate_ref, up_ref, gate_scale_ref, up_scale_ref, sems):
    core = lax.bitwise_and(exp_ref[0], 1)
    width, cols = gate_ref.shape
    rows = width // (2 * ctx_count)
    pairs = [(gate_scale_hbm, gate_scale_ref), (up_scale_hbm, up_scale_ref)]
    for step in range(ctx_count):
        at = pl.ds(step * 2 * rows, 2 * rows)
        pairs += [(gate_hbm.at[0, at], gate_ref.at[at]), (up_hbm.at[0, at], up_ref.at[at])]
    copies = copy_all(sems, pairs)
    for copy in copies[:2]:
        copy.wait()
    for step in range(ctx_count):
        for half, (ref, scale_ref) in enumerate(((gate_ref, gate_scale_ref), (up_ref, up_scale_ref))):
            copies[2 + 2 * step + half].wait()
            for out_ref, side in ((give_ref, 1 - core), (own_ref, core)):
                first = (2 * step + side) * (rows // WB)
                for i in range(rows // WB):
                    row = pl.multiple_of((2 * step + side) * rows + i * WB, WB)
                    for j in range(cols // WB):
                        factor = block_factor(scale_ref[j, 0, first + i], WB)
                        out_ref[pl.ds(step * rows + i * WB, WB), pl.ds(half * cols + j * WB, WB)] = (
                            ref[pl.ds(row, WB), pl.ds(j * WB, WB)] * factor
                        )


def deq_in(my_exp, gate_weight, gate_scale, up_weight, up_scale, ctx_count, after):
    width, hidden = gate_weight.shape[1:]
    shape = jax.ShapeDtypeStruct((width // 2, 2 * hidden), jnp.bfloat16)
    gate_scale = jnp.transpose(gate_scale, (2, 0, 1))
    up_scale = jnp.transpose(up_scale, (2, 0, 1))
    return pl.pallas_call(
        functools.partial(deq_in_kernel, ctx_count),
        in_specs=[pl.BlockSpec(memory_space=pltpu.SMEM)]
        + [pl.BlockSpec(memory_space=pltpu.HBM)] * 4
        + [pl.BlockSpec(memory_space=pl.ANY)],
        out_specs=[pl.BlockSpec(memory_space=pltpu.VMEM)] * 2,
        out_shape=[shape, shape],
        scratch_shapes=[
            pltpu.VMEM((width, hidden), jnp.bfloat16),
            pltpu.VMEM((width, hidden), jnp.bfloat16),
            pltpu.SMEM(gate_scale.shape, jnp.int32),
            pltpu.SMEM(up_scale.shape, jnp.int32),
            pltpu.SemaphoreType.DMA((2 + 2 * ctx_count,)),
        ],
        compiler_params=pltpu.CompilerParams(vmem_limit_bytes=20 * MIB),
        cost_estimate=pl.CostEstimate(
            flops=2 * width * hidden, bytes_accessed=8 * width * hidden, transcendentals=0
        ),
        name="dequant_in",
    )(my_exp, *in_hbm(gate_scale, up_scale, gate_weight, up_weight), after)


def deq_down_kernel(ctx_count, exp_ref, scale_hbm, down_hbm, _, own_ref, give_ref, down_ref, scale_ref, sems):
    core = lax.bitwise_and(exp_ref[0], 1)
    rows, width = down_ref.shape
    cols = width // (2 * ctx_count)
    pairs = [(scale_hbm, scale_ref)]
    for step in range(ctx_count):
        at = pl.ds(step * 2 * cols, 2 * cols)
        pairs.append((down_hbm.at[0, :, at], down_ref.at[:, at]))
    copies = copy_all(sems, pairs)
    copies[0].wait()
    for step in range(ctx_count):
        copies[1 + step].wait()
        for out_ref, side in ((give_ref, 1 - core), (own_ref, core)):
            first = (2 * step + side) * (cols // WB)
            for j in range(cols // WB):
                col = pl.multiple_of((2 * step + side) * cols + j * WB, WB)
                for i in range(rows // WB):
                    factor = block_factor(scale_ref[i, 0, first + j], WB)
                    out_ref[pl.ds(i * WB, WB), pl.ds(step * cols + j * WB, WB)] = (
                        down_ref[pl.ds(i * WB, WB), pl.ds(col, WB)] * factor
                    )


def deq_down(my_exp, down_weight, down_scale, ctx_count, after):
    hidden, width = down_weight.shape[1:]
    shape = jax.ShapeDtypeStruct((hidden, width // 2), jnp.bfloat16)
    down_scale = jnp.transpose(down_scale, (1, 0, 2))
    return pl.pallas_call(
        functools.partial(deq_down_kernel, ctx_count),
        in_specs=[pl.BlockSpec(memory_space=pltpu.SMEM)]
        + [pl.BlockSpec(memory_space=pltpu.HBM)] * 2
        + [pl.BlockSpec(memory_space=pl.ANY)],
        out_specs=[pl.BlockSpec(memory_space=pltpu.VMEM)] * 2,
        out_shape=[shape, shape],
        scratch_shapes=[
            pltpu.VMEM((hidden, width), jnp.bfloat16),
            pltpu.SMEM(down_scale.shape, jnp.int32),
            pltpu.SemaphoreType.DMA((1 + ctx_count,)),
        ],
        compiler_params=pltpu.CompilerParams(vmem_limit_bytes=12 * MIB),
        cost_estimate=pl.CostEstimate(
            flops=width * hidden, bytes_accessed=4 * width * hidden, transcendentals=0
        ),
        name="dequant_down",
    )(my_exp, *in_hbm(down_scale, down_weight), after)


def attend_kernel(plan, ctx_ref, exp_ref, order_ref, *refs):
    ctx_count, exp_count, tok, heads, attend_at = plan
    packed_at, places_of = [at for at, _ in attend_at], [place for _, place in attend_at]
    array_count = 1 + max(array for array, _ in packed_at)
    span = exp_count * tok
    packed_refs, refs = refs[:array_count], refs[array_count:]
    packed = []
    for array, row in packed_at:
        packed.append(packed_refs[array].at[pl.ds(row, span)])
    weight_ref, rest = refs[0], refs[2:]
    x_count = exp_count // 2
    keep_refs, give_ref = rest[:x_count], rest[x_count]
    key_scr, value_scr, place_scr, att_scr = rest[x_count + 1 :]
    positions = ctx_count * span
    my_ctx, my_exp = ctx_ref[0], exp_ref[0]
    my_x, my_core = lax.shift_right_logical(my_exp, 1), lax.bitwise_and(my_exp, 1)
    lane = lax.broadcasted_iota(jnp.int32, (8, positions), 1)
    places = lane % span
    for offset, ref in enumerate(packed):
        key_scr[pl.ds(offset * span, span), :] = ref[:, 0:HEAD_SIZE]
        value_scr[pl.ds(offset * span, span), 0:HEAD_SIZE] = ref[:, HEAD_SIZE : 2 * HEAD_SIZE]
        base = order_ref[lax.bitwise_xor(my_ctx, by_core(my_core, places_of[offset], 0))] * span
        places = places + jnp.where(lane // span == offset, base, 0)
    place_scr[...] = places
    scale = math.log2(math.e) / math.sqrt(HEAD_SIZE)
    value_scr[:, HEAD_SIZE:] = jnp.ones((positions, HEAD_SIZE), jnp.bfloat16)
    for offset, ref in enumerate(packed):
        source = lax.bitwise_xor(my_ctx, by_core(my_core, places_of[offset], 0))
        queries = jnp.concatenate(
            [ref[:, (h + 2) * HEAD_SIZE : (h + 3) * HEAD_SIZE] for h in range(heads)], axis=0
        )
        scores = lax.dot_general(
            queries, key_scr[...], (((1,), (1,)), ((), ())), preferred_element_type=jnp.float32
        )
        own_place = order_ref[source] * span + lax.broadcasted_iota(jnp.int32, (span, positions), 0)
        bias = jnp.where(place_scr[0:1, :] <= own_place, 0.0, -1e30)
        scores = scores.reshape(heads, span, positions) * scale + bias[None]
        exps = jnp.exp2(scores - jnp.max(scores, axis=-1, keepdims=True))
        mixed = jnp.dot(
            exps.astype(jnp.bfloat16).reshape(heads * span, positions),
            value_scr[...],
            preferred_element_type=jnp.float32,
        )
        mixed = mixed[:, :HEAD_SIZE] * (1.0 / mixed[:, HEAD_SIZE : HEAD_SIZE + 1])
        mixed = mixed.astype(jnp.bfloat16).reshape(heads, span, HEAD_SIZE)
        for owner in range(exp_count):
            x_off = lax.bitwise_xor(my_x, owner // 2)
            row = pl.multiple_of(((x_off * ctx_count + source) * 2 + owner % 2) * tok, tok)
            for head in range(heads):
                att_scr[pl.ds(row, tok), pl.ds(head * HEAD_SIZE, HEAD_SIZE)] = mixed[
                    head, owner * tok : (owner + 1) * tok, :
                ]

    cols = weight_ref.shape[1] // 2
    per_x = 2 * ctx_count * tok
    for x_off in range(x_count):
        rows = pl.ds(x_off * per_x, per_x)
        for which in (1, 0):
            side = lax.bitwise_xor(my_core, which)
            weight = weight_ref[:, pl.ds(pl.multiple_of(side * cols, cols), cols)]
            part = jnp.dot(att_scr[rows, :], weight, preferred_element_type=jnp.float32)
            out_ref = give_ref if which else keep_refs[x_off]
            out_ref[pl.ds(x_off * per_x if which else 0, per_x), :] = part.astype(out_ref.dtype)


def finish_kernel(plan, ctx_ref, exp_ref, keep_in, give_in, *refs):
    ctx_count, x_count, tok, piece_places, places_of = plan
    piece_refs, (keep_ref, give_ref, own_route_ref) = refs[:-3], refs[-3:]
    my_ctx, my_exp = ctx_ref[0], exp_ref[0]
    my_x, my_core = lax.shift_right_logical(my_exp, 1), lax.bitwise_and(my_exp, 1)
    cols = keep_ref.shape[1]
    route_base = give_in.shape[0]
    keep_ref[...] = keep_in[...]
    give_ref[0:route_base, :] = give_in[...]
    blocks = [jnp.zeros((tok, HEAD_SIZE), jnp.float32)] * x_count
    lane = lax.broadcasted_iota(jnp.int32, (tok, HEAD_SIZE), 1)
    for (array, place), place_of in zip(piece_places, places_of):
        source = lax.bitwise_xor(my_ctx, by_core(my_core, place_of, 0))
        at = pl.ds(pl.multiple_of((source * 2 + my_core) * tok, tok), tok)
        for which, ref in enumerate((keep_ref, give_ref)):
            side = lax.bitwise_xor(my_core, which)
            piece = piece_refs[array][place, :, pl.ds(pl.multiple_of(side * cols, cols), cols)]
            value = ref[at, :].astype(jnp.float32) + piece.astype(jnp.float32)
            ref[at, :] = value.astype(ref.dtype)
        block = piece_refs[array][place, :, 2 * cols :].astype(jnp.float32)
        for x_off in range(x_count):
            for part in range(2):
                wanted = lax.bitwise_xor(my_x, x_off) + part * x_count
                column = jnp.sum(jnp.where(lane == wanted, block, 0.0), axis=1, keepdims=True)
                blocks[x_off] = jnp.where(lane == source + part * ctx_count, column, blocks[x_off])
    for x_off, block in enumerate(blocks):
        for ref, base in ((give_ref, route_base), (own_route_ref, 0)):
            at = pl.ds(base + x_off * tok, tok)
            ref[at, 0:HEAD_SIZE] = block.astype(jnp.bfloat16)
            if cols > HEAD_SIZE:
                ref[at, HEAD_SIZE:] = jnp.zeros((tok, cols - HEAD_SIZE), jnp.bfloat16)


def fill_rows(plan, ctx_ref, exp_ref, gain_ref, chunk_refs, places, rows_scr, square_ref, groups):
    ctx_count, x_count, tok, bit = plan
    my_ctx = ctx_ref[0]
    my_core = lax.bitwise_and(exp_ref[0], 1)
    mine = side_of(my_ctx, bit)
    cols = chunk_refs[0].shape[1]
    rows = ctx_count * tok
    for (array, first_row), place_of in places:
        ref = chunk_refs[array]
        source = lax.bitwise_xor(my_ctx, by_core(my_core, place_of, 0))
        x_off = by_core(my_core, place_of, 1)
        gain_at = pl.multiple_of((source * 2 + my_core) * cols, cols)
        gain = gain_ref[:, pl.ds(gain_at, cols)]
        col = pl.multiple_of(without(source, bit) * cols, cols)
        for place, group in enumerate(groups):
            for start, low, length in runs(ctx_count, bit, mine if group == 1 else 1 - mine, 2 * tok):
                chunk = ref[pl.ds(first_row + start, length), :].astype(jnp.float32)
                row = (place * x_count + x_off) * rows + low
                at = pl.ds(pl.multiple_of(row, 2 * tok), length)
                rows_scr[at, pl.ds(col, cols)] = (chunk * gain).astype(jnp.bfloat16)
                square_ref[at, :] = square_ref[at, :] + jnp.sum(chunk * chunk, axis=-1, keepdims=True)


def product(plan, side, rows_scr, weight_ref, cols):
    ctx_count, _, _, bit = plan
    total = None
    for start, low, length in runs(ctx_count, bit, side, cols):
        part = jnp.dot(
            rows_scr[:, low : low + length],
            weight_ref[pl.ds(start, length), :],
            preferred_element_type=jnp.float32,
        )
        total = part if total is None else total + part
    return total


def experts_in_first(plan, offsets, ctx_ref, exp_ref, *refs):
    chunk_refs, (gain_ref, own_ref, other_ref, _, act_ref, square_ref, rows_scr) = refs[:-7], refs[-7:]
    square_ref[...] = jnp.zeros(square_ref.shape, jnp.float32)
    fill_rows(plan, ctx_ref, exp_ref, gain_ref, chunk_refs, offsets, rows_scr, square_ref, (0, 1))
    width, side = own_ref.shape[1], side_of(ctx_ref[0], plan[3])
    for place, ref in enumerate((own_ref, other_ref)):
        act_ref[:, place * width : (place + 1) * width] = product(
            plan, side, rows_scr, ref, chunk_refs[0].shape[1]
        )


def experts_in_second(plan, offsets, group, ctx_ref, exp_ref, *refs):
    chunk_refs, rest = refs[:-9], refs[-9:]
    gain_ref, own_ref, other_ref, first_ref, square_ref, _, act_ref, rows_scr, sum_scr = rest
    count, width = rows_scr.shape[0], own_ref.shape[1]
    sum_scr[...] = square_ref[group * count : (group + 1) * count, :]
    fill_rows(plan, ctx_ref, exp_ref, gain_ref, chunk_refs, offsets, rows_scr, sum_scr, (group,))
    lane = lax.broadcasted_iota(jnp.int32, (1, HEAD_SIZE), 1)
    square = sum_scr[...]
    high = square.astype(jnp.bfloat16).astype(jnp.float32)
    act_ref[:, 2 * width :] = jnp.where(lane == 0, high, square - high).astype(jnp.bfloat16)
    side = 1 - side_of(ctx_ref[0], plan[3])
    for place, ref in enumerate((own_ref, other_ref)):
        cols = slice(place * width, (place + 1) * width)
        act = first_ref[group * count : (group + 1) * count, cols] + product(
            plan, side, rows_scr, ref, chunk_refs[0].shape[1]
        )
        act_ref[:, cols] = act.astype(jnp.bfloat16)


def experts_out_kernel(plan, group, places, state_at, route_at, model_width, ctx_ref, exp_ref, act_ref, came_ref, *refs):
    ctx_count, exp_count, tok, bit = plan
    x_count, half = exp_count // 2, ctx_count // 2
    route_refs, refs = refs[: x_count + 1], refs[x_count + 1 :]
    (own_ref, other_ref, _), rest = refs[:3], refs[3:]
    state_count = 1 + max((array for pair in state_at for array, _ in pair), default=-1)
    state_refs, rest = rest[:state_count], rest[state_count:]
    out_refs, hidden_scr = rest[:-1], rest[-1]
    my_ctx = ctx_ref[0]
    my_core = lax.bitwise_and(exp_ref[0], 1)
    mine = side_of(my_ctx, bit)
    side = mine if group == 1 else 1 - mine
    width = (act_ref.shape[1] - HEAD_SIZE) // 2
    hidden = width // 2
    lane = lax.broadcasted_iota(jnp.int32, (tok, HEAD_SIZE), 1)
    blocks = []
    for array, row in route_at:
        blocks.append(route_refs[array][row : row + tok, 0:HEAD_SIZE].astype(jnp.float32))
    columns = []
    for x_off in range(x_count):
        for low in range(half):
            for core in range(2):
                same, swapped = blocks[2 * x_off + core], blocks[2 * x_off + 1 - core]
                block = jnp.where(my_core == 0, same, swapped)
                number = (low >> bit << bit + 1) + (low & ((1 << bit) - 1)) + side * (1 << bit)
                picked = jnp.where(lane % ctx_count == number, block, 0.0)
                columns.append(jnp.sum(picked, axis=1, keepdims=True))
    route = jnp.concatenate(columns, axis=0)
    squares = act_ref[:, 2 * width :].astype(jnp.float32) + came_ref[:, 2 * width :].astype(jnp.float32)
    norm = lax.rsqrt((squares[:, 0:1] + squares[:, 1:2]) / model_width + 1e-06)
    scaled_route = norm * route
    for part in range(2):
        acts = act_ref[:, part * width : (part + 1) * width].astype(jnp.float32) + came_ref[
            :, (1 - part) * width : (2 - part) * width
        ].astype(jnp.float32)
        gate = acts[:, :hidden] * norm
        value = gate / (1.0 + jnp.exp(-gate)) * (acts[:, hidden:] * scaled_route)
        hidden_scr[:, part * hidden : (part + 1) * hidden] = value.astype(jnp.bfloat16)
    picked = []
    for place in places:
        x_off = by_core(my_core, place, 1)
        low = without(lax.bitwise_xor(my_ctx, by_core(my_core, place, 0)), bit)
        row = pl.multiple_of((x_off * half + low) * (2 * tok), 2 * tok)
        picked.append(hidden_scr[pl.ds(row, 2 * tok), :])
    picked = jnp.concatenate(picked, axis=0)
    out_cols = own_ref.shape[1]
    step = min(512, out_cols)
    for col in range(0, out_cols, step):
        at = pl.ds(col, step)
        out = jnp.dot(picked[:, :hidden], own_ref[:, at], preferred_element_type=jnp.float32)
        out = out + jnp.dot(picked[:, hidden:], other_ref[:, at], preferred_element_type=jnp.float32)
        for place, ref in enumerate(out_refs):
            ref[:, at] = out[place * 2 * tok : (place + 1) * 2 * tok, :].astype(ref.dtype)
    for place, ref in zip(places, out_refs):
        if place[0] == (0, 0):
            for c_off, pair in enumerate(state_at):
                states = []
                for array, first_row in pair:
                    own_row = pl.multiple_of(first_row + my_ctx * (2 * tok), 2 * tok)
                    states.append(state_refs[array][pl.ds(own_row, 2 * tok), :].astype(jnp.float32))
                state = states[0] if pair[0] == pair[1] else jnp.where(my_core == 0, *states)
                cols = state.shape[1]
                at = pl.ds(pl.multiple_of(lax.bitwise_xor(my_ctx, c_off) * cols, cols), cols)
                ref[:, at] = ref[:, at] + state


def shards(
    residual,
    encoded_query_rows,
    quantized_key_rows,
    quantized_value_rows,
    key_block_exponent,
    value_block_exponent,
    block_order,
    out_weight,
    norm_gain,
    expert_ids,
    route_weight,
    gate_weight,
    gate_scale,
    up_weight,
    up_scale,
    down_weight,
    down_scale,
):
    f32, bf16 = jnp.float32, jnp.bfloat16
    vmem = pl.BlockSpec(memory_space=pltpu.VMEM)
    smem = pl.BlockSpec(memory_space=pltpu.SMEM)
    anywhere = pl.BlockSpec(memory_space=pl.ANY)
    span, query_width = encoded_query_rows.shape
    heads = query_width // HEAD_SIZE
    group = QUERY_HEADS // KEY_VALUE_HEADS
    ctx_count = lax.axis_size("ctx")
    exp_count = lax.axis_size("exp")
    x_count = exp_count // 2
    experts = ctx_count * x_count
    tok, model_width = residual.shape
    half_width = model_width // 2
    cols = half_width // ctx_count
    my_ctx = lax.axis_index("ctx").astype(jnp.int32).reshape(1)
    my_exp = lax.axis_index("exp").astype(jnp.int32).reshape(1)
    route, places = gather_route(ctx_count, x_count)

    hbm = pl.BlockSpec(memory_space=pltpu.HBM)
    piece_shape = jax.ShapeDtypeStruct((ctx_count // 2, tok, 2 * cols + HEAD_SIZE), bf16)
    row_route, row_places = gather_route(ctx_count, x_count, rows_only=True)
    names = sorted(row_places)
    piece_names = [[key for key in names if bool(key[0] & 2) == sent] for sent in (False, True)]
    piece_places = tuple(tuple(row_places[key] for key in keys) for keys in piece_names)
    packed, near, far = pl.pallas_call(
        functools.partial(pack_kernel, (heads, group, x_count, piece_places)),
        in_specs=[smem] * 2 + [hbm] * 8,
        out_specs=[vmem] * 3,
        out_shape=[
            jax.ShapeDtypeStruct((span, query_width + 2 * HEAD_SIZE), bf16),
            piece_shape,
            piece_shape,
        ],
        scratch_shapes=[
            pltpu.VMEM(key_block_exponent.shape, jnp.int32),
            pltpu.VMEM(key_block_exponent.shape, jnp.int32),
            pltpu.VMEM((span, HEAD_SIZE), bf16),
            pltpu.VMEM((span, HEAD_SIZE), bf16),
            pltpu.VMEM((TOP, tok), jnp.int32),
            pltpu.VMEM((TOP, tok), f32),
            pltpu.SemaphoreType.DMA((7 + ctx_count,)),
        ],
        compiler_params=pltpu.CompilerParams(vmem_limit_bytes=8 * MIB),
        name="pack",
    )(
        my_ctx,
        my_exp,
        *in_hbm(
            key_block_exponent,
            value_block_exponent,
            encoded_query_rows,
            quantized_key_rows,
            quantized_value_rows,
            jnp.transpose(expert_ids),
            jnp.transpose(route_weight),
            residual,
        ),
    )
    piece_arrays = [near]
    piece_at = {(0, key[0]): (0, place) for place, key in enumerate(piece_names[0])}
    piece_bits = [1, 0, *range(bits_of(ctx_count) - 1, 1, -1)]
    sending, weights = far, {}

    def beside(number, came):
        nonlocal sending
        bit = 1 << piece_bits[number]
        moves = {1: ((2, 0), (1, 0)), 0: ((1, 0), (2, 0))}.get(piece_bits[number], ((bit, 0),) * 2)
        if number == 0:
            keys = [(0, key[0]) for key in piece_names[1]]
        else:
            keys = sorted(key for key in piece_at if key[1] & bit)
            sending = jnp.stack([piece_arrays[array][place] for array, place in map(piece_at.pop, keys)])
        pieces = follow(sending, moves)
        if number == 0:
            own, give = deq_in(my_exp, gate_weight, gate_scale, up_weight, up_scale, ctx_count, packed)
            *came, pieces, weights["in_own"], weights["in_give"] = together(*came, pieces, own, give)
        elif number == 1:
            other = from_offset(weights["in_give"], 1)
            own, give = deq_down(my_exp, down_weight, down_scale, ctx_count, piece_arrays[-1])
            *came, pieces, weights["in_other"], weights["down_own"], weights["down_give"] = together(
                *came, pieces, other, own, give
            )
        elif number < len(piece_bits) - 1:
            *came, pieces = together(*came, pieces)
        for place, (source, target) in enumerate(keys):
            piece_at[source ^ bit, target ^ bit] = (len(piece_arrays), place)
        piece_arrays.append(pieces)
        return came

    packed, packed_at = spread(packed, stages_of(row_route), beside)
    attend_at = tuple((packed_at[key], row_places[key]) for key in names)
    attend_pieces = tuple(piece_at[key[0], 0] for key in names)
    in_own, in_other, down_own = weights["in_own"], weights["in_other"], weights["down_own"]
    down_other = from_offset(weights["down_give"], 1)

    positions = ctx_count * span
    per_x = 2 * ctx_count * tok
    *keeps, give = pl.pallas_call(
        functools.partial(attend_kernel, (ctx_count, exp_count, tok, heads, attend_at)),
        in_specs=[smem] * 3 + [vmem] * (len(packed) + 1) + [anywhere],
        out_specs=[vmem] * (1 + x_count),
        out_shape=[jax.ShapeDtypeStruct((per_x, cols), f32)] * x_count
        + [jax.ShapeDtypeStruct((x_count * per_x, cols), bf16)],
        scratch_shapes=[
            pltpu.VMEM((positions, HEAD_SIZE), bf16),
            pltpu.VMEM((positions, 2 * HEAD_SIZE), bf16),
            pltpu.VMEM((8, positions), jnp.int32),
            pltpu.VMEM((positions, query_width), bf16),
        ],
        compiler_params=pltpu.CompilerParams(vmem_limit_bytes=3 * ctx_count * MIB),
        cost_estimate=pl.CostEstimate(
            flops=4 * positions * positions * query_width + 4 * positions * query_width * cols,
            bytes_accessed=8 * MIB,
            transcendentals=heads * positions * positions,
        ),
        name="attend",
    )(my_ctx, my_exp, block_order, *packed, out_weight, down_other)
    keeps[0], give, own_route = pl.pallas_call(
        functools.partial(
            finish_kernel,
            (ctx_count, x_count, tok, attend_pieces, tuple(place for _, place in attend_at)),
        ),
        in_specs=[smem] * 2 + [vmem] * (2 + len(piece_arrays)),
        out_specs=[vmem] * 3,
        out_shape=[
            jax.ShapeDtypeStruct((per_x, cols), f32),
            jax.ShapeDtypeStruct((x_count * (per_x + tok), cols), bf16),
            jax.ShapeDtypeStruct((x_count * tok, cols), bf16),
        ],
        compiler_params=pltpu.CompilerParams(vmem_limit_bytes=8 * MIB),
        name="finish",
    )(my_ctx, my_exp, keeps[0], give, *piece_arrays)

    given = from_offset(give, 1)
    routes, route_at, state = [own_route, given], [(0, 0), (1, x_count * per_x)], keeps[0]
    state = state + given[:per_x].astype(f32)
    for x_off in range(1, x_count):
        part = keeps[x_off] + given[x_off * per_x : (x_off + 1) * per_x].astype(f32)
        row = x_count * per_x + x_off * tok
        own = own_route[x_off * tok : (x_off + 1) * tok]
        sent = jnp.concatenate([part.astype(bf16), own, given[row : row + tok]], axis=0)
        came = from_offset(sent, 2 * x_off)
        state = state + came[:per_x].astype(f32)
        route_at += [(len(routes), per_x), (len(routes), per_x + tok)]
        routes.append(came)
    state = state.astype(bf16)

    stages = stages_of(route)
    chunks, chunk_at = spread(state, stages)
    gain = norm_gain.reshape(1, model_width)
    rows = x_count * per_x
    in_width = in_own.shape[1]
    bit = 1 if (ctx_count, x_count) == (8, 2) else bits_of(ctx_count) - 1
    near = tuple(sorted(key for key in places if not side_of(key[0], bit)))
    far = tuple(sorted(key for key in places if side_of(key[0], bit)))

    def picked(keys):
        arrays = sorted({chunk_at[key][0] for key in keys})
        at = tuple(((arrays.index(chunk_at[key][0]), chunk_at[key][1]), places[key]) for key in keys)
        return [chunks[array] for array in arrays], at

    near_chunks, near_places = picked(near)
    far_chunks, far_places = picked(far)
    first_act, first_square = pl.pallas_call(
        functools.partial(experts_in_first, (ctx_count, x_count, tok, bit), near_places),
        in_specs=[smem] * 2 + [vmem] * (len(near_chunks) + 3) + [anywhere],
        out_specs=[vmem] * 2,
        out_shape=[
            jax.ShapeDtypeStruct((rows, 2 * in_width), f32),
            jax.ShapeDtypeStruct((rows, 1), f32),
        ],
        scratch_shapes=[pltpu.VMEM((rows, half_width // 2), bf16)],
        compiler_params=pltpu.CompilerParams(vmem_limit_bytes=2 * ctx_count * MIB),
        cost_estimate=pl.CostEstimate(
            flops=2 * rows * half_width * in_width, bytes_accessed=8 * MIB, transcendentals=0
        ),
        name="experts_in_first",
    )(my_ctx, my_exp, *near_chunks, gain, in_own, in_other, down_other)
    acts = []
    for part in range(2):
        acts.append(
            pl.pallas_call(
                functools.partial(experts_in_second, (ctx_count, x_count, tok, bit), far_places, part),
                in_specs=[smem] * 2 + [vmem] * (len(far_chunks) + 5) + [anywhere],
                out_specs=vmem,
                out_shape=jax.ShapeDtypeStruct((rows // 2, 2 * in_width + HEAD_SIZE), bf16),
                scratch_shapes=[
                    pltpu.VMEM((rows // 2, half_width // 2), bf16),
                    pltpu.VMEM((rows // 2, 1), f32),
                ],
                compiler_params=pltpu.CompilerParams(vmem_limit_bytes=2 * ctx_count * MIB),
                cost_estimate=pl.CostEstimate(
                    flops=rows * half_width * in_width, bytes_accessed=8 * MIB, transcendentals=0
                ),
                name="experts_in_second",
            )(
                my_ctx,
                my_exp,
                *far_chunks,
                gain,
                in_own,
                in_other,
                first_act,
                first_square,
                acts[0] if part else first_square,
            )
        )
    leaves = set(places) - {source for _, source, _, _ in route}
    sums = {}
    for part in range(2):
        slots = near if part == 1 else far
        state_keys = [
            next(key for key in places if places[key][core] == (offset, 0))
            for offset in (range(ctx_count) if part == 1 else ())
            for core in range(2)
        ]
        states, state_at = picked(state_keys)
        state_at = tuple((state_at[i][0], state_at[i + 1][0]) for i in range(0, len(state_at), 2))
        outs = pl.pallas_call(
            functools.partial(
                experts_out_kernel,
                (ctx_count, exp_count, tok, bit),
                part,
                tuple(places[key] for key in slots),
                state_at,
                tuple(route_at),
                model_width,
            ),
            in_specs=[smem] * 2 + [vmem] * (5 + x_count) + [anywhere] + [vmem] * len(states),
            out_specs=[vmem] * len(slots),
            out_shape=[
                jax.ShapeDtypeStruct((2 * tok, half_width), bf16 if slot in leaves else f32)
                for slot in slots
            ],
            scratch_shapes=[pltpu.VMEM((rows // 2, in_width), bf16)],
            compiler_params=pltpu.CompilerParams(vmem_limit_bytes=2 * ctx_count * MIB),
            cost_estimate=pl.CostEstimate(
                flops=rows * half_width * in_width,
                bytes_accessed=8 * MIB,
                transcendentals=rows * in_width // 2,
            ),
            name="experts_out",
        )(
            my_ctx,
            my_exp,
            acts[part],
            from_offset(acts[part], 1),
            *routes,
            down_own,
            down_other,
            sums[slots_done[0]] if part else acts[1],
            *states,
        )
        slots_done = slots
        sums.update(zip(slots, outs))

    for number, sends in enumerate(reversed(stages)):
        came = []
        for moves, _, targets in sends:
            sent = [sums[key].astype(bf16) for key in targets]
            came.append(follow(sent[0] if len(sent) == 1 else jnp.concatenate(sent, axis=0), moves))
        if number < len(stages) - 1:
            waiting = list(near) if number == 0 else []
            values = together(*came, *[sums[key] for key in waiting])
            came = values[: len(came)]
            sums.update(zip(waiting, values[len(came) :]))
        for (_, sources, _), array in zip(sends, came):
            for place, key in enumerate(sources):
                part = array[place * 2 * tok : (place + 1) * 2 * tok]
                sums[key] = sums[key] + part.astype(f32)
    total = sums[0, 0]
    core = lax.bitwise_and(my_exp[0], 1)
    mine = jnp.where(core == 0, total[:tok], total[tok:]).astype(bf16)
    came = from_offset(jnp.where(core == 0, total[tok:], total[:tok]).astype(bf16), 1)
    mine = mine.reshape(tok, ctx_count, 1, cols)
    came = came.reshape(tok, ctx_count, 1, cols)
    result = jnp.where(core == 0, jnp.concatenate([mine, came], axis=2), jnp.concatenate([came, mine], axis=2))
    return result.reshape(tok, model_width)


def solution(mesh):
    return jax.shard_map(
        shards,
        mesh=mesh,
        in_specs=(
            P(("dp", "ctx", "exp"), None),
            P(("dp", "ctx"), "exp"),
            P(("dp", "ctx"), None),
            P(("dp", "ctx"), None),
            P(("dp", "ctx"), None),
            P(("dp", "ctx"), None),
            P(),
            P("exp", "ctx"),
            P(),
            P(("dp", "ctx", "exp"), None),
            P(("dp", "ctx", "exp"), None),
            P(("ctx", "exp"), None, None),
            P(("ctx", "exp"), None, None),
            P(("ctx", "exp"), None, None),
            P(("ctx", "exp"), None, None),
            P(("ctx", "exp"), None, None),
            P(("ctx", "exp"), None, None),
        ),
        out_specs=P(("dp", "ctx", "exp"), None),
        check_vma=False,
    )
```

```python
import functools
import math

import jax
import jax.numpy as jnp
from jax import lax
from jax.experimental import pallas as pl
from jax.experimental.pallas import tpu as pltpu
from jax.sharding import PartitionSpec as P

QUERY_HEADS = 32
KEY_VALUE_HEADS = 4
HEAD_SIZE = 128
TOP = 8
SCALE_POSITIONS = 64
WB = 128
MIB = 1 << 20


def bits_of(count):
    return count.bit_length() - 1


def from_offset(array, offset):
    return lax.ppermute(array, "exp", [(i, i ^ offset) for i in range(lax.axis_size("exp"))])


def from_ctx(array, offset):
    return lax.ppermute(array, "ctx", [(i, i ^ offset) for i in range(lax.axis_size("ctx"))])


def moved(offset, move):
    return (offset[0] ^ move[0], offset[1] ^ move[1])


def gather_route(ctx_count, x_count, rows_only=False):
    transfers, arrival, places = [], {(0, 0): 0}, {(0, 0): ((0, 0), (0, 0))}

    def go(source, moves, delay=0):
        reached = tuple(moved(place, (c, e >> 1)) for place, (c, e) in zip(places[source], moves))
        target = reached[0]
        arrival[target], places[target] = arrival[source] + 1 + delay, reached
        transfers.append((arrival[target], source, target, moves))
        return target

    bits = bits_of(ctx_count)
    y_move = (1, 0)
    if (ctx_count, x_count) == (8, 2) and not rows_only:
        z_far, z_near = ((4, 0),) * 2, ((2, 0),) * 2
        first, second, both = ((0, 2), y_move), (y_move, (0, 2)), ((1, 2),) * 2
        at = {"0": (0, 0)}
        for stage, moves, hops in (
            (1, z_far, "0>4"),
            (1, z_near, "0>2"),
            (1, first, "0>0a"),
            (1, second, "0>0b"),
            (1, both, "0>0ab"),
            (2, z_far, "0ab>4ab"),
            (2, z_near, "4>6"),
            (2, first, "2>2a 4>4a"),
            (2, second, "2>2b 4>4b"),
            (3, z_near, "4ab>6ab"),
            (3, first, "6>6a"),
            (3, second, "6>6b 2a>2ab"),
        ):
            for hop in hops.split():
                source, target = hop.split(">")
                at[target] = go(at[source], moves, stage - 1 - arrival[at[source]])
        return sorted(transfers, key=lambda transfer: transfer[0]), places
    if rows_only:
        shared, steps = range(bits - 1, 1, -1), [(2, 0), y_move]
    else:
        shared, steps = range(bits - 1, 0, -1), [(0, 2 << bit) for bit in range(bits_of(x_count))] + [y_move]
    pairs = list(zip(steps, reversed(steps)))
    for bit in shared:
        for source in list(arrival):
            go(source, ((1 << bit, 0),) * 2)
    for first in sorted(arrival):
        held = [first]
        for moves in pairs:
            held = held + [go(source, moves) for source in held]
    return sorted(transfers, key=lambda transfer: transfer[0]), places


def follow(array, moves):
    exp_count = lax.axis_size("exp")
    pairs = []
    for c in range(lax.axis_size("ctx")):
        for e in range(exp_count):
            far = moved((c, e), moves[e % 2])
            pairs.append((far[0] * exp_count + far[1], c * exp_count + e))
    return lax.ppermute(array, ("ctx", "exp"), pairs)


def side_of(index, bit):
    return (index >> bit) & 1


def without(index, bit):
    return (index & ((1 << bit) - 1)) | ((index >> bit + 1) << bit)


def runs(ctx_count, bit, side, each):
    length = each << bit
    return [
        (pl.multiple_of((2 * k + side) * length, length), k * length, length) for k in range(ctx_count >> bit + 1)
    ]


def by_core(core, place, part):
    first, second = place[0][part], place[1][part]
    return first if first == second else jnp.where(core == 0, first, second)


def stages_of(route):
    stages, arrays = [], [((0, 0),)]
    top = max(moves[0][0] for _, _, _, moves in route)
    for stage in sorted({transfer[0] for transfer in route}):
        sends = []
        for moves in sorted({t[3] for t in route if t[0] == stage}):
            left = {source: target for number, source, target, way in route if (number, way) == (stage, moves)}
            groups = [group for group in arrays if len(group) > 1 and all(key in left for key in group)]
            rest = tuple(sorted(key for key in left if not any(key in group for group in groups)))
            for group in groups + [rest] * bool(rest):
                sends.append((moves, group, tuple(left[key] for key in group)))
        def order(send):
            moves, group, _ = send
            shared, far = moves[0] == moves[1], moves[0][0] == top > 2
            rank = (0 if shared else 1) if len(group) == 1 else (1 if shared else 2 * moves[0][0])
            return -len(group) * (2 if far else 1), -1 if far else rank

        sends.sort(key=order)
        arrays = arrays + [send[2] for send in sends]
        stages.append(sends)
    return stages


def spread(block, stages, beside=None):
    arrays, at, joined = [block], {(0, 0): (0, 0)}, {}
    rows = block.shape[0]
    for number, sends in enumerate(stages):
        came = []
        for moves, group, _ in sends:
            first, row = at[group[0]]
            whole = row == 0 and arrays[first].shape[0] == len(group) * rows
            if whole and all(at[key] == (first, place * rows) for place, key in enumerate(group)):
                joined[group] = arrays[first]
            elif group not in joined:
                parts = [arrays[at[key][0]][at[key][1] : at[key][1] + rows] for key in group]
                joined[group] = jnp.concatenate(parts, axis=0)
            came.append(follow(joined[group], moves))
        came = beside(number, came, arrays, at) if beside else (together(*came) if number < len(stages) - 1 else came)
        for (_, _, targets), array in zip(sends, came):
            at.update({key: (len(arrays), place * rows) for place, key in enumerate(targets)})
            arrays.append(array)
    return arrays, at


def together(*values):
    return lax.optimization_barrier(values)


def block_factor(exponent, width):
    factor = jnp.where(exponent < 0, 0.5, jnp.where(exponent > 0, 2.0, 1.0))
    return jnp.full((1, width), factor, jnp.float32).astype(jnp.bfloat16)


def in_hbm(*arrays):
    return [pltpu.with_memory_space_constraint(array, pltpu.HBM) for array in arrays]


def copy_all(sems, pairs):
    copies = [pltpu.make_async_copy(src, dst, sems.at[i]) for i, (src, dst) in enumerate(pairs)]
    for copy in copies:
        copy.start()
    return copies


def pack_kernel(plan, ctx_ref, exp_ref, key_scale_hbm, value_scale_hbm, query_hbm, key_hbm, value_hbm, ids_hbm,
                route_hbm, residual_hbm, packed_ref, near_ref, far_ref, key_scale_ref, value_scale_ref,
                key_ref, value_ref, ids_ref, route_ref, sems):
    heads, group, x_count, piece_places = plan
    span, width = query_hbm.shape
    half, tok, cols = near_ref.shape
    cols = cols - HEAD_SIZE
    my_ctx, my_exp = ctx_ref[0], exp_ref[0]
    kv_head = my_exp * heads // group
    at = pl.ds(pl.multiple_of(kv_head * HEAD_SIZE, HEAD_SIZE), HEAD_SIZE)
    pairs = [
        (key_scale_hbm, key_scale_ref),
        (value_scale_hbm, value_scale_ref),
        (key_hbm.at[:, at], key_ref),
        (value_hbm.at[:, at], value_ref),
        (ids_hbm, ids_ref),
        (route_hbm, route_ref),
        (query_hbm, packed_ref.at[:, 2 * HEAD_SIZE : 2 * HEAD_SIZE + width]),
    ]
    core = lax.bitwise_and(my_exp, 1)
    for ref, places in zip((near_ref, far_ref), piece_places):
        for number, place in enumerate(places):
            col = pl.multiple_of(lax.bitwise_xor(my_ctx, by_core(core, place, 0)) * cols, cols)
            pairs.append((residual_hbm.at[:, pl.ds(col, cols)], ref.at[number, :, 0:cols]))
    copies = copy_all(sems, pairs)
    for copy in copies[:6]:
        copy.wait()
    lane = lax.broadcasted_iota(jnp.int32, key_scale_ref.shape, 1)
    blocks = key_scale_ref.shape[0]
    for place, (ref, scale_ref) in enumerate(((key_ref, key_scale_ref), (value_ref, value_scale_ref))):
        exponent = scale_ref[...]
        factor = jnp.where(
            exponent < -1, 0.25, jnp.where(exponent < 0, 0.5, jnp.where(exponent < 1, 1.0, 2.0))
        )
        factor = jnp.sum(jnp.where(lane == kv_head, factor, 0.0), axis=1, keepdims=True)
        for block in range(blocks):
            rows = pl.ds(block * (span // blocks), span // blocks)
            scaled = ref[rows, :].astype(jnp.float32) * factor[block : block + 1, :]
            packed_ref[rows, pl.ds(place * HEAD_SIZE, HEAD_SIZE)] = scaled.astype(jnp.bfloat16)
    number = lax.broadcasted_iota(jnp.int32, (128, tok), 0)
    dense = jnp.zeros((128, tok), jnp.float32)
    for k in range(TOP):
        dense = dense + jnp.where(ids_ref[k : k + 1, :] == number, route_ref[k : k + 1, :], 0.0)
    dense = jnp.concatenate([dense, jnp.zeros((128, 128 - tok), jnp.float32)], axis=1)
    dense = jnp.transpose(dense)[:tok, :]
    lane = lax.broadcasted_iota(jnp.int32, (tok, HEAD_SIZE), 1)
    for ref, places in zip((near_ref, far_ref), piece_places):
        for number, place in enumerate(places):
            expert = lax.bitwise_xor(my_ctx, by_core(core, place, 0)) * x_count
            block = jnp.zeros((tok, HEAD_SIZE), jnp.float32)
            for x in range(x_count):
                column = jnp.sum(jnp.where(lane == expert + x, dense, 0.0), axis=1, keepdims=True)
                high = column.astype(jnp.bfloat16).astype(jnp.float32)
                block = jnp.where(lane == x, high, jnp.where(lane == x_count + x, column - high, block))
            ref[number, :, cols:] = block.astype(jnp.bfloat16)
    for copy in copies[6:]:
        copy.wait()


def deq_in_kernel(ctx_count, exp_ref, gate_scale_hbm, up_scale_hbm, gate_hbm, up_hbm, _, own_ref, give_ref,
                  gate_ref, up_ref, gate_scale_ref, up_scale_ref, sems):
    core = lax.bitwise_and(exp_ref[0], 1)
    width, cols = gate_ref.shape
    rows = width // (2 * ctx_count)
    pairs = [(gate_scale_hbm, gate_scale_ref), (up_scale_hbm, up_scale_ref)]
    for step in range(ctx_count):
        at = pl.ds(step * 2 * rows, 2 * rows)
        pairs += [(gate_hbm.at[0, at], gate_ref.at[at]), (up_hbm.at[0, at], up_ref.at[at])]
    copies = copy_all(sems, pairs)
    for copy in copies[:2]:
        copy.wait()
    for step in range(ctx_count):
        for half, (ref, scale_ref) in enumerate(((gate_ref, gate_scale_ref), (up_ref, up_scale_ref))):
            copies[2 + 2 * step + half].wait()
            for out_ref, side in ((give_ref, 1 - core), (own_ref, core)):
                first = (2 * step + side) * (rows // WB)
                for i in range(rows // WB):
                    row = pl.multiple_of((2 * step + side) * rows + i * WB, WB)
                    for j in range(cols // WB):
                        factor = block_factor(scale_ref[j, 0, first + i], WB)
                        out_ref[pl.ds(step * rows + i * WB, WB), pl.ds(half * cols + j * WB, WB)] = (
                            ref[pl.ds(row, WB), pl.ds(j * WB, WB)] * factor
                        )


def deq_in(my_exp, gate_weight, gate_scale, up_weight, up_scale, ctx_count, after):
    width, hidden = gate_weight.shape[1:]
    shape = jax.ShapeDtypeStruct((width // 2, 2 * hidden), jnp.bfloat16)
    gate_scale = jnp.transpose(gate_scale, (2, 0, 1))
    up_scale = jnp.transpose(up_scale, (2, 0, 1))
    return pl.pallas_call(
        functools.partial(deq_in_kernel, ctx_count),
        in_specs=[pl.BlockSpec(memory_space=pltpu.SMEM)]
        + [pl.BlockSpec(memory_space=pltpu.HBM)] * 4
        + [pl.BlockSpec(memory_space=pl.ANY)],
        out_specs=[pl.BlockSpec(memory_space=pltpu.VMEM)] * 2,
        out_shape=[shape, shape],
        scratch_shapes=[
            pltpu.VMEM((width, hidden), jnp.bfloat16),
            pltpu.VMEM((width, hidden), jnp.bfloat16),
            pltpu.SMEM(gate_scale.shape, jnp.int32),
            pltpu.SMEM(up_scale.shape, jnp.int32),
            pltpu.SemaphoreType.DMA((2 + 2 * ctx_count,)),
        ],
        compiler_params=pltpu.CompilerParams(vmem_limit_bytes=20 * MIB),
        cost_estimate=pl.CostEstimate(
            flops=2 * width * hidden, bytes_accessed=8 * width * hidden, transcendentals=0
        ),
        name="dequant_in",
    )(my_exp, *in_hbm(gate_scale, up_scale, gate_weight, up_weight), after)


def deq_down_kernel(ctx_count, exp_ref, scale_hbm, down_hbm, _, own_ref, give_ref, down_ref, scale_ref, sems):
    core = lax.bitwise_and(exp_ref[0], 1)
    rows, width = down_ref.shape
    cols = width // (2 * ctx_count)
    pairs = [(scale_hbm, scale_ref)]
    for step in range(ctx_count):
        at = pl.ds(step * 2 * cols, 2 * cols)
        pairs.append((down_hbm.at[0, :, at], down_ref.at[:, at]))
    copies = copy_all(sems, pairs)
    copies[0].wait()
    for step in range(ctx_count):
        copies[1 + step].wait()
        for out_ref, side in ((give_ref, 1 - core), (own_ref, core)):
            first = (2 * step + side) * (cols // WB)
            for j in range(cols // WB):
                col = pl.multiple_of((2 * step + side) * cols + j * WB, WB)
                for i in range(rows // WB):
                    factor = block_factor(scale_ref[i, 0, first + j], WB)
                    out_ref[pl.ds(i * WB, WB), pl.ds(step * cols + j * WB, WB)] = (
                        down_ref[pl.ds(i * WB, WB), pl.ds(col, WB)] * factor
                    )


def deq_down(my_exp, down_weight, down_scale, ctx_count, after):
    hidden, width = down_weight.shape[1:]
    shape = jax.ShapeDtypeStruct((hidden, width // 2), jnp.bfloat16)
    down_scale = jnp.transpose(down_scale, (1, 0, 2))
    return pl.pallas_call(
        functools.partial(deq_down_kernel, ctx_count),
        in_specs=[pl.BlockSpec(memory_space=pltpu.SMEM)]
        + [pl.BlockSpec(memory_space=pltpu.HBM)] * 2
        + [pl.BlockSpec(memory_space=pl.ANY)],
        out_specs=[pl.BlockSpec(memory_space=pltpu.VMEM)] * 2,
        out_shape=[shape, shape],
        scratch_shapes=[
            pltpu.VMEM((hidden, width), jnp.bfloat16),
            pltpu.SMEM(down_scale.shape, jnp.int32),
            pltpu.SemaphoreType.DMA((1 + ctx_count,)),
        ],
        compiler_params=pltpu.CompilerParams(vmem_limit_bytes=12 * MIB),
        cost_estimate=pl.CostEstimate(
            flops=width * hidden, bytes_accessed=4 * width * hidden, transcendentals=0
        ),
        name="dequant_down",
    )(my_exp, *in_hbm(down_scale, down_weight), after)


def attend_kernel(plan, ctx_ref, exp_ref, order_ref, *refs):
    ctx_count, exp_count, tok, heads, attend_at, slots, kv_apart, more, final = plan
    packed_at, places_of = [at for at, _ in attend_at], [place for _, place in attend_at]
    array_count = 1 + max(at[0] for at in packed_at if at)
    span = exp_count * tok
    packed_refs, refs = refs[:array_count], refs[array_count:]
    packed = [packed_refs[at[0]].at[pl.ds(at[1], span)] if at else None for at in packed_at]
    kv_refs = list(packed)
    if kv_apart:
        kv_refs[packed_at.index(None)], refs = refs[0], refs[1:]
    if more:
        more_ref, refs = refs[0], refs[1:]
    x_count = exp_count // 2
    if final:
        weight_ref, rest = refs[0], refs[2:]
        keep_refs, give_ref = rest[:x_count], rest[x_count]
    key_scr, value_scr, place_scr, att_ref = refs[-4:] if final else (*refs[1:], refs[0])
    if more:
        att_ref[...] = more_ref[...]
    positions = ctx_count * span
    my_ctx, my_exp = ctx_ref[0], exp_ref[0]
    my_x, my_core = lax.shift_right_logical(my_exp, 1), lax.bitwise_and(my_exp, 1)
    lane = lax.broadcasted_iota(jnp.int32, (8, positions), 1)
    places = lane % span
    for offset, ref in enumerate(kv_refs):
        key_scr[pl.ds(offset * span, span), :] = ref[:, 0:HEAD_SIZE]
        value_scr[pl.ds(offset * span, span), 0:HEAD_SIZE] = ref[:, HEAD_SIZE : 2 * HEAD_SIZE]
        base = order_ref[lax.bitwise_xor(my_ctx, by_core(my_core, places_of[offset], 0))] * span
        places = places + jnp.where(lane // span == offset, base, 0)
    place_scr[...] = places
    scale = math.log2(math.e) / math.sqrt(HEAD_SIZE)
    value_scr[:, HEAD_SIZE:] = jnp.ones((positions, HEAD_SIZE), jnp.bfloat16)
    for offset in slots:
        ref = packed[offset]
        source = lax.bitwise_xor(my_ctx, by_core(my_core, places_of[offset], 0))
        queries = jnp.concatenate(
            [ref[:, (h + 2) * HEAD_SIZE : (h + 3) * HEAD_SIZE] for h in range(heads)], axis=0
        )
        scores = lax.dot_general(
            queries, key_scr[...], (((1,), (1,)), ((), ())), preferred_element_type=jnp.float32
        )
        own_place = order_ref[source] * span + lax.broadcasted_iota(jnp.int32, (span, positions), 0)
        bias = jnp.where(place_scr[0:1, :] <= own_place, 0.0, -1e30)
        scores = scores.reshape(heads, span, positions) * scale + bias[None]
        exps = jnp.exp2(scores - jnp.max(scores, axis=-1, keepdims=True))
        mixed = jnp.dot(
            exps.astype(jnp.bfloat16).reshape(heads * span, positions),
            value_scr[...],
            preferred_element_type=jnp.float32,
        )
        mixed = mixed[:, :HEAD_SIZE] * (1.0 / mixed[:, HEAD_SIZE : HEAD_SIZE + 1])
        mixed = mixed.astype(jnp.bfloat16).reshape(heads, span, HEAD_SIZE)
        for owner in range(exp_count):
            x_off = lax.bitwise_xor(my_x, owner // 2)
            row = pl.multiple_of(((x_off * ctx_count + source) * 2 + owner % 2) * tok, tok)
            for head in range(heads):
                att_ref[pl.ds(row, tok), pl.ds(head * HEAD_SIZE, HEAD_SIZE)] = mixed[
                    head, owner * tok : (owner + 1) * tok, :
                ]

    if not final:
        return
    cols = weight_ref.shape[1] // 2
    per_x = 2 * ctx_count * tok
    for x_off in range(x_count):
        rows = pl.ds(x_off * per_x, per_x)
        for which in (1, 0):
            side = lax.bitwise_xor(my_core, which)
            weight = weight_ref[:, pl.ds(pl.multiple_of(side * cols, cols), cols)]
            part = jnp.dot(att_ref[rows, :], weight, preferred_element_type=jnp.float32)
            out_ref = give_ref if which else keep_refs[x_off]
            out_ref[pl.ds(x_off * per_x if which else 0, per_x), :] = part.astype(out_ref.dtype)


def finish_kernel(plan, ctx_ref, exp_ref, keep_in, give_in, *refs):
    ctx_count, x_count, tok, piece_places, places_of = plan
    piece_refs, (keep_ref, give_ref, own_route_ref) = refs[:-3], refs[-3:]
    my_ctx, my_exp = ctx_ref[0], exp_ref[0]
    my_x, my_core = lax.shift_right_logical(my_exp, 1), lax.bitwise_and(my_exp, 1)
    cols = keep_ref.shape[1]
    route_base = give_in.shape[0]
    keep_ref[...] = keep_in[...]
    give_ref[0:route_base, :] = give_in[...]
    blocks = [jnp.zeros((tok, HEAD_SIZE), jnp.float32)] * x_count
    lane = lax.broadcasted_iota(jnp.int32, (tok, HEAD_SIZE), 1)
    for (array, place), place_of in zip(piece_places, places_of):
        source = lax.bitwise_xor(my_ctx, by_core(my_core, place_of, 0))
        at = pl.ds(pl.multiple_of((source * 2 + my_core) * tok, tok), tok)
        for which, ref in enumerate((keep_ref, give_ref)):
            side = lax.bitwise_xor(my_core, which)
            piece = piece_refs[array][place, :, pl.ds(pl.multiple_of(side * cols, cols), cols)]
            value = ref[at, :].astype(jnp.float32) + piece.astype(jnp.float32)
            ref[at, :] = value.astype(ref.dtype)
        block = piece_refs[array][place, :, 2 * cols :].astype(jnp.float32)
        for x_off in range(x_count):
            for part in range(2):
                wanted = lax.bitwise_xor(my_x, x_off) + part * x_count
                column = jnp.sum(jnp.where(lane == wanted, block, 0.0), axis=1, keepdims=True)
                blocks[x_off] = jnp.where(lane == source + part * ctx_count, column, blocks[x_off])
    for x_off, block in enumerate(blocks):
        for ref, base in ((give_ref, route_base), (own_route_ref, 0)):
            at = pl.ds(base + x_off * tok, tok)
            ref[at, 0:HEAD_SIZE] = block.astype(jnp.bfloat16)
            if cols > HEAD_SIZE:
                ref[at, HEAD_SIZE:] = jnp.zeros((tok, cols - HEAD_SIZE), jnp.bfloat16)


def fill_rows(plan, ctx_ref, exp_ref, gain_ref, chunk_refs, places, rows_scr, square_ref, groups):
    ctx_count, x_count, tok, bit = plan
    my_ctx = ctx_ref[0]
    my_core = lax.bitwise_and(exp_ref[0], 1)
    mine = side_of(my_ctx, bit)
    cols = chunk_refs[0].shape[1]
    rows = ctx_count * tok
    for (array, first_row), place_of in places:
        ref = chunk_refs[array]
        source = lax.bitwise_xor(my_ctx, by_core(my_core, place_of, 0))
        x_off = by_core(my_core, place_of, 1)
        gain_at = pl.multiple_of((source * 2 + my_core) * cols, cols)
        gain = gain_ref[:, pl.ds(gain_at, cols)]
        col = pl.multiple_of(without(source, bit) * cols, cols)
        for place, group in enumerate(groups):
            for start, low, length in runs(ctx_count, bit, mine if group == 1 else 1 - mine, 2 * tok):
                chunk = ref[pl.ds(first_row + start, length), :].astype(jnp.float32)
                row = (place * x_count + x_off) * rows + low
                at = pl.ds(pl.multiple_of(row, 2 * tok), length)
                rows_scr[at, pl.ds(col, cols)] = (chunk * gain).astype(jnp.bfloat16)
                square_ref[at, :] = square_ref[at, :] + jnp.sum(chunk * chunk, axis=-1, keepdims=True)


def product(plan, side, rows_scr, weight_ref, cols):
    ctx_count, _, _, bit = plan
    total = None
    for start, low, length in runs(ctx_count, bit, side, cols):
        part = jnp.dot(
            rows_scr[:, low : low + length],
            weight_ref[pl.ds(start, length), :],
            preferred_element_type=jnp.float32,
        )
        total = part if total is None else total + part
    return total


def experts_in_first(plan, offsets, ctx_ref, exp_ref, *refs):
    chunk_refs, (gain_ref, own_ref, other_ref, _, act_ref, square_ref, rows_scr) = refs[:-7], refs[-7:]
    square_ref[...] = jnp.zeros(square_ref.shape, jnp.float32)
    fill_rows(plan, ctx_ref, exp_ref, gain_ref, chunk_refs, offsets, rows_scr, square_ref, (0, 1))
    width, side = own_ref.shape[1], side_of(ctx_ref[0], plan[3])
    for place, ref in enumerate((own_ref, other_ref)):
        act_ref[:, place * width : (place + 1) * width] = product(
            plan, side, rows_scr, ref, chunk_refs[0].shape[1]
        )


def experts_in_second(plan, offsets, group, ctx_ref, exp_ref, *refs):
    chunk_refs, rest = refs[:-9], refs[-9:]
    gain_ref, own_ref, other_ref, first_ref, square_ref, _, act_ref, rows_scr, sum_scr = rest
    count, width = rows_scr.shape[0], own_ref.shape[1]
    sum_scr[...] = square_ref[group * count : (group + 1) * count, :]
    fill_rows(plan, ctx_ref, exp_ref, gain_ref, chunk_refs, offsets, rows_scr, sum_scr, (group,))
    lane = lax.broadcasted_iota(jnp.int32, (1, HEAD_SIZE), 1)
    square = sum_scr[...]
    high = square.astype(jnp.bfloat16).astype(jnp.float32)
    act_ref[:, 2 * width :] = jnp.where(lane == 0, high, square - high).astype(jnp.bfloat16)
    side = 1 - side_of(ctx_ref[0], plan[3])
    for place, ref in enumerate((own_ref, other_ref)):
        cols = slice(place * width, (place + 1) * width)
        act = first_ref[group * count : (group + 1) * count, cols] + product(
            plan, side, rows_scr, ref, chunk_refs[0].shape[1]
        )
        act_ref[:, cols] = act.astype(jnp.bfloat16)


def experts_out_kernel(plan, group, places, state_at, route_at, model_width, ctx_ref, exp_ref, act_ref, came_ref, *refs):
    ctx_count, exp_count, tok, bit = plan
    x_count, half = exp_count // 2, ctx_count // 2
    route_refs, refs = refs[: x_count + 1], refs[x_count + 1 :]
    (own_ref, other_ref, _), rest = refs[:3], refs[3:]
    state_count = 1 + max((array for pair in state_at for array, _ in pair), default=-1)
    state_refs, rest = rest[:state_count], rest[state_count:]
    out_refs, hidden_scr = rest[:-1], rest[-1]
    my_ctx = ctx_ref[0]
    my_core = lax.bitwise_and(exp_ref[0], 1)
    mine = side_of(my_ctx, bit)
    side = mine if group == 1 else 1 - mine
    width = (act_ref.shape[1] - HEAD_SIZE) // 2
    hidden = width // 2
    lane = lax.broadcasted_iota(jnp.int32, (tok, HEAD_SIZE), 1)
    blocks = []
    for array, row in route_at:
        blocks.append(route_refs[array][row : row + tok, 0:HEAD_SIZE].astype(jnp.float32))
    columns = []
    for x_off in range(x_count):
        for low in range(half):
            for core in range(2):
                same, swapped = blocks[2 * x_off + core], blocks[2 * x_off + 1 - core]
                block = jnp.where(my_core == 0, same, swapped)
                number = (low >> bit << bit + 1) + (low & ((1 << bit) - 1)) + side * (1 << bit)
                picked = jnp.where(lane % ctx_count == number, block, 0.0)
                columns.append(jnp.sum(picked, axis=1, keepdims=True))
    route = jnp.concatenate(columns, axis=0)
    squares = act_ref[:, 2 * width :].astype(jnp.float32) + came_ref[:, 2 * width :].astype(jnp.float32)
    norm = lax.rsqrt((squares[:, 0:1] + squares[:, 1:2]) / model_width + 1e-06)
    scaled_route = norm * route
    for part in range(2):
        acts = act_ref[:, part * width : (part + 1) * width].astype(jnp.float32) + came_ref[
            :, (1 - part) * width : (2 - part) * width
        ].astype(jnp.float32)
        gate = acts[:, :hidden] * norm
        value = gate / (1.0 + jnp.exp(-gate)) * (acts[:, hidden:] * scaled_route)
        hidden_scr[:, part * hidden : (part + 1) * hidden] = value.astype(jnp.bfloat16)
    picked = []
    for place in places:
        x_off = by_core(my_core, place, 1)
        low = without(lax.bitwise_xor(my_ctx, by_core(my_core, place, 0)), bit)
        row = pl.multiple_of((x_off * half + low) * (2 * tok), 2 * tok)
        picked.append(hidden_scr[pl.ds(row, 2 * tok), :])
    picked = jnp.concatenate(picked, axis=0)
    out_cols = own_ref.shape[1]
    step = min(512, out_cols)
    for col in range(0, out_cols, step):
        at = pl.ds(col, step)
        out = jnp.dot(picked[:, :hidden], own_ref[:, at], preferred_element_type=jnp.float32)
        out = out + jnp.dot(picked[:, hidden:], other_ref[:, at], preferred_element_type=jnp.float32)
        for place, ref in enumerate(out_refs):
            ref[:, at] = out[place * 2 * tok : (place + 1) * 2 * tok, :].astype(ref.dtype)
    for place, ref in zip(places, out_refs):
        if place[0] == (0, 0):
            for c_off, pair in enumerate(state_at):
                states = []
                for array, first_row in pair:
                    own_row = pl.multiple_of(first_row + my_ctx * (2 * tok), 2 * tok)
                    states.append(state_refs[array][pl.ds(own_row, 2 * tok), :].astype(jnp.float32))
                state = states[0] if pair[0] == pair[1] else jnp.where(my_core == 0, *states)
                cols = state.shape[1]
                at = pl.ds(pl.multiple_of(lax.bitwise_xor(my_ctx, c_off) * cols, cols), cols)
                ref[:, at] = ref[:, at] + state


def shards(
    residual,
    encoded_query_rows,
    quantized_key_rows,
    quantized_value_rows,
    key_block_exponent,
    value_block_exponent,
    block_order,
    out_weight,
    norm_gain,
    expert_ids,
    route_weight,
    gate_weight,
    gate_scale,
    up_weight,
    up_scale,
    down_weight,
    down_scale,
):
    f32, bf16 = jnp.float32, jnp.bfloat16
    vmem = pl.BlockSpec(memory_space=pltpu.VMEM)
    smem = pl.BlockSpec(memory_space=pltpu.SMEM)
    anywhere = pl.BlockSpec(memory_space=pl.ANY)
    span, query_width = encoded_query_rows.shape
    heads = query_width // HEAD_SIZE
    group = QUERY_HEADS // KEY_VALUE_HEADS
    ctx_count = lax.axis_size("ctx")
    exp_count = lax.axis_size("exp")
    x_count = exp_count // 2
    experts = ctx_count * x_count
    tok, model_width = residual.shape
    half_width = model_width // 2
    cols = half_width // ctx_count
    my_ctx = lax.axis_index("ctx").astype(jnp.int32).reshape(1)
    my_exp = lax.axis_index("exp").astype(jnp.int32).reshape(1)
    route, places = gather_route(ctx_count, x_count)

    hbm = pl.BlockSpec(memory_space=pltpu.HBM)
    piece_shape = jax.ShapeDtypeStruct((ctx_count // 2, tok, 2 * cols + HEAD_SIZE), bf16)
    row_route, row_places = gather_route(ctx_count, x_count, rows_only=True)
    names = sorted(row_places)
    piece_names = [[key for key in names if bool(key[0] & 2) == sent] for sent in (False, True)]
    piece_places = tuple(tuple(row_places[key] for key in keys) for keys in piece_names)
    packed, near, far = pl.pallas_call(
        functools.partial(pack_kernel, (heads, group, x_count, piece_places)),
        in_specs=[smem] * 2 + [hbm] * 8,
        out_specs=[vmem] * 3,
        out_shape=[
            jax.ShapeDtypeStruct((span, query_width + 2 * HEAD_SIZE), bf16),
            piece_shape,
            piece_shape,
        ],
        scratch_shapes=[
            pltpu.VMEM(key_block_exponent.shape, jnp.int32),
            pltpu.VMEM(key_block_exponent.shape, jnp.int32),
            pltpu.VMEM((span, HEAD_SIZE), bf16),
            pltpu.VMEM((span, HEAD_SIZE), bf16),
            pltpu.VMEM((TOP, tok), jnp.int32),
            pltpu.VMEM((TOP, tok), f32),
            pltpu.SemaphoreType.DMA((7 + ctx_count,)),
        ],
        compiler_params=pltpu.CompilerParams(vmem_limit_bytes=8 * MIB),
        name="pack",
    )(
        my_ctx,
        my_exp,
        *in_hbm(
            key_block_exponent,
            value_block_exponent,
            encoded_query_rows,
            quantized_key_rows,
            quantized_value_rows,
            jnp.transpose(expert_ids),
            jnp.transpose(route_weight),
            residual,
        ),
    )
    piece_arrays = [near]
    piece_at = {(0, key[0]): (0, place) for place, key in enumerate(piece_names[0])}
    piece_bits = [1, 0, *range(bits_of(ctx_count) - 1, 1, -1)]
    sending, weights = far, {}
    early, last_kv = ctx_count == 8, []

    def beside(number, came, arrays, at):
        nonlocal sending
        bit = 1 << piece_bits[number]
        moves = {1: ((2, 0), (1, 0)), 0: ((1, 0), (2, 0))}.get(piece_bits[number], ((bit, 0),) * 2)
        if number == 0:
            keys = [(0, key[0]) for key in piece_names[1]]
        else:
            keys = sorted(key for key in piece_at if key[1] & bit)
            sending = jnp.stack([piece_arrays[array][place] for array, place in map(piece_at.pop, keys)])
        pieces = follow(sending, moves)
        if number == 0:
            own, give = deq_in(my_exp, gate_weight, gate_scale, up_weight, up_scale, ctx_count, packed)
            *came, pieces, weights["in_own"], weights["in_give"] = together(*came, pieces, own, give)
        elif number == 1:
            other = from_offset(weights["in_give"], 1)
            own, give = deq_down(my_exp, down_weight, down_scale, ctx_count, piece_arrays[-1])
            if early:
                array, row = at[4, 0]
                last_kv.append(follow(arrays[array][row : row + span, : 2 * HEAD_SIZE], ((3, 0),) * 2))
            held = together(*came, pieces, other, own, give, *last_kv)
            *came, pieces, other, own, give = held[: len(held) - len(last_kv)]
            last_kv[:] = held[len(held) - len(last_kv) :]
            weights.update(in_other=other, down_own=own, down_give=give)
        elif number < len(piece_bits) - 1:
            *came, pieces = together(*came, pieces)
        for place, (source, target) in enumerate(keys):
            piece_at[source ^ bit, target ^ bit] = (len(piece_arrays), place)
        piece_arrays.append(pieces)
        return came

    packed, packed_at = spread(packed, stages_of(row_route), beside)
    attend_at = tuple((packed_at[key], row_places[key]) for key in names)
    attend_pieces = tuple(piece_at[key[0], 0] for key in names)
    in_own, in_other, down_own = weights["in_own"], weights["in_other"], weights["down_own"]
    down_other = from_offset(weights["down_give"], 1)

    positions = ctx_count * span
    per_x = 2 * ctx_count * tok
    def attend(arrays, at, slots, kv, more, final):
        scratch = [
            pltpu.VMEM((positions, HEAD_SIZE), bf16),
            pltpu.VMEM((positions, 2 * HEAD_SIZE), bf16),
            pltpu.VMEM((8, positions), jnp.int32),
        ]
        rows_shape = (positions, query_width)
        out_shape = [jax.ShapeDtypeStruct(rows_shape, bf16)]
        if final:
            out_shape = [jax.ShapeDtypeStruct((per_x, cols), f32)] * x_count
            out_shape += [jax.ShapeDtypeStruct((x_count * per_x, cols), bf16)]
            scratch.append(pltpu.VMEM(rows_shape, bf16))
        operands = [*arrays, *kv, *more, *([out_weight] if final else [])]
        return pl.pallas_call(
            functools.partial(
                attend_kernel,
                (ctx_count, exp_count, tok, heads, at, slots, bool(kv), bool(more), final),
            ),
            in_specs=[smem] * 3 + [vmem] * len(operands) + [anywhere] * final,
            out_specs=[vmem] * len(out_shape),
            out_shape=out_shape,
            scratch_shapes=scratch,
            compiler_params=pltpu.CompilerParams(vmem_limit_bytes=3 * ctx_count * MIB),
            cost_estimate=pl.CostEstimate(
                flops=4 * positions * len(slots) * span * query_width
                + 4 * positions * query_width * cols * final,
                bytes_accessed=4 * MIB,
                transcendentals=heads * positions * len(slots) * span,
            ),
            name="attend",
        )(my_ctx, my_exp, block_order, *operands, *([down_other] if final else []))

    more, slots = [], tuple(range(ctx_count))
    if early:
        late = max(packed_at[key][0] for key in names)
        early_at = tuple((None if at[0] == late else at, place) for at, place in attend_at)
        slots = tuple(i for i, (at, _) in enumerate(early_at) if at is None)
        rest = tuple(i for i, (at, _) in enumerate(early_at) if at is not None)
        more = attend(packed[:late], early_at, rest, last_kv, [], False)
    *keeps, give = attend(packed, attend_at, slots, [], more, True)
    keeps[0], give, own_route = pl.pallas_call(
        functools.partial(
            finish_kernel,
            (ctx_count, x_count, tok, attend_pieces, tuple(place for _, place in attend_at)),
        ),
        in_specs=[smem] * 2 + [vmem] * (2 + len(piece_arrays)),
        out_specs=[vmem] * 3,
        out_shape=[
            jax.ShapeDtypeStruct((per_x, cols), f32),
            jax.ShapeDtypeStruct((x_count * (per_x + tok), cols), bf16),
            jax.ShapeDtypeStruct((x_count * tok, cols), bf16),
        ],
        compiler_params=pltpu.CompilerParams(vmem_limit_bytes=8 * MIB),
        name="finish",
    )(my_ctx, my_exp, keeps[0], give, *piece_arrays)

    given = from_offset(give, 1)
    routes, route_at, state = [own_route, given], [(0, 0), (1, x_count * per_x)], keeps[0]
    state = state + given[:per_x].astype(f32)
    for x_off in range(1, x_count):
        part = keeps[x_off] + given[x_off * per_x : (x_off + 1) * per_x].astype(f32)
        row = x_count * per_x + x_off * tok
        own = own_route[x_off * tok : (x_off + 1) * tok]
        sent = jnp.concatenate([part.astype(bf16), own, given[row : row + tok]], axis=0)
        came = from_offset(sent, 2 * x_off)
        state = state + came[:per_x].astype(f32)
        route_at += [(len(routes), per_x), (len(routes), per_x + tok)]
        routes.append(came)
    state = state.astype(bf16)

    stages = stages_of(route)
    chunks, chunk_at = spread(state, stages)
    gain = norm_gain.reshape(1, model_width)
    rows = x_count * per_x
    in_width = in_own.shape[1]
    bit = 1 if (ctx_count, x_count) == (8, 2) else bits_of(ctx_count) - 1
    near = tuple(sorted(key for key in places if not side_of(key[0], bit)))
    far = tuple(sorted(key for key in places if side_of(key[0], bit)))

    def picked(keys):
        arrays = sorted({chunk_at[key][0] for key in keys})
        at = tuple(((arrays.index(chunk_at[key][0]), chunk_at[key][1]), places[key]) for key in keys)
        return [chunks[array] for array in arrays], at

    near_chunks, near_places = picked(near)
    far_chunks, far_places = picked(far)
    first_act, first_square = pl.pallas_call(
        functools.partial(experts_in_first, (ctx_count, x_count, tok, bit), near_places),
        in_specs=[smem] * 2 + [vmem] * (len(near_chunks) + 3) + [anywhere],
        out_specs=[vmem] * 2,
        out_shape=[
            jax.ShapeDtypeStruct((rows, 2 * in_width), f32),
            jax.ShapeDtypeStruct((rows, 1), f32),
        ],
        scratch_shapes=[pltpu.VMEM((rows, half_width // 2), bf16)],
        compiler_params=pltpu.CompilerParams(vmem_limit_bytes=2 * ctx_count * MIB),
        cost_estimate=pl.CostEstimate(
            flops=2 * rows * half_width * in_width, bytes_accessed=8 * MIB, transcendentals=0
        ),
        name="experts_in_first",
    )(my_ctx, my_exp, *near_chunks, gain, in_own, in_other, down_other)
    acts = []
    for part in range(2):
        acts.append(
            pl.pallas_call(
                functools.partial(experts_in_second, (ctx_count, x_count, tok, bit), far_places, part),
                in_specs=[smem] * 2 + [vmem] * (len(far_chunks) + 5) + [anywhere],
                out_specs=vmem,
                out_shape=jax.ShapeDtypeStruct((rows // 2, 2 * in_width + HEAD_SIZE), bf16),
                scratch_shapes=[
                    pltpu.VMEM((rows // 2, half_width // 2), bf16),
                    pltpu.VMEM((rows // 2, 1), f32),
                ],
                compiler_params=pltpu.CompilerParams(vmem_limit_bytes=2 * ctx_count * MIB),
                cost_estimate=pl.CostEstimate(
                    flops=rows * half_width * in_width, bytes_accessed=8 * MIB, transcendentals=0
                ),
                name="experts_in_second",
            )(
                my_ctx,
                my_exp,
                *far_chunks,
                gain,
                in_own,
                in_other,
                first_act,
                first_square,
                acts[0] if part else first_square,
            )
        )
    leaves = set(places) - {source for _, source, _, _ in route}
    sums = {}
    for part in range(2):
        slots = near if part == 1 else far
        state_keys = [
            next(key for key in places if places[key][core] == (offset, 0))
            for offset in (range(ctx_count) if part == 1 else ())
            for core in range(2)
        ]
        states, state_at = picked(state_keys)
        state_at = tuple((state_at[i][0], state_at[i + 1][0]) for i in range(0, len(state_at), 2))
        outs = pl.pallas_call(
            functools.partial(
                experts_out_kernel,
                (ctx_count, exp_count, tok, bit),
                part,
                tuple(places[key] for key in slots),
                state_at,
                tuple(route_at),
                model_width,
            ),
            in_specs=[smem] * 2 + [vmem] * (5 + x_count) + [anywhere] + [vmem] * len(states),
            out_specs=[vmem] * len(slots),
            out_shape=[
                jax.ShapeDtypeStruct((2 * tok, half_width), bf16 if slot in leaves else f32)
                for slot in slots
            ],
            scratch_shapes=[pltpu.VMEM((rows // 2, in_width), bf16)],
            compiler_params=pltpu.CompilerParams(vmem_limit_bytes=2 * ctx_count * MIB),
            cost_estimate=pl.CostEstimate(
                flops=rows * half_width * in_width,
                bytes_accessed=8 * MIB,
                transcendentals=rows * in_width // 2,
            ),
            name="experts_out",
        )(
            my_ctx,
            my_exp,
            acts[part],
            from_offset(acts[part], 1),
            *routes,
            down_own,
            down_other,
            sums[slots_done[0]] if part else acts[1],
            *states,
        )
        slots_done = slots
        sums.update(zip(slots, outs))

    for number, sends in enumerate(reversed(stages)):
        came = []
        for moves, _, targets in sends:
            sent = [sums[key].astype(bf16) for key in targets]
            came.append(follow(sent[0] if len(sent) == 1 else jnp.concatenate(sent, axis=0), moves))
        if number < len(stages) - 1:
            waiting = list(near) if number == 0 else []
            values = together(*came, *[sums[key] for key in waiting])
            came = values[: len(came)]
            sums.update(zip(waiting, values[len(came) :]))
        for (_, sources, _), array in zip(sends, came):
            for place, key in enumerate(sources):
                part = array[place * 2 * tok : (place + 1) * 2 * tok]
                sums[key] = sums[key] + part.astype(f32)
    total = sums[0, 0]
    core = lax.bitwise_and(my_exp[0], 1)
    mine = jnp.where(core == 0, total[:tok], total[tok:]).astype(bf16)
    came = from_offset(jnp.where(core == 0, total[tok:], total[:tok]).astype(bf16), 1)
    mine = mine.reshape(tok, ctx_count, 1, cols)
    came = came.reshape(tok, ctx_count, 1, cols)
    result = jnp.where(core == 0, jnp.concatenate([mine, came], axis=2), jnp.concatenate([came, mine], axis=2))
    return result.reshape(tok, model_width)


def solution(mesh):
    return jax.shard_map(
        shards,
        mesh=mesh,
        in_specs=(
            P(("dp", "ctx", "exp"), None),
            P(("dp", "ctx"), "exp"),
            P(("dp", "ctx"), None),
            P(("dp", "ctx"), None),
            P(("dp", "ctx"), None),
            P(("dp", "ctx"), None),
            P(),
            P("exp", "ctx"),
            P(),
            P(("dp", "ctx", "exp"), None),
            P(("dp", "ctx", "exp"), None),
            P(("ctx", "exp"), None, None),
            P(("ctx", "exp"), None, None),
            P(("ctx", "exp"), None, None),
            P(("ctx", "exp"), None, None),
            P(("ctx", "exp"), None, None),
            P(("ctx", "exp"), None, None),
        ),
        out_specs=P(("dp", "ctx", "exp"), None),
        check_vma=False,
    )
```

```python
import functools
import math

import jax
import jax.numpy as jnp
from jax import lax
from jax.experimental import pallas as pl
from jax.experimental.pallas import tpu as pltpu
from jax.sharding import PartitionSpec as P

QUERY_HEADS = 32
KEY_VALUE_HEADS = 4
HEAD_SIZE = 128
TOP = 8
SCALE_POSITIONS = 64
WB = 128
MIB = 1 << 20


def bits_of(count):
    return count.bit_length() - 1


def from_offset(array, offset):
    return lax.ppermute(array, "exp", [(i, i ^ offset) for i in range(lax.axis_size("exp"))])


def from_ctx(array, offset):
    return lax.ppermute(array, "ctx", [(i, i ^ offset) for i in range(lax.axis_size("ctx"))])


def moved(offset, move):
    return (offset[0] ^ move[0], offset[1] ^ move[1])


def gather_route(ctx_count, x_count, rows_only=False):
    transfers, arrival, places = [], {(0, 0): 0}, {(0, 0): ((0, 0), (0, 0))}

    def go(source, moves, delay=0):
        reached = tuple(moved(place, (c, e >> 1)) for place, (c, e) in zip(places[source], moves))
        target = reached[0]
        arrival[target], places[target] = arrival[source] + 1 + delay, reached
        transfers.append((arrival[target], source, target, moves))
        return target

    bits = bits_of(ctx_count)
    y_move = (1, 0)
    if (ctx_count, x_count) == (8, 2) and not rows_only:
        z_far, z_near = ((4, 0),) * 2, ((2, 0),) * 2
        first, second, both = ((0, 2), y_move), (y_move, (0, 2)), ((1, 2),) * 2
        at = {"0": (0, 0)}
        for stage, moves, hops in (
            (1, z_far, "0>4"),
            (1, z_near, "0>2"),
            (1, first, "0>0a"),
            (1, second, "0>0b"),
            (1, both, "0>0ab"),
            (2, z_far, "0ab>4ab"),
            (2, z_near, "4>6"),
            (2, first, "2>2a 4>4a"),
            (2, second, "2>2b 4>4b"),
            (3, z_near, "4ab>6ab"),
            (3, first, "6>6a"),
            (3, second, "6>6b 2a>2ab"),
        ):
            for hop in hops.split():
                source, target = hop.split(">")
                at[target] = go(at[source], moves, stage - 1 - arrival[at[source]])
        return sorted(transfers, key=lambda transfer: transfer[0]), places
    if rows_only:
        shared, steps = range(bits - 1, 1, -1), [(2, 0), y_move]
    else:
        shared, steps = range(bits - 1, 0, -1), [(0, 2 << bit) for bit in range(bits_of(x_count))] + [y_move]
    pairs = list(zip(steps, reversed(steps)))
    for bit in shared:
        for source in list(arrival):
            go(source, ((1 << bit, 0),) * 2)
    for first in sorted(arrival):
        held = [first]
        for moves in pairs:
            held = held + [go(source, moves) for source in held]
    return sorted(transfers, key=lambda transfer: transfer[0]), places


def follow(array, moves):
    exp_count = lax.axis_size("exp")
    pairs = []
    for c in range(lax.axis_size("ctx")):
        for e in range(exp_count):
            far = moved((c, e), moves[e % 2])
            pairs.append((far[0] * exp_count + far[1], c * exp_count + e))
    return lax.ppermute(array, ("ctx", "exp"), pairs)


def side_of(index, bit):
    return (index >> bit) & 1


def without(index, bit):
    return (index & ((1 << bit) - 1)) | ((index >> bit + 1) << bit)


def runs(ctx_count, bit, side, each):
    length = each << bit
    return [
        (pl.multiple_of((2 * k + side) * length, length), k * length, length) for k in range(ctx_count >> bit + 1)
    ]


def by_core(core, place, part):
    first, second = place[0][part], place[1][part]
    return first if first == second else jnp.where(core == 0, first, second)


def stages_of(route):
    stages, arrays = [], [((0, 0),)]
    top = max(moves[0][0] for _, _, _, moves in route)
    for stage in sorted({transfer[0] for transfer in route}):
        sends = []
        for moves in sorted({t[3] for t in route if t[0] == stage}):
            left = {source: target for number, source, target, way in route if (number, way) == (stage, moves)}
            groups = [group for group in arrays if len(group) > 1 and all(key in left for key in group)]
            rest = tuple(sorted(key for key in left if not any(key in group for group in groups)))
            for group in groups + [rest] * bool(rest):
                sends.append((moves, group, tuple(left[key] for key in group)))
        def order(send):
            moves, group, _ = send
            shared, far = moves[0] == moves[1], moves[0][0] == top > 2
            rank = (0 if shared else 1) if len(group) == 1 else (1 if shared else 2 * moves[0][0])
            return -len(group) * (2 if far else 1), -1 if far else rank

        sends.sort(key=order)
        arrays = arrays + [send[2] for send in sends]
        stages.append(sends)
    return stages


def spread(block, stages, beside=None):
    arrays, at, joined = [block], {(0, 0): (0, 0)}, {}
    rows = block.shape[0]
    for number, sends in enumerate(stages):
        came = []
        for moves, group, _ in sends:
            first, row = at[group[0]]
            whole = row == 0 and arrays[first].shape[0] == len(group) * rows
            if whole and all(at[key] == (first, place * rows) for place, key in enumerate(group)):
                joined[group] = arrays[first]
            elif group not in joined:
                parts = [arrays[at[key][0]][at[key][1] : at[key][1] + rows] for key in group]
                joined[group] = jnp.concatenate(parts, axis=0)
            came.append(follow(joined[group], moves))
        came = beside(number, came, arrays, at) if beside else (together(*came) if number < len(stages) - 1 else came)
        for (_, _, targets), array in zip(sends, came):
            at.update({key: (len(arrays), place * rows) for place, key in enumerate(targets)})
            arrays.append(array)
    return arrays, at


def together(*values):
    return lax.optimization_barrier(values)


def block_factor(exponent, width):
    factor = jnp.where(exponent < 0, 0.5, jnp.where(exponent > 0, 2.0, 1.0))
    return jnp.full((1, width), factor, jnp.float32).astype(jnp.bfloat16)


def in_hbm(*arrays):
    return [pltpu.with_memory_space_constraint(array, pltpu.HBM) for array in arrays]


def copy_all(sems, pairs):
    copies = [pltpu.make_async_copy(src, dst, sems.at[i]) for i, (src, dst) in enumerate(pairs)]
    for copy in copies:
        copy.start()
    return copies


def pack_kernel(plan, ctx_ref, exp_ref, key_scale_hbm, value_scale_hbm, query_hbm, key_hbm, value_hbm, ids_hbm,
                route_hbm, residual_hbm, packed_ref, near_ref, far_ref, key_scale_ref, value_scale_ref,
                key_ref, value_ref, ids_ref, route_ref, sems):
    heads, group, x_count, piece_places = plan
    span, width = query_hbm.shape
    half, tok, cols = near_ref.shape
    cols = cols - HEAD_SIZE
    my_ctx, my_exp = ctx_ref[0], exp_ref[0]
    kv_head = my_exp * heads // group
    at = pl.ds(pl.multiple_of(kv_head * HEAD_SIZE, HEAD_SIZE), HEAD_SIZE)
    pairs = [
        (key_scale_hbm, key_scale_ref),
        (value_scale_hbm, value_scale_ref),
        (key_hbm.at[:, at], key_ref),
        (value_hbm.at[:, at], value_ref),
        (ids_hbm, ids_ref),
        (route_hbm, route_ref),
        (query_hbm, packed_ref.at[:, 2 * HEAD_SIZE : 2 * HEAD_SIZE + width]),
    ]
    core = lax.bitwise_and(my_exp, 1)
    for ref, places in zip((near_ref, far_ref), piece_places):
        for number, place in enumerate(places):
            col = pl.multiple_of(lax.bitwise_xor(my_ctx, by_core(core, place, 0)) * cols, cols)
            pairs.append((residual_hbm.at[:, pl.ds(col, cols)], ref.at[number, :, 0:cols]))
    copies = copy_all(sems, pairs)
    for copy in copies[:6]:
        copy.wait()
    lane = lax.broadcasted_iota(jnp.int32, key_scale_ref.shape, 1)
    blocks = key_scale_ref.shape[0]
    for place, (ref, scale_ref) in enumerate(((key_ref, key_scale_ref), (value_ref, value_scale_ref))):
        exponent = scale_ref[...]
        factor = jnp.where(
            exponent < -1, 0.25, jnp.where(exponent < 0, 0.5, jnp.where(exponent < 1, 1.0, 2.0))
        )
        factor = jnp.sum(jnp.where(lane == kv_head, factor, 0.0), axis=1, keepdims=True)
        for block in range(blocks):
            rows = pl.ds(block * (span // blocks), span // blocks)
            scaled = ref[rows, :].astype(jnp.float32) * factor[block : block + 1, :]
            packed_ref[rows, pl.ds(place * HEAD_SIZE, HEAD_SIZE)] = scaled.astype(jnp.bfloat16)
    number = lax.broadcasted_iota(jnp.int32, (128, tok), 0)
    dense = jnp.zeros((128, tok), jnp.float32)
    for k in range(TOP):
        dense = dense + jnp.where(ids_ref[k : k + 1, :] == number, route_ref[k : k + 1, :], 0.0)
    dense = jnp.concatenate([dense, jnp.zeros((128, 128 - tok), jnp.float32)], axis=1)
    dense = jnp.transpose(dense)[:tok, :]
    lane = lax.broadcasted_iota(jnp.int32, (tok, HEAD_SIZE), 1)
    for ref, places in zip((near_ref, far_ref), piece_places):
        for number, place in enumerate(places):
            expert = lax.bitwise_xor(my_ctx, by_core(core, place, 0)) * x_count
            block = jnp.zeros((tok, HEAD_SIZE), jnp.float32)
            for x in range(x_count):
                column = jnp.sum(jnp.where(lane == expert + x, dense, 0.0), axis=1, keepdims=True)
                high = column.astype(jnp.bfloat16).astype(jnp.float32)
                block = jnp.where(lane == x, high, jnp.where(lane == x_count + x, column - high, block))
            ref[number, :, cols:] = block.astype(jnp.bfloat16)
    for copy in copies[6:]:
        copy.wait()


def deq_in_kernel(ctx_count, exp_ref, gate_scale_hbm, up_scale_hbm, gate_hbm, up_hbm, _, own_ref, give_ref,
                  gate_ref, up_ref, gate_scale_ref, up_scale_ref, sems):
    core = lax.bitwise_and(exp_ref[0], 1)
    width, cols = gate_ref.shape
    rows = width // (2 * ctx_count)
    pairs = [(gate_scale_hbm, gate_scale_ref), (up_scale_hbm, up_scale_ref)]
    for step in range(ctx_count):
        at = pl.ds(step * 2 * rows, 2 * rows)
        pairs += [(gate_hbm.at[0, at], gate_ref.at[at]), (up_hbm.at[0, at], up_ref.at[at])]
    copies = copy_all(sems, pairs)
    for copy in copies[:2]:
        copy.wait()
    for step in range(ctx_count):
        for half, (ref, scale_ref) in enumerate(((gate_ref, gate_scale_ref), (up_ref, up_scale_ref))):
            copies[2 + 2 * step + half].wait()
            for out_ref, side in ((give_ref, 1 - core), (own_ref, core)):
                first = (2 * step + side) * (rows // WB)
                for i in range(rows // WB):
                    row = pl.multiple_of((2 * step + side) * rows + i * WB, WB)
                    for j in range(cols // WB):
                        factor = block_factor(scale_ref[j, 0, first + i], WB)
                        out_ref[pl.ds(step * rows + i * WB, WB), pl.ds(half * cols + j * WB, WB)] = (
                            ref[pl.ds(row, WB), pl.ds(j * WB, WB)] * factor
                        )


def deq_in(my_exp, gate_weight, gate_scale, up_weight, up_scale, ctx_count, after):
    width, hidden = gate_weight.shape[1:]
    shape = jax.ShapeDtypeStruct((width // 2, 2 * hidden), jnp.bfloat16)
    gate_scale = jnp.transpose(gate_scale, (2, 0, 1))
    up_scale = jnp.transpose(up_scale, (2, 0, 1))
    return pl.pallas_call(
        functools.partial(deq_in_kernel, ctx_count),
        in_specs=[pl.BlockSpec(memory_space=pltpu.SMEM)]
        + [pl.BlockSpec(memory_space=pltpu.HBM)] * 4
        + [pl.BlockSpec(memory_space=pl.ANY)],
        out_specs=[pl.BlockSpec(memory_space=pltpu.VMEM)] * 2,
        out_shape=[shape, shape],
        scratch_shapes=[
            pltpu.VMEM((width, hidden), jnp.bfloat16),
            pltpu.VMEM((width, hidden), jnp.bfloat16),
            pltpu.SMEM(gate_scale.shape, jnp.int32),
            pltpu.SMEM(up_scale.shape, jnp.int32),
            pltpu.SemaphoreType.DMA((2 + 2 * ctx_count,)),
        ],
        compiler_params=pltpu.CompilerParams(vmem_limit_bytes=20 * MIB),
        cost_estimate=pl.CostEstimate(
            flops=2 * width * hidden, bytes_accessed=8 * width * hidden, transcendentals=0
        ),
        name="dequant_in",
    )(my_exp, *in_hbm(gate_scale, up_scale, gate_weight, up_weight), after)


def deq_down_kernel(ctx_count, exp_ref, scale_hbm, down_hbm, _, own_ref, give_ref, down_ref, scale_ref, sems):
    core = lax.bitwise_and(exp_ref[0], 1)
    rows, width = down_ref.shape
    cols = width // (2 * ctx_count)
    pairs = [(scale_hbm, scale_ref)]
    for step in range(ctx_count):
        at = pl.ds(step * 2 * cols, 2 * cols)
        pairs.append((down_hbm.at[0, :, at], down_ref.at[:, at]))
    copies = copy_all(sems, pairs)
    copies[0].wait()
    for step in range(ctx_count):
        copies[1 + step].wait()
        for out_ref, side in ((give_ref, 1 - core), (own_ref, core)):
            first = (2 * step + side) * (cols // WB)
            for j in range(cols // WB):
                col = pl.multiple_of((2 * step + side) * cols + j * WB, WB)
                for i in range(rows // WB):
                    factor = block_factor(scale_ref[i, 0, first + j], WB)
                    out_ref[pl.ds(i * WB, WB), pl.ds(step * cols + j * WB, WB)] = (
                        down_ref[pl.ds(i * WB, WB), pl.ds(col, WB)] * factor
                    )


def deq_down(my_exp, down_weight, down_scale, ctx_count, after):
    hidden, width = down_weight.shape[1:]
    shape = jax.ShapeDtypeStruct((hidden, width // 2), jnp.bfloat16)
    down_scale = jnp.transpose(down_scale, (1, 0, 2))
    return pl.pallas_call(
        functools.partial(deq_down_kernel, ctx_count),
        in_specs=[pl.BlockSpec(memory_space=pltpu.SMEM)]
        + [pl.BlockSpec(memory_space=pltpu.HBM)] * 2
        + [pl.BlockSpec(memory_space=pl.ANY)],
        out_specs=[pl.BlockSpec(memory_space=pltpu.VMEM)] * 2,
        out_shape=[shape, shape],
        scratch_shapes=[
            pltpu.VMEM((hidden, width), jnp.bfloat16),
            pltpu.SMEM(down_scale.shape, jnp.int32),
            pltpu.SemaphoreType.DMA((1 + ctx_count,)),
        ],
        compiler_params=pltpu.CompilerParams(vmem_limit_bytes=12 * MIB),
        cost_estimate=pl.CostEstimate(
            flops=width * hidden, bytes_accessed=4 * width * hidden, transcendentals=0
        ),
        name="dequant_down",
    )(my_exp, *in_hbm(down_scale, down_weight), after)


def attend_kernel(plan, ctx_ref, exp_ref, order_ref, *refs):
    ctx_count, exp_count, tok, heads, attend_at, slots, kv_apart, more, final = plan
    packed_at, places_of = [at for at, _ in attend_at], [place for _, place in attend_at]
    array_count = 1 + max(at[0] for at in packed_at if at)
    span = exp_count * tok
    packed_refs, refs = refs[:array_count], refs[array_count:]
    packed = [packed_refs[at[0]].at[pl.ds(at[1], span)] if at else None for at in packed_at]
    kv_refs = list(packed)
    if kv_apart:
        kv_refs[packed_at.index(None)], refs = refs[0], refs[1:]
    if more:
        more_ref, refs = refs[0], refs[1:]
    x_count = exp_count // 2
    if final:
        weight_ref, rest = refs[0], refs[2:]
        keep_refs, give_ref = rest[:x_count], rest[x_count]
    key_scr, value_scr, place_scr, att_ref = refs[-4:] if final else (*refs[1:], refs[0])
    if more:
        att_ref[...] = more_ref[...]
    positions = ctx_count * span
    my_ctx, my_exp = ctx_ref[0], exp_ref[0]
    my_x, my_core = lax.shift_right_logical(my_exp, 1), lax.bitwise_and(my_exp, 1)
    lane = lax.broadcasted_iota(jnp.int32, (8, positions), 1)
    places = lane % span
    for offset, ref in enumerate(kv_refs):
        key_scr[pl.ds(offset * span, span), :] = ref[:, 0:HEAD_SIZE]
        value_scr[pl.ds(offset * span, span), 0:HEAD_SIZE] = ref[:, HEAD_SIZE : 2 * HEAD_SIZE]
        base = order_ref[lax.bitwise_xor(my_ctx, by_core(my_core, places_of[offset], 0))] * span
        places = places + jnp.where(lane // span == offset, base, 0)
    place_scr[...] = places
    scale = math.log2(math.e) / math.sqrt(HEAD_SIZE)
    value_scr[:, HEAD_SIZE:] = jnp.ones((positions, HEAD_SIZE), jnp.bfloat16)
    for offset in slots:
        ref = packed[offset]
        source = lax.bitwise_xor(my_ctx, by_core(my_core, places_of[offset], 0))
        queries = jnp.concatenate(
            [ref[:, (h + 2) * HEAD_SIZE : (h + 3) * HEAD_SIZE] for h in range(heads)], axis=0
        )
        scores = lax.dot_general(
            queries, key_scr[...], (((1,), (1,)), ((), ())), preferred_element_type=jnp.float32
        )
        own_place = order_ref[source] * span + lax.broadcasted_iota(jnp.int32, (span, positions), 0)
        bias = jnp.where(place_scr[0:1, :] <= own_place, 0.0, -1e30)
        scores = scores.reshape(heads, span, positions) * scale + bias[None]
        exps = jnp.exp2(scores - jnp.max(scores, axis=-1, keepdims=True))
        mixed = jnp.dot(
            exps.astype(jnp.bfloat16).reshape(heads * span, positions),
            value_scr[...],
            preferred_element_type=jnp.float32,
        )
        mixed = mixed[:, :HEAD_SIZE] * (1.0 / mixed[:, HEAD_SIZE : HEAD_SIZE + 1])
        mixed = mixed.astype(jnp.bfloat16).reshape(heads, span, HEAD_SIZE)
        for owner in range(exp_count):
            x_off = lax.bitwise_xor(my_x, owner // 2)
            row = pl.multiple_of(((x_off * ctx_count + source) * 2 + owner % 2) * tok, tok)
            for head in range(heads):
                att_ref[pl.ds(row, tok), pl.ds(head * HEAD_SIZE, HEAD_SIZE)] = mixed[
                    head, owner * tok : (owner + 1) * tok, :
                ]

    if not final:
        return
    cols = weight_ref.shape[1] // 2
    per_x = 2 * ctx_count * tok
    for which in (1, 0):
        side = lax.bitwise_xor(my_core, which)
        weight = weight_ref[:, pl.ds(pl.multiple_of(side * cols, cols), cols)]
        part = jnp.dot(att_ref[...], weight, preferred_element_type=jnp.float32)
        if which:
            give_ref[...] = part.astype(give_ref.dtype)
        else:
            for x_off, keep_ref in enumerate(keep_refs):
                keep_ref[...] = part[x_off * per_x : (x_off + 1) * per_x]


def finish_kernel(plan, ctx_ref, exp_ref, keep_in, give_in, *refs):
    ctx_count, x_count, tok, piece_places, places_of = plan
    piece_refs, (keep_ref, give_ref, own_route_ref) = refs[:-3], refs[-3:]
    my_ctx, my_exp = ctx_ref[0], exp_ref[0]
    my_x, my_core = lax.shift_right_logical(my_exp, 1), lax.bitwise_and(my_exp, 1)
    cols = keep_ref.shape[1]
    route_base = give_in.shape[0]
    keep_ref[...] = keep_in[...]
    give_ref[0:route_base, :] = give_in[...]
    blocks = [jnp.zeros((tok, HEAD_SIZE), jnp.float32)] * x_count
    lane = lax.broadcasted_iota(jnp.int32, (tok, HEAD_SIZE), 1)
    for (array, place), place_of in zip(piece_places, places_of):
        source = lax.bitwise_xor(my_ctx, by_core(my_core, place_of, 0))
        at = pl.ds(pl.multiple_of((source * 2 + my_core) * tok, tok), tok)
        for which, ref in enumerate((keep_ref, give_ref)):
            side = lax.bitwise_xor(my_core, which)
            piece = piece_refs[array][place, :, pl.ds(pl.multiple_of(side * cols, cols), cols)]
            value = ref[at, :].astype(jnp.float32) + piece.astype(jnp.float32)
            ref[at, :] = value.astype(ref.dtype)
        block = piece_refs[array][place, :, 2 * cols :].astype(jnp.float32)
        for x_off in range(x_count):
            for part in range(2):
                wanted = lax.bitwise_xor(my_x, x_off) + part * x_count
                column = jnp.sum(jnp.where(lane == wanted, block, 0.0), axis=1, keepdims=True)
                blocks[x_off] = jnp.where(lane == source + part * ctx_count, column, blocks[x_off])
    for x_off, block in enumerate(blocks):
        for ref, base in ((give_ref, route_base), (own_route_ref, 0)):
            at = pl.ds(base + x_off * tok, tok)
            ref[at, 0:HEAD_SIZE] = block.astype(jnp.bfloat16)
            if cols > HEAD_SIZE:
                ref[at, HEAD_SIZE:] = jnp.zeros((tok, cols - HEAD_SIZE), jnp.bfloat16)


def fill_rows(plan, ctx_ref, exp_ref, gain_ref, chunk_refs, places, rows_scr, square_ref, groups):
    ctx_count, x_count, tok, bit = plan
    my_ctx = ctx_ref[0]
    my_core = lax.bitwise_and(exp_ref[0], 1)
    mine = side_of(my_ctx, bit)
    cols = chunk_refs[0].shape[1]
    rows = ctx_count * tok
    for (array, first_row), place_of in places:
        ref = chunk_refs[array]
        source = lax.bitwise_xor(my_ctx, by_core(my_core, place_of, 0))
        x_off = by_core(my_core, place_of, 1)
        gain_at = pl.multiple_of((source * 2 + my_core) * cols, cols)
        gain = gain_ref[:, pl.ds(gain_at, cols)]
        col = pl.multiple_of(without(source, bit) * cols, cols)
        for place, group in enumerate(groups):
            for start, low, length in runs(ctx_count, bit, mine if group == 1 else 1 - mine, 2 * tok):
                chunk = ref[pl.ds(first_row + start, length), :].astype(jnp.float32)
                row = (place * x_count + x_off) * rows + low
                at = pl.ds(pl.multiple_of(row, 2 * tok), length)
                rows_scr[at, pl.ds(col, cols)] = (chunk * gain).astype(jnp.bfloat16)
                square_ref[at, :] = square_ref[at, :] + jnp.sum(chunk * chunk, axis=-1, keepdims=True)


def product(plan, side, rows_scr, weight_ref, cols):
    ctx_count, _, _, bit = plan
    total = None
    for start, low, length in runs(ctx_count, bit, side, cols):
        part = jnp.dot(
            rows_scr[:, low : low + length],
            weight_ref[pl.ds(start, length), :],
            preferred_element_type=jnp.float32,
        )
        total = part if total is None else total + part
    return total


def experts_in_first(plan, offsets, ctx_ref, exp_ref, *refs):
    chunk_refs, (gain_ref, own_ref, other_ref, _, act_ref, square_ref, rows_scr) = refs[:-7], refs[-7:]
    square_ref[...] = jnp.zeros(square_ref.shape, jnp.float32)
    fill_rows(plan, ctx_ref, exp_ref, gain_ref, chunk_refs, offsets, rows_scr, square_ref, (0, 1))
    width, side = own_ref.shape[1], side_of(ctx_ref[0], plan[3])
    for place, ref in enumerate((own_ref, other_ref)):
        act_ref[:, place * width : (place + 1) * width] = product(
            plan, side, rows_scr, ref, chunk_refs[0].shape[1]
        )


def experts_in_second(plan, offsets, group, ctx_ref, exp_ref, *refs):
    chunk_refs, rest = refs[:-9], refs[-9:]
    gain_ref, own_ref, other_ref, first_ref, square_ref, _, act_ref, rows_scr, sum_scr = rest
    count, width = rows_scr.shape[0], own_ref.shape[1]
    sum_scr[...] = square_ref[group * count : (group + 1) * count, :]
    fill_rows(plan, ctx_ref, exp_ref, gain_ref, chunk_refs, offsets, rows_scr, sum_scr, (group,))
    lane = lax.broadcasted_iota(jnp.int32, (1, HEAD_SIZE), 1)
    square = sum_scr[...]
    high = square.astype(jnp.bfloat16).astype(jnp.float32)
    act_ref[:, 2 * width :] = jnp.where(lane == 0, high, square - high).astype(jnp.bfloat16)
    side = 1 - side_of(ctx_ref[0], plan[3])
    for place, ref in enumerate((own_ref, other_ref)):
        cols = slice(place * width, (place + 1) * width)
        act = first_ref[group * count : (group + 1) * count, cols] + product(
            plan, side, rows_scr, ref, chunk_refs[0].shape[1]
        )
        act_ref[:, cols] = act.astype(jnp.bfloat16)


def experts_out_kernel(plan, group, places, state_at, route_at, model_width, ctx_ref, exp_ref, act_ref, came_ref, *refs):
    ctx_count, exp_count, tok, bit = plan
    x_count, half = exp_count // 2, ctx_count // 2
    route_refs, refs = refs[: x_count + 1], refs[x_count + 1 :]
    (own_ref, other_ref, _), rest = refs[:3], refs[3:]
    state_count = 1 + max((array for pair in state_at for array, _ in pair), default=-1)
    state_refs, rest = rest[:state_count], rest[state_count:]
    out_refs, hidden_scr = rest[:-1], rest[-1]
    my_ctx = ctx_ref[0]
    my_core = lax.bitwise_and(exp_ref[0], 1)
    mine = side_of(my_ctx, bit)
    side = mine if group == 1 else 1 - mine
    width = (act_ref.shape[1] - HEAD_SIZE) // 2
    hidden = width // 2
    lane = lax.broadcasted_iota(jnp.int32, (tok, HEAD_SIZE), 1)
    blocks = []
    for array, row in route_at:
        blocks.append(route_refs[array][row : row + tok, 0:HEAD_SIZE].astype(jnp.float32))
    columns = []
    for x_off in range(x_count):
        for low in range(half):
            for core in range(2):
                same, swapped = blocks[2 * x_off + core], blocks[2 * x_off + 1 - core]
                block = jnp.where(my_core == 0, same, swapped)
                number = (low >> bit << bit + 1) + (low & ((1 << bit) - 1)) + side * (1 << bit)
                picked = jnp.where(lane % ctx_count == number, block, 0.0)
                columns.append(jnp.sum(picked, axis=1, keepdims=True))
    route = jnp.concatenate(columns, axis=0)
    squares = act_ref[:, 2 * width :].astype(jnp.float32) + came_ref[:, 2 * width :].astype(jnp.float32)
    norm = lax.rsqrt((squares[:, 0:1] + squares[:, 1:2]) / model_width + 1e-06)
    scaled_route = norm * route
    for part in range(2):
        acts = act_ref[:, part * width : (part + 1) * width].astype(jnp.float32) + came_ref[
            :, (1 - part) * width : (2 - part) * width
        ].astype(jnp.float32)
        gate = acts[:, :hidden] * norm
        value = gate / (1.0 + jnp.exp(-gate)) * (acts[:, hidden:] * scaled_route)
        hidden_scr[:, part * hidden : (part + 1) * hidden] = value.astype(jnp.bfloat16)
    picked = []
    for place in places:
        x_off = by_core(my_core, place, 1)
        low = without(lax.bitwise_xor(my_ctx, by_core(my_core, place, 0)), bit)
        row = pl.multiple_of((x_off * half + low) * (2 * tok), 2 * tok)
        picked.append(hidden_scr[pl.ds(row, 2 * tok), :])
    picked = jnp.concatenate(picked, axis=0)
    out_cols = own_ref.shape[1]
    step = min(512, out_cols)
    for col in range(0, out_cols, step):
        at = pl.ds(col, step)
        out = jnp.dot(picked[:, :hidden], own_ref[:, at], preferred_element_type=jnp.float32)
        out = out + jnp.dot(picked[:, hidden:], other_ref[:, at], preferred_element_type=jnp.float32)
        for place, ref in enumerate(out_refs):
            ref[:, at] = out[place * 2 * tok : (place + 1) * 2 * tok, :].astype(ref.dtype)
    for place, ref in zip(places, out_refs):
        if place[0] == (0, 0):
            for c_off, pair in enumerate(state_at):
                states = []
                for array, first_row in pair:
                    own_row = pl.multiple_of(first_row + my_ctx * (2 * tok), 2 * tok)
                    states.append(state_refs[array][pl.ds(own_row, 2 * tok), :].astype(jnp.float32))
                state = states[0] if pair[0] == pair[1] else jnp.where(my_core == 0, *states)
                cols = state.shape[1]
                at = pl.ds(pl.multiple_of(lax.bitwise_xor(my_ctx, c_off) * cols, cols), cols)
                ref[:, at] = ref[:, at] + state


def shards(
    residual,
    encoded_query_rows,
    quantized_key_rows,
    quantized_value_rows,
    key_block_exponent,
    value_block_exponent,
    block_order,
    out_weight,
    norm_gain,
    expert_ids,
    route_weight,
    gate_weight,
    gate_scale,
    up_weight,
    up_scale,
    down_weight,
    down_scale,
):
    f32, bf16 = jnp.float32, jnp.bfloat16
    vmem = pl.BlockSpec(memory_space=pltpu.VMEM)
    smem = pl.BlockSpec(memory_space=pltpu.SMEM)
    anywhere = pl.BlockSpec(memory_space=pl.ANY)
    span, query_width = encoded_query_rows.shape
    heads = query_width // HEAD_SIZE
    group = QUERY_HEADS // KEY_VALUE_HEADS
    ctx_count = lax.axis_size("ctx")
    exp_count = lax.axis_size("exp")
    x_count = exp_count // 2
    experts = ctx_count * x_count
    tok, model_width = residual.shape
    half_width = model_width // 2
    cols = half_width // ctx_count
    my_ctx = lax.axis_index("ctx").astype(jnp.int32).reshape(1)
    my_exp = lax.axis_index("exp").astype(jnp.int32).reshape(1)
    route, places = gather_route(ctx_count, x_count)

    hbm = pl.BlockSpec(memory_space=pltpu.HBM)
    piece_shape = jax.ShapeDtypeStruct((ctx_count // 2, tok, 2 * cols + HEAD_SIZE), bf16)
    row_route, row_places = gather_route(ctx_count, x_count, rows_only=True)
    names = sorted(row_places)
    piece_names = [[key for key in names if bool(key[0] & 2) == sent] for sent in (False, True)]
    piece_places = tuple(tuple(row_places[key] for key in keys) for keys in piece_names)
    packed, near, far = pl.pallas_call(
        functools.partial(pack_kernel, (heads, group, x_count, piece_places)),
        in_specs=[smem] * 2 + [hbm] * 8,
        out_specs=[vmem] * 3,
        out_shape=[
            jax.ShapeDtypeStruct((span, query_width + 2 * HEAD_SIZE), bf16),
            piece_shape,
            piece_shape,
        ],
        scratch_shapes=[
            pltpu.VMEM(key_block_exponent.shape, jnp.int32),
            pltpu.VMEM(key_block_exponent.shape, jnp.int32),
            pltpu.VMEM((span, HEAD_SIZE), bf16),
            pltpu.VMEM((span, HEAD_SIZE), bf16),
            pltpu.VMEM((TOP, tok), jnp.int32),
            pltpu.VMEM((TOP, tok), f32),
            pltpu.SemaphoreType.DMA((7 + ctx_count,)),
        ],
        compiler_params=pltpu.CompilerParams(vmem_limit_bytes=8 * MIB),
        name="pack",
    )(
        my_ctx,
        my_exp,
        *in_hbm(
            key_block_exponent,
            value_block_exponent,
            encoded_query_rows,
            quantized_key_rows,
            quantized_value_rows,
            jnp.transpose(expert_ids),
            jnp.transpose(route_weight),
            residual,
        ),
    )
    piece_arrays = [near]
    piece_at = {(0, key[0]): (0, place) for place, key in enumerate(piece_names[0])}
    piece_bits = [1, 0, *range(bits_of(ctx_count) - 1, 1, -1)]
    sending, weights = far, {}
    early, last_kv = ctx_count == 8, []

    def beside(number, came, arrays, at):
        nonlocal sending
        bit = 1 << piece_bits[number]
        moves = {1: ((2, 0), (1, 0)), 0: ((1, 0), (2, 0))}.get(piece_bits[number], ((bit, 0),) * 2)
        if number == 0:
            keys = [(0, key[0]) for key in piece_names[1]]
        else:
            keys = sorted(key for key in piece_at if key[1] & bit)
            sending = jnp.stack([piece_arrays[array][place] for array, place in map(piece_at.pop, keys)])
        pieces = follow(sending, moves)
        if number == 0:
            own, give = deq_in(my_exp, gate_weight, gate_scale, up_weight, up_scale, ctx_count, packed)
            *came, pieces, weights["in_own"], weights["in_give"] = together(*came, pieces, own, give)
        elif number == 1:
            other = from_offset(weights["in_give"], 1)
            own, give = deq_down(my_exp, down_weight, down_scale, ctx_count, piece_arrays[-1])
            if early:
                array, row = at[4, 0]
                last_kv.append(follow(arrays[array][row : row + span, : 2 * HEAD_SIZE], ((3, 0),) * 2))
            held = together(*came, pieces, other, own, give, *last_kv)
            *came, pieces, other, own, give = held[: len(held) - len(last_kv)]
            last_kv[:] = held[len(held) - len(last_kv) :]
            weights.update(in_other=other, down_own=own, down_give=give)
        elif number < len(piece_bits) - 1:
            *came, pieces = together(*came, pieces)
        for place, (source, target) in enumerate(keys):
            piece_at[source ^ bit, target ^ bit] = (len(piece_arrays), place)
        piece_arrays.append(pieces)
        return came

    packed, packed_at = spread(packed, stages_of(row_route), beside)
    attend_at = tuple((packed_at[key], row_places[key]) for key in names)
    attend_pieces = tuple(piece_at[key[0], 0] for key in names)
    in_own, in_other, down_own = weights["in_own"], weights["in_other"], weights["down_own"]
    down_other = from_offset(weights["down_give"], 1)

    positions = ctx_count * span
    per_x = 2 * ctx_count * tok
    def attend(arrays, at, slots, kv, more, final):
        scratch = [
            pltpu.VMEM((positions, HEAD_SIZE), bf16),
            pltpu.VMEM((positions, 2 * HEAD_SIZE), bf16),
            pltpu.VMEM((8, positions), jnp.int32),
        ]
        rows_shape = (positions, query_width)
        out_shape = [jax.ShapeDtypeStruct(rows_shape, bf16)]
        if final:
            out_shape = [jax.ShapeDtypeStruct((per_x, cols), f32)] * x_count
            out_shape += [jax.ShapeDtypeStruct((x_count * per_x, cols), bf16)]
            scratch.append(pltpu.VMEM(rows_shape, bf16))
        operands = [*arrays, *kv, *more, *([out_weight] if final else [])]
        return pl.pallas_call(
            functools.partial(
                attend_kernel,
                (ctx_count, exp_count, tok, heads, at, slots, bool(kv), bool(more), final),
            ),
            in_specs=[smem] * 3 + [vmem] * len(operands) + [anywhere] * final,
            out_specs=[vmem] * len(out_shape),
            out_shape=out_shape,
            scratch_shapes=scratch,
            compiler_params=pltpu.CompilerParams(vmem_limit_bytes=3 * ctx_count * MIB),
            cost_estimate=pl.CostEstimate(
                flops=4 * positions * len(slots) * span * query_width
                + 4 * positions * query_width * cols * final,
                bytes_accessed=4 * MIB,
                transcendentals=heads * positions * len(slots) * span,
            ),
            name="attend",
        )(my_ctx, my_exp, block_order, *operands, *([down_other] if final else []))

    more, slots = [], tuple(range(ctx_count))
    if early:
        late = max(packed_at[key][0] for key in names)
        early_at = tuple((None if at[0] == late else at, place) for at, place in attend_at)
        slots = tuple(i for i, (at, _) in enumerate(early_at) if at is None)
        rest = tuple(i for i, (at, _) in enumerate(early_at) if at is not None)
        more = attend(packed[:late], early_at, rest, last_kv, [], False)
    *keeps, give = attend(packed, attend_at, slots, [], more, True)
    keeps[0], give, own_route = pl.pallas_call(
        functools.partial(
            finish_kernel,
            (ctx_count, x_count, tok, attend_pieces, tuple(place for _, place in attend_at)),
        ),
        in_specs=[smem] * 2 + [vmem] * (2 + len(piece_arrays)),
        out_specs=[vmem] * 3,
        out_shape=[
            jax.ShapeDtypeStruct((per_x, cols), f32),
            jax.ShapeDtypeStruct((x_count * (per_x + tok), cols), bf16),
            jax.ShapeDtypeStruct((x_count * tok, cols), bf16),
        ],
        compiler_params=pltpu.CompilerParams(vmem_limit_bytes=8 * MIB),
        name="finish",
    )(my_ctx, my_exp, keeps[0], give, *piece_arrays)

    given = from_offset(give, 1)
    routes, route_at, state = [own_route, given], [(0, 0), (1, x_count * per_x)], keeps[0]
    state = state + given[:per_x].astype(f32)
    for x_off in range(1, x_count):
        part = keeps[x_off] + given[x_off * per_x : (x_off + 1) * per_x].astype(f32)
        row = x_count * per_x + x_off * tok
        own = own_route[x_off * tok : (x_off + 1) * tok]
        sent = jnp.concatenate([part.astype(bf16), own, given[row : row + tok]], axis=0)
        came = from_offset(sent, 2 * x_off)
        state = state + came[:per_x].astype(f32)
        route_at += [(len(routes), per_x), (len(routes), per_x + tok)]
        routes.append(came)
    state = state.astype(bf16)

    stages = stages_of(route)
    chunks, chunk_at = spread(state, stages)
    gain = norm_gain.reshape(1, model_width)
    rows = x_count * per_x
    in_width = in_own.shape[1]
    bit = 1 if (ctx_count, x_count) == (8, 2) else bits_of(ctx_count) - 1
    near = tuple(sorted(key for key in places if not side_of(key[0], bit)))
    far = tuple(sorted(key for key in places if side_of(key[0], bit)))

    def picked(keys):
        arrays = sorted({chunk_at[key][0] for key in keys})
        at = tuple(((arrays.index(chunk_at[key][0]), chunk_at[key][1]), places[key]) for key in keys)
        return [chunks[array] for array in arrays], at

    near_chunks, near_places = picked(near)
    far_chunks, far_places = picked(far)
    first_act, first_square = pl.pallas_call(
        functools.partial(experts_in_first, (ctx_count, x_count, tok, bit), near_places),
        in_specs=[smem] * 2 + [vmem] * (len(near_chunks) + 3) + [anywhere],
        out_specs=[vmem] * 2,
        out_shape=[
            jax.ShapeDtypeStruct((rows, 2 * in_width), f32),
            jax.ShapeDtypeStruct((rows, 1), f32),
        ],
        scratch_shapes=[pltpu.VMEM((rows, half_width // 2), bf16)],
        compiler_params=pltpu.CompilerParams(vmem_limit_bytes=2 * ctx_count * MIB),
        cost_estimate=pl.CostEstimate(
            flops=2 * rows * half_width * in_width, bytes_accessed=8 * MIB, transcendentals=0
        ),
        name="experts_in_first",
    )(my_ctx, my_exp, *near_chunks, gain, in_own, in_other, down_other)
    acts = []
    for part in range(2):
        acts.append(
            pl.pallas_call(
                functools.partial(experts_in_second, (ctx_count, x_count, tok, bit), far_places, part),
                in_specs=[smem] * 2 + [vmem] * (len(far_chunks) + 5) + [anywhere],
                out_specs=vmem,
                out_shape=jax.ShapeDtypeStruct((rows // 2, 2 * in_width + HEAD_SIZE), bf16),
                scratch_shapes=[
                    pltpu.VMEM((rows // 2, half_width // 2), bf16),
                    pltpu.VMEM((rows // 2, 1), f32),
                ],
                compiler_params=pltpu.CompilerParams(vmem_limit_bytes=2 * ctx_count * MIB),
                cost_estimate=pl.CostEstimate(
                    flops=rows * half_width * in_width, bytes_accessed=8 * MIB, transcendentals=0
                ),
                name="experts_in_second",
            )(
                my_ctx,
                my_exp,
                *far_chunks,
                gain,
                in_own,
                in_other,
                first_act,
                first_square,
                acts[0] if part else first_square,
            )
        )
    leaves = set(places) - {source for _, source, _, _ in route}
    sums = {}
    for part in range(2):
        slots = near if part == 1 else far
        state_keys = [
            next(key for key in places if places[key][core] == (offset, 0))
            for offset in (range(ctx_count) if part == 1 else ())
            for core in range(2)
        ]
        states, state_at = picked(state_keys)
        state_at = tuple((state_at[i][0], state_at[i + 1][0]) for i in range(0, len(state_at), 2))
        outs = pl.pallas_call(
            functools.partial(
                experts_out_kernel,
                (ctx_count, exp_count, tok, bit),
                part,
                tuple(places[key] for key in slots),
                state_at,
                tuple(route_at),
                model_width,
            ),
            in_specs=[smem] * 2 + [vmem] * (5 + x_count) + [anywhere] + [vmem] * len(states),
            out_specs=[vmem] * len(slots),
            out_shape=[
                jax.ShapeDtypeStruct((2 * tok, half_width), bf16 if slot in leaves else f32)
                for slot in slots
            ],
            scratch_shapes=[pltpu.VMEM((rows // 2, in_width), bf16)],
            compiler_params=pltpu.CompilerParams(vmem_limit_bytes=2 * ctx_count * MIB),
            cost_estimate=pl.CostEstimate(
                flops=rows * half_width * in_width,
                bytes_accessed=8 * MIB,
                transcendentals=rows * in_width // 2,
            ),
            name="experts_out",
        )(
            my_ctx,
            my_exp,
            acts[part],
            from_offset(acts[part], 1),
            *routes,
            down_own,
            down_other,
            sums[slots_done[0]] if part else acts[1],
            *states,
        )
        slots_done = slots
        sums.update(zip(slots, outs))

    for number, sends in enumerate(reversed(stages)):
        came = []
        for moves, _, targets in sends:
            sent = [sums[key].astype(bf16) for key in targets]
            came.append(follow(sent[0] if len(sent) == 1 else jnp.concatenate(sent, axis=0), moves))
        if number < len(stages) - 1:
            waiting = list(near) if number == 0 else []
            values = together(*came, *[sums[key] for key in waiting])
            came = values[: len(came)]
            sums.update(zip(waiting, values[len(came) :]))
        for (_, sources, _), array in zip(sends, came):
            for place, key in enumerate(sources):
                part = array[place * 2 * tok : (place + 1) * 2 * tok]
                sums[key] = sums[key] + part.astype(f32)
    total = sums[0, 0]
    core = lax.bitwise_and(my_exp[0], 1)
    mine = jnp.where(core == 0, total[:tok], total[tok:]).astype(bf16)
    came = from_offset(jnp.where(core == 0, total[tok:], total[:tok]).astype(bf16), 1)
    mine = mine.reshape(tok, ctx_count, 1, cols)
    came = came.reshape(tok, ctx_count, 1, cols)
    result = jnp.where(core == 0, jnp.concatenate([mine, came], axis=2), jnp.concatenate([came, mine], axis=2))
    return result.reshape(tok, model_width)


def solution(mesh):
    return jax.shard_map(
        shards,
        mesh=mesh,
        in_specs=(
            P(("dp", "ctx", "exp"), None),
            P(("dp", "ctx"), "exp"),
            P(("dp", "ctx"), None),
            P(("dp", "ctx"), None),
            P(("dp", "ctx"), None),
            P(("dp", "ctx"), None),
            P(),
            P("exp", "ctx"),
            P(),
            P(("dp", "ctx", "exp"), None),
            P(("dp", "ctx", "exp"), None),
            P(("ctx", "exp"), None, None),
            P(("ctx", "exp"), None, None),
            P(("ctx", "exp"), None, None),
            P(("ctx", "exp"), None, None),
            P(("ctx", "exp"), None, None),
            P(("ctx", "exp"), None, None),
        ),
        out_specs=P(("dp", "ctx", "exp"), None),
        check_vma=False,
    )
```

```python
import functools
import math

import jax
import jax.numpy as jnp
from jax import lax
from jax.experimental import pallas as pl
from jax.experimental.pallas import tpu as pltpu
from jax.sharding import PartitionSpec as P

QUERY_HEADS = 32
KEY_VALUE_HEADS = 4
HEAD_SIZE = 128
TOP = 8
SCALE_POSITIONS = 64
WB = 128
MIB = 1 << 20


def bits_of(count):
    return count.bit_length() - 1


def from_offset(array, offset):
    return lax.ppermute(array, "exp", [(i, i ^ offset) for i in range(lax.axis_size("exp"))])


def from_ctx(array, offset):
    return lax.ppermute(array, "ctx", [(i, i ^ offset) for i in range(lax.axis_size("ctx"))])


def moved(offset, move):
    return (offset[0] ^ move[0], offset[1] ^ move[1])


def gather_route(ctx_count, x_count, rows_only=False):
    transfers, arrival, places = [], {(0, 0): 0}, {(0, 0): ((0, 0), (0, 0))}

    def go(source, moves, delay=0):
        reached = tuple(moved(place, (c, e >> 1)) for place, (c, e) in zip(places[source], moves))
        target = reached[0]
        arrival[target], places[target] = arrival[source] + 1 + delay, reached
        transfers.append((arrival[target], source, target, moves))
        return target

    bits = bits_of(ctx_count)
    y_move = (1, 0)
    if (ctx_count, x_count) == (8, 2) and not rows_only:
        z_far, z_near = ((4, 0),) * 2, ((2, 0),) * 2
        first, second, both = ((0, 2), y_move), (y_move, (0, 2)), ((1, 2),) * 2
        at = {"0": (0, 0)}
        for stage, moves, hops in (
            (1, z_far, "0>4"),
            (1, z_near, "0>2"),
            (1, first, "0>0a"),
            (1, second, "0>0b"),
            (1, both, "0>0ab"),
            (2, z_far, "0ab>4ab"),
            (2, z_near, "4>6"),
            (2, first, "2>2a 4>4a"),
            (2, second, "2>2b 4>4b"),
            (3, z_near, "4ab>6ab"),
            (3, first, "6>6a"),
            (3, second, "6>6b 2a>2ab"),
        ):
            for hop in hops.split():
                source, target = hop.split(">")
                at[target] = go(at[source], moves, stage - 1 - arrival[at[source]])
        return sorted(transfers, key=lambda transfer: transfer[0]), places
    if rows_only:
        shared, steps = range(bits - 1, 1, -1), [(2, 0), y_move]
    else:
        shared, steps = range(bits - 1, 0, -1), [(0, 2 << bit) for bit in range(bits_of(x_count))] + [y_move]
    pairs = list(zip(steps, reversed(steps)))
    for bit in shared:
        for source in list(arrival):
            go(source, ((1 << bit, 0),) * 2)
    for first in sorted(arrival):
        held = [first]
        for moves in pairs:
            held = held + [go(source, moves) for source in held]
    return sorted(transfers, key=lambda transfer: transfer[0]), places


def follow(array, moves):
    exp_count = lax.axis_size("exp")
    pairs = []
    for c in range(lax.axis_size("ctx")):
        for e in range(exp_count):
            far = moved((c, e), moves[e % 2])
            pairs.append((far[0] * exp_count + far[1], c * exp_count + e))
    return lax.ppermute(array, ("ctx", "exp"), pairs)


def side_of(index, bit):
    return (index >> bit) & 1


def without(index, bit):
    return (index & ((1 << bit) - 1)) | ((index >> bit + 1) << bit)


def runs(ctx_count, bit, side, each):
    length = each << bit
    return [
        (pl.multiple_of((2 * k + side) * length, length), k * length, length) for k in range(ctx_count >> bit + 1)
    ]


def by_core(core, place, part):
    first, second = place[0][part], place[1][part]
    return first if first == second else jnp.where(core == 0, first, second)


def stages_of(route):
    stages, arrays = [], [((0, 0),)]
    top = max(moves[0][0] for _, _, _, moves in route)
    for stage in sorted({transfer[0] for transfer in route}):
        sends = []
        for moves in sorted({t[3] for t in route if t[0] == stage}):
            left = {source: target for number, source, target, way in route if (number, way) == (stage, moves)}
            groups = [group for group in arrays if len(group) > 1 and all(key in left for key in group)]
            rest = tuple(sorted(key for key in left if not any(key in group for group in groups)))
            for group in groups + [rest] * bool(rest):
                sends.append((moves, group, tuple(left[key] for key in group)))
        def order(send):
            moves, group, _ = send
            shared, far = moves[0] == moves[1], moves[0][0] == top > 2
            rank = (0 if shared else 1) if len(group) == 1 else (1 if shared else 2 * moves[0][0])
            return -len(group) * (2 if far else 1), -1 if far else rank

        sends.sort(key=order)
        arrays = arrays + [send[2] for send in sends]
        stages.append(sends)
    return stages


def spread(block, stages, beside=None):
    arrays, at, joined = [block], {(0, 0): (0, 0)}, {}
    rows = block.shape[0]
    for number, sends in enumerate(stages):
        came = []
        for moves, group, _ in sends:
            first, row = at[group[0]]
            whole = row == 0 and arrays[first].shape[0] == len(group) * rows
            if whole and all(at[key] == (first, place * rows) for place, key in enumerate(group)):
                joined[group] = arrays[first]
            elif group not in joined:
                parts = [arrays[at[key][0]][at[key][1] : at[key][1] + rows] for key in group]
                joined[group] = jnp.concatenate(parts, axis=0)
            came.append(follow(joined[group], moves))
        came = beside(number, came, arrays, at) if beside else (together(*came) if number < len(stages) - 1 else came)
        for (_, _, targets), array in zip(sends, came):
            at.update({key: (len(arrays), place * rows) for place, key in enumerate(targets)})
            arrays.append(array)
    return arrays, at


def together(*values):
    return lax.optimization_barrier(values)


def block_factor(exponent, width):
    factor = jnp.where(exponent < 0, 0.5, jnp.where(exponent > 0, 2.0, 1.0))
    return jnp.full((1, width), factor, jnp.float32).astype(jnp.bfloat16)


def in_hbm(*arrays):
    return [pltpu.with_memory_space_constraint(array, pltpu.HBM) for array in arrays]


def copy_all(sems, pairs):
    copies = [pltpu.make_async_copy(src, dst, sems.at[i]) for i, (src, dst) in enumerate(pairs)]
    for copy in copies:
        copy.start()
    return copies


def pack_kernel(plan, ctx_ref, exp_ref, key_scale_hbm, value_scale_hbm, query_hbm, key_hbm, value_hbm, ids_hbm,
                route_hbm, residual_hbm, packed_ref, near_ref, far_ref, key_scale_ref, value_scale_ref,
                key_ref, value_ref, ids_ref, route_ref, sems):
    heads, group, x_count, piece_places = plan
    span, width = query_hbm.shape
    half, tok, cols = near_ref.shape
    cols = cols - HEAD_SIZE
    my_ctx, my_exp = ctx_ref[0], exp_ref[0]
    kv_head = my_exp * heads // group
    at = pl.ds(pl.multiple_of(kv_head * HEAD_SIZE, HEAD_SIZE), HEAD_SIZE)
    pairs = [
        (key_scale_hbm, key_scale_ref),
        (value_scale_hbm, value_scale_ref),
        (key_hbm.at[:, at], key_ref),
        (value_hbm.at[:, at], value_ref),
        (ids_hbm, ids_ref),
        (route_hbm, route_ref),
        (query_hbm, packed_ref.at[:, 2 * HEAD_SIZE : 2 * HEAD_SIZE + width]),
    ]
    core = lax.bitwise_and(my_exp, 1)
    for ref, places in zip((near_ref, far_ref), piece_places):
        for number, place in enumerate(places):
            col = pl.multiple_of(lax.bitwise_xor(my_ctx, by_core(core, place, 0)) * cols, cols)
            pairs.append((residual_hbm.at[:, pl.ds(col, cols)], ref.at[number, :, 0:cols]))
    copies = copy_all(sems, pairs)
    for copy in copies[:6]:
        copy.wait()
    lane = lax.broadcasted_iota(jnp.int32, key_scale_ref.shape, 1)
    blocks = key_scale_ref.shape[0]
    for place, (ref, scale_ref) in enumerate(((key_ref, key_scale_ref), (value_ref, value_scale_ref))):
        exponent = scale_ref[...]
        factor = jnp.where(
            exponent < -1, 0.25, jnp.where(exponent < 0, 0.5, jnp.where(exponent < 1, 1.0, 2.0))
        )
        factor = jnp.sum(jnp.where(lane == kv_head, factor, 0.0), axis=1, keepdims=True)
        for block in range(blocks):
            rows = pl.ds(block * (span // blocks), span // blocks)
            scaled = ref[rows, :].astype(jnp.float32) * factor[block : block + 1, :]
            packed_ref[rows, pl.ds(place * HEAD_SIZE, HEAD_SIZE)] = scaled.astype(jnp.bfloat16)
    number = lax.broadcasted_iota(jnp.int32, (128, tok), 0)
    dense = jnp.zeros((128, tok), jnp.float32)
    for k in range(TOP):
        dense = dense + jnp.where(ids_ref[k : k + 1, :] == number, route_ref[k : k + 1, :], 0.0)
    dense = jnp.concatenate([dense, jnp.zeros((128, 128 - tok), jnp.float32)], axis=1)
    dense = jnp.transpose(dense)[:tok, :]
    lane = lax.broadcasted_iota(jnp.int32, (tok, HEAD_SIZE), 1)
    for ref, places in zip((near_ref, far_ref), piece_places):
        for number, place in enumerate(places):
            expert = lax.bitwise_xor(my_ctx, by_core(core, place, 0)) * x_count
            block = jnp.zeros((tok, HEAD_SIZE), jnp.float32)
            for x in range(x_count):
                column = jnp.sum(jnp.where(lane == expert + x, dense, 0.0), axis=1, keepdims=True)
                high = column.astype(jnp.bfloat16).astype(jnp.float32)
                block = jnp.where(lane == x, high, jnp.where(lane == x_count + x, column - high, block))
            ref[number, :, cols:] = block.astype(jnp.bfloat16)
    for copy in copies[6:]:
        copy.wait()


def deq_in_kernel(ctx_count, exp_ref, gate_scale_hbm, up_scale_hbm, gate_hbm, up_hbm, _, own_ref, give_ref,
                  gate_ref, up_ref, gate_scale_ref, up_scale_ref, sems):
    core = lax.bitwise_and(exp_ref[0], 1)
    width, cols = gate_ref.shape
    rows = width // (2 * ctx_count)
    pairs = [(gate_scale_hbm, gate_scale_ref), (up_scale_hbm, up_scale_ref)]
    for step in range(ctx_count):
        at = pl.ds(step * 2 * rows, 2 * rows)
        pairs += [(gate_hbm.at[0, at], gate_ref.at[at]), (up_hbm.at[0, at], up_ref.at[at])]
    copies = copy_all(sems, pairs)
    for copy in copies[:2]:
        copy.wait()
    for step in range(ctx_count):
        for half, (ref, scale_ref) in enumerate(((gate_ref, gate_scale_ref), (up_ref, up_scale_ref))):
            copies[2 + 2 * step + half].wait()
            for out_ref, side in ((give_ref, 1 - core), (own_ref, core)):
                first = (2 * step + side) * (rows // WB)
                for i in range(rows // WB):
                    row = pl.multiple_of((2 * step + side) * rows + i * WB, WB)
                    for j in range(cols // WB):
                        factor = block_factor(scale_ref[j, 0, first + i], WB)
                        out_ref[pl.ds(step * rows + i * WB, WB), pl.ds(half * cols + j * WB, WB)] = (
                            ref[pl.ds(row, WB), pl.ds(j * WB, WB)] * factor
                        )


def deq_in(my_exp, gate_weight, gate_scale, up_weight, up_scale, ctx_count, after):
    width, hidden = gate_weight.shape[1:]
    shape = jax.ShapeDtypeStruct((width // 2, 2 * hidden), jnp.bfloat16)
    gate_scale = jnp.transpose(gate_scale, (2, 0, 1))
    up_scale = jnp.transpose(up_scale, (2, 0, 1))
    return pl.pallas_call(
        functools.partial(deq_in_kernel, ctx_count),
        in_specs=[pl.BlockSpec(memory_space=pltpu.SMEM)]
        + [pl.BlockSpec(memory_space=pltpu.HBM)] * 4
        + [pl.BlockSpec(memory_space=pl.ANY)],
        out_specs=[pl.BlockSpec(memory_space=pltpu.VMEM)] * 2,
        out_shape=[shape, shape],
        scratch_shapes=[
            pltpu.VMEM((width, hidden), jnp.bfloat16),
            pltpu.VMEM((width, hidden), jnp.bfloat16),
            pltpu.SMEM(gate_scale.shape, jnp.int32),
            pltpu.SMEM(up_scale.shape, jnp.int32),
            pltpu.SemaphoreType.DMA((2 + 2 * ctx_count,)),
        ],
        compiler_params=pltpu.CompilerParams(vmem_limit_bytes=20 * MIB),
        cost_estimate=pl.CostEstimate(
            flops=2 * width * hidden, bytes_accessed=8 * width * hidden, transcendentals=0
        ),
        name="dequant_in",
    )(my_exp, *in_hbm(gate_scale, up_scale, gate_weight, up_weight), after)


def deq_down_kernel(ctx_count, exp_ref, scale_hbm, down_hbm, _, own_ref, give_ref, down_ref, scale_ref, sems):
    core = lax.bitwise_and(exp_ref[0], 1)
    rows, width = down_ref.shape
    cols = width // (2 * ctx_count)
    pairs = [(scale_hbm, scale_ref)]
    for step in range(ctx_count):
        at = pl.ds(step * 2 * cols, 2 * cols)
        pairs.append((down_hbm.at[0, :, at], down_ref.at[:, at]))
    copies = copy_all(sems, pairs)
    copies[0].wait()
    for step in range(ctx_count):
        copies[1 + step].wait()
        for out_ref, side in ((give_ref, 1 - core), (own_ref, core)):
            first = (2 * step + side) * (cols // WB)
            for j in range(cols // WB):
                col = pl.multiple_of((2 * step + side) * cols + j * WB, WB)
                for i in range(rows // WB):
                    factor = block_factor(scale_ref[i, 0, first + j], WB)
                    out_ref[pl.ds(i * WB, WB), pl.ds(step * cols + j * WB, WB)] = (
                        down_ref[pl.ds(i * WB, WB), pl.ds(col, WB)] * factor
                    )


def deq_down(my_exp, down_weight, down_scale, ctx_count, after):
    hidden, width = down_weight.shape[1:]
    shape = jax.ShapeDtypeStruct((hidden, width // 2), jnp.bfloat16)
    down_scale = jnp.transpose(down_scale, (1, 0, 2))
    return pl.pallas_call(
        functools.partial(deq_down_kernel, ctx_count),
        in_specs=[pl.BlockSpec(memory_space=pltpu.SMEM)]
        + [pl.BlockSpec(memory_space=pltpu.HBM)] * 2
        + [pl.BlockSpec(memory_space=pl.ANY)],
        out_specs=[pl.BlockSpec(memory_space=pltpu.VMEM)] * 2,
        out_shape=[shape, shape],
        scratch_shapes=[
            pltpu.VMEM((hidden, width), jnp.bfloat16),
            pltpu.SMEM(down_scale.shape, jnp.int32),
            pltpu.SemaphoreType.DMA((1 + ctx_count,)),
        ],
        compiler_params=pltpu.CompilerParams(vmem_limit_bytes=12 * MIB),
        cost_estimate=pl.CostEstimate(
            flops=width * hidden, bytes_accessed=4 * width * hidden, transcendentals=0
        ),
        name="dequant_down",
    )(my_exp, *in_hbm(down_scale, down_weight), after)


def attend_kernel(plan, ctx_ref, exp_ref, order_ref, *refs):
    ctx_count, exp_count, tok, heads, attend_at, slots, kv_apart, more, final = plan
    packed_at, places_of = [at for at, _ in attend_at], [place for _, place in attend_at]
    array_count = 1 + max(at[0] for at in packed_at if at)
    span = exp_count * tok
    packed_refs, refs = refs[:array_count], refs[array_count:]
    packed = [packed_refs[at[0]].at[pl.ds(at[1], span)] if at else None for at in packed_at]
    kv_refs = list(packed)
    if kv_apart:
        kv_refs[packed_at.index(None)], refs = refs[0], refs[1:]
    if more:
        more_ref, refs = refs[0], refs[1:]
    x_count = exp_count // 2
    if final:
        weight_ref, rest = refs[0], refs[2:]
        keep_refs, give_ref = rest[:x_count], rest[x_count]
    key_scr, value_scr, place_scr, att_ref = refs[-4:] if final else (*refs[1:], refs[0])
    if more:
        att_ref[...] = more_ref[...]
    positions = ctx_count * span
    my_ctx, my_exp = ctx_ref[0], exp_ref[0]
    my_x, my_core = lax.shift_right_logical(my_exp, 1), lax.bitwise_and(my_exp, 1)
    lane = lax.broadcasted_iota(jnp.int32, (8, positions), 1)
    places = lane % span
    for offset, ref in enumerate(kv_refs):
        key_scr[pl.ds(offset * span, span), :] = ref[:, 0:HEAD_SIZE]
        value_scr[pl.ds(offset * span, span), 0:HEAD_SIZE] = ref[:, HEAD_SIZE : 2 * HEAD_SIZE]
        base = order_ref[lax.bitwise_xor(my_ctx, by_core(my_core, places_of[offset], 0))] * span
        places = places + jnp.where(lane // span == offset, base, 0)
    place_scr[...] = places
    scale = math.log2(math.e) / math.sqrt(HEAD_SIZE)
    value_scr[:, HEAD_SIZE:] = jnp.ones((positions, HEAD_SIZE), jnp.bfloat16)
    for offset in slots:
        ref = packed[offset]
        source = lax.bitwise_xor(my_ctx, by_core(my_core, places_of[offset], 0))
        queries = jnp.concatenate(
            [ref[:, (h + 2) * HEAD_SIZE : (h + 3) * HEAD_SIZE] for h in range(heads)], axis=0
        )
        scores = lax.dot_general(
            queries, key_scr[...], (((1,), (1,)), ((), ())), preferred_element_type=jnp.float32
        )
        own_place = order_ref[source] * span + lax.broadcasted_iota(jnp.int32, (span, positions), 0)
        bias = jnp.where(place_scr[0:1, :] <= own_place, 0.0, -1e30)
        scores = scores.reshape(heads, span, positions) * scale + bias[None]
        exps = jnp.exp2(scores - jnp.max(scores, axis=-1, keepdims=True))
        mixed = jnp.dot(
            exps.astype(jnp.bfloat16).reshape(heads * span, positions),
            value_scr[...],
            preferred_element_type=jnp.float32,
        )
        mixed = mixed[:, :HEAD_SIZE] * (1.0 / mixed[:, HEAD_SIZE : HEAD_SIZE + 1])
        mixed = mixed.astype(jnp.bfloat16).reshape(heads, span, HEAD_SIZE)
        for owner in range(exp_count):
            x_off = lax.bitwise_xor(my_x, owner // 2)
            row = pl.multiple_of(((x_off * ctx_count + source) * 2 + owner % 2) * tok, tok)
            for head in range(heads):
                att_ref[pl.ds(row, tok), pl.ds(head * HEAD_SIZE, HEAD_SIZE)] = mixed[
                    head, owner * tok : (owner + 1) * tok, :
                ]

    if not final:
        return
    cols = weight_ref.shape[1] // 2
    per_x = 2 * ctx_count * tok
    for which in (1, 0):
        side = lax.bitwise_xor(my_core, which)
        weight = weight_ref[:, pl.ds(pl.multiple_of(side * cols, cols), cols)]
        part = jnp.dot(att_ref[...], weight, preferred_element_type=jnp.float32)
        if which:
            give_ref[...] = part.astype(give_ref.dtype)
        else:
            for x_off, keep_ref in enumerate(keep_refs):
                keep_ref[...] = part[x_off * per_x : (x_off + 1) * per_x]


def finish_kernel(plan, ctx_ref, exp_ref, keep_in, give_in, *refs):
    ctx_count, x_count, tok, piece_places, places_of = plan
    piece_refs, (keep_ref, give_ref, own_route_ref) = refs[:-3], refs[-3:]
    my_ctx, my_exp = ctx_ref[0], exp_ref[0]
    my_x, my_core = lax.shift_right_logical(my_exp, 1), lax.bitwise_and(my_exp, 1)
    cols = keep_ref.shape[1]
    route_base = give_in.shape[0]
    keep_ref[...] = keep_in[...]
    give_ref[0:route_base, :] = give_in[...]
    blocks = [jnp.zeros((tok, HEAD_SIZE), jnp.float32)] * x_count
    lane = lax.broadcasted_iota(jnp.int32, (tok, HEAD_SIZE), 1)
    for (array, place), place_of in zip(piece_places, places_of):
        source = lax.bitwise_xor(my_ctx, by_core(my_core, place_of, 0))
        at = pl.ds(pl.multiple_of((source * 2 + my_core) * tok, tok), tok)
        for which, ref in enumerate((keep_ref, give_ref)):
            side = lax.bitwise_xor(my_core, which)
            piece = piece_refs[array][place, :, pl.ds(pl.multiple_of(side * cols, cols), cols)]
            value = ref[at, :].astype(jnp.float32) + piece.astype(jnp.float32)
            ref[at, :] = value.astype(ref.dtype)
        block = piece_refs[array][place, :, 2 * cols :].astype(jnp.float32)
        for x_off in range(x_count):
            for part in range(2):
                wanted = lax.bitwise_xor(my_x, x_off) + part * x_count
                column = jnp.sum(jnp.where(lane == wanted, block, 0.0), axis=1, keepdims=True)
                blocks[x_off] = jnp.where(lane == source + part * ctx_count, column, blocks[x_off])
    for x_off, block in enumerate(blocks):
        for ref, base in ((give_ref, route_base), (own_route_ref, 0)):
            at = pl.ds(base + x_off * tok, tok)
            ref[at, 0:HEAD_SIZE] = block.astype(jnp.bfloat16)
            if cols > HEAD_SIZE:
                ref[at, HEAD_SIZE:] = jnp.zeros((tok, cols - HEAD_SIZE), jnp.bfloat16)


def fill_rows(plan, ctx_ref, exp_ref, gain_ref, chunk_refs, places, rows_scr, square_ref, groups):
    ctx_count, x_count, tok, bit = plan
    my_ctx = ctx_ref[0]
    my_core = lax.bitwise_and(exp_ref[0], 1)
    mine = side_of(my_ctx, bit)
    cols = chunk_refs[0].shape[1]
    rows = ctx_count * tok
    for (array, first_row), place_of in places:
        ref = chunk_refs[array]
        source = lax.bitwise_xor(my_ctx, by_core(my_core, place_of, 0))
        x_off = by_core(my_core, place_of, 1)
        gain_at = pl.multiple_of((source * 2 + my_core) * cols, cols)
        gain = gain_ref[:, pl.ds(gain_at, cols)]
        col = pl.multiple_of(without(source, bit) * cols, cols)
        for place, group in enumerate(groups):
            for start, low, length in runs(ctx_count, bit, mine if group == 1 else 1 - mine, 2 * tok):
                chunk = ref[pl.ds(first_row + start, length), :].astype(jnp.float32)
                row = (place * x_count + x_off) * rows + low
                at = pl.ds(pl.multiple_of(row, 2 * tok), length)
                rows_scr[at, pl.ds(col, cols)] = (chunk * gain).astype(jnp.bfloat16)
                square_ref[at, :] = square_ref[at, :] + jnp.sum(chunk * chunk, axis=-1, keepdims=True)


def product(plan, side, rows_scr, weight_ref, cols):
    ctx_count, _, _, bit = plan
    total = None
    for start, low, length in runs(ctx_count, bit, side, cols):
        part = jnp.dot(
            rows_scr[:, low : low + length],
            weight_ref[pl.ds(start, length), :],
            preferred_element_type=jnp.float32,
        )
        total = part if total is None else total + part
    return total


def experts_in_first(plan, offsets, ctx_ref, exp_ref, *refs):
    chunk_refs, (gain_ref, own_ref, other_ref, _, act_ref, square_ref, rows_scr) = refs[:-7], refs[-7:]
    square_ref[...] = jnp.zeros(square_ref.shape, jnp.float32)
    fill_rows(plan, ctx_ref, exp_ref, gain_ref, chunk_refs, offsets, rows_scr, square_ref, (0, 1))
    width, side = own_ref.shape[1], side_of(ctx_ref[0], plan[3])
    for place, ref in enumerate((own_ref, other_ref)):
        act_ref[:, place * width : (place + 1) * width] = product(
            plan, side, rows_scr, ref, chunk_refs[0].shape[1]
        )


def experts_in_second(plan, offsets, group, ctx_ref, exp_ref, *refs):
    chunk_refs, rest = refs[:-9], refs[-9:]
    gain_ref, own_ref, other_ref, first_ref, square_ref, _, act_ref, rows_scr, sum_scr = rest
    count, width = rows_scr.shape[0], own_ref.shape[1]
    sum_scr[...] = square_ref[group * count : (group + 1) * count, :]
    fill_rows(plan, ctx_ref, exp_ref, gain_ref, chunk_refs, offsets, rows_scr, sum_scr, (group,))
    lane = lax.broadcasted_iota(jnp.int32, (1, HEAD_SIZE), 1)
    square = sum_scr[...]
    high = square.astype(jnp.bfloat16).astype(jnp.float32)
    act_ref[:, 2 * width :] = jnp.where(lane == 0, high, square - high).astype(jnp.bfloat16)
    side = 1 - side_of(ctx_ref[0], plan[3])
    for place, ref in enumerate((own_ref, other_ref)):
        cols = slice(place * width, (place + 1) * width)
        act = first_ref[group * count : (group + 1) * count, cols] + product(
            plan, side, rows_scr, ref, chunk_refs[0].shape[1]
        )
        act_ref[:, cols] = act.astype(jnp.bfloat16)


def experts_out_kernel(plan, group, places, state_at, route_at, model_width, ctx_ref, exp_ref, act_ref, came_ref, *refs):
    ctx_count, exp_count, tok, bit = plan
    x_count, half = exp_count // 2, ctx_count // 2
    route_refs, refs = refs[: x_count + 1], refs[x_count + 1 :]
    (own_ref, other_ref, _), rest = refs[:3], refs[3:]
    state_count = 1 + max((array for pair in state_at for array, _ in pair), default=-1)
    state_refs, rest = rest[:state_count], rest[state_count:]
    out_refs, hidden_scr = rest[:-1], rest[-1]
    my_ctx = ctx_ref[0]
    my_core = lax.bitwise_and(exp_ref[0], 1)
    mine = side_of(my_ctx, bit)
    side = mine if group == 1 else 1 - mine
    width = (act_ref.shape[1] - HEAD_SIZE) // 2
    hidden = width // 2
    lane = lax.broadcasted_iota(jnp.int32, (tok, HEAD_SIZE), 1)
    blocks = []
    for array, row in route_at:
        blocks.append(route_refs[array][row : row + tok, 0:HEAD_SIZE].astype(jnp.float32))
    columns = []
    for x_off in range(x_count):
        for low in range(half):
            for core in range(2):
                same, swapped = blocks[2 * x_off + core], blocks[2 * x_off + 1 - core]
                block = jnp.where(my_core == 0, same, swapped)
                number = (low >> bit << bit + 1) + (low & ((1 << bit) - 1)) + side * (1 << bit)
                picked = jnp.where(lane % ctx_count == number, block, 0.0)
                columns.append(jnp.sum(picked, axis=1, keepdims=True))
    route = jnp.concatenate(columns, axis=0)
    squares = act_ref[:, 2 * width :].astype(jnp.float32) + came_ref[:, 2 * width :].astype(jnp.float32)
    norm = lax.rsqrt((squares[:, 0:1] + squares[:, 1:2]) / model_width + 1e-06)
    scaled_route = norm * route
    for part in range(2):
        acts = act_ref[:, part * width : (part + 1) * width].astype(jnp.float32) + came_ref[
            :, (1 - part) * width : (2 - part) * width
        ].astype(jnp.float32)
        gate = acts[:, :hidden] * norm
        value = gate / (1.0 + jnp.exp(-gate)) * (acts[:, hidden:] * scaled_route)
        hidden_scr[:, part * hidden : (part + 1) * hidden] = value.astype(jnp.bfloat16)
    picked = []
    for place in places:
        x_off = by_core(my_core, place, 1)
        low = without(lax.bitwise_xor(my_ctx, by_core(my_core, place, 0)), bit)
        row = pl.multiple_of((x_off * half + low) * (2 * tok), 2 * tok)
        picked.append(hidden_scr[pl.ds(row, 2 * tok), :])
    picked = jnp.concatenate(picked, axis=0)
    out_cols = own_ref.shape[1]
    step = min(512, out_cols)
    for col in range(0, out_cols, step):
        at = pl.ds(col, step)
        out = jnp.dot(picked[:, :hidden], own_ref[:, at], preferred_element_type=jnp.float32)
        out = out + jnp.dot(picked[:, hidden:], other_ref[:, at], preferred_element_type=jnp.float32)
        for place, ref in enumerate(out_refs):
            ref[:, at] = out[place * 2 * tok : (place + 1) * 2 * tok, :].astype(ref.dtype)
    for place, ref in zip(places, out_refs):
        if place[0] == (0, 0):
            for c_off, pair in enumerate(state_at):
                states = []
                for array, first_row in pair:
                    own_row = pl.multiple_of(first_row + my_ctx * (2 * tok), 2 * tok)
                    states.append(state_refs[array][pl.ds(own_row, 2 * tok), :].astype(jnp.float32))
                state = states[0] if pair[0] == pair[1] else jnp.where(my_core == 0, *states)
                cols = state.shape[1]
                at = pl.ds(pl.multiple_of(lax.bitwise_xor(my_ctx, c_off) * cols, cols), cols)
                ref[:, at] = ref[:, at] + state


def join_kernel(ctx_count, exp_ref, mine_ref, came_ref, out_ref):
    core = lax.bitwise_and(exp_ref[0], 1)
    cols = mine_ref.shape[1] // ctx_count
    for c in range(ctx_count):
        for which, ref in enumerate((mine_ref, came_ref)):
            at = pl.multiple_of((2 * c + lax.bitwise_xor(core, which)) * cols, cols)
            out_ref[:, pl.ds(at, cols)] = ref[:, c * cols : (c + 1) * cols]


def shards(
    residual,
    encoded_query_rows,
    quantized_key_rows,
    quantized_value_rows,
    key_block_exponent,
    value_block_exponent,
    block_order,
    out_weight,
    norm_gain,
    expert_ids,
    route_weight,
    gate_weight,
    gate_scale,
    up_weight,
    up_scale,
    down_weight,
    down_scale,
):
    f32, bf16 = jnp.float32, jnp.bfloat16
    vmem = pl.BlockSpec(memory_space=pltpu.VMEM)
    smem = pl.BlockSpec(memory_space=pltpu.SMEM)
    anywhere = pl.BlockSpec(memory_space=pl.ANY)
    span, query_width = encoded_query_rows.shape
    heads = query_width // HEAD_SIZE
    group = QUERY_HEADS // KEY_VALUE_HEADS
    ctx_count = lax.axis_size("ctx")
    exp_count = lax.axis_size("exp")
    x_count = exp_count // 2
    experts = ctx_count * x_count
    tok, model_width = residual.shape
    half_width = model_width // 2
    cols = half_width // ctx_count
    my_ctx = lax.axis_index("ctx").astype(jnp.int32).reshape(1)
    my_exp = lax.axis_index("exp").astype(jnp.int32).reshape(1)
    route, places = gather_route(ctx_count, x_count)

    hbm = pl.BlockSpec(memory_space=pltpu.HBM)
    piece_shape = jax.ShapeDtypeStruct((ctx_count // 2, tok, 2 * cols + HEAD_SIZE), bf16)
    row_route, row_places = gather_route(ctx_count, x_count, rows_only=True)
    names = sorted(row_places)
    piece_names = [[key for key in names if bool(key[0] & 2) == sent] for sent in (False, True)]
    piece_places = tuple(tuple(row_places[key] for key in keys) for keys in piece_names)
    packed, near, far = pl.pallas_call(
        functools.partial(pack_kernel, (heads, group, x_count, piece_places)),
        in_specs=[smem] * 2 + [hbm] * 8,
        out_specs=[vmem] * 3,
        out_shape=[
            jax.ShapeDtypeStruct((span, query_width + 2 * HEAD_SIZE), bf16),
            piece_shape,
            piece_shape,
        ],
        scratch_shapes=[
            pltpu.VMEM(key_block_exponent.shape, jnp.int32),
            pltpu.VMEM(key_block_exponent.shape, jnp.int32),
            pltpu.VMEM((span, HEAD_SIZE), bf16),
            pltpu.VMEM((span, HEAD_SIZE), bf16),
            pltpu.VMEM((TOP, tok), jnp.int32),
            pltpu.VMEM((TOP, tok), f32),
            pltpu.SemaphoreType.DMA((7 + ctx_count,)),
        ],
        compiler_params=pltpu.CompilerParams(vmem_limit_bytes=8 * MIB),
        name="pack",
    )(
        my_ctx,
        my_exp,
        *in_hbm(
            key_block_exponent,
            value_block_exponent,
            encoded_query_rows,
            quantized_key_rows,
            quantized_value_rows,
            jnp.transpose(expert_ids),
            jnp.transpose(route_weight),
            residual,
        ),
    )
    piece_arrays = [near]
    piece_at = {(0, key[0]): (0, place) for place, key in enumerate(piece_names[0])}
    piece_bits = [1, 0, *range(bits_of(ctx_count) - 1, 1, -1)]
    sending, weights = far, {}
    early, last_kv = ctx_count == 8, []

    def beside(number, came, arrays, at):
        nonlocal sending
        bit = 1 << piece_bits[number]
        moves = {1: ((2, 0), (1, 0)), 0: ((1, 0), (2, 0))}.get(piece_bits[number], ((bit, 0),) * 2)
        if number == 0:
            keys = [(0, key[0]) for key in piece_names[1]]
        else:
            keys = sorted(key for key in piece_at if key[1] & bit)
            sending = jnp.stack([piece_arrays[array][place] for array, place in map(piece_at.pop, keys)])
        pieces = follow(sending, moves)
        if number == 0:
            own, give = deq_in(my_exp, gate_weight, gate_scale, up_weight, up_scale, ctx_count, packed)
            *came, pieces, weights["in_own"], weights["in_give"] = together(*came, pieces, own, give)
        elif number == 1:
            other = from_offset(weights["in_give"], 1)
            own, give = deq_down(my_exp, down_weight, down_scale, ctx_count, piece_arrays[-1])
            if early:
                array, row = at[4, 0]
                last_kv.append(follow(arrays[array][row : row + span, : 2 * HEAD_SIZE], ((3, 0),) * 2))
            held = together(*came, pieces, other, own, give, *last_kv)
            *came, pieces, other, own, give = held[: len(held) - len(last_kv)]
            last_kv[:] = held[len(held) - len(last_kv) :]
            weights.update(in_other=other, down_own=own, down_give=give)
        elif number < len(piece_bits) - 1:
            *came, pieces = together(*came, pieces)
        for place, (source, target) in enumerate(keys):
            piece_at[source ^ bit, target ^ bit] = (len(piece_arrays), place)
        piece_arrays.append(pieces)
        return came

    packed, packed_at = spread(packed, stages_of(row_route), beside)
    attend_at = tuple((packed_at[key], row_places[key]) for key in names)
    attend_pieces = tuple(piece_at[key[0], 0] for key in names)
    in_own, in_other, down_own = weights["in_own"], weights["in_other"], weights["down_own"]
    down_other = from_offset(weights["down_give"], 1)

    positions = ctx_count * span
    per_x = 2 * ctx_count * tok
    def attend(arrays, at, slots, kv, more, final):
        scratch = [
            pltpu.VMEM((positions, HEAD_SIZE), bf16),
            pltpu.VMEM((positions, 2 * HEAD_SIZE), bf16),
            pltpu.VMEM((8, positions), jnp.int32),
        ]
        rows_shape = (positions, query_width)
        out_shape = [jax.ShapeDtypeStruct(rows_shape, bf16)]
        if final:
            out_shape = [jax.ShapeDtypeStruct((per_x, cols), f32)] * x_count
            out_shape += [jax.ShapeDtypeStruct((x_count * per_x, cols), bf16)]
            scratch.append(pltpu.VMEM(rows_shape, bf16))
        operands = [*arrays, *kv, *more, *([out_weight] if final else [])]
        return pl.pallas_call(
            functools.partial(
                attend_kernel,
                (ctx_count, exp_count, tok, heads, at, slots, bool(kv), bool(more), final),
            ),
            in_specs=[smem] * 3 + [vmem] * len(operands) + [anywhere] * final,
            out_specs=[vmem] * len(out_shape),
            out_shape=out_shape,
            scratch_shapes=scratch,
            compiler_params=pltpu.CompilerParams(vmem_limit_bytes=3 * ctx_count * MIB),
            cost_estimate=pl.CostEstimate(
                flops=4 * positions * len(slots) * span * query_width
                + 4 * positions * query_width * cols * final,
                bytes_accessed=4 * MIB,
                transcendentals=heads * positions * len(slots) * span,
            ),
            name="attend",
        )(my_ctx, my_exp, block_order, *operands, *([down_other] if final else []))

    more, slots = [], tuple(range(ctx_count))
    if early:
        late = max(packed_at[key][0] for key in names)
        early_at = tuple((None if at[0] == late else at, place) for at, place in attend_at)
        slots = tuple(i for i, (at, _) in enumerate(early_at) if at is None)
        rest = tuple(i for i, (at, _) in enumerate(early_at) if at is not None)
        more = attend(packed[:late], early_at, rest, last_kv, [], False)
    *keeps, give = attend(packed, attend_at, slots, [], more, True)
    keeps[0], give, own_route = pl.pallas_call(
        functools.partial(
            finish_kernel,
            (ctx_count, x_count, tok, attend_pieces, tuple(place for _, place in attend_at)),
        ),
        in_specs=[smem] * 2 + [vmem] * (2 + len(piece_arrays)),
        out_specs=[vmem] * 3,
        out_shape=[
            jax.ShapeDtypeStruct((per_x, cols), f32),
            jax.ShapeDtypeStruct((x_count * (per_x + tok), cols), bf16),
            jax.ShapeDtypeStruct((x_count * tok, cols), bf16),
        ],
        compiler_params=pltpu.CompilerParams(vmem_limit_bytes=8 * MIB),
        name="finish",
    )(my_ctx, my_exp, keeps[0], give, *piece_arrays)

    given = from_offset(give, 1)
    routes, route_at, state = [own_route, given], [(0, 0), (1, x_count * per_x)], keeps[0]
    state = state + given[:per_x].astype(f32)
    for x_off in range(1, x_count):
        part = keeps[x_off] + given[x_off * per_x : (x_off + 1) * per_x].astype(f32)
        row = x_count * per_x + x_off * tok
        own = own_route[x_off * tok : (x_off + 1) * tok]
        sent = jnp.concatenate([part.astype(bf16), own, given[row : row + tok]], axis=0)
        came = from_offset(sent, 2 * x_off)
        state = state + came[:per_x].astype(f32)
        route_at += [(len(routes), per_x), (len(routes), per_x + tok)]
        routes.append(came)
    state = state.astype(bf16)

    stages = stages_of(route)
    chunks, chunk_at = spread(state, stages)
    gain = norm_gain.reshape(1, model_width)
    rows = x_count * per_x
    in_width = in_own.shape[1]
    bit = 1 if (ctx_count, x_count) == (8, 2) else bits_of(ctx_count) - 1
    near = tuple(sorted(key for key in places if not side_of(key[0], bit)))
    far = tuple(sorted(key for key in places if side_of(key[0], bit)))

    def picked(keys):
        arrays = sorted({chunk_at[key][0] for key in keys})
        at = tuple(((arrays.index(chunk_at[key][0]), chunk_at[key][1]), places[key]) for key in keys)
        return [chunks[array] for array in arrays], at

    near_chunks, near_places = picked(near)
    far_chunks, far_places = picked(far)
    first_act, first_square = pl.pallas_call(
        functools.partial(experts_in_first, (ctx_count, x_count, tok, bit), near_places),
        in_specs=[smem] * 2 + [vmem] * (len(near_chunks) + 3) + [anywhere],
        out_specs=[vmem] * 2,
        out_shape=[
            jax.ShapeDtypeStruct((rows, 2 * in_width), f32),
            jax.ShapeDtypeStruct((rows, 1), f32),
        ],
        scratch_shapes=[pltpu.VMEM((rows, half_width // 2), bf16)],
        compiler_params=pltpu.CompilerParams(vmem_limit_bytes=2 * ctx_count * MIB),
        cost_estimate=pl.CostEstimate(
            flops=2 * rows * half_width * in_width, bytes_accessed=8 * MIB, transcendentals=0
        ),
        name="experts_in_first",
    )(my_ctx, my_exp, *near_chunks, gain, in_own, in_other, down_other)
    acts = []
    for part in range(2):
        acts.append(
            pl.pallas_call(
                functools.partial(experts_in_second, (ctx_count, x_count, tok, bit), far_places, part),
                in_specs=[smem] * 2 + [vmem] * (len(far_chunks) + 5) + [anywhere],
                out_specs=vmem,
                out_shape=jax.ShapeDtypeStruct((rows // 2, 2 * in_width + HEAD_SIZE), bf16),
                scratch_shapes=[
                    pltpu.VMEM((rows // 2, half_width // 2), bf16),
                    pltpu.VMEM((rows // 2, 1), f32),
                ],
                compiler_params=pltpu.CompilerParams(vmem_limit_bytes=2 * ctx_count * MIB),
                cost_estimate=pl.CostEstimate(
                    flops=rows * half_width * in_width, bytes_accessed=8 * MIB, transcendentals=0
                ),
                name="experts_in_second",
            )(
                my_ctx,
                my_exp,
                *far_chunks,
                gain,
                in_own,
                in_other,
                first_act,
                first_square,
                acts[0] if part else first_square,
            )
        )
    leaves = set(places) - {source for _, source, _, _ in route}
    sums = {}
    for part in range(2):
        slots = near if part == 1 else far
        state_keys = [
            next(key for key in places if places[key][core] == (offset, 0))
            for offset in (range(ctx_count) if part == 1 else ())
            for core in range(2)
        ]
        states, state_at = picked(state_keys)
        state_at = tuple((state_at[i][0], state_at[i + 1][0]) for i in range(0, len(state_at), 2))
        outs = pl.pallas_call(
            functools.partial(
                experts_out_kernel,
                (ctx_count, exp_count, tok, bit),
                part,
                tuple(places[key] for key in slots),
                state_at,
                tuple(route_at),
                model_width,
            ),
            in_specs=[smem] * 2 + [vmem] * (5 + x_count) + [anywhere] + [vmem] * len(states),
            out_specs=[vmem] * len(slots),
            out_shape=[
                jax.ShapeDtypeStruct((2 * tok, half_width), bf16 if slot in leaves else f32)
                for slot in slots
            ],
            scratch_shapes=[pltpu.VMEM((rows // 2, in_width), bf16)],
            compiler_params=pltpu.CompilerParams(vmem_limit_bytes=2 * ctx_count * MIB),
            cost_estimate=pl.CostEstimate(
                flops=rows * half_width * in_width,
                bytes_accessed=8 * MIB,
                transcendentals=rows * in_width // 2,
            ),
            name="experts_out",
        )(
            my_ctx,
            my_exp,
            acts[part],
            from_offset(acts[part], 1),
            *routes,
            down_own,
            down_other,
            sums[slots_done[0]] if part else acts[1],
            *states,
        )
        slots_done = slots
        sums.update(zip(slots, outs))

    for number, sends in enumerate(reversed(stages)):
        came = []
        for moves, _, targets in sends:
            sent = [sums[key].astype(bf16) for key in targets]
            came.append(follow(sent[0] if len(sent) == 1 else jnp.concatenate(sent, axis=0), moves))
        if number < len(stages) - 1:
            waiting = list(near) if number == 0 else []
            values = together(*came, *[sums[key] for key in waiting])
            came = values[: len(came)]
            sums.update(zip(waiting, values[len(came) :]))
        for (_, sources, _), array in zip(sends, came):
            for place, key in enumerate(sources):
                part = array[place * 2 * tok : (place + 1) * 2 * tok]
                sums[key] = sums[key] + part.astype(f32)
    total = sums[0, 0]
    core = lax.bitwise_and(my_exp[0], 1)
    mine = jnp.where(core == 0, total[:tok], total[tok:]).astype(bf16)
    came = from_offset(jnp.where(core == 0, total[tok:], total[:tok]).astype(bf16), 1)
    return pl.pallas_call(
        functools.partial(join_kernel, ctx_count),
        in_specs=[smem, vmem, vmem],
        out_specs=vmem,
        out_shape=jax.ShapeDtypeStruct((tok, model_width), bf16),
        name="join",
    )(my_exp, mine, came)


def solution(mesh):
    return jax.shard_map(
        shards,
        mesh=mesh,
        in_specs=(
            P(("dp", "ctx", "exp"), None),
            P(("dp", "ctx"), "exp"),
            P(("dp", "ctx"), None),
            P(("dp", "ctx"), None),
            P(("dp", "ctx"), None),
            P(("dp", "ctx"), None),
            P(),
            P("exp", "ctx"),
            P(),
            P(("dp", "ctx", "exp"), None),
            P(("dp", "ctx", "exp"), None),
            P(("ctx", "exp"), None, None),
            P(("ctx", "exp"), None, None),
            P(("ctx", "exp"), None, None),
            P(("ctx", "exp"), None, None),
            P(("ctx", "exp"), None, None),
            P(("ctx", "exp"), None, None),
        ),
        out_specs=P(("dp", "ctx", "exp"), None),
        check_vma=False,
    )
```
